128 devices in a mesh: seq: 4 (over x_lo, core), blk: 32 (over y, z, x_hi).
Axes of the slice: x: 4 (x_hi: 2, x_lo: 2; x = x_hi * 2 + x_lo), y: 4, z: 4, core: 2. Of those that a mesh axis runs over, the one named last changes fastest.
Arguments:
- tokens: bfloat16 [8, 2048, 768], P('seq', 'blk'), may hold values from -6 to 6
- cotangent: bfloat16 [8, 2048, 768], P('seq', 'blk'), may hold values from -6 to 6
- group_of_seq: int32 [8], P('seq'), may hold values from 0 to 3
- group_weight: float32 [4], replicated, may hold values from 0.25 to 4
- norm_attn: float32 [768], replicated, may hold values from 0.5 to 1.5
- w_query: bfloat16 [768, 768], replicated, may hold values from -0.21875 to 0.21875
- w_qrope: bfloat16 [768, 768], replicated, may hold values from -0.21875 to 0.21875
- w_latent: bfloat16 [768, 512], replicated, may hold values from -0.21875 to 0.21875
- w_krope: bfloat16 [768, 64], replicated, may hold values from -0.21875 to 0.21875
- w_upkey: bfloat16 [2, 256, 384], replicated, may hold values from -0.375 to 0.375
- w_upval: bfloat16 [2, 256, 384], replicated, may hold values from -0.375 to 0.375
- w_out: bfloat16 [768, 768], replicated, may hold values from -0.875 to 0.875
- norm_mlp: float32 [768], replicated, may hold values from 0.5 to 1.5
- w_gate: bfloat16 [768, 2048], replicated, may hold values from -0.21875 to 0.21875
- w_up: bfloat16 [768, 2048], replicated, may hold values from -0.21875 to 0.21875
- w_down: bfloat16 [2048, 768], replicated, may hold values from -0.125 to 0.125
Outputs:
- layer_out: bfloat16 [8, 2048, 768], P('seq', 'blk')
- grad_tokens: float32 [8, 2048, 768], P('seq', 'blk')
- grad_norm_attn: float32 [768], replicated
- grad_w_query: float32 [768, 768], replicated
- grad_w_qrope: float32 [768, 768], replicated
- grad_w_latent: float32 [768, 512], replicated
- grad_w_krope: float32 [768, 64], replicated
- grad_w_upkey: float32 [2, 256, 384], replicated
- grad_w_upval: float32 [2, 256, 384], replicated
- grad_w_out: float32 [768, 768], replicated
- grad_norm_mlp: float32 [768], replicated
- grad_w_gate: float32 [768, 2048], replicated
- grad_w_up: float32 [768, 2048], replicated
- grad_w_down: float32 [2048, 768], replicated
The draws below stay inside these ranges and needn't reach their ends.
All inputs are finite; a program needn't handle non-finite values.
Results may differ from the reference program's by a relative error of at most 0.023.
Values may be sent and summed in bfloat16 or wider, within the bound.
A program may use at most 192 MiB of HBM per device.

```python
import math
import jax
import jax.numpy as jnp
from jax import lax

D = 768
HEADS = 12
HEAD = 64
LAT_HEADS = 2
LATENT = 256
ROPE = 64
FF = 2048
SEQ_LEN = 2048
GROUPS = 4
SEQS = 8
N_BLK = 32


def set_ends(result, own_key, least, top_value):
    place = [jax.random.randint(jax.random.fold_in(own_key, axis), (), 0, length) for axis, length in enumerate(result.shape)]
    main_axis = result.shape.index(max(result.shape))
    beside = place[:main_axis] + [(place[main_axis] + 1) % result.shape[main_axis]] + place[main_axis + 1:]
    return result.at[tuple(place)].set(least).at[tuple(beside)].set(top_value)


def steps_of(key, extent, shards, low, largest):
    factor_of, own = 1.0, jax.random.fold_in(key, 6)
    for position, parts in shards:
        draws = jnp.exp(jax.random.uniform(jax.random.fold_in(own, position), (parts,), jnp.float32, low / len(shards), largest / len(shards)))
        factor_of = factor_of * jnp.repeat(draws, extent[position] // parts).reshape([-1 if axis == position else 1 for axis in range(len(extent))])
    return factor_of


def gaussian(key, extent, spread, reach, split=(), held_as=jnp.bfloat16):
    factor_of = steps_of(key, extent, split, -0.22, 0.18) if split else 1.0
    result = jax.random.normal(key, extent, jnp.float32) * spread * factor_of
    return jnp.minimum(jnp.maximum(result, -reach), reach).astype(held_as)


def setup_inputs(seed: int = 0) -> dict:
    key_of = jax.random.split(jax.random.key(seed), 17)
    tokens = gaussian(key_of[0], (SEQS, SEQ_LEN, D), 1.0, 6.0, ((0, 4), (1, 32)))
    cotangent = gaussian(key_of[1], (SEQS, SEQ_LEN, D), 1.0, 6.0, ((0, 4), (1, 32)))
    group_of_seq = set_ends(jax.random.randint(key_of[2], (SEQS,), 0, GROUPS), jax.random.fold_in(key_of[2], 1), 0, GROUPS - 1).astype(jnp.int32)
    group_weight = jnp.clip(jnp.exp(jax.random.uniform(key_of[3], (GROUPS,), jnp.float32, math.log(0.25), math.log(4.0))), 0.25, 4.0)
    norm_attn = jnp.clip(1.0 + 0.1 * jax.random.normal(key_of[4], (D,), jnp.float32), 0.5, 1.5)
    w_query = gaussian(key_of[5], (D, HEADS * HEAD), D ** -0.5, 0.21875)
    w_qrope = gaussian(key_of[6], (D, HEADS * ROPE), D ** -0.5, 0.21875)
    w_latent = gaussian(key_of[7], (D, LAT_HEADS * LATENT), D ** -0.5, 0.21875)
    w_krope = gaussian(key_of[8], (D, ROPE), D ** -0.5, 0.21875)
    w_upkey = gaussian(key_of[9], (LAT_HEADS, LATENT, HEADS // LAT_HEADS * HEAD), LATENT ** -0.5, 0.375)
    w_upval = gaussian(key_of[10], (LAT_HEADS, LATENT, HEADS // LAT_HEADS * HEAD), LATENT ** -0.5, 0.375)
    w_out = gaussian(key_of[11], (HEADS * HEAD, D), (HEADS * HEAD // 16) ** -0.5, 0.875)
    norm_mlp = jnp.clip(1.0 + 0.1 * jax.random.normal(key_of[12], (D,), jnp.float32), 0.5, 1.5)
    w_gate = gaussian(key_of[13], (D, FF), D ** -0.5, 0.21875)
    w_up = gaussian(key_of[14], (D, FF), D ** -0.5, 0.21875)
    w_down = gaussian(key_of[15], (FF, D), FF ** -0.5, 0.125)
    return {"tokens": tokens, "cotangent": cotangent, "group_of_seq": group_of_seq, "group_weight": group_weight, "norm_attn": norm_attn, "w_query": w_query, "w_qrope": w_qrope, "w_latent": w_latent, "w_krope": w_krope, "w_upkey": w_upkey, "w_upval": w_upval, "w_out": w_out, "norm_mlp": norm_mlp, "w_gate": w_gate, "w_up": w_up, "w_down": w_down}


@jax.custom_vjp
def low(v):
    return lax.optimization_barrier(v.astype(jnp.bfloat16)).astype(jnp.float32)

@jax.custom_vjp
def low_back(v):
    return v

def low_keep(v):
    return (low(v), None)

def low_pass(kept, grad):
    return (grad,)

def back_keep(v):
    return (v, None)

def back_low(kept, grad):
    return (low(grad),)
low.defvjp(low_keep, low_pass)
low_back.defvjp(back_keep, back_low)
epsilon = 1e-06
rope_base = 10000.0
masked_score = -1e+30

def matmul(left, right):
    return jnp.dot(left, right, precision=lax.Precision.HIGHEST, preferred_element_type=jnp.float32)

def contract(formula, left, right):
    return jnp.einsum(formula, left, right, precision=lax.Precision.HIGHEST, preferred_element_type=jnp.float32)

def rms_norm(values, gain):
    inverse = lax.rsqrt(lax.optimization_barrier(jnp.mean(values * values, axis=-1, keepdims=True)) + epsilon)
    return values * inverse * gain

def angles(positions):
    halves = ROPE // 2
    freq_list = rope_base ** (-(jnp.arange(halves, dtype=jnp.float32) * 2.0 / ROPE))
    phases = positions[:, None] * freq_list[None, :]
    return (jnp.cos(phases), jnp.sin(phases))

def rotate(values, cosine, sine):
    halves = values.shape[-1] // 2
    front = values[..., :halves]
    back_half = values[..., halves:]
    return jnp.concatenate([front * cosine - back_half * sine, front * sine + back_half * cosine], axis=-1)

def forward(params, inputs):
    norm_attn, w_query, w_qrope, w_latent, w_krope, w_upkey, w_upval, w_out, norm_mlp, w_gate, w_up, w_down = params
    length = inputs.shape[0]
    block_len = length // N_BLK
    factor = (HEAD + ROPE) ** (-0.5)
    cosine, sine = angles(jnp.arange(length).astype(jnp.float32))
    normed = low(rms_norm(inputs, norm_attn))
    queries = low_back(low(matmul(normed, w_query))).reshape(length, HEADS, HEAD)
    query_pre = low_back(matmul(normed, w_qrope)).reshape(length, HEADS, ROPE)
    query_rot = low(rotate(query_pre, cosine[:, None, :], sine[:, None, :]))
    latents = low_back(low(matmul(normed, w_latent))).reshape(length, LAT_HEADS, LATENT)
    key_rot = low(rotate(low_back(matmul(normed, w_krope)), cosine, sine))
    keys = low(contract('lgc,gcf->lgf', latents, w_upkey).reshape(length, HEADS, HEAD))
    values = low(contract('lgc,gcf->lgf', latents, w_upval).reshape(length, HEADS, HEAD))
    key_pos = jnp.arange(length).astype(jnp.int32)

    def attend(start):
        query_blk = lax.dynamic_slice_in_dim(queries, start, block_len, 0)
        rot_blk = lax.dynamic_slice_in_dim(query_rot, start, block_len, 0)
        key_blk = low_back(keys)
        value_blk = low_back(values)
        raw = contract('qhe,khe->hqk', query_blk, key_blk) + contract('qhr,kr->hqk', rot_blk, key_rot)
        scores = low_back(raw * factor)
        query_pos = start + jnp.arange(block_len).astype(jnp.int32)
        allowed = key_pos[None, :] <= query_pos[:, None]
        scores = jnp.where(allowed[None, :, :], scores, masked_score)
        highest = lax.optimization_barrier(jnp.max(scores, axis=-1, keepdims=True))
        summed = lax.optimization_barrier(jnp.sum(jnp.exp(scores - highest), axis=-1, keepdims=True))
        weights = jnp.exp(scores - highest - jnp.log(summed))
        mixed_blk = contract('hqk,khe->qhe', low(weights), value_blk)
        return mixed_blk.reshape(block_len, HEADS * HEAD)
    starts = jnp.arange(N_BLK).astype(jnp.int32) * block_len
    mixed = lax.map(jax.checkpoint(attend), starts).reshape(length, HEADS * HEAD)
    attn_out = low_back(low(mixed))
    middle = inputs + low_back(matmul(attn_out, w_out))
    normed_mlp = low(rms_norm(middle, norm_mlp))
    gate_pre = low_back(matmul(normed_mlp, w_gate))
    up_pre = low_back(matmul(normed_mlp, w_up))
    hidden = low(jax.nn.silu(gate_pre) * up_pre)
    return middle + low_back(matmul(hidden, w_down))

def add_pair(left, right):
    return left + right

def reference(tokens, cotangent, group_of_seq, group_weight, norm_attn, w_query, w_qrope, w_latent, w_krope, w_upkey, w_upval, w_out, norm_mlp, w_gate, w_up, w_down):
    params = (norm_attn.astype(jnp.float32), w_query.astype(jnp.float32), w_qrope.astype(jnp.float32), w_latent.astype(jnp.float32), w_krope.astype(jnp.float32), w_upkey.astype(jnp.float32), w_upval.astype(jnp.float32), w_out.astype(jnp.float32), norm_mlp.astype(jnp.float32), w_gate.astype(jnp.float32), w_up.astype(jnp.float32), w_down.astype(jnp.float32))
    seq_weight = group_weight[group_of_seq].astype(jnp.float32)

    def one_sequence(totals, item):
        inputs, grad_in, weight = item
        outputs, pullback = jax.vjp(forward, params, inputs.astype(jnp.float32))
        grads, input_grad = pullback(grad_in.astype(jnp.float32) * weight)
        totals = jax.tree.map(add_pair, totals, grads)
        return (totals, (outputs.astype(jnp.bfloat16), input_grad))
    zeros = jax.tree.map(jnp.zeros_like, params)
    totals, (layer_out, grad_tokens) = lax.scan(one_sequence, zeros, (tokens, cotangent, seq_weight))
    return (layer_out, grad_tokens, totals[0], totals[1], totals[2], totals[3], totals[4], totals[5], totals[6], totals[7], totals[8], totals[9], totals[10], totals[11])
```

```python
import functools
import jax
import jax.numpy as jnp
from jax import lax
from jax.sharding import PartitionSpec as P
from jax.experimental import pallas as pl
from jax.experimental.pallas import tpu as pltpu

MESH = pl.DeviceIdType.MESH
BF = jnp.bfloat16
F32 = jnp.float32


def coords():
    s = lax.axis_index("seq")
    b = lax.axis_index("blk")
    core = lax.rem(s, 2)
    x = lax.rem(b, 2) * 2 + lax.div(s, 2)
    return x, lax.div(b, 8), lax.rem(lax.div(b, 2), 4), core


def device(x, y, z, core):
    return (lax.rem(x, 2) * 2 + core, y * 8 + z * 2 + lax.div(x, 2))


def on_ring(place, axis, step):
    spot = list(place)
    spot[axis] = lax.rem(place[axis] + step, 4)
    return device(*spot)


def greet(place, peers):
    barrier = pltpu.get_barrier_semaphore()
    for peer in peers:
        pl.semaphore_signal(barrier, inc=1, device_id=peer, device_id_type=MESH)
    pl.semaphore_wait(barrier, len(peers))


ORDERS = ((0, 1, 2), (1, 2, 0), (2, 0, 1))


class Reduction:
    def __init__(self, place, total, done, first, second, third, send, recv):
        self.place = place
        self.total, self.done = total, done
        self.first, self.second, self.third = first, second, third
        self.send, self.recv = send, recv
        self.n = total.shape[2]

    def spots(self, o):
        a, b, c = ORDERS[o]
        return self.place[a], self.place[b], self.place[c]

    def copies(self, o, stage):
        i, j, k = self.spots(o)
        made = []
        for step in (1, 2, 3):
            axis = ORDERS[o][(0, 1, 2, 2, 1, 0)[stage]]
            to = lax.rem(self.place[axis] + step, 4)
            if stage == 0:
                src, dst = self.total.at[o, to], self.first.at[o, step - 1]
            elif stage == 1:
                src = self.total.at[o, i, :, pl.ds(pl.multiple_of(to * 64, 64), 64)]
                dst = self.second.at[o, step - 1]
            elif stage == 2:
                src = self.total.at[o, i, :, pl.ds(pl.multiple_of(j * 64 + to * 16, 16), 16)]
                dst = self.third.at[o, step - 1]
            elif stage == 3:
                src = dst = self.done.at[o, i, :, pl.ds(pl.multiple_of(j * 64 + k * 16, 16), 16)]
            elif stage == 4:
                src = dst = self.done.at[o, i, :, pl.ds(pl.multiple_of(j * 64, 64), 64)]
            else:
                src = dst = self.done.at[o, i]
            made.append(
                pltpu.make_async_remote_copy(
                    src_ref=src,
                    dst_ref=dst,
                    send_sem=self.send.at[o, stage, step - 1],
                    recv_sem=self.recv.at[o, stage, step - 1],
                    device_id=on_ring(self.place, axis, step),
                    device_id_type=MESH,
                )
            )
        return made

    def start(self, o, stage):
        for copy in self.copies(o, stage):
            copy.start()

    def finish(self, o, stage):
        for copy in self.copies(o, stage):
            copy.wait()
        if stage > 2:
            return
        i, j, k = self.spots(o)
        rows = (64, 64, 16)[stage]
        base = (0, j * 64, j * 64 + k * 16)[stage]
        arrived = (self.first, self.second, self.third)[stage]

        def add(step, _):
            m = lax.div(step, 4) if stage == 0 else step
            r = lax.rem(step, 4) * 64 if stage == 0 else 0
            here = pl.ds(pl.multiple_of(base + r, 16), rows)
            there = pl.ds(pl.multiple_of(r, 16) if stage == 0 else 0, rows)
            acc = self.total[o, i, m, here, :].astype(F32)
            for slot in range(3):
                acc = acc + arrived[o, slot, m, there, :].astype(F32)
            summed = self.done if stage == 2 else self.total
            summed[o, i, m, here, :] = acc.astype(BF)
            return _

        lax.fori_loop(0, self.n * (4 if stage == 0 else 1), add, 0)


def reduction_scratch(n, width):
    return [
        pltpu.VMEM((3, 4, n, 256, width), BF),
        pltpu.VMEM((3, 4, n, 256, width), BF),
        pltpu.VMEM((3, 3, n, 256, width), BF),
        pltpu.VMEM((3, 3, n, 64, width), BF),
        pltpu.VMEM((3, 3, n, 16, width), BF),
        pltpu.SemaphoreType.DMA((3, 6, 3)),
        pltpu.SemaphoreType.DMA((3, 6, 3)),
    ]


def all_peers(place):
    peers = [on_ring(place, axis, step) for axis in range(3) for step in (1, 2, 3)]
    x, y, z, core = place
    return peers + [device(x, y, z, 1 - core)]


def ar_kernel(parts_ref, out_ref, total, done, first, second, third, send, recv, local_sem, pair, psem):
    place = coords()
    x, y, z, core = place
    sibling = device(x, y, z, 1 - core)
    greet(place, all_peers(place))
    own = pltpu.make_async_copy(parts_ref.at[core], total, local_sem.at[0])
    own.start()
    cp = pltpu.make_async_remote_copy(
        src_ref=parts_ref.at[1 - core], dst_ref=pair, send_sem=psem.at[0], recv_sem=psem.at[1], device_id=sibling, device_id_type=MESH)
    cp.start()
    own.wait()
    cp.wait()
    n = total.shape[2]

    def add(step, _):
        o = lax.div(step, 4 * n)
        i = lax.rem(lax.div(step, n), 4)
        m = lax.rem(step, n)
        total[o, i, m] = (total[o, i, m].astype(F32) + pair[o, i, m].astype(F32)).astype(BF)
        return _
    lax.fori_loop(0, 12 * n, add, 0)
    red = Reduction(place, total, done, first, second, third, send, recv)
    for stage in range(6):
        for o in range(3):
            red.start(o, stage)
        for o in range(3):
            red.finish(o, stage)
    mine = pltpu.make_async_copy(done, out_ref.at[core], local_sem.at[0])
    mine.start()
    cp = pltpu.make_async_remote_copy(
        src_ref=done, dst_ref=out_ref.at[core], send_sem=psem.at[2], recv_sem=psem.at[3], device_id=sibling, device_id_type=MESH)
    cp.start()
    cp.wait()
    mine.wait()


def all_reduce(parts, cid):
    _, _, _, n, _, width = parts.shape
    return pl.pallas_call(
        ar_kernel,
        out_shape=jax.ShapeDtypeStruct(parts.shape, BF),
        in_specs=[pl.BlockSpec(memory_space=pl.ANY)],
        out_specs=pl.BlockSpec(memory_space=pl.ANY),
        scratch_shapes=reduction_scratch(n, width) + [pltpu.SemaphoreType.DMA((1,)), pltpu.VMEM((3, 4, n, 256, width), BF), pltpu.SemaphoreType.DMA((4,))],
        compiler_params=pltpu.CompilerParams(collective_id=cid, has_side_effects=True, vmem_limit_bytes=60 * 2**20),
    )(parts)


HEADS = 12
HEAD = 64
LAT_HEADS = 2
LATENT = 256
ROPE = 64
KEY_BLK = 512
GROUPS = 4


epsilon = 1e-06
rope_base = 10000.0
masked_score = -1e30


def angles(positions):
    halves = ROPE // 2
    freq_list = rope_base ** (-(jnp.arange(halves, dtype=jnp.float32) * 2.0 / ROPE))
    phases = positions[:, None] * freq_list[None, :]
    return (jnp.cos(phases), jnp.sin(phases))


def rotate(values, cosine, sine):
    halves = values.shape[-1] // 2
    front = values[..., :halves]
    back_half = values[..., halves:]
    return jnp.concatenate(
        [front * cosine - back_half * sine, front * sine + back_half * cosine], axis=-1
    )


def unrotate(grads, cosine, sine):
    halves = grads.shape[-1] // 2
    front = grads[..., :halves]
    back_half = grads[..., halves:]
    return jnp.concatenate(
        [front * cosine + back_half * sine, back_half * cosine - front * sine], axis=-1
    )


def norm_forward(values, gain):
    inverse = lax.rsqrt(jnp.mean(values * values, axis=-1, keepdims=True) + epsilon)
    unit_rows = values * inverse
    return (unit_rows, inverse, unit_rows * gain)


def norm_backward(grads, unit_rows, inverse, gain):
    scaled = grads * gain
    gain_grad = jnp.sum(grads * unit_rows, axis=0)
    input_grad = inverse * (
        scaled - unit_rows * jnp.mean(scaled * unit_rows, axis=-1, keepdims=True)
    )
    return (input_grad, gain_grad)


def product(left, right):
    return jnp.dot(left, right, preferred_element_type=jnp.float32)


def outer_sum(left, right):
    return lax.dot_general(
        left, right, (((0,), (0,)), ((), ())), preferred_element_type=jnp.float32
    )


def times_transpose(left, right):
    return lax.dot_general(
        left, right, (((1,), (1,)), ((), ())), preferred_element_type=jnp.float32
    )


def up_project(latents, w_upkey, w_upval):
    row_count = latents.shape[0]
    grouped = latents.reshape(row_count, LAT_HEADS, LATENT)
    keys = jnp.einsum("ngc,gcf->ngf", grouped, w_upkey, preferred_element_type=jnp.float32)
    values = jnp.einsum("ngc,gcf->ngf", grouped, w_upval, preferred_element_type=jnp.float32)
    return (
        keys.astype(jnp.bfloat16).reshape(row_count, HEADS * HEAD),
        values.astype(jnp.bfloat16).reshape(row_count, HEADS * HEAD),
    )


def block_scores(queries, query_rot, keys, key_rot, query_first, position):
    query_len = queries.shape[0]
    offset = position * KEY_BLK
    key_blk = lax.dynamic_slice_in_dim(keys, offset, KEY_BLK, 0).reshape(KEY_BLK, HEADS, HEAD)
    rot_blk = lax.dynamic_slice_in_dim(key_rot, offset, KEY_BLK, 0)
    raw = jnp.einsum("qhe,khe->hqk", queries, key_blk, preferred_element_type=jnp.float32)
    raw = raw + jnp.einsum("qhr,kr->hqk", query_rot, rot_blk, preferred_element_type=jnp.float32)
    key_pos = offset + jnp.arange(KEY_BLK, dtype=jnp.int32)
    query_pos = query_first + jnp.arange(query_len, dtype=jnp.int32)
    allowed = key_pos[None, :] <= query_pos[:, None]
    scores = jnp.where(allowed[None, :, :], raw * (HEAD + ROPE) ** (-0.5), masked_score)
    return (scores, key_blk, rot_blk)


def value_block(values, position):
    return lax.dynamic_slice_in_dim(values, position * KEY_BLK, KEY_BLK, 0).reshape(
        KEY_BLK, HEADS, HEAD
    )


def attend_forward(queries, query_rot, keys, values, key_rot, query_first, block_count):
    query_len = queries.shape[0]

    def sweep(position, carried):
        highest, summed = carried
        scores = block_scores(queries, query_rot, keys, key_rot, query_first, position)[0]
        new_high = jnp.maximum(highest, jnp.max(scores, axis=-1))
        summed = summed * jnp.exp(highest - new_high) + jnp.sum(
            jnp.exp(scores - new_high[..., None]), axis=-1
        )
        return (new_high, summed)

    start_state = (
        jnp.full((HEADS, query_len), masked_score, jnp.float32),
        jnp.zeros((HEADS, query_len), jnp.float32),
    )
    highest, summed = lax.fori_loop(0, block_count, sweep, start_state)
    log_total = highest + jnp.log(summed)

    def weigh_values(position, acc):
        scores = block_scores(queries, query_rot, keys, key_rot, query_first, position)[0]
        weights = jnp.exp(scores - log_total[..., None]).astype(jnp.bfloat16)
        return acc + jnp.einsum(
            "hqk,khe->qhe",
            weights,
            value_block(values, position),
            preferred_element_type=jnp.float32,
        )

    mixed = lax.fori_loop(
        0, block_count, weigh_values, jnp.zeros((query_len, HEADS, HEAD), jnp.float32)
    )
    return (mixed, log_total)


def attend_backward(
    queries, query_rot, keys, values, key_rot, log_total, grad_mixed, query_first, block_count
):
    query_len = queries.shape[0]
    length = keys.shape[0]
    factor = (HEAD + ROPE) ** (-0.5)

    def row_terms(position, acc):
        scores = block_scores(queries, query_rot, keys, key_rot, query_first, position)[0]
        weights = jnp.exp(scores - log_total[..., None])
        dprob = jnp.einsum(
            "qhe,khe->hqk",
            grad_mixed,
            value_block(values, position),
            preferred_element_type=jnp.float32,
        )
        return acc + jnp.sum(weights * dprob, axis=-1)

    delta = lax.fori_loop(0, block_count, row_terms, jnp.zeros((HEADS, query_len), jnp.float32))

    def accumulate(position, carried):
        grad_q, grad_qr, grad_keys, grad_values, grad_rot = carried
        scores, key_blk, rot_blk = block_scores(
            queries, query_rot, keys, key_rot, query_first, position
        )
        weights = jnp.exp(scores - log_total[..., None])
        dprob = jnp.einsum(
            "qhe,khe->hqk",
            grad_mixed,
            value_block(values, position),
            preferred_element_type=jnp.float32,
        )
        dscore = (weights * (dprob - delta[..., None])).astype(jnp.bfloat16)
        grad_q = grad_q + jnp.einsum(
            "hqk,khe->qhe", dscore, key_blk, preferred_element_type=jnp.float32
        )
        grad_qr = grad_qr + jnp.einsum(
            "hqk,kr->qhr", dscore, rot_blk, preferred_element_type=jnp.float32
        )
        key_part = factor * jnp.einsum(
            "hqk,qhe->khe", dscore, queries, preferred_element_type=jnp.float32
        )
        rot_part = factor * jnp.einsum(
            "hqk,qhr->kr", dscore, query_rot, preferred_element_type=jnp.float32
        )
        value_part = jnp.einsum(
            "hqk,qhe->khe",
            weights.astype(jnp.bfloat16),
            grad_mixed,
            preferred_element_type=jnp.float32,
        )
        offset = position * KEY_BLK
        grad_keys = lax.dynamic_update_slice_in_dim(
            grad_keys, key_part.astype(jnp.bfloat16).reshape(KEY_BLK, HEADS * HEAD), offset, 0
        )
        grad_values = lax.dynamic_update_slice_in_dim(
            grad_values, value_part.astype(jnp.bfloat16).reshape(KEY_BLK, HEADS * HEAD), offset, 0
        )
        grad_rot = lax.dynamic_update_slice_in_dim(grad_rot, rot_part, offset, 0)
        return (grad_q, grad_qr, grad_keys, grad_values, grad_rot)

    start_state = (
        jnp.zeros((query_len, HEADS, HEAD), jnp.float32),
        jnp.zeros((query_len, HEADS, ROPE), jnp.float32),
        jnp.zeros((length, HEADS * HEAD), jnp.bfloat16),
        jnp.zeros((length, HEADS * HEAD), jnp.bfloat16),
        jnp.zeros((length, ROPE), jnp.float32),
    )
    grad_q, grad_qr, grad_keys, grad_values, grad_rot = lax.fori_loop(
        0, block_count, accumulate, start_state
    )
    return (factor * grad_q, factor * grad_qr, grad_keys, grad_values, grad_rot)


def halves(grad, blocks, width):
    grad = grad.reshape(3, 256, 2, blocks, width)
    return jnp.transpose(grad, (2, 0, 3, 1, 4)).astype(BF)


def whole(blocks):
    _, _, count, _, width = blocks.shape
    return jnp.transpose(blocks, (1, 3, 0, 2, 4)).reshape(768, 2 * count * width)


def up_blocks(grad):
    return jnp.transpose(grad.reshape(2, 256, 3, 128), (0, 2, 1, 3))[:, :, None].astype(BF)


def summed(grads):
    g_norm, g_query, g_qrope, g_latent, g_krope, g_upkey, g_upval, g_out, g_norm2, g_gate, g_up, g_down = grads
    down = jnp.transpose(g_down.reshape(2, 4, 256, 3, 256), (0, 3, 1, 2, 4)).astype(BF)
    wide = jnp.stack([halves(g_gate, 4, 256), halves(g_up, 4, 256), down], axis=3)
    wide = all_reduce(wide, 1)
    column = jnp.concatenate([g_krope, g_norm[:, None], g_norm2[:, None], jnp.zeros((768, 62), jnp.float32)], axis=1)
    column = jnp.broadcast_to(column.reshape(1, 3, 1, 256, 128), (2, 3, 1, 256, 128)).astype(BF)
    column = column * (lax.broadcasted_iota(jnp.int32, (2, 1, 1, 1, 1), 0) == 0)
    column = column.astype(BF)
    narrow = jnp.stack(
        [
            jnp.concatenate([halves(g_query, 3, 128), up_blocks(g_upkey)], axis=2),
            jnp.concatenate([halves(g_qrope, 3, 128), up_blocks(g_upval)], axis=2),
            jnp.concatenate([halves(g_out, 3, 128), column], axis=2),
            jnp.concatenate([halves(g_latent, 2, 128)] * 2, axis=2),
        ],
        axis=3,
    )
    narrow = all_reduce(narrow, 2)
    wide = wide.astype(jnp.float32)
    narrow = narrow.astype(jnp.float32)
    column = narrow[0, :, 3, 2].reshape(768, 128)
    ups = lambda m: jnp.transpose(narrow[:, :, 3, m], (0, 2, 1, 3)).reshape(2, 256, 384)
    return (
        column[:, 64],
        whole(narrow[:, :, :3, 0]),
        whole(narrow[:, :, :3, 1]),
        whole(narrow[:, :, :2, 3]),
        column[:, :64],
        ups(0),
        ups(1),
        whole(narrow[:, :, :3, 2]),
        column[:, 65],
        whole(wide[:, :, :, 0]),
        whole(wide[:, :, :, 1]),
        jnp.transpose(wide[:, :, :, 2], (0, 2, 3, 1, 4)).reshape(2048, 768),
    )


def local(
    tokens,
    cotangent,
    group_of_seq,
    group_weight,
    norm_attn,
    w_query,
    w_qrope,
    w_latent,
    w_krope,
    w_upkey,
    w_upval,
    w_out,
    norm_mlp,
    w_gate,
    w_up,
    w_down,
):
    seq_count, blk_width, model_width = tokens.shape
    row_count = seq_count * blk_width
    group_heads = HEADS // LAT_HEADS
    query_first = lax.axis_index("blk") * blk_width
    block_count = (query_first + blk_width + KEY_BLK - 1) // KEY_BLK
    cosine, sine = angles(
        (query_first + jnp.arange(blk_width, dtype=jnp.int32)).astype(jnp.float32)
    )
    cos_heads = cosine[None, :, None, :]
    sin_heads = sine[None, :, None, :]
    inputs = tokens.astype(jnp.float32).reshape(row_count, model_width)
    unit_attn, inv_attn, pre_attn = norm_forward(inputs, norm_attn)
    normed = pre_attn.astype(jnp.bfloat16)
    queries = product(normed, w_query).astype(jnp.bfloat16)
    query_pre = product(normed, w_qrope).reshape(seq_count, blk_width, HEADS, ROPE)
    query_rot = rotate(query_pre, cos_heads, sin_heads).astype(jnp.bfloat16)
    latents = product(normed, w_latent).astype(jnp.bfloat16)
    key_rot = rotate(
        product(normed, w_krope).reshape(seq_count, blk_width, ROPE), cosine[None], sine[None]
    ).astype(jnp.bfloat16)
    own_keys, own_values = up_project(latents, w_upkey, w_upval)
    keys_all, values_all, rot_all = (
        lax.all_gather(
            own_keys.reshape(seq_count, blk_width, HEADS * HEAD), "blk", axis=1, tiled=True
        ),
        lax.all_gather(
            own_values.reshape(seq_count, blk_width, HEADS * HEAD), "blk", axis=1, tiled=True
        ),
        lax.all_gather(key_rot, "blk", axis=1, tiled=True),
    )
    query_heads = queries.reshape(seq_count, blk_width, HEADS, HEAD)
    mixed, log_total = jax.vmap(attend_forward, in_axes=(0, 0, 0, 0, 0, None, None))(
        query_heads, query_rot, keys_all, values_all, rot_all, query_first, block_count
    )
    attn_out = mixed.reshape(row_count, HEADS * HEAD).astype(jnp.bfloat16)
    middle = inputs + product(attn_out, w_out)
    unit_mlp, inv_mlp, pre_mlp = norm_forward(middle, norm_mlp)
    normed_mlp = pre_mlp.astype(jnp.bfloat16)
    gate_pre = product(normed_mlp, w_gate)
    up_pre = product(normed_mlp, w_up)
    sigmoid_gate = jax.nn.sigmoid(gate_pre)
    silu_gate = gate_pre * sigmoid_gate
    hidden = (silu_gate * up_pre).astype(jnp.bfloat16)
    layer_out = (
        (middle + product(hidden, w_down))
        .astype(jnp.bfloat16)
        .reshape(seq_count, blk_width, model_width)
    )
    matches = group_of_seq[:, None] == jnp.arange(GROUPS, dtype=jnp.int32)[None, :]
    seq_weight = jnp.sum(jnp.where(matches, group_weight[None, :], 0.0), axis=1)
    grad_out = (cotangent.astype(jnp.float32) * seq_weight[:, None, None]).reshape(
        row_count, model_width
    )
    grad_branch = grad_out.astype(jnp.bfloat16)
    grad_w_down = outer_sum(hidden, grad_branch)
    grad_hidden = times_transpose(grad_branch, w_down)
    grad_gate = (
        grad_hidden * up_pre * sigmoid_gate * (1.0 + gate_pre * (1.0 - sigmoid_gate))
    ).astype(jnp.bfloat16)
    grad_upper = (grad_hidden * silu_gate).astype(jnp.bfloat16)
    grad_w_gate = outer_sum(normed_mlp, grad_gate)
    grad_w_up = outer_sum(normed_mlp, grad_upper)
    grad_nm = times_transpose(grad_gate, w_gate) + times_transpose(grad_upper, w_up)
    grad_mid_norm, grad_norm_mlp = norm_backward(grad_nm, unit_mlp, inv_mlp, norm_mlp)
    grad_middle = grad_out + grad_mid_norm
    grad_attn = grad_middle.astype(jnp.bfloat16)
    grad_w_out = outer_sum(attn_out, grad_attn)
    grad_mixed = (
        times_transpose(grad_attn, w_out)
        .astype(jnp.bfloat16)
        .reshape(seq_count, blk_width, HEADS, HEAD)
    )
    grad_q, grad_qr, grad_keys, grad_values, grad_rot = jax.vmap(
        attend_backward, in_axes=(0, 0, 0, 0, 0, 0, 0, None, None)
    )(
        query_heads,
        query_rot,
        keys_all,
        values_all,
        rot_all,
        log_total,
        grad_mixed,
        query_first,
        block_count,
    )
    key_total, value_total, grad_krot = (
        lax.psum_scatter(
            grad_keys.astype(jnp.float32).astype(jnp.bfloat16),
            "blk",
            scatter_dimension=1,
            tiled=True,
        ).astype(jnp.float32),
        lax.psum_scatter(
            grad_values.astype(jnp.float32).astype(jnp.bfloat16),
            "blk",
            scatter_dimension=1,
            tiled=True,
        ).astype(jnp.float32),
        lax.psum_scatter(
            grad_rot.astype(jnp.bfloat16), "blk", scatter_dimension=1, tiled=True
        ).astype(jnp.float32),
    )
    keys_grouped = key_total.reshape(row_count, LAT_HEADS, group_heads * HEAD)
    values_grouped = value_total.reshape(row_count, LAT_HEADS, group_heads * HEAD)
    upkey_wide = w_upkey.astype(jnp.float32)
    upval_wide = w_upval.astype(jnp.float32)
    grad_lat = jnp.einsum(
        "ngf,gcf->ngc",
        keys_grouped,
        upkey_wide,
        precision=lax.Precision.HIGHEST,
        preferred_element_type=jnp.float32,
    )
    grad_lat = grad_lat + jnp.einsum(
        "ngf,gcf->ngc",
        values_grouped,
        upval_wide,
        precision=lax.Precision.HIGHEST,
        preferred_element_type=jnp.float32,
    )
    lat_wide = latents.astype(jnp.float32).reshape(row_count, LAT_HEADS, LATENT)
    grad_w_upkey = jnp.einsum(
        "ngc,ngf->gcf",
        lat_wide,
        keys_grouped,
        precision=lax.Precision.HIGHEST,
        preferred_element_type=jnp.float32,
    )
    grad_w_upval = jnp.einsum(
        "ngc,ngf->gcf",
        lat_wide,
        values_grouped,
        precision=lax.Precision.HIGHEST,
        preferred_element_type=jnp.float32,
    )
    grad_latents = grad_lat.reshape(row_count, LAT_HEADS * LATENT).astype(jnp.bfloat16)
    grad_kpre = (
        unrotate(grad_krot, cosine[None], sine[None]).reshape(row_count, ROPE).astype(jnp.bfloat16)
    )
    grad_queries = grad_q.reshape(row_count, HEADS * HEAD).astype(jnp.bfloat16)
    grad_qpre = (
        unrotate(grad_qr, cos_heads, sin_heads)
        .reshape(row_count, HEADS * ROPE)
        .astype(jnp.bfloat16)
    )
    grad_w_query = outer_sum(normed, grad_queries)
    grad_w_qrope = outer_sum(normed, grad_qpre)
    grad_w_latent = outer_sum(normed, grad_latents)
    grad_w_krope = outer_sum(normed, grad_kpre)
    grad_normed = times_transpose(grad_queries, w_query) + times_transpose(grad_qpre, w_qrope)
    grad_normed = (
        grad_normed + times_transpose(grad_latents, w_latent) + times_transpose(grad_kpre, w_krope)
    )
    grad_in_norm, grad_norm_attn = norm_backward(grad_normed, unit_attn, inv_attn, norm_attn)
    grad_tokens = (grad_middle + grad_in_norm).reshape(seq_count, blk_width, model_width)
    totals = summed(
        (
            grad_norm_attn,
            grad_w_query,
            grad_w_qrope,
            grad_w_latent,
            grad_w_krope,
            grad_w_upkey,
            grad_w_upval,
            grad_w_out,
            grad_norm_mlp,
            grad_w_gate,
            grad_w_up,
            grad_w_down,
        ),
    )
    return (
        layer_out,
        grad_tokens,
        totals[0],
        totals[1],
        totals[2],
        totals[3],
        totals[4],
        totals[5],
        totals[6],
        totals[7],
        totals[8],
        totals[9],
        totals[10],
        totals[11],
    )


def solution(mesh):
    in_specs = (
        P("seq", "blk", None),
        P("seq", "blk", None),
        P("seq"),
        P(),
        P(),
        P(),
        P(),
        P(),
        P(),
        P(),
        P(),
        P(),
        P(),
        P(),
        P(),
        P(),
    )
    out_specs = (
        P("seq", "blk", None),
        P("seq", "blk", None),
        P(),
        P(),
        P(),
        P(),
        P(),
        P(),
        P(),
        P(),
        P(),
        P(),
        P(),
        P(),
    )
    return jax.shard_map(local, mesh=mesh, in_specs=in_specs, out_specs=out_specs, check_vma=False)
```

```python
import jax
import jax.numpy as jnp
from jax import lax
from jax.sharding import PartitionSpec as P
from jax.experimental import pallas as pl
from jax.experimental.pallas import tpu as pltpu

MESH = pl.DeviceIdType.MESH
BF = jnp.bfloat16
F32 = jnp.float32
EPSILON = 1e-06
ROPE = 64
GROUPS = 4
FACTOR = 128.0**-0.5
LOG2E = 1.4426950408889634
HIDDEN_SCORE = -1e30
ORDERS = ((0, 1, 2), (1, 2, 0), (2, 0, 1))


def coords():
    s = lax.axis_index("seq")
    b = lax.axis_index("blk")
    x = lax.rem(b, 2) * 2 + lax.div(s, 2)
    return x, lax.div(b, 8), lax.rem(lax.div(b, 2), 4), lax.rem(s, 2)


def device(x, y, z, core):
    return (lax.rem(x, 2) * 2 + core, y * 8 + z * 2 + lax.div(x, 2))


def on_ring(place, axis, step):
    spot = list(place)
    spot[axis] = lax.rem(place[axis] + step, 4)
    return device(*spot)


def remote(src, dst, send, recv, peer):
    return pltpu.make_async_remote_copy(
        src_ref=src, dst_ref=dst, send_sem=send, recv_sem=recv, device_id=peer, device_id_type=MESH
    )


def rows_at(start, size, multiple=16):
    return pl.ds(pl.multiple_of(start, multiple), size)


def dot(left, right):
    return jnp.dot(left, right, preferred_element_type=F32)


def dot_nt(left, right):
    return lax.dot_general(left, right, (((1,), (1,)), ((), ())), preferred_element_type=F32)


def dot_tn(left, right):
    return lax.dot_general(left, right, (((0,), (0,)), ((), ())), preferred_element_type=F32)


class Reduction:
    def __init__(self, place, total, first, second, third, chunk, send, recv, keep, outs, tall):
        self.place = place
        self.total, self.first, self.second, self.third, self.chunk = total, first, second, third, chunk
        self.send, self.recv, self.keep, self.outs, self.tall = send, recv, keep, outs, tall
        self.n, self.width = total.shape[2], total.shape[4]

    def spots(self, o):
        a, b, c = ORDERS[o]
        return self.place[a], self.place[b], self.place[c]

    def region(self, o, m, i, row, rows, count=1):
        core, width = self.place[3], self.width
        if self.tall[m]:
            if count == 4:
                return self.outs[m].at[rows_at(core * 4 * 256, 1024), pl.ds(o * width, width)]
            return self.outs[m].at[rows_at((core * 4 + i) * 256 + row, rows), pl.ds(o * width, width)]
        return self.outs[m].at[rows_at(o * 256 + row, rows), rows_at((core * 4 + i) * width, count * width, 128)]

    def copies(self, o, stage):
        i, j, k = self.spots(o)
        made = []
        if stage == 6:
            x, y, z, core = self.place
            for m in range(self.n):
                here = self.region(o, m, 0, 0, 256, 4)
                made.append(
                    remote(here, here, self.send.at[o, 6, 0, m], self.recv.at[o, 6, 0, m], device(x, y, z, 1 - core))
                )
            return made
        axis = ORDERS[o][(0, 1, 2, 2, 1, 0)[stage]]
        for step in (1, 2, 3):
            to = lax.rem(self.place[axis] + step, 4)
            peer = on_ring(self.place, axis, step)
            if stage < 3:
                if stage == 0:
                    src, dst = self.total.at[o, to], self.first.at[o, step - 1]
                elif stage == 1:
                    src, dst = self.total.at[o, i, :, rows_at(to * 64, 64)], self.second.at[o, step - 1]
                else:
                    src, dst = self.total.at[o, i, :, rows_at(j * 64 + to * 16, 16)], self.third.at[o, step - 1]
                made.append(
                    remote(src, dst, self.send.at[o, stage, step - 1, 0], self.recv.at[o, stage, step - 1, 0], peer)
                )
                continue
            row, rows = ((j * 64 + k * 16, 16), (j * 64, 64), (0, 256))[stage - 3]
            for m in range(self.n):
                here = self.region(o, m, i, row, rows)
                src = self.chunk.at[o, m] if stage == 3 else here
                made.append(
                    remote(src, here, self.send.at[o, stage, step - 1, m], self.recv.at[o, stage, step - 1, m], peer)
                )
        return made

    def kept(self, o):
        i, j, k = self.spots(o)
        return [
            pltpu.make_async_copy(
                self.chunk.at[o, m], self.region(o, m, i, j * 64 + k * 16, 16), self.keep.at[o, m]
            )
            for m in range(self.n)
        ]

    def start(self, stage, orders=(0, 1, 2)):
        for o in orders:
            for copy in self.copies(o, stage):
                copy.start()
            if stage == 3:
                for copy in self.kept(o):
                    copy.start()

    def finish(self, stage, orders=(0, 1, 2)):
        for o in orders:
            for copy in self.copies(o, stage):
                copy.wait()
            if stage == 3:
                for copy in self.kept(o):
                    copy.wait()
            if stage < 3:
                self.add(o, stage)

    def step(self, stage):
        for o in range(3):
            self.finish(stage, (o,))
            self.start(stage + 1, (o,))

    def add(self, o, stage):
        i, j, k = self.spots(o)
        rows = (64, 64, 16)[stage]
        base = (0, j * 64, j * 64 + k * 16)[stage]
        arrived = (self.first, self.second, self.third)[stage]
        parts = 4 if stage == 0 else 1

        def body(step, carried):
            m = lax.div(step, parts)
            shift = lax.rem(step, parts) * 64
            here, there = rows_at(base + shift, rows), rows_at(shift, rows)
            acc = self.total[o, i, m, here, :].astype(F32)
            for slot in range(3):
                acc = acc + arrived[o, slot, m, there, :].astype(F32)
            if stage == 2:
                self.chunk[o, m] = acc.astype(BF)
            else:
                self.total[o, i, m, here, :] = acc.astype(BF)
            return carried

        lax.fori_loop(0, self.n * parts, body, 0)


def reduction_scratch(name, n, width):
    return {
        name + "_total": pltpu.VMEM((3, 4, n, 256, width), BF),
        name + "_first": pltpu.VMEM((3, 3, n, 256, width), BF),
        name + "_second": pltpu.VMEM((3, 3, n, 64, width), BF),
        name + "_third": pltpu.VMEM((3, 3, n, 16, width), BF),
        name + "_chunk": pltpu.VMEM((3, n, 16, width), BF),
        name + "_send": pltpu.SemaphoreType.DMA((3, 7, 3, n)),
        name + "_recv": pltpu.SemaphoreType.DMA((3, 7, 3, n)),
        name + "_keep": pltpu.SemaphoreType.DMA((3, n)),
    }


WEIGHTS = {
    "w_latent": (768, 512),
    "w_krope": (768, 64),
    "w_query": (768, 768),
    "w_qrope": (768, 768),
    "w_upkey": (2, 256, 384),
    "w_upval": (2, 256, 384),
    "w_out": (768, 768),
    "w_gate": (768, 2048),
    "w_up": (768, 2048),
    "w_down": (2048, 768),
}
SMALL = ("tokens", "cotangent", "seq_weight", "cosine", "sine", "norm_attn", "norm_mlp")
OUTS = {
    "layer_out": ((2, 64, 768), BF),
    "grad_tokens": ((2, 64, 768), F32),
    "g_gate": ((768, 2048), BF),
    "g_up": ((768, 2048), BF),
    "g_down": ((2048, 768), BF),
    "g_query": ((768, 1024), BF),
    "g_qrope": ((768, 1024), BF),
    "g_out": ((768, 1024), BF),
    "g_late": ((768, 1024), BF),
}


def scratch():
    vmem, dma = pltpu.VMEM, pltpu.SemaphoreType.DMA
    made = {"v" + name[1:]: vmem(shape, BF) for name, shape in WEIGHTS.items()}
    made.update(
        load_sem=dma((len(WEIGHTS),)),
        swap_sem=dma((4, 2)),
        pair_sem=dma((12, 2)),
        ag_sem=dma((2, 2, 2, 3, 2)),
        rs_sem=dma((2, 2, 2, 3, 2)),
        xbuf=vmem((128, 768), BF),
        cbuf=vmem((128, 768), BF),
        norm2=vmem((256, 768), BF),
        normt=vmem((768, 256), BF),
        krd=vmem((128, 128), F32),
        q=vmem((128, 768), BF),
        qr=vmem((128, 768), BF),
        lat=vmem((4, 4, 4, 64, 256), BF),
        kr=vmem((4, 4, 64, 128), BF),
        latt=vmem((4, 4, 4, 64, 256), BF),
        krt=vmem((2, 4, 128, 256), BF),
        rel=vmem((2, 256, 384), jnp.int32),
        qs=vmem((4, 384, 256), BF),
        ga=vmem((4, 384, 256), BF),
        qrx=vmem((2, 4, 384, 128), BF),
        acc=vmem((4, 256, 384), F32),
        ctx=vmem((4, 256, 384), BF),
        logs=vmem((4, 8, 384), F32),
        delta=vmem((4, 8, 384), F32),
        aof=vmem((128, 768), F32),
        ao2=vmem((256, 768), BF),
        middle=vmem((128, 768), F32),
        nm2=vmem((256, 768), BF),
        nmt=vmem((768, 256), BF),
        gb2=vmem((256, 768), BF),
        acts=vmem((3, 256, 1024), BF),
        other=vmem((3, 128, 1024), BF),
        hidt=vmem((1024, 256), BF),
        outacc=vmem((128, 768), F32),
        gnm=vmem((128, 768), F32),
        outbf=vmem((128, 768), BF),
        gattn=vmem((2, 256, 384), BF),
        gmix=vmem((128, 768), BF),
        dqr=vmem((4, 128, 384), F32),
        dlat=vmem((4, 4, 256, 256), F32),
        dkr=vmem((4, 256, 128), F32),
        skr=vmem((4, 4, 64, 128), BF),
        ro1=vmem((3, 2, 4, 64, 256), BF),
        rk1=vmem((3, 4, 64, 128), BF),
        rt1=vmem((3, 2, 4, 64, 256), BF),
        so1=vmem((2, 4, 64, 256), BF),
        ks1=vmem((4, 64, 128), BF),
        st1=vmem((2, 4, 64, 256), BF),
        ro2=vmem((3, 2, 64, 256), BF),
        rk2=vmem((3, 64, 128), BF),
        rt2=vmem((3, 2, 64, 256), BF),
        gq2=vmem((2, 256, 384), BF),
        gqp2=vmem((2, 256, 384), BF),
        gl2=vmem((2, 256, 256), BF),
        dup=vmem((2, 2, 3, 256, 128), BF),
        sup=vmem((2, 3, 256, 128), BF),
        gmid=vmem((128, 768), F32),
        gains=vmem((16, 128), F32),
    )
    made.update(reduction_scratch("wide", 3, 256))
    made.update(reduction_scratch("early", 3, 128))
    made.update(reduction_scratch("late", 1, 128))
    return made


class Refs:
    pass


def swap_halves(values):
    lanes = values.shape[-1]
    low = lax.rem(lax.broadcasted_iota(jnp.int32, values.shape, 1), 64) < 32
    return jnp.where(low, pltpu.roll(values, lanes - 32, 1), pltpu.roll(values, 32, 1))


def layer_kernel(*args):
    r = Refs()
    shapes = scratch()
    names = list(SMALL) + list(WEIGHTS) + list(OUTS) + list(shapes)
    for name, ref in zip(names, args, strict=True):
        setattr(r, name, ref)
    place = coords()
    x, y, z, core = place
    x_hi = lax.div(x, 2)
    blk = y * 8 + z * 2 + x_hi
    slot = y * 4 + z
    sibling = device(x, y, z, 1 - core)
    partner = device(lax.rem(x + 2, 4), 3 - y, 3 - z, core)
    peers = [on_ring(place, axis, step) for axis in range(3) for step in (1, 2, 3)] + [sibling, partner]
    low64 = lambda rows: lax.broadcasted_iota(jnp.int32, (rows, 128), 1) < 64
    diagonal = (lax.broadcasted_iota(jnp.int32, (128, 128), 0) < 64) == low64(128)

    def both(value):
        return jnp.where(diagonal, jnp.concatenate([value, value], axis=0), jnp.zeros((), value.dtype))

    def pick(value):
        return jnp.where(low64(64), value[0:64], value[64:128])

    loads = {}
    for at, name in enumerate(WEIGHTS):
        loads[name] = pltpu.make_async_copy(getattr(r, name), getattr(r, "v" + name[1:]), r.load_sem.at[at])
        loads[name].start()
    barrier = pltpu.get_barrier_semaphore()
    for peer in peers:
        pl.semaphore_signal(barrier, inc=1, device_id=peer, device_id_type=MESH)
    pl.semaphore_wait(barrier, len(peers))

    def swap(at, src, dst):
        return remote(src, dst, r.swap_sem.at[at, 0], r.swap_sem.at[at, 1], partner)

    def paired(at, src, dst):
        return remote(src, dst, r.pair_sem.at[at, 0], r.pair_sem.at[at, 1], sibling)

    swap_x = swap(0, r.tokens.at[1 - x_hi], r.xbuf.at[pl.ds(64, 64)])
    swap_c = swap(1, r.cotangent.at[1 - x_hi], r.cbuf.at[pl.ds(64, 64)])
    swap_x.start()
    swap_c.start()
    r.xbuf[0:64] = r.tokens[x_hi]
    r.cbuf[0:64] = r.cotangent[x_hi]
    key_row = lax.broadcasted_iota(jnp.int32, (256, 384), 0)
    query_lane = lax.rem(lax.broadcasted_iota(jnp.int32, (256, 384), 1), 64)
    within = lax.rem(key_row, 64) - query_lane
    r.rel[0] = 128 * lax.div(key_row, 64) + within
    r.rel[1] = within - 128 * lax.div(key_row, 64)
    swap_x.wait()

    def unit_of(values):
        inverse = lax.rsqrt(jnp.mean(values * values, axis=-1, keepdims=True) + EPSILON)
        return values * inverse, inverse

    unit = unit_of(r.xbuf[...].astype(F32))[0]
    normed = (unit * r.norm_attn[...]).astype(BF)
    r.norm2[0:128] = normed
    send_norm = paired(0, r.norm2.at[pl.ds(0, 128)], r.norm2.at[pl.ds(128, 128)])
    send_norm.start()
    loads["w_latent"].wait()
    loads["w_krope"].wait()
    key_pre = dot(normed, r.v_krope[...])
    r.krd[:, 0:64] = key_pre
    r.krd[:, 64:128] = key_pre
    key_pre = r.krd[...]
    key_rot = (key_pre * r.cosine[...] + swap_halves(key_pre) * r.sine[...]).astype(BF)
    r.kr[y, z] = pick(key_rot)
    latents = dot(normed, r.v_latent[...]).astype(BF)
    for half in range(2):
        for g in range(2):
            r.lat[half * 2 + g, y, z] = latents[half * 64 : half * 64 + 64, g * 256 : g * 256 + 256]

    def gather(part, phase):
        made = []
        axis = (2, 1)[(part + phase) % 2]
        for step in (1, 2, 3):
            peer = on_ring(place, axis, step)
            two = pl.ds(part * 2, 2)
            if phase == 0:
                pieces = [r.lat.at[two, y, z], r.kr.at[y, z]]
            elif part == 0:
                pieces = [r.lat.at[two, y], r.kr.at[y]]
            else:
                pieces = [r.lat.at[two, :, z], None]
            for at, piece in enumerate(pieces if part == 0 else pieces[:1]):
                sem = r.ag_sem.at[part, phase, at, step - 1]
                made.append(remote(piece, piece, sem.at[0], sem.at[1], peer))
        return made

    for part in range(2):
        for copy in gather(part, 0):
            copy.start()

    loads["w_query"].wait()
    r.q[...] = dot(normed, r.v_query[...]).astype(BF)
    loads["w_qrope"].wait()
    query_pre = dot(normed, r.v_qrope[...])
    for p in range(6):
        lanes = slice(p * 128, p * 128 + 128)
        piece = query_pre[:, lanes]
        r.qr[:, lanes] = (piece * r.cosine[...] + swap_halves(piece) * r.sine[...]).astype(BF)
    loads["w_upkey"].wait()

    def to_latent(source, weights, target):
        for half in range(2):
            for g in range(2):
                for j in range(3):
                    p = g * 3 + j
                    block = both(source[half * 64 : half * 64 + 64, p * 128 : p * 128 + 128])
                    rows = dot_nt(block, weights[g, :, j * 128 : j * 128 + 128])
                    target[half * 2 + g, j * 128 : j * 128 + 128] = rows.astype(BF)

    to_latent(r.q, r.v_upkey, r.qs)
    for half in range(2):
        for p in range(6):
            pair = r.qr[half * 64 : half * 64 + 64, p * 128 : p * 128 + 128].astype(F32)
            turned = pltpu.roll(pair, 64, 1)
            for odd in range(2):
                front, back = (turned, pair) if odd else (pair, turned)
                at = (p % 3) * 128 + odd * 64
                here = (half * 2 + p // 3, slice(at, at + 64))
                r.qrx[(0,) + here] = jnp.where(low64(64), front, 0.0).astype(BF)
                r.qrx[(1,) + here] = jnp.where(low64(64), 0.0, back).astype(BF)

    for part in range(2):
        for copy in gather(part, 0):
            copy.wait()
        for copy in gather(part, 1):
            copy.start()
    for part in range(2):
        for copy in gather(part, 1):
            copy.wait()

    def transpose_latents(step, carried):
        j, c = lax.div(step, 4), lax.rem(step, 4)
        r.latt[j, c] = r.lat[j, c].reshape(256, 256).T.reshape(4, 64, 256)
        return carried

    lax.fori_loop(0, 16, transpose_latents, 0)
    top = lax.broadcasted_iota(jnp.int32, (128, 256), 0) < 64
    for c in range(4):
        turned = r.kr[c].reshape(256, 128).astype(F32).T
        r.krt[0, c] = jnp.where(top, turned, 0.0).astype(BF)
        r.krt[1, c] = jnp.where(top, 0.0, turned).astype(BF)

    own_count = (y + 1, lax.div(16 - x_hi - slot + 3, 4))
    far_count = (lax.div(slot + x_hi + 3, 4), 4 - y)
    query_blk = (blk, 31 - blk)

    def chosen(half, pair):
        return jnp.where(half == 0, pair[0], pair[1])

    def key_chunk(half, step):
        near = chosen(half, own_count)
        far = (step >= near).astype(jnp.int32)
        chunk = jnp.where(step < near, step, 4 - chosen(half, far_count) + step - near)
        first = chosen(half, query_blk) * 64
        edge = jnp.where(far == 0, first - 512 * chunk - 64 * x_hi, first - 1984 + 512 * chunk + 64 * x_hi)
        return far, chunk, r.rel[far] <= edge

    def raw_scores(at, far, chunk, g):
        keys = r.lat[far * 2 + g, chunk].reshape(256, 256)
        rot = r.kr[chunk].reshape(256, 128)
        return dot_nt(keys, r.qs[at]) + dot_nt(rot, r.qrx[far, at]), keys

    r.acc[...] = jnp.zeros_like(r.acc)

    def forward_half(half, carried):
        def chunk_step(step, state):
            far, chunk, allowed = key_chunk(half, step)
            result = []
            for g in range(2):
                at = half * 2 + g
                high, total = state[g]
                raw = raw_scores(at, far, chunk, g)[0]
                raw = jnp.where(allowed, raw, HIDDEN_SCORE)
                new_high = jnp.maximum(high, jnp.max(raw, axis=0, keepdims=True))
                shrink = jnp.exp2((high - new_high) * (FACTOR * LOG2E))
                weights = jnp.exp2((raw - new_high) * (FACTOR * LOG2E))
                total = total * shrink + jnp.sum(weights, axis=0, keepdims=True)
                r.acc[at] = r.acc[at] * shrink + dot(r.latt[far * 2 + g, chunk].reshape(256, 256), weights.astype(BF))
                result.append((new_high, total))
            return tuple(result)

        empty = (jnp.full((1, 384), HIDDEN_SCORE, F32), jnp.zeros((1, 384), F32))
        count = chosen(half, own_count) + chosen(half, far_count)
        state = lax.fori_loop(0, count, chunk_step, (empty, empty))
        for g in range(2):
            high, total = state[g]
            at = half * 2 + g
            r.ctx[at] = (r.acc[at] * (1.0 / total)).astype(BF)
            r.logs[at] = jnp.broadcast_to(high * (FACTOR * LOG2E) + jnp.log2(total), (8, 384))
        return carried

    lax.fori_loop(0, 2, forward_half, 0)
    loads["w_upval"].wait()

    def from_latent(source, weights, half, p):
        g, j = p // 3, p % 3
        lanes = slice(j * 128, j * 128 + 128)
        return pick(dot_tn(source[half * 2 + g, :, lanes].astype(BF), weights[g, :, lanes]))

    for half in range(2):
        for p in range(6):
            r.aof[half * 64 : half * 64 + 64, p * 128 : p * 128 + 128] = from_latent(r.ctx, r.v_upval, half, p)
    r.ao2[0:128] = r.aof[...].astype(BF)
    send_ao = paired(1, r.ao2.at[pl.ds(0, 128)], r.ao2.at[pl.ds(128, 128)])
    send_ao.start()

    loads["w_out"].wait()
    middle = r.xbuf[...].astype(F32) + dot(r.ao2[0:128], r.v_out[...])
    r.middle[...] = middle
    unit_mlp = unit_of(middle)[0]
    r.nm2[0:128] = (unit_mlp * r.norm_mlp[...]).astype(BF)
    send_nm = paired(2, r.nm2.at[pl.ds(0, 128)], r.nm2.at[pl.ds(128, 128)])
    send_nm.start()
    swap_c.wait()
    weight = jnp.where(x_hi == 0, r.seq_weight[0:1, 0:1], r.seq_weight[1:2, 0:1])
    r.gb2[0:128] = (r.cbuf[...].astype(F32) * weight).astype(BF)
    send_gb = paired(3, r.gb2.at[pl.ds(0, 128)], r.gb2.at[pl.ds(128, 128)])
    send_gb.start()
    r.outacc[...] = middle
    r.gnm[...] = jnp.zeros_like(r.gnm)
    for name in ("w_gate", "w_up", "w_down"):
        loads[name].wait()

    def feed(half, target):
        def tile(step, carried):
            at = rows_at(half * 1024 + step * 256, 256, 256)
            cols = rows_at(step * 256, 256, 256)
            act = r.nm2[0:128]
            gate = dot(act, r.v_gate[:, at])
            up = dot(act, r.v_up[:, at])
            sig = jax.nn.sigmoid(gate)
            silu = gate * sig
            hidden = (silu * up).astype(BF)
            grad_hidden = dot_nt(r.gb2[0:128], r.v_down[at, :])
            grad_gate = (grad_hidden * up * sig * (1.0 + gate * (1.0 - sig))).astype(BF)
            grad_up = (grad_hidden * silu).astype(BF)
            target[0, 0:128, cols] = hidden
            target[1, 0:128, cols] = grad_gate
            target[2, 0:128, cols] = grad_up
            r.outacc[...] += dot(hidden, r.v_down[at, :])
            r.gnm[...] += dot_nt(grad_gate, r.v_gate[:, at]) + dot_nt(grad_up, r.v_up[:, at])
            return carried

        lax.fori_loop(0, 4, tile, 0)

    feed(1 - core, r.other)
    send_acts = paired(4, r.other, r.acts.at[:, pl.ds(128, 128)])
    send_acts.start()
    feed(core, r.acts)
    r.outbf[...] = r.outacc[...].astype(BF)
    r.layer_out[x_hi] = r.outbf[0:64]
    swap_out = swap(2, r.outbf.at[pl.ds(64, 64)], r.layer_out.at[x_hi])
    swap_out.start()

    def norm_back(grads, values, gain):
        unit_rows, inverse = unit_of(values)
        scaled = grads * gain
        gain_grad = jnp.sum(grads * unit_rows, axis=0, keepdims=True)
        mean = jnp.mean(scaled * unit_rows, axis=-1, keepdims=True)
        return inverse * (scaled - unit_rows * mean), gain_grad

    back, gain_mlp = norm_back(r.gnm[...], r.middle[...], r.norm_mlp[...])
    r.gmid[...] = r.cbuf[...].astype(F32) * weight + back
    gain_row = lax.broadcasted_iota(jnp.int32, (16, 128), 0)
    gains = jnp.zeros((16, 128), F32)
    for p in range(6):
        gains = gains + jnp.where(gain_row == 6 + p, gain_mlp[:, p * 128 : p * 128 + 128], 0.0)
    r.gains[...] = gains
    grad_attn = r.gmid[...].astype(BF)
    for half in range(2):
        r.gattn[half, 0:128] = grad_attn[:, half * 384 : half * 384 + 384]
    send_ga = paired(5, r.gattn.at[1 - core, pl.ds(0, 128)], r.gattn.at[1 - core, pl.ds(128, 128)])
    send_ga.start()
    mixed = dot_nt(grad_attn, r.v_out[...])
    r.gmix[...] = mixed.astype(BF)
    to_latent(r.gmix, r.v_upval, r.ga)
    ones = jnp.ones((8, 128), F32)
    for half in range(2):
        for p in range(6):
            here = (slice(half * 64, half * 64 + 64), slice(p * 128, p * 128 + 128))
            block = both(r.gmix[here].astype(F32) * r.aof[here])
            sums = lax.dot_general(
                ones, block, (((1,), (1,)), ((), ())), precision=lax.Precision.HIGHEST, preferred_element_type=F32
            )
            r.delta[half * 2 + p // 3, :, (p % 3) * 128 : (p % 3) * 128 + 128] = sums

    wide = Reduction(
        place, r.wide_total, r.wide_first, r.wide_second, r.wide_third, r.wide_chunk, r.wide_send, r.wide_recv,
        r.wide_keep, (r.g_gate, r.g_up, r.g_down), (False, False, True),
    )
    early = Reduction(
        place, r.early_total, r.early_first, r.early_second, r.early_third, r.early_chunk, r.early_send,
        r.early_recv, r.early_keep, (r.g_query, r.g_qrope, r.g_out), (False, False, False),
    )
    late = Reduction(
        place, r.late_total, r.late_first, r.late_second, r.late_third, r.late_chunk, r.late_send, r.late_recv,
        r.late_keep, (r.g_late,), (False,),
    )
    for copy in (send_nm, send_gb, send_acts):
        copy.wait()
    r.nmt[...] = r.nm2[...].T
    r.hidt[...] = r.acts[0].T
    for o in range(3):

        def wide_tile(i, carried):
            cols = rows_at(i * 256, 256, 256)
            left = r.nmt[o * 256 : o * 256 + 256]
            r.wide_total[o, i, 0] = dot(left, r.acts[1, :, cols]).astype(BF)
            r.wide_total[o, i, 1] = dot(left, r.acts[2, :, cols]).astype(BF)
            r.wide_total[o, i, 2] = dot(r.hidt[cols, :], r.gb2[:, o * 256 : o * 256 + 256]).astype(BF)
            return carried

        lax.fori_loop(0, 4, wide_tile, 0)
        wide.start(0, (o,))

    r.acc[...] = jnp.zeros_like(r.acc)
    r.dqr[...] = jnp.zeros_like(r.dqr)
    r.dlat[...] = jnp.zeros_like(r.dlat)
    r.dkr[...] = jnp.zeros_like(r.dkr)

    def backward_half(half, carried):
        def chunk_step(step, inner):
            far, chunk, allowed = key_chunk(half, step)
            for g in range(2):
                at = half * 2 + g
                raw, keys = raw_scores(at, far, chunk, g)
                weights = jnp.exp2(raw * (FACTOR * LOG2E) - r.logs[at, 0:1])
                weights = jnp.where(allowed, weights, 0.0)
                dprob = dot_nt(keys, r.ga[at])
                dscore = (weights * (dprob - r.delta[at, 0:1])).astype(BF)
                weights = weights.astype(BF)
                r.acc[at] += dot(r.latt[far * 2 + g, chunk].reshape(256, 256), dscore)
                r.dqr[at] += dot(r.krt[far, chunk], dscore)
                r.dlat[far * 2 + g, chunk] += FACTOR * dot(dscore, r.qs[at]) + dot(weights, r.ga[at])
                r.dkr[chunk] += FACTOR * dot(dscore, r.qrx[far, at])
            return inner

        count = chosen(half, own_count) + chosen(half, far_count)
        lax.fori_loop(0, count, chunk_step, 0)
        return carried

    lax.fori_loop(0, 2, backward_half, 0)

    def narrow(step, carried):
        j, c = lax.div(step, 4), lax.rem(step, 4)
        r.latt[j, c] = r.dlat[j, c].astype(BF).reshape(4, 64, 256)
        return carried

    lax.fori_loop(0, 16, narrow, 0)
    for c in range(4):
        r.skr[c] = r.dkr[c].astype(BF).reshape(4, 64, 128)

    def scatter(part, phase):
        made = []
        axis = (1, 2)[(part + phase) % 2]
        for step in (1, 2, 3):
            peer = on_ring(place, axis, step)
            to = lax.rem(place[axis] + step, 4)
            at = step - 1
            if part == 0 and phase == 0:
                pieces = [(r.latt.at[pl.ds(0, 2), to], r.ro1.at[at]), (r.skr.at[to], r.rk1.at[at])]
            elif part == 0:
                pieces = [(r.so1.at[:, to], r.ro2.at[at]), (r.ks1.at[to], r.rk2.at[at])]
            elif phase == 0:
                pieces = [(r.latt.at[pl.ds(2, 2), :, to], r.rt1.at[at])]
            else:
                pieces = [(r.st1.at[:, to], r.rt2.at[at])]
            for k, (src, dst) in enumerate(pieces):
                sem = r.rs_sem.at[part, phase, k, at]
                made.append(remote(src, dst, sem.at[0], sem.at[1], peer))
        return made

    for part in range(2):
        for copy in scatter(part, 0):
            copy.start()

    for half in range(2):
        for p in range(6):
            rows, lanes = slice(half * 64, half * 64 + 64), slice((p % 3) * 128, (p % 3) * 128 + 128)
            at = half * 2 + p // 3
            piece = (FACTOR * from_latent(r.acc, r.v_upkey, half, p)).astype(BF)
            r.gq2[p // 3, rows, lanes] = piece
            turned = FACTOR * r.dqr[at, :, lanes].T
            turned = pick(turned + pltpu.roll(turned, 64, 1))
            turned = turned * r.cosine[rows, :] - swap_halves(turned) * r.sine[rows, :]
            r.gqp2[p // 3, rows, lanes] = turned.astype(BF)
    send_gq = paired(6, r.gq2.at[1 - core, pl.ds(0, 128)], r.gq2.at[1 - core, pl.ds(128, 128)])
    send_gqp = paired(7, r.gqp2.at[1 - core, pl.ds(0, 128)], r.gqp2.at[1 - core, pl.ds(128, 128)])
    send_gq.start()
    send_gqp.start()
    for g in range(2):
        for j in range(3):
            lanes = slice(j * 128, j * 128 + 128)
            wide_lanes = slice((g * 3 + j) * 128, (g * 3 + j) * 128 + 128)
            key_sum, value_sum = jnp.zeros((256, 128), F32), jnp.zeros((256, 128), F32)
            for half in range(2):
                rows = slice(half * 64, half * 64 + 64)
                key_sum += FACTOR * dot(r.acc[half * 2 + g, :, lanes].astype(BF), both(r.q[rows, wide_lanes]))
                value_sum += dot(r.ctx[half * 2 + g, :, lanes], both(r.gmix[rows, wide_lanes]))
            r.dup[g, 0, j] = key_sum.astype(BF)
            r.dup[g, 1, j] = value_sum.astype(BF)
    send_up = paired(8, r.dup.at[1 - core], r.sup)
    send_up.start()
    wide.step(0)
    grad_normed = dot_nt(r.gq2[0, 0:128], r.v_query[:, 0:384]) + dot_nt(r.gq2[1, 0:128], r.v_query[:, 384:768])
    grad_normed += dot_nt(r.gqp2[0, 0:128], r.v_qrope[:, 0:384]) + dot_nt(r.gqp2[1, 0:128], r.v_qrope[:, 384:768])
    r.gnm[...] = grad_normed
    send_norm.wait()
    r.normt[...] = r.norm2[...].T
    send_ao.wait()
    send_ga.wait()
    send_gq.wait()
    send_gqp.wait()
    send_up.wait()
    r.nmt[...] = r.ao2[...].T
    for o in range(3):
        rows = slice(o * 256, o * 256 + 256)
        for m, (left, right) in enumerate(((r.normt, r.gq2), (r.normt, r.gqp2), (r.nmt, r.gattn))):
            block = dot(left[rows], right[core]).astype(BF)
            for i in range(3):
                r.early_total[o, i, m] = block[:, i * 128 : i * 128 + 128]
        for m in range(2):
            r.early_total[o, 3, m] = (r.dup[core, m, o].astype(F32) + r.sup[m, o].astype(F32)).astype(BF)
        r.early_total[o, 3, 2] = jnp.zeros((256, 128), BF)
        early.start(0, (o,))

    wide.step(1)
    for copy in scatter(0, 0) + scatter(1, 0):
        copy.wait()

    def fold(at, carried):
        for g in range(2):
            near = r.dlat[g, y, rows_at(at * 64, 64), :]
            far = r.dlat[2 + g, at, rows_at(z * 64, 64), :]
            for k in range(3):
                near = near + r.ro1[k, g, at].astype(F32)
                far = far + r.rt1[k, g, at].astype(F32)
            r.so1[g, at] = near.astype(BF)
            r.st1[g, at] = far.astype(BF)
        rot = r.dkr[y, rows_at(at * 64, 64), :]
        for k in range(3):
            rot = rot + r.rk1[k, at].astype(F32)
        r.ks1[at] = rot.astype(BF)
        return carried

    lax.fori_loop(0, 4, fold, 0)
    for part in range(2):
        for copy in scatter(part, 1):
            copy.start()
    wide.step(2)
    for copy in scatter(0, 1) + scatter(1, 1):
        copy.wait()
    grad_latents = []
    for g in range(2):
        near = r.so1[g, z].astype(F32)
        far = r.st1[g, y].astype(F32)
        for k in range(3):
            near = near + r.ro2[k, g].astype(F32)
            far = far + r.rt2[k, g].astype(F32)
        piece = jnp.concatenate([near, far], axis=0).astype(BF)
        grad_latents.append(piece)
        r.gl2[g, 0:128] = piece
    send_gl = paired(9, r.gl2.at[1 - core, pl.ds(0, 128)], r.gl2.at[1 - core, pl.ds(128, 128)])
    send_gl.start()
    rot = r.ks1[z].astype(F32)
    for k in range(3):
        rot = rot + r.rk2[k].astype(F32)
    turned = pltpu.roll(rot, 64, 1)
    rot = jnp.concatenate([jnp.where(low64(64), rot, turned), jnp.where(low64(64), turned, rot)], axis=0)
    grad_kpre = (rot * r.cosine[...] - swap_halves(rot) * r.sine[...]).astype(BF)
    grad_normed = r.gnm[...] + dot_nt(grad_kpre[:, 0:64], r.v_krope[...])
    for g in range(2):
        grad_normed = grad_normed + dot_nt(grad_latents[g], r.v_latent[:, g * 256 : g * 256 + 256])
    back, gain_attn = norm_back(grad_normed, r.xbuf[...].astype(F32), r.norm_attn[...])
    r.outacc[...] = r.gmid[...] + back
    r.grad_tokens[x_hi] = r.outacc[0:64]
    swap_grad = swap(3, r.outacc.at[pl.ds(64, 64)], r.grad_tokens.at[x_hi])
    swap_grad.start()
    gains = r.gains[...]
    for p in range(6):
        gains = gains + jnp.where(gain_row == p, gain_attn[:, p * 128 : p * 128 + 128], 0.0)
    for o in range(3):
        r.late_total[o, 3, 0] = jnp.zeros((256, 128), BF)
    r.late_total[0, 3, 0, 0:16] = gains.astype(BF)
    send_gl.wait()
    for o in range(3):
        rows = slice(o * 256, o * 256 + 256)
        block = dot(r.normt[rows], r.gl2[core]).astype(BF)
        for i in range(2):
            r.late_total[o, i, 0] = block[:, i * 128 : i * 128 + 128]
        r.late_total[o, 2, 0] = dot(r.normt[rows, 0:128], grad_kpre).astype(BF)
        late.start(0, (o,))
    wide.step(3)
    early.step(0)
    late.step(0)
    wide.step(4)
    early.step(1)
    late.step(1)
    early.step(2)
    late.step(2)
    early.step(3)
    late.step(3)
    early.step(4)
    late.step(4)
    wide.step(5)
    early.step(5)
    late.step(5)
    swap_out.wait()
    swap_grad.wait()
    for reduction in (wide, early, late):
        reduction.finish(6)


def layer(small, weights):
    vmem = pl.BlockSpec(memory_space=pltpu.VMEM)
    hbm = pl.BlockSpec(memory_space=pl.ANY)
    return pl.pallas_call(
        layer_kernel,
        out_shape=[jax.ShapeDtypeStruct(shape, kind) for shape, kind in OUTS.values()],
        in_specs=[vmem] * len(small) + [hbm] * len(weights),
        out_specs=[vmem, vmem] + [hbm] * (len(OUTS) - 2),
        scratch_shapes=list(scratch().values()),
        compiler_params=pltpu.CompilerParams(
            collective_id=1, has_side_effects=True, vmem_limit_bytes=63 * 2**20
        ),
    )(*small, *weights)


def local(
    tokens, cotangent, group_of_seq, group_weight, norm_attn, w_query, w_qrope, w_latent, w_krope, w_upkey, w_upval,
    w_out, norm_mlp, w_gate, w_up, w_down,
):
    blk = lax.axis_index("blk")
    within = jnp.arange(64, dtype=jnp.int32)
    positions = jnp.concatenate([blk * 64 + within, (31 - blk) * 64 + within]).astype(F32)
    halves = ROPE // 2
    freq_list = 10000.0 ** (-(jnp.arange(halves, dtype=F32) * 2.0 / ROPE))
    phases = positions[:, None] * freq_list[None, :]
    cosine, sine = jnp.cos(phases), jnp.sin(phases)
    cosine = jnp.concatenate([cosine] * 4, axis=1)
    sine = jnp.concatenate([-sine, sine, -sine, sine], axis=1)
    matches = group_of_seq[:, None] == jnp.arange(GROUPS, dtype=jnp.int32)[None, :]
    seq_weight = jnp.sum(jnp.where(matches, group_weight[None, :], 0.0), axis=1)
    seq_weight = jnp.broadcast_to(seq_weight[:, None], (2, 128))
    small = (tokens, cotangent, seq_weight, cosine, sine, norm_attn[None, :], norm_mlp[None, :])
    weights = (w_latent, w_krope, w_query, w_qrope, w_upkey, w_upval, w_out, w_gate, w_up, w_down)
    layer_out, grad_tokens, g_gate, g_up, g_down, g_query, g_qrope, g_out, g_late = layer(small, weights)

    def joined(grad, width):
        return jnp.concatenate([grad[:, 0:width], grad[:, 512 : 512 + width]], axis=1).astype(F32)

    def up_part(grad):
        both = jnp.stack([grad[:, 384:512], grad[:, 896:1024]]).reshape(2, 3, 256, 128)
        return jnp.transpose(both, (0, 2, 1, 3)).reshape(2, 256, 384).astype(F32)

    extra = g_late[:, 256:512].astype(F32) + g_late[:, 768:1024].astype(F32)
    gains = extra[0:12, 128:256].reshape(2, 768)
    return (
        layer_out,
        grad_tokens,
        gains[0],
        joined(g_query, 384),
        joined(g_qrope, 384),
        joined(g_late, 256),
        extra[:, 0:64],
        up_part(g_query),
        up_part(g_qrope),
        joined(g_out, 384),
        gains[1],
        g_gate.astype(F32),
        g_up.astype(F32),
        g_down.astype(F32),
    )


def solution(mesh):
    split = P("seq", "blk", None)
    in_specs = (split, split, P("seq")) + (P(),) * 13
    out_specs = (split, split) + (P(),) * 12
    return jax.shard_map(local, mesh=mesh, in_specs=in_specs, out_specs=out_specs, check_vma=False)
```

```python
import jax
import jax.numpy as jnp
import numpy as np
from jax import lax
from jax.sharding import PartitionSpec as P
from jax.experimental import pallas as pl
from jax.experimental.pallas import tpu as pltpu

MESH = pl.DeviceIdType.MESH
BF = jnp.bfloat16
F32 = jnp.float32
EPSILON = 1e-06
ROPE = 64
GROUPS = 4
FACTOR = 128.0**-0.5
LOG2E = 1.4426950408889634
HIDDEN_SCORE = -1e30
ORDERS = ((0, 1, 2), (1, 2, 0), (2, 0, 1))


def coords():
    s = lax.axis_index("seq")
    b = lax.axis_index("blk")
    x = lax.rem(b, 2) * 2 + lax.div(s, 2)
    return x, lax.div(b, 8), lax.rem(lax.div(b, 2), 4), lax.rem(s, 2)


def device(x, y, z, core):
    return (lax.rem(x, 2) * 2 + core, y * 8 + z * 2 + lax.div(x, 2))


def on_ring(place, axis, step):
    spot = list(place)
    spot[axis] = lax.rem(place[axis] + step, 4)
    return device(*spot)


def remote(src, dst, send, recv, peer):
    return pltpu.make_async_remote_copy(
        src_ref=src, dst_ref=dst, send_sem=send, recv_sem=recv, device_id=peer, device_id_type=MESH
    )


def rows_at(start, size, multiple=16):
    return pl.ds(pl.multiple_of(start, multiple), size)


def dot(left, right):
    return jnp.dot(left, right, preferred_element_type=F32)


def dot_nt(left, right):
    return lax.dot_general(left, right, (((1,), (1,)), ((), ())), preferred_element_type=F32)


def dot_tn(left, right):
    return lax.dot_general(left, right, (((0,), (0,)), ((), ())), preferred_element_type=F32)


class Reduction:
    def __init__(self, r, name, place, outs, tall=None, halving=True):
        self.place, self.outs, self.halving = place, outs, halving
        for part in ("total", "first", "second", "third", "chunk", "send", "recv", "keep"):
            setattr(self, part, getattr(r, name + "_" + part))
        self.n, self.width = self.total.shape[2], self.total.shape[4]
        self.tall = tall or (False,) * self.n

    def spots(self, o):
        a, b, c = ORDERS[o]
        return self.place[a], self.place[b], self.place[c]

    def sides(self, o, s):
        me = self.place[ORDERS[o][0]]
        odd = lax.rem(me, 2)
        near, far = 1 + 2 * odd, 3 - 2 * odd
        steps = (near, far) if s == 0 else (far, near)
        return steps, lax.rem(me + steps[0], 4), lax.rem(me + steps[1], 4), lax.rem(me + 2, 4)

    def region(self, o, m, i, row, rows, count=1):
        core, width = self.place[3], self.width
        if self.tall[m]:
            if count == 4:
                return self.outs[m].at[rows_at(core * 4 * 256, 1024), pl.ds(o * width, width)]
            return self.outs[m].at[rows_at((core * 4 + i) * 256 + row, rows), pl.ds(o * width, width)]
        return self.outs[m].at[rows_at(o * 256 + row, rows), rows_at((core * 4 + i) * width, count * width, 128)]

    def moves(self, o, stage):
        i, j, k = self.spots(o)
        every = range(self.n)
        if stage == 8:
            x, y, z, core = self.place
            here = [self.region(o, m, 0, 0, 256, 4) for m in every]
            return [(spot, spot, device(x, y, z, 1 - core)) for spot in here]
        made = []
        axis = ORDERS[o][(0, 0, 1, 2, 2, 1, 0, 0)[stage]]
        if stage in (0, 1, 6, 7) and self.halving:
            for s in range(2):
                steps, front, last, across = self.sides(o, s)
                half = pl.ds(s * 128, 128)
                peer = on_ring(self.place, axis, steps[0 if stage in (0, 7) else 1])
                if stage == 0:
                    made.append((self.total.at[o, front, :, half], self.first.at[o, s, 0], peer))
                    made.append((self.total.at[o, across, :, half], self.first.at[o, s, 1], peer))
                elif stage == 1:
                    made.append((self.total.at[o, last, :, half], self.first.at[o, s, 2], peer))
                else:
                    for spot in (i, last) if stage == 7 else (i,):
                        here = [self.region(o, m, spot, s * 128, 128) for m in every]
                        made += [(where, where, peer) for where in here]
            return made
        if stage in (1, 6):
            return made
        for step in (1, 2, 3):
            to = lax.rem(self.place[axis] + step, 4)
            peer = on_ring(self.place, axis, step)
            at = step - 1
            if stage == 0:
                made.append((self.total.at[o, to], self.first.at[o, at], peer))
            elif stage == 2:
                made.append((self.total.at[o, i, :, rows_at(to * 64, 64)], self.second.at[o, at], peer))
            elif stage == 3:
                made.append((self.total.at[o, i, :, rows_at(j * 64 + to * 16, 16)], self.third.at[o, at], peer))
            else:
                row, rows = {4: (j * 64 + k * 16, 16), 5: (j * 64, 64), 7: (0, 256)}[stage]
                for m in every:
                    here = self.region(o, m, i, row, rows)
                    made.append((self.chunk.at[o, m] if stage == 4 else here, here, peer))
        return made

    def copies(self, o, stage):
        return [
            remote(src, dst, self.send.at[o, stage, at], self.recv.at[o, stage, at], peer)
            for at, (src, dst, peer) in enumerate(self.moves(o, stage))
        ]

    def kept(self, o):
        i, j, k = self.spots(o)
        return [
            pltpu.make_async_copy(
                self.chunk.at[o, m], self.region(o, m, i, j * 64 + k * 16, 16), self.keep.at[o, m]
            )
            for m in range(self.n)
        ]

    def start(self, stage, orders=(0, 1, 2)):
        for o in orders:
            for copy in self.copies(o, stage):
                copy.start()
            if stage == 4:
                for copy in self.kept(o):
                    copy.start()

    def finish(self, stage, orders=(0, 1, 2)):
        for o in orders:
            for copy in self.copies(o, stage):
                copy.wait()
            if stage == 4:
                for copy in self.kept(o):
                    copy.wait()
            if stage < 4:
                self.add(o, stage)

    def step(self, *stages):
        for stage in stages:
            for o in range(3):
                self.finish(stage, (o,))
                self.start(stage + 1, (o,))

    def add(self, o, stage):
        i, j, k = self.spots(o)

        def body(m, carried):
            if stage < 2 and self.halving:
                for s in range(2):
                    _, _, last, _ = self.sides(o, s)
                    half = slice(s * 128, s * 128 + 128)
                    for spot, slot in ((i, 0), (last, 1)) if stage == 0 else ((i, 2),):
                        acc = self.total[o, spot, m, half, :].astype(F32) + self.first[o, s, slot, m].astype(F32)
                        self.total[o, spot, m, half, :] = acc.astype(BF)
            elif stage == 0:
                for part in range(4):
                    rows = slice(part * 64, part * 64 + 64)
                    acc = self.total[o, i, m, rows, :].astype(F32)
                    for slot in range(3):
                        acc = acc + self.first[o, slot, m, rows, :].astype(F32)
                    self.total[o, i, m, rows, :] = acc.astype(BF)
            elif stage == 2:
                rows = rows_at(j * 64, 64)
                acc = self.total[o, i, m, rows, :].astype(F32)
                for slot in range(3):
                    acc = acc + self.second[o, slot, m].astype(F32)
                self.total[o, i, m, rows, :] = acc.astype(BF)
            elif stage == 3:
                acc = self.total[o, i, m, rows_at(j * 64 + k * 16, 16), :].astype(F32)
                for slot in range(3):
                    acc = acc + self.third[o, slot, m].astype(F32)
                self.chunk[o, m] = acc.astype(BF)
            return carried

        lax.fori_loop(0, self.n, body, 0)


def reduction_scratch(name, n, width, halving=True):
    copies = max(4 * n, 3 * n, 4)
    return {
        name + "_total": pltpu.VMEM((3, 4, n, 256, width), BF),
        name + "_first": pltpu.VMEM((3, 2, 3, n, 128, width) if halving else (3, 3, n, 256, width), BF),
        name + "_second": pltpu.VMEM((3, 3, n, 64, width), BF),
        name + "_third": pltpu.VMEM((3, 3, n, 16, width), BF),
        name + "_chunk": pltpu.VMEM((3, n, 16, width), BF),
        name + "_send": pltpu.SemaphoreType.DMA((3, 9, copies)),
        name + "_recv": pltpu.SemaphoreType.DMA((3, 9, copies)),
        name + "_keep": pltpu.SemaphoreType.DMA((3, n)),
    }


WEIGHTS = {
    "w_latent": (768, 512),
    "w_krope": (64, 768),
    "w_query": (768, 768),
    "w_qrope": (768, 768),
    "w_upkey": (2, 256, 384),
    "w_upval": (2, 256, 384),
    "w_out": (768, 768),
    "w_gate": (768, 1024),
    "w_up": (768, 1024),
    "w_down": (1024, 768),
}
SMALL = ("tokens", "cotangent", "norm_attn", "norm_mlp", "group_of_seq", "group_weight")
OUTS = {
    "layer_out": ((2, 64, 768), BF),
    "grad_tokens": ((2, 64, 768), F32),
    "g_gate": ((768, 2048), BF),
    "g_up": ((768, 2048), BF),
    "g_down": ((2048, 768), BF),
    "g_query": ((768, 1024), BF),
    "g_qrope": ((768, 1024), BF),
    "g_out": ((768, 1024), BF),
    "g_late": ((768, 1024), BF),
}


def scratch():
    vmem, dma = pltpu.VMEM, pltpu.SemaphoreType.DMA
    made = {"v" + name[1:]: vmem(shape, BF) for name, shape in WEIGHTS.items()}
    made.update(
        load_sem=dma((len(WEIGHTS),)),
        table_sem=dma((2,)),
        turns=vmem((128, 128), F32),
        cosine=vmem((128, 128), F32),
        sine=vmem((128, 128), F32),
        swap_sem=dma((4, 2)),
        pair_sem=dma((12, 2)),
        ag_sem=dma((2, 2, 2, 3, 2)),
        rs_sem=dma((2, 2, 2, 3, 2)),
        xbuf=vmem((128, 768), BF),
        cbuf=vmem((128, 768), BF),
        norm2=vmem((256, 768), BF),
        normt=vmem((768, 256), BF),
        krd=vmem((128, 128), F32),
        q=vmem((128, 768), BF),
        qr=vmem((128, 768), BF),
        lat=vmem((4, 4, 4, 64, 256), BF),
        kr=vmem((4, 4, 64, 128), BF),
        latt=vmem((4, 4, 4, 64, 256), BF),
        krt=vmem((2, 4, 128, 256), BF),
        rel=vmem((2, 256, 384), jnp.int32),
        qs=vmem((4, 384, 256), BF),
        ga=vmem((4, 384, 256), BF),
        qrx=vmem((2, 4, 384, 128), BF),
        acc=vmem((4, 256, 384), F32),
        ctx=vmem((4, 256, 384), BF),
        logs=vmem((4, 8, 384), F32),
        delta=vmem((4, 8, 384), F32),
        aof=vmem((128, 768), F32),
        ao2=vmem((256, 768), BF),
        middle=vmem((128, 768), F32),
        nm2=vmem((256, 768), BF),
        nmt=vmem((768, 256), BF),
        gb2=vmem((256, 768), BF),
        acts=vmem((3, 256, 1024), BF),
        hidt=vmem((1024, 256), BF),
        outacc=vmem((256, 768), F32),
        gnm=vmem((256, 768), F32),
        outx=vmem((128, 768), F32),
        gnmx=vmem((128, 768), F32),
        outbf=vmem((128, 768), BF),
        gattn=vmem((2, 256, 384), BF),
        gmix=vmem((128, 768), BF),
        dqr=vmem((4, 128, 384), F32),
        dlat=vmem((4, 4, 256, 256), F32),
        dkr=vmem((4, 256, 128), F32),
        skr=vmem((4, 4, 64, 128), BF),
        ro1=vmem((3, 2, 4, 64, 256), BF),
        rk1=vmem((3, 4, 64, 128), BF),
        rt1=vmem((3, 2, 4, 64, 256), BF),
        so1=vmem((2, 4, 64, 256), BF),
        ks1=vmem((4, 64, 128), BF),
        st1=vmem((2, 4, 64, 256), BF),
        ro2=vmem((3, 2, 64, 256), BF),
        rk2=vmem((3, 64, 128), BF),
        rt2=vmem((3, 2, 64, 256), BF),
        gq2=vmem((2, 256, 384), BF),
        gqp2=vmem((2, 256, 384), BF),
        gl2=vmem((2, 256, 256), BF),
        dup=vmem((2, 2, 3, 256, 128), BF),
        sup=vmem((2, 3, 256, 128), BF),
        gmid=vmem((128, 768), F32),
        gains=vmem((16, 128), F32),
    )
    made.update(reduction_scratch("wide", 3, 256))
    made.update(reduction_scratch("out", 1, 128))
    made.update(reduction_scratch("early", 2, 128))
    made.update(reduction_scratch("late", 1, 128, False))
    return made


class Refs:
    pass


def swap_halves(values):
    lanes = values.shape[-1]
    low = lax.rem(lax.broadcasted_iota(jnp.int32, values.shape, 1), 64) < 32
    return jnp.where(low, pltpu.roll(values, lanes - 32, 1), pltpu.roll(values, 32, 1))


def layer_kernel(*args):
    r = Refs()
    shapes = scratch()
    names = list(SMALL) + ["table"] + list(WEIGHTS) + list(OUTS) + list(shapes)
    for name, ref in zip(names, args, strict=True):
        setattr(r, name, ref)
    place = coords()
    x, y, z, core = place
    x_hi = lax.div(x, 2)
    blk = y * 8 + z * 2 + x_hi
    slot = y * 4 + z
    sibling = device(x, y, z, 1 - core)
    partner = device(lax.rem(x + 2, 4), 3 - y, 3 - z, core)
    peers = [on_ring(place, axis, step) for axis in range(3) for step in (1, 2, 3)] + [sibling, partner]
    low64 = lambda rows: lax.broadcasted_iota(jnp.int32, (rows, 128), 1) < 64
    diagonal = (lax.broadcasted_iota(jnp.int32, (128, 128), 0) < 64) == low64(128)

    def gain_of(ref):
        return ref[...].reshape(1, 768)

    def both(value):
        return jnp.where(diagonal, jnp.concatenate([value, value], axis=0), jnp.zeros((), value.dtype))

    def pick(value):
        return jnp.where(low64(64), value[0:64], value[64:128])

    loads = {}
    for at, name in enumerate(WEIGHTS):
        source = getattr(r, name)
        if name in ("w_gate", "w_up"):
            source = source.at[:, rows_at(core * 1024, 1024, 128)]
        elif name == "w_down":
            source = source.at[rows_at(core * 1024, 1024), :]
        loads[name] = pltpu.make_async_copy(source, getattr(r, "v" + name[1:]), r.load_sem.at[at])
    tables = [
        pltpu.make_async_copy(
            r.table.at[rows_at(where * 64, 64)], r.turns.at[pl.ds(half * 64, 64)], r.table_sem.at[half]
        )
        for half, where in enumerate((blk, 31 - blk))
    ]
    loads["w_latent"].start()
    loads["w_krope"].start()
    for table in tables:
        table.start()
    barrier = pltpu.get_barrier_semaphore()
    for peer in peers:
        pl.semaphore_signal(barrier, inc=1, device_id=peer, device_id_type=MESH)
    pl.semaphore_wait(barrier, len(peers))

    def swap(at, src, dst):
        return remote(src, dst, r.swap_sem.at[at, 0], r.swap_sem.at[at, 1], partner)

    def paired(at, src, dst):
        return remote(src, dst, r.pair_sem.at[at, 0], r.pair_sem.at[at, 1], sibling)

    swap_x = swap(0, r.tokens.at[1 - x_hi], r.xbuf.at[pl.ds(64, 64)])
    swap_c = swap(1, r.cotangent.at[1 - x_hi], r.cbuf.at[pl.ds(64, 64)])
    swap_x.start()
    swap_c.start()
    for name in ("w_query", "w_qrope", "w_upkey"):
        loads[name].start()
    r.xbuf[0:64] = r.tokens[x_hi]
    r.cbuf[0:64] = r.cotangent[x_hi]
    key_row = lax.broadcasted_iota(jnp.int32, (256, 384), 0)
    query_lane = lax.rem(lax.broadcasted_iota(jnp.int32, (256, 384), 1), 64)
    within = lax.rem(key_row, 64) - query_lane
    r.rel[0] = 128 * lax.div(key_row, 64) + within
    r.rel[1] = within - 128 * lax.div(key_row, 64)
    for table in tables:
        table.wait()
    turns = r.turns[...]
    other = pltpu.roll(turns, 64, 1)
    r.cosine[...] = jnp.where(low64(128), turns, other)
    r.sine[...] = jnp.where(low64(128), other, turns)
    swap_x.wait()

    def unit_of(values):
        inverse = lax.rsqrt(jnp.mean(values * values, axis=-1, keepdims=True) + EPSILON)
        return values * inverse, inverse

    unit = unit_of(r.xbuf[...].astype(F32))[0]
    normed = (unit * gain_of(r.norm_attn)).astype(BF)
    r.norm2[0:128] = normed
    send_norm = paired(0, r.norm2.at[pl.ds(0, 128)], r.norm2.at[pl.ds(128, 128)])
    send_norm.start()
    loads["w_latent"].wait()
    loads["w_krope"].wait()
    key_pre = dot_nt(normed, r.v_krope[...])
    r.krd[:, 0:64] = key_pre
    r.krd[:, 64:128] = key_pre
    key_pre = r.krd[...]
    key_rot = (key_pre * r.cosine[...] + swap_halves(key_pre) * r.sine[...]).astype(BF)
    r.kr[y, z] = pick(key_rot)
    latents = dot(normed, r.v_latent[...]).astype(BF)
    for half in range(2):
        for g in range(2):
            r.lat[half * 2 + g, y, z] = latents[half * 64 : half * 64 + 64, g * 256 : g * 256 + 256]

    def gather(part, phase):
        made = []
        axis = (2, 1)[(part + phase) % 2]
        for step in (1, 2, 3):
            peer = on_ring(place, axis, step)
            two = pl.ds(part * 2, 2)
            if phase == 0:
                pieces = [r.lat.at[two, y, z], r.kr.at[y, z]]
            elif part == 0:
                pieces = [r.lat.at[two, y], r.kr.at[y]]
            else:
                pieces = [r.lat.at[two, :, z], None]
            for at, piece in enumerate(pieces if part == 0 else pieces[:1]):
                sem = r.ag_sem.at[part, phase, at, step - 1]
                made.append(remote(piece, piece, sem.at[0], sem.at[1], peer))
        return made

    for part in range(2):
        for copy in gather(part, 0):
            copy.start()
    for name in ("w_upval", "w_out", "w_gate", "w_up", "w_down"):
        loads[name].start()

    loads["w_query"].wait()
    r.q[...] = dot(normed, r.v_query[...]).astype(BF)
    loads["w_qrope"].wait()
    query_pre = dot(normed, r.v_qrope[...])
    for p in range(6):
        lanes = slice(p * 128, p * 128 + 128)
        piece = query_pre[:, lanes]
        r.qr[:, lanes] = (piece * r.cosine[...] + swap_halves(piece) * r.sine[...]).astype(BF)
    loads["w_upkey"].wait()

    def to_latent(source, weights, target):
        for half in range(2):
            for g in range(2):
                for j in range(3):
                    p = g * 3 + j
                    block = both(source[half * 64 : half * 64 + 64, p * 128 : p * 128 + 128])
                    rows = dot_nt(block, weights[g, :, j * 128 : j * 128 + 128])
                    target[half * 2 + g, j * 128 : j * 128 + 128] = rows.astype(BF)

    to_latent(r.q, r.v_upkey, r.qs)
    for half in range(2):
        for p in range(6):
            pair = r.qr[half * 64 : half * 64 + 64, p * 128 : p * 128 + 128].astype(F32)
            turned = pltpu.roll(pair, 64, 1)
            for odd in range(2):
                front, back = (turned, pair) if odd else (pair, turned)
                at = (p % 3) * 128 + odd * 64
                here = (half * 2 + p // 3, slice(at, at + 64))
                r.qrx[(0,) + here] = jnp.where(low64(64), front, 0.0).astype(BF)
                r.qrx[(1,) + here] = jnp.where(low64(64), 0.0, back).astype(BF)

    for part in range(2):
        for copy in gather(part, 0):
            copy.wait()
        for copy in gather(part, 1):
            copy.start()
    for part in range(2):
        for copy in gather(part, 1):
            copy.wait()

    def transpose_latents(step, carried):
        j, c = lax.div(step, 4), lax.rem(step, 4)
        r.latt[j, c] = r.lat[j, c].reshape(256, 256).T.reshape(4, 64, 256)
        return carried

    lax.fori_loop(0, 16, transpose_latents, 0)
    top = lax.broadcasted_iota(jnp.int32, (128, 256), 0) < 64
    for c in range(4):
        turned = r.kr[c].reshape(256, 128).astype(F32).T
        r.krt[0, c] = jnp.where(top, turned, 0.0).astype(BF)
        r.krt[1, c] = jnp.where(top, 0.0, turned).astype(BF)

    own_count = (y + 1, lax.div(16 - x_hi - slot + 3, 4))
    far_count = (lax.div(slot + x_hi + 3, 4), 4 - y)
    query_blk = (blk, 31 - blk)

    def chosen(half, pair):
        return jnp.where(half == 0, pair[0], pair[1])

    def key_chunk(half, step):
        near = chosen(half, own_count)
        far = (step >= near).astype(jnp.int32)
        chunk = jnp.where(step < near, step, 4 - chosen(half, far_count) + step - near)
        first = chosen(half, query_blk) * 64
        edge = jnp.where(far == 0, first - 512 * chunk - 64 * x_hi, first - 1984 + 512 * chunk + 64 * x_hi)
        return far, chunk, r.rel[far] <= edge

    def raw_scores(at, far, chunk, g):
        keys = r.lat[far * 2 + g, chunk].reshape(256, 256)
        rot = r.kr[chunk].reshape(256, 128)
        return dot_nt(keys, r.qs[at]) + dot_nt(rot, r.qrx[far, at]), keys

    r.acc[...] = jnp.zeros_like(r.acc)

    def forward_half(half, carried):
        def chunk_step(step, state):
            far, chunk, allowed = key_chunk(half, step)
            result = []
            for g in range(2):
                at = half * 2 + g
                high, total = state[g]
                raw = raw_scores(at, far, chunk, g)[0]
                raw = jnp.where(allowed, raw, HIDDEN_SCORE)
                new_high = jnp.maximum(high, jnp.max(raw, axis=0, keepdims=True))
                shrink = jnp.exp2((high - new_high) * (FACTOR * LOG2E))
                weights = jnp.exp2((raw - new_high) * (FACTOR * LOG2E))
                total = total * shrink + jnp.sum(weights, axis=0, keepdims=True)
                r.acc[at] = r.acc[at] * shrink + dot(r.latt[far * 2 + g, chunk].reshape(256, 256), weights.astype(BF))
                result.append((new_high, total))
            return tuple(result)

        empty = (jnp.full((1, 384), HIDDEN_SCORE, F32), jnp.zeros((1, 384), F32))
        count = chosen(half, own_count) + chosen(half, far_count)
        state = lax.fori_loop(0, count, chunk_step, (empty, empty))
        for g in range(2):
            high, total = state[g]
            at = half * 2 + g
            r.ctx[at] = (r.acc[at] * (1.0 / total)).astype(BF)
            r.logs[at] = jnp.broadcast_to(high * (FACTOR * LOG2E) + jnp.log2(total), (8, 384))
        return carried

    lax.fori_loop(0, 2, forward_half, 0)
    loads["w_upval"].wait()

    def from_latent(source, weights, half, p):
        g, j = p // 3, p % 3
        lanes = slice(j * 128, j * 128 + 128)
        return pick(dot_tn(source[half * 2 + g, :, lanes].astype(BF), weights[g, :, lanes]))

    for half in range(2):
        for p in range(6):
            r.aof[half * 64 : half * 64 + 64, p * 128 : p * 128 + 128] = from_latent(r.ctx, r.v_upval, half, p)
    r.ao2[0:128] = r.aof[...].astype(BF)
    send_ao = paired(1, r.ao2.at[pl.ds(0, 128)], r.ao2.at[pl.ds(128, 128)])
    send_ao.start()

    loads["w_out"].wait()
    middle = r.xbuf[...].astype(F32) + dot(r.ao2[0:128], r.v_out[...])
    r.middle[...] = middle
    unit_mlp = unit_of(middle)[0]
    r.nm2[0:128] = (unit_mlp * gain_of(r.norm_mlp)).astype(BF)
    send_nm = paired(2, r.nm2.at[pl.ds(0, 128)], r.nm2.at[pl.ds(128, 128)])
    send_nm.start()
    swap_c.wait()
    group = jnp.where(x_hi == 0, r.group_of_seq[0], r.group_of_seq[1])
    weight = r.group_weight[0]
    for g in range(1, GROUPS):
        weight = jnp.where(group == g, r.group_weight[g], weight)
    r.gb2[0:128] = (r.cbuf[...].astype(F32) * weight).astype(BF)
    send_gb = paired(3, r.gb2.at[pl.ds(0, 128)], r.gb2.at[pl.ds(128, 128)])
    send_gb.start()
    r.outacc[...] = jnp.zeros_like(r.outacc)
    r.gnm[...] = jnp.zeros_like(r.gnm)
    for name in ("w_gate", "w_up", "w_down"):
        loads[name].wait()
    send_nm.wait()
    send_gb.wait()

    def tile(step, carried):
        at = rows_at(step * 256, 256, 256)
        act = r.nm2[...]
        gate = dot(act, r.v_gate[:, at])
        up = dot(act, r.v_up[:, at])
        sig = jax.nn.sigmoid(gate)
        silu = gate * sig
        hidden = (silu * up).astype(BF)
        grad_hidden = dot_nt(r.gb2[...], r.v_down[at, :])
        grad_gate = (grad_hidden * up * sig * (1.0 + gate * (1.0 - sig))).astype(BF)
        grad_up = (grad_hidden * silu).astype(BF)
        r.acts[0, :, at] = hidden
        r.acts[1, :, at] = grad_gate
        r.acts[2, :, at] = grad_up
        r.outacc[...] += dot(hidden, r.v_down[at, :])
        r.gnm[...] += dot_nt(grad_gate, r.v_gate[:, at]) + dot_nt(grad_up, r.v_up[:, at])
        return carried

    lax.fori_loop(0, 4, tile, 0)
    send_gnm = paired(4, r.gnm.at[pl.ds(128, 128)], r.gnmx)
    send_out = paired(10, r.outacc.at[pl.ds(128, 128)], r.outx)
    send_gnm.start()
    send_out.start()

    wide = Reduction(r, "wide", place, (r.g_gate, r.g_up, r.g_down), (False, False, True))
    outer = Reduction(r, "out", place, (r.g_out,))
    early = Reduction(r, "early", place, (r.g_query, r.g_qrope))
    late = Reduction(r, "late", place, (r.g_late,), halving=False)
    r.nmt[...] = r.nm2[...].T
    r.hidt[...] = r.acts[0].T
    for o in range(3):

        def wide_tile(i, carried):
            cols = rows_at(i * 256, 256, 256)
            left = r.nmt[o * 256 : o * 256 + 256]
            r.wide_total[o, i, 0] = dot(left, r.acts[1, :, cols]).astype(BF)
            r.wide_total[o, i, 1] = dot(left, r.acts[2, :, cols]).astype(BF)
            r.wide_total[o, i, 2] = dot(r.hidt[cols, :], r.gb2[:, o * 256 : o * 256 + 256]).astype(BF)
            return carried

        lax.fori_loop(0, 4, wide_tile, 0)
        wide.start(0, (o,))

    def norm_back(grads, values, gain):
        unit_rows, inverse = unit_of(values)
        scaled = grads * gain
        gain_grad = jnp.sum(grads * unit_rows, axis=0, keepdims=True)
        mean = jnp.mean(scaled * unit_rows, axis=-1, keepdims=True)
        return inverse * (scaled - unit_rows * mean), gain_grad

    send_gnm.wait()
    back, gain_mlp = norm_back(r.gnm[0:128] + r.gnmx[...], r.middle[...], gain_of(r.norm_mlp))
    r.gmid[...] = r.cbuf[...].astype(F32) * weight + back
    gain_row = lax.broadcasted_iota(jnp.int32, (16, 128), 0)
    gains = jnp.zeros((16, 128), F32)
    for p in range(6):
        gains = gains + jnp.where(gain_row == 6 + p, gain_mlp[:, p * 128 : p * 128 + 128], 0.0)
    r.gains[...] = gains
    grad_attn = r.gmid[...].astype(BF)
    for half in range(2):
        r.gattn[half, 0:128] = grad_attn[:, half * 384 : half * 384 + 384]
    send_ga = paired(5, r.gattn.at[1 - core, pl.ds(0, 128)], r.gattn.at[1 - core, pl.ds(128, 128)])
    send_ga.start()
    mixed = dot_nt(grad_attn, r.v_out[...])
    r.gmix[...] = mixed.astype(BF)
    to_latent(r.gmix, r.v_upval, r.ga)
    send_out.wait()
    r.outbf[...] = (r.middle[...] + r.outacc[0:128] + r.outx[...]).astype(BF)
    r.layer_out[x_hi] = r.outbf[0:64]
    swap_out = swap(2, r.outbf.at[pl.ds(64, 64)], r.layer_out.at[x_hi])
    swap_out.start()
    ones = jnp.ones((8, 128), F32)
    for half in range(2):
        for p in range(6):
            here = (slice(half * 64, half * 64 + 64), slice(p * 128, p * 128 + 128))
            block = both(r.gmix[here].astype(F32) * r.aof[here])
            sums = lax.dot_general(
                ones, block, (((1,), (1,)), ((), ())), precision=lax.Precision.HIGHEST, preferred_element_type=F32
            )
            r.delta[half * 2 + p // 3, :, (p % 3) * 128 : (p % 3) * 128 + 128] = sums

    send_ao.wait()
    send_ga.wait()
    r.nmt[...] = r.ao2[...].T
    for o in range(3):
        block = dot(r.nmt[o * 256 : o * 256 + 256], r.gattn[core]).astype(BF)
        for i in range(3):
            r.out_total[o, i, 0] = block[:, i * 128 : i * 128 + 128]
        r.out_total[o, 3, 0] = jnp.zeros((256, 128), BF)
    outer.start(0)

    r.acc[...] = jnp.zeros_like(r.acc)
    r.dqr[...] = jnp.zeros_like(r.dqr)
    r.dlat[...] = jnp.zeros_like(r.dlat)
    r.dkr[...] = jnp.zeros_like(r.dkr)

    def backward_half(half):
        def chunk_step(step, inner):
            far, chunk, allowed = key_chunk(half, step)
            for g in range(2):
                at = half * 2 + g
                raw, keys = raw_scores(at, far, chunk, g)
                weights = jnp.exp2(raw * (FACTOR * LOG2E) - r.logs[at, 0:1])
                weights = jnp.where(allowed, weights, 0.0)
                dprob = dot_nt(keys, r.ga[at])
                dscore = (weights * (dprob - r.delta[at, 0:1])).astype(BF)
                weights = weights.astype(BF)
                r.acc[at] += dot(r.latt[far * 2 + g, chunk].reshape(256, 256), dscore)
                r.dqr[at] += dot(r.krt[far, chunk], dscore)
                r.dlat[far * 2 + g, chunk] += FACTOR * dot(dscore, r.qs[at]) + dot(weights, r.ga[at])
                r.dkr[chunk] += FACTOR * dot(dscore, r.qrx[far, at])
            return inner

        count = chosen(half, own_count) + chosen(half, far_count)
        lax.fori_loop(0, count, chunk_step, 0)

    backward_half(0)
    wide.step(0)
    backward_half(1)

    def narrow(step, carried):
        j, c = lax.div(step, 4), lax.rem(step, 4)
        r.latt[j, c] = r.dlat[j, c].astype(BF).reshape(4, 64, 256)
        return carried

    lax.fori_loop(0, 16, narrow, 0)
    for c in range(4):
        r.skr[c] = r.dkr[c].astype(BF).reshape(4, 64, 128)

    def scatter(part, phase):
        made = []
        axis = (1, 2)[(part + phase) % 2]
        for step in (1, 2, 3):
            peer = on_ring(place, axis, step)
            to = lax.rem(place[axis] + step, 4)
            at = step - 1
            if part == 0 and phase == 0:
                pieces = [(r.latt.at[pl.ds(0, 2), to], r.ro1.at[at]), (r.skr.at[to], r.rk1.at[at])]
            elif part == 0:
                pieces = [(r.so1.at[:, to], r.ro2.at[at]), (r.ks1.at[to], r.rk2.at[at])]
            elif phase == 0:
                pieces = [(r.latt.at[pl.ds(2, 2), :, to], r.rt1.at[at])]
            else:
                pieces = [(r.st1.at[:, to], r.rt2.at[at])]
            for k, (src, dst) in enumerate(pieces):
                sem = r.rs_sem.at[part, phase, k, at]
                made.append(remote(src, dst, sem.at[0], sem.at[1], peer))
        return made

    for part in range(2):
        for copy in scatter(part, 0):
            copy.start()

    wide.step(1)
    outer.step(0)

    for half in range(2):
        for p in range(6):
            rows, lanes = slice(half * 64, half * 64 + 64), slice((p % 3) * 128, (p % 3) * 128 + 128)
            at = half * 2 + p // 3
            piece = (FACTOR * from_latent(r.acc, r.v_upkey, half, p)).astype(BF)
            r.gq2[p // 3, rows, lanes] = piece
            turned = FACTOR * r.dqr[at, :, lanes].T
            turned = pick(turned + pltpu.roll(turned, 64, 1))
            turned = turned * r.cosine[rows, :] - swap_halves(turned) * r.sine[rows, :]
            r.gqp2[p // 3, rows, lanes] = turned.astype(BF)
    send_gq = paired(6, r.gq2.at[1 - core, pl.ds(0, 128)], r.gq2.at[1 - core, pl.ds(128, 128)])
    send_gqp = paired(7, r.gqp2.at[1 - core, pl.ds(0, 128)], r.gqp2.at[1 - core, pl.ds(128, 128)])
    send_gq.start()
    send_gqp.start()
    for g in range(2):
        for j in range(3):
            lanes = slice(j * 128, j * 128 + 128)
            wide_lanes = slice((g * 3 + j) * 128, (g * 3 + j) * 128 + 128)
            key_sum, value_sum = jnp.zeros((256, 128), F32), jnp.zeros((256, 128), F32)
            for half in range(2):
                rows = slice(half * 64, half * 64 + 64)
                key_sum += FACTOR * dot(r.acc[half * 2 + g, :, lanes].astype(BF), both(r.q[rows, wide_lanes]))
                value_sum += dot(r.ctx[half * 2 + g, :, lanes], both(r.gmix[rows, wide_lanes]))
            r.dup[g, 0, j] = key_sum.astype(BF)
            r.dup[g, 1, j] = value_sum.astype(BF)
    send_up = paired(8, r.dup.at[1 - core], r.sup)
    send_up.start()
    wide.step(2)
    grad_normed = dot_nt(r.gq2[0, 0:128], r.v_query[:, 0:384]) + dot_nt(r.gq2[1, 0:128], r.v_query[:, 384:768])
    grad_normed += dot_nt(r.gqp2[0, 0:128], r.v_qrope[:, 0:384]) + dot_nt(r.gqp2[1, 0:128], r.v_qrope[:, 384:768])
    r.gnm[0:128] = grad_normed
    send_norm.wait()
    r.normt[...] = r.norm2[...].T
    send_gq.wait()
    send_gqp.wait()
    send_up.wait()
    for o in range(3):
        rows = slice(o * 256, o * 256 + 256)
        for m, right in enumerate((r.gq2, r.gqp2)):
            block = dot(r.normt[rows], right[core]).astype(BF)
            for i in range(3):
                r.early_total[o, i, m] = block[:, i * 128 : i * 128 + 128]
            r.early_total[o, 3, m] = (r.dup[core, m, o].astype(F32) + r.sup[m, o].astype(F32)).astype(BF)
        early.start(0, (o,))

    outer.step(1)
    wide.step(3)
    for copy in scatter(0, 0) + scatter(1, 0):
        copy.wait()

    def fold(at, carried):
        for g in range(2):
            near = r.dlat[g, y, rows_at(at * 64, 64), :]
            far = r.dlat[2 + g, at, rows_at(z * 64, 64), :]
            for k in range(3):
                near = near + r.ro1[k, g, at].astype(F32)
                far = far + r.rt1[k, g, at].astype(F32)
            r.so1[g, at] = near.astype(BF)
            r.st1[g, at] = far.astype(BF)
        rot = r.dkr[y, rows_at(at * 64, 64), :]
        for k in range(3):
            rot = rot + r.rk1[k, at].astype(F32)
        r.ks1[at] = rot.astype(BF)
        return carried

    lax.fori_loop(0, 4, fold, 0)
    for part in range(2):
        for copy in scatter(part, 1):
            copy.start()
    outer.step(2)
    wide.step(4)
    early.step(0)
    for copy in scatter(0, 1) + scatter(1, 1):
        copy.wait()
    grad_latents = []
    for g in range(2):
        near = r.so1[g, z].astype(F32)
        far = r.st1[g, y].astype(F32)
        for k in range(3):
            near = near + r.ro2[k, g].astype(F32)
            far = far + r.rt2[k, g].astype(F32)
        piece = jnp.concatenate([near, far], axis=0).astype(BF)
        grad_latents.append(piece)
        r.gl2[g, 0:128] = piece
    send_gl = paired(9, r.gl2.at[1 - core, pl.ds(0, 128)], r.gl2.at[1 - core, pl.ds(128, 128)])
    send_gl.start()
    rot = r.ks1[z].astype(F32)
    for k in range(3):
        rot = rot + r.rk2[k].astype(F32)
    turned = pltpu.roll(rot, 64, 1)
    rot = jnp.concatenate([jnp.where(low64(64), rot, turned), jnp.where(low64(64), turned, rot)], axis=0)
    grad_kpre = (rot * r.cosine[...] - swap_halves(rot) * r.sine[...]).astype(BF)
    grad_normed = r.gnm[0:128] + dot(grad_kpre[:, 0:64], r.v_krope[...])
    for g in range(2):
        grad_normed = grad_normed + dot_nt(grad_latents[g], r.v_latent[:, g * 256 : g * 256 + 256])
    back, gain_attn = norm_back(grad_normed, r.xbuf[...].astype(F32), gain_of(r.norm_attn))
    r.outacc[0:128] = r.gmid[...] + back
    r.grad_tokens[x_hi] = r.outacc[0:64]
    swap_grad = swap(3, r.outacc.at[pl.ds(64, 64)], r.grad_tokens.at[x_hi])
    swap_grad.start()
    gains = r.gains[...]
    for p in range(6):
        gains = gains + jnp.where(gain_row == p, gain_attn[:, p * 128 : p * 128 + 128], 0.0)
    for o in range(3):
        r.late_total[o, 3, 0] = jnp.zeros((256, 128), BF)
    r.late_total[0, 3, 0, 0:16] = gains.astype(BF)
    send_gl.wait()
    for o in range(3):
        rows = slice(o * 256, o * 256 + 256)
        block = dot(r.normt[rows], r.gl2[core]).astype(BF)
        for i in range(2):
            r.late_total[o, i, 0] = block[:, i * 128 : i * 128 + 128]
        r.late_total[o, 2, 0] = dot(r.normt[rows, 0:128], grad_kpre).astype(BF)
        late.start(0, (o,))
    wide.step(5)
    outer.step(3)
    early.step(1)
    late.step(0, 1)
    wide.step(6)
    outer.step(4)
    early.step(2)
    late.step(2)
    outer.step(5)
    early.step(3)
    late.step(3)
    outer.step(6)
    early.step(4)
    late.step(4)
    wide.step(7)
    outer.step(7)
    early.step(5)
    late.step(5, 6)
    early.step(6)
    late.step(7)
    early.step(7)
    swap_out.wait()
    swap_grad.wait()
    for reduction in (wide, outer, early, late):
        reduction.finish(8)


def layer(small, weights):
    vmem = pl.BlockSpec(memory_space=pltpu.VMEM)
    hbm = pl.BlockSpec(memory_space=pl.ANY)
    smem = pl.BlockSpec(memory_space=pltpu.SMEM)
    return pl.pallas_call(
        layer_kernel,
        out_shape=[jax.ShapeDtypeStruct(shape, kind) for shape, kind in OUTS.values()],
        in_specs=[vmem] * 4 + [smem] * 2 + [hbm] * (1 + len(weights)),
        out_specs=[vmem, vmem] + [hbm] * (len(OUTS) - 2),
        scratch_shapes=list(scratch().values()),
        compiler_params=pltpu.CompilerParams(
            collective_id=1, has_side_effects=True, vmem_limit_bytes=63 * 2**20
        ),
    )(*small, jnp.asarray(rotary_table()), *weights)


def rotary_table():
    halves = ROPE // 2
    powers = -(np.arange(halves, dtype=np.float32) * np.float32(2.0) / np.float32(ROPE))
    freq_list = np.power(np.float32(10000.0), powers, dtype=np.float32)
    phases = (np.arange(2048, dtype=np.float32)[:, None] * freq_list[None, :]).astype(np.float32)
    cosine, sine = np.cos(phases), np.sin(phases)
    return np.concatenate([cosine, cosine, -sine, sine], axis=1).astype(np.float32)


CAST_STEPS = 12


def cast_kernel(
    gate, up, down, query, qrope, out, late,
    o_gate, o_up, o_down, o_query, o_qrope, o_out, o_latent, o_krope, o_upkey, o_upval, o_gains,
):
    o_gate[...] = gate[...].astype(F32)
    o_up[...] = up[...].astype(F32)
    o_down[...] = down[...].astype(F32)
    for source, target, width in ((query, o_query, 384), (qrope, o_qrope, 384), (out, o_out, 384), (late, o_latent, 256)):
        target[:, 0:width] = source[:, 0:width].astype(F32)
        target[:, width : 2 * width] = source[:, 512 : 512 + width].astype(F32)
    for source, target in ((query, o_upkey), (qrope, o_upval)):
        target[0] = source[:, 384:512].astype(F32)
        target[1] = source[:, 896:1024].astype(F32)
    o_krope[...] = late[:, 256:320].astype(F32) + late[:, 768:832].astype(F32)

    @pl.when(pl.program_id(0) == 0)
    def _():
        o_gains[...] = late[0:16, 384:512].astype(F32) + late[0:16, 896:1024].astype(F32)


def cast_sums(sums):
    rows = lambda width: pl.BlockSpec((64, width), lambda i: (i, 0))
    tall = pl.BlockSpec((1024, 128), lambda i: (lax.rem(i, 2), lax.div(i, 2)))
    ups = pl.BlockSpec((2, 64, 128), lambda i: (0, lax.rem(i, 4), lax.div(i, 4)))
    shapes = (
        (768, 2048), (768, 2048), (2048, 768), (768, 768), (768, 768), (768, 768), (768, 512), (768, 64),
        (2, 256, 384), (2, 256, 384), (16, 128),
    )
    return pl.pallas_call(
        cast_kernel,
        grid=(CAST_STEPS,),
        out_shape=[jax.ShapeDtypeStruct(shape, F32) for shape in shapes],
        in_specs=[rows(2048), rows(2048), tall] + [rows(1024)] * 4,
        out_specs=[rows(2048), rows(2048), tall] + [rows(768)] * 3 + [rows(512), rows(64), ups, ups]
        + [pl.BlockSpec((16, 128), lambda i: (0, 0))],
        compiler_params=pltpu.CompilerParams(vmem_limit_bytes=40 * 2**20),
    )(*sums)


def local(
    tokens, cotangent, group_of_seq, group_weight, norm_attn, w_query, w_qrope, w_latent, w_krope, w_upkey, w_upval,
    w_out, norm_mlp, w_gate, w_up, w_down,
):
    small = (tokens, cotangent, norm_attn, norm_mlp, group_of_seq, group_weight)
    weights = (w_latent, w_krope.T, w_query, w_qrope, w_upkey, w_upval, w_out, w_gate, w_up, w_down)
    layer_out, grad_tokens, *sums = layer(small, weights)
    gate, up, down, query, qrope, out, latent, krope, upkey, upval, gains = cast_sums(sums)
    return (
        layer_out,
        grad_tokens,
        gains[0:6].reshape(768),
        query,
        qrope,
        latent,
        krope,
        upkey,
        upval,
        out,
        gains[6:12].reshape(768),
        gate,
        up,
        down,
    )


def solution(mesh):
    split = P("seq", "blk", None)
    in_specs = (split, split, P("seq")) + (P(),) * 13
    out_specs = (split, split) + (P(),) * 12
    return jax.shard_map(local, mesh=mesh, in_specs=in_specs, out_specs=out_specs, check_vma=False)
```

```python
import jax
import jax.numpy as jnp
import numpy as np
from jax import lax
from jax.sharding import PartitionSpec as P
from jax.experimental import pallas as pl
from jax.experimental.pallas import tpu as pltpu

MESH = pl.DeviceIdType.MESH
BF = jnp.bfloat16
F32 = jnp.float32
EPSILON = 1e-06
ROPE = 64
GROUPS = 4
FACTOR = 128.0**-0.5
LOG2E = 1.4426950408889634
HIDDEN_SCORE = -1e30
ORDERS = ((0, 1, 2), (1, 2, 0), (2, 0, 1))
X_FIRST = ((0, 1, 2), (0, 2, 1), (0, 1, 2))


def coords():
    s = lax.axis_index("seq")
    b = lax.axis_index("blk")
    x = lax.rem(b, 2) * 2 + lax.div(s, 2)
    return x, lax.div(b, 8), lax.rem(lax.div(b, 2), 4), lax.rem(s, 2)


def device(x, y, z, core):
    return (lax.rem(x, 2) * 2 + core, y * 8 + z * 2 + lax.div(x, 2))


def on_ring(place, axis, step):
    spot = list(place)
    spot[axis] = lax.rem(place[axis] + step, 4)
    return device(*spot)


def remote(src, dst, send, recv, peer):
    return pltpu.make_async_remote_copy(
        src_ref=src, dst_ref=dst, send_sem=send, recv_sem=recv, device_id=peer, device_id_type=MESH
    )


def rows_at(start, size, multiple=16):
    return pl.ds(pl.multiple_of(start, multiple), size)


def dot(left, right):
    return jnp.dot(left, right, preferred_element_type=F32)


def dot_nt(left, right):
    return lax.dot_general(left, right, (((1,), (1,)), ((), ())), preferred_element_type=F32)


def dot_tn(left, right):
    return lax.dot_general(left, right, (((0,), (0,)), ((), ())), preferred_element_type=F32)


class Reduction:
    def __init__(self, r, name, place, out, halving, flat=False, orders=ORDERS):
        self.place, self.out, self.halving, self.flat, self.orders = place, out, halving, flat, orders
        for part in ("total", "first", "second", "third", "chunk", "send", "recv", "keep"):
            setattr(self, part, getattr(r, name + "_" + part))
        self.n, self.width = self.total.shape[2], self.total.shape[4]
        counts = stage_counts(halving, flat)
        self.base = [sum(counts[:stage]) for stage in range(9)]

    def spots(self, o):
        a, b, c = self.orders[o]
        return self.place[a], self.place[b], self.place[c]

    def sides(self, o, s):
        me = self.place[self.orders[o][0]]
        odd = lax.rem(me, 2)
        near, far = 1 + 2 * odd, 3 - 2 * odd
        steps = (near, far) if s == 0 else (far, near)
        return steps, lax.rem(me + steps[0], 4), lax.rem(me + steps[1], 4), lax.rem(me + 2, 4)

    def region(self, o, i, row, rows, count=1):
        core, width = self.place[3], self.width
        return self.out.at[:, rows_at(o * 256 + row, rows), rows_at((core * 4 + i) * width, count * width, 128)]

    def moves(self, o, stage):
        i, j, k = self.spots(o)
        if stage == 8:
            x, y, z, core = self.place
            here = self.region(o, 0, 0, 256, 4)
            return [(here, here, device(x, y, z, 1 - core))]
        made = []
        axis = self.orders[o][(0, 0, 1, 2, 2, 1, 0, 0)[stage]]
        if stage in (0, 1, 6, 7) and self.halving:
            for s in range(2):
                steps, front, last, across = self.sides(o, s)
                half = pl.ds(s * 128, 128)
                peer = on_ring(self.place, axis, steps[0 if stage in (0, 7) else 1])
                if stage == 0:
                    made.append((self.total.at[o, front, :, half], self.first.at[o, s, 0], peer))
                    made.append((self.total.at[o, across, :, half], self.first.at[o, s, 1], peer))
                elif stage == 1:
                    made.append((self.total.at[o, last, :, half], self.first.at[o, s, 2], peer))
                else:
                    for spot in (i, last) if stage == 7 else (i,):
                        here = self.region(o, spot, s * 128, 128)
                        made.append((here, here, peer))
            return made
        if stage in (1, 6) or (stage == 4 and self.flat):
            return made
        for step in (1, 2, 3):
            to = lax.rem(self.place[axis] + step, 4)
            peer = on_ring(self.place, axis, step)
            at = step - 1
            if stage == 0:
                made.append((self.total.at[o, to], self.first.at[o, at], peer))
            elif stage == 2:
                made.append((self.total.at[o, i, :, rows_at(to * 64, 64)], self.second.at[o, at], peer))
            elif stage == 3 and self.flat:
                made.append((self.total.at[o, i, :, rows_at(j * 64, 64)], self.third.at[o, k], peer))
            elif stage == 3:
                made.append((self.total.at[o, i, :, rows_at(j * 64 + to * 16, 16)], self.third.at[o, at], peer))
            elif stage == 4:
                made.append((self.chunk.at[o], self.region(o, i, j * 64 + k * 16, 16), peer))
            elif stage == 5:
                here = self.region(o, i, j * 64, 64)
                made.append((self.chunk.at[o] if self.flat else here, here, peer))
            else:
                here = self.region(o, i, 0, 256)
                made.append((here, here, peer))
        return made

    def copies(self, o, stage):
        return [
            remote(src, dst, self.send.at[o, at], self.recv.at[o, self.base[stage] + at], peer)
            for at, (src, dst, peer) in enumerate(self.moves(o, stage))
        ]

    def kept(self, o):
        i, j, k = self.spots(o)
        row, rows = (j * 64, 64) if self.flat else (j * 64 + k * 16, 16)
        return pltpu.make_async_copy(self.chunk.at[o], self.region(o, i, row, rows), self.keep.at[o])

    def start(self, stage, orders=(0, 1, 2)):
        for o in orders:
            for copy in self.copies(o, stage):
                copy.start()
            if stage == 4:
                self.kept(o).start()

    def finish(self, stage, orders=(0, 1, 2)):
        for o in orders:
            for copy in self.copies(o, stage):
                copy.wait()
            if stage == 4:
                self.kept(o).wait()
            if stage < 4:
                self.add(o, stage)

    def step(self, *stages):
        for stage in stages:
            for o in range(3):
                self.finish(stage, (o,))
                self.start(stage + 1, (o,))

    def add(self, o, stage):
        i, j, k = self.spots(o)
        if stage == 1 and not self.halving:
            return

        def body(m, carried):
            if stage < 2 and self.halving:
                for s in range(2):
                    _, _, last, _ = self.sides(o, s)
                    half = slice(s * 128, s * 128 + 128)
                    for spot, slot in ((i, 0), (last, 1)) if stage == 0 else ((i, 2),):
                        acc = self.total[o, spot, m, half, :].astype(F32) + self.first[o, s, slot, m].astype(F32)
                        self.total[o, spot, m, half, :] = acc.astype(BF)
            elif stage == 0:
                for part in range(4):
                    rows = slice(part * 64, part * 64 + 64)
                    acc = self.total[o, i, m, rows, :].astype(F32)
                    for slot in range(3):
                        acc = acc + self.first[o, slot, m, rows, :].astype(F32)
                    self.total[o, i, m, rows, :] = acc.astype(BF)
            elif stage == 2:
                rows = rows_at(j * 64, 64)
                acc = self.total[o, i, m, rows, :].astype(F32)
                for slot in range(3):
                    acc = acc + self.second[o, slot, m].astype(F32)
                self.total[o, i, m, rows, :] = acc.astype(BF)
            elif self.flat:
                self.third[o, k, m] = self.total[o, i, m, rows_at(j * 64, 64), :]
                acc = self.third[o, 0, m].astype(F32)
                for slot in range(1, 4):
                    acc = acc + self.third[o, slot, m].astype(F32)
                self.chunk[o, m] = acc.astype(BF)
            else:
                acc = self.total[o, i, m, rows_at(j * 64 + k * 16, 16), :].astype(F32)
                for slot in range(3):
                    acc = acc + self.third[o, slot, m].astype(F32)
                self.chunk[o, m] = acc.astype(BF)
            return carried

        lax.fori_loop(0, self.n, body, 0)


def stage_counts(halving, flat):
    return (4 if halving else 3, 2 if halving else 0, 3, 3, 0 if flat else 3, 3, 2 if halving else 0, 4 if halving else 3, 1)


def reduction_scratch(name, n, width, halving, flat=False):
    return {
        name + "_total": pltpu.VMEM((3, 4, n, 256, width), BF),
        name + "_first": pltpu.VMEM((3, 2, 3, n, 128, width) if halving else (3, 3, n, 256, width), BF),
        name + "_second": pltpu.VMEM((3, 3, n, 64, width), BF),
        name + "_third": pltpu.VMEM((3, 4, n, 64, width) if flat else (3, 3, n, 16, width), BF),
        name + "_chunk": pltpu.VMEM((3, n, 64 if flat else 16, width), BF),
        name + "_send": pltpu.SemaphoreType.DMA((3, 4)),
        name + "_recv": pltpu.SemaphoreType.DMA((3, sum(stage_counts(halving, flat)))),
        name + "_keep": pltpu.SemaphoreType.DMA((3,)),
    }


WEIGHTS = {
    "w_latent": (768, 512),
    "w_krope": (64, 768),
    "w_query": (768, 768),
    "w_qrope": (768, 768),
    "w_upkey": (2, 256, 384),
    "w_upval": (2, 256, 384),
    "w_out": (768, 768),
    "w_gate": (768, 1024),
    "w_up": (768, 1024),
    "w_down": (1024, 768),
}
SMALL = ("tokens", "cotangent", "norm_attn", "norm_mlp", "group_of_seq", "group_weight")
OUTS = {
    "layer_out": ((2, 64, 768), BF),
    "grad_tokens": ((2, 64, 768), F32),
    "g_wide": ((3, 768, 2048), BF),
    "g_out": ((1, 768, 1024), BF),
    "g_early": ((2, 768, 1024), BF),
    "g_late": ((1, 768, 1024), BF),
}


def scratch():
    vmem, dma = pltpu.VMEM, pltpu.SemaphoreType.DMA
    made = {"v" + name[1:]: vmem(shape, BF) for name, shape in WEIGHTS.items()}
    made.update(
        load_sem=dma((len(WEIGHTS),)),
        table_sem=dma((2,)),
        turns=vmem((128, 128), F32),
        cosine=vmem((128, 128), F32),
        sine=vmem((128, 128), F32),
        swap_sem=dma((4, 2)),
        pair_sem=dma((12, 2)),
        lat_send=dma((2, 2, 3)),
        lat_recv=dma((2, 2, 2, 2, 3)),
        xbuf=vmem((128, 768), BF),
        cbuf=vmem((128, 768), BF),
        norm2=vmem((256, 768), BF),
        normt=vmem((768, 256), BF),
        krd=vmem((128, 128), F32),
        q=vmem((128, 768), BF),
        qr=vmem((128, 768), BF),
        lat=vmem((4, 4, 4, 64, 256), BF),
        kr=vmem((4, 4, 64, 128), BF),
        latt=vmem((4, 4, 4, 64, 256), BF),
        krt=vmem((2, 4, 128, 256), BF),
        rel=vmem((2, 256, 384), jnp.int32),
        qs=vmem((4, 384, 256), BF),
        ga=vmem((4, 384, 256), BF),
        qrx=vmem((2, 4, 384, 128), BF),
        acc=vmem((4, 256, 384), F32),
        ctx=vmem((4, 256, 384), BF),
        logs=vmem((4, 8, 384), F32),
        delta=vmem((4, 8, 384), F32),
        aof=vmem((128, 768), F32),
        ao2=vmem((256, 768), BF),
        middle=vmem((128, 768), F32),
        nm2=vmem((256, 768), BF),
        nmt=vmem((768, 256), BF),
        gb2=vmem((256, 768), BF),
        acts=vmem((3, 256, 1024), BF),
        hidt=vmem((1024, 256), BF),
        outacc=vmem((256, 768), F32),
        gnm=vmem((256, 768), F32),
        outx=vmem((128, 768), F32),
        gnmx=vmem((128, 768), F32),
        outbf=vmem((128, 768), BF),
        gattn=vmem((2, 256, 384), BF),
        gmix=vmem((128, 768), BF),
        dqr=vmem((4, 128, 384), F32),
        dlat=vmem((4, 4, 256, 256), F32),
        dkr=vmem((4, 256, 128), F32),
        skr=vmem((4, 4, 64, 128), BF),
        ro1=vmem((3, 2, 4, 64, 256), BF),
        rk1=vmem((3, 4, 64, 128), BF),
        rt1=vmem((3, 2, 4, 64, 256), BF),
        so1=vmem((2, 4, 64, 256), BF),
        ks1=vmem((4, 64, 128), BF),
        st1=vmem((2, 4, 64, 256), BF),
        ro2=vmem((3, 2, 64, 256), BF),
        rk2=vmem((3, 64, 128), BF),
        rt2=vmem((3, 2, 64, 256), BF),
        gq2=vmem((2, 256, 384), BF),
        gqp2=vmem((2, 256, 384), BF),
        gl2=vmem((2, 256, 256), BF),
        dup=vmem((2, 2, 3, 256, 128), BF),
        sup=vmem((2, 3, 256, 128), BF),
        gmid=vmem((128, 768), F32),
        gains=vmem((16, 128), F32),
    )
    made.update(reduction_scratch("wide", 3, 256, True))
    made.update(reduction_scratch("out", 1, 128, False))
    made.update(reduction_scratch("early", 2, 128, False, True))
    made.update(reduction_scratch("late", 1, 128, False, True))
    return made


class Refs:
    pass


def swap_halves(values):
    lanes = values.shape[-1]
    low = lax.rem(lax.broadcasted_iota(jnp.int32, values.shape, 1), 64) < 32
    return jnp.where(low, pltpu.roll(values, lanes - 32, 1), pltpu.roll(values, 32, 1))


def layer_kernel(*args):
    r = Refs()
    shapes = scratch()
    names = list(SMALL) + ["table"] + list(WEIGHTS) + list(OUTS) + list(shapes)
    for name, ref in zip(names, args, strict=True):
        setattr(r, name, ref)
    place = coords()
    x, y, z, core = place
    x_hi = lax.div(x, 2)
    blk = y * 8 + z * 2 + x_hi
    slot = y * 4 + z
    sibling = device(x, y, z, 1 - core)
    partner = device(lax.rem(x + 2, 4), 3 - y, 3 - z, core)
    peers = [on_ring(place, axis, step) for axis in range(3) for step in (1, 2, 3)] + [sibling, partner]
    low64 = lambda rows: lax.broadcasted_iota(jnp.int32, (rows, 128), 1) < 64
    diagonal = (lax.broadcasted_iota(jnp.int32, (128, 128), 0) < 64) == low64(128)

    def gain_of(ref):
        return ref[...].reshape(1, 768)

    def both(value):
        return jnp.where(diagonal, jnp.concatenate([value, value], axis=0), jnp.zeros((), value.dtype))

    def pick(value):
        return jnp.where(low64(64), value[0:64], value[64:128])

    loads = {}
    for at, name in enumerate(WEIGHTS):
        source = getattr(r, name)
        if name in ("w_gate", "w_up"):
            source = source.at[:, rows_at(core * 1024, 1024, 128)]
        elif name == "w_down":
            source = source.at[rows_at(core * 1024, 1024), :]
        loads[name] = pltpu.make_async_copy(source, getattr(r, "v" + name[1:]), r.load_sem.at[at])
    tables = [
        pltpu.make_async_copy(
            r.table.at[rows_at(where * 64, 64)], r.turns.at[pl.ds(half * 64, 64)], r.table_sem.at[half]
        )
        for half, where in enumerate((blk, 31 - blk))
    ]
    loads["w_latent"].start()
    loads["w_krope"].start()
    for table in tables:
        table.start()
    barrier = pltpu.get_barrier_semaphore()
    for peer in peers:
        pl.semaphore_signal(barrier, inc=1, device_id=peer, device_id_type=MESH)
    pl.semaphore_wait(barrier, len(peers))

    def swap(at, src, dst):
        return remote(src, dst, r.swap_sem.at[at, 0], r.swap_sem.at[at, 1], partner)

    def paired(at, src, dst):
        return remote(src, dst, r.pair_sem.at[at, 0], r.pair_sem.at[at, 1], sibling)

    swap_x = swap(0, r.tokens.at[1 - x_hi], r.xbuf.at[pl.ds(64, 64)])
    swap_c = swap(1, r.cotangent.at[1 - x_hi], r.cbuf.at[pl.ds(64, 64)])
    swap_x.start()
    swap_c.start()
    for name in ("w_query", "w_qrope", "w_upkey"):
        loads[name].start()
    r.xbuf[0:64] = r.tokens[x_hi]
    r.cbuf[0:64] = r.cotangent[x_hi]
    key_row = lax.broadcasted_iota(jnp.int32, (256, 384), 0)
    query_lane = lax.rem(lax.broadcasted_iota(jnp.int32, (256, 384), 1), 64)
    within = lax.rem(key_row, 64) - query_lane
    r.rel[0] = 128 * lax.div(key_row, 64) + within
    r.rel[1] = within - 128 * lax.div(key_row, 64)
    for table in tables:
        table.wait()
    turns = r.turns[...]
    other = pltpu.roll(turns, 64, 1)
    r.cosine[...] = jnp.where(low64(128), turns, other)
    r.sine[...] = jnp.where(low64(128), other, turns)
    swap_x.wait()

    def unit_of(values):
        inverse = lax.rsqrt(jnp.mean(values * values, axis=-1, keepdims=True) + EPSILON)
        return values * inverse, inverse

    unit = unit_of(r.xbuf[...].astype(F32))[0]
    normed = (unit * gain_of(r.norm_attn)).astype(BF)
    r.norm2[0:128] = normed
    send_norm = paired(0, r.norm2.at[pl.ds(0, 128)], r.norm2.at[pl.ds(128, 128)])
    send_norm.start()
    loads["w_latent"].wait()
    loads["w_krope"].wait()
    key_pre = dot_nt(normed, r.v_krope[...])
    r.krd[:, 0:64] = key_pre
    r.krd[:, 64:128] = key_pre
    key_pre = r.krd[...]
    key_rot = (key_pre * r.cosine[...] + swap_halves(key_pre) * r.sine[...]).astype(BF)
    r.kr[y, z] = pick(key_rot)
    latents = dot(normed, r.v_latent[...]).astype(BF)
    for half in range(2):
        for g in range(2):
            r.lat[half * 2 + g, y, z] = latents[half * 64 : half * 64 + 64, g * 256 : g * 256 + 256]

    def gather(part, phase):
        made = []
        axis = (2, 1)[(part + phase) % 2]
        for step in (1, 2, 3):
            peer = on_ring(place, axis, step)
            two = pl.ds(part * 2, 2)
            if phase == 0:
                pieces = [r.lat.at[two, y, z], r.kr.at[y, z]]
            elif part == 0:
                pieces = [r.lat.at[two, y], r.kr.at[y]]
            else:
                pieces = [r.lat.at[two, :, z], None]
            for at, piece in enumerate(pieces if part == 0 else pieces[:1]):
                send = r.lat_send.at[part, at, step - 1]
                made.append(remote(piece, piece, send, r.lat_recv.at[0, part, phase, at, step - 1], peer))
        return made

    for part in range(2):
        for copy in gather(part, 0):
            copy.start()
    for name in ("w_upval", "w_out", "w_gate", "w_up", "w_down"):
        loads[name].start()

    loads["w_query"].wait()
    r.q[...] = dot(normed, r.v_query[...]).astype(BF)
    loads["w_qrope"].wait()
    query_pre = dot(normed, r.v_qrope[...])
    for p in range(6):
        lanes = slice(p * 128, p * 128 + 128)
        piece = query_pre[:, lanes]
        r.qr[:, lanes] = (piece * r.cosine[...] + swap_halves(piece) * r.sine[...]).astype(BF)
    loads["w_upkey"].wait()

    def to_latent(source, weights, target):
        for half in range(2):
            for g in range(2):
                for j in range(3):
                    p = g * 3 + j
                    block = both(source[half * 64 : half * 64 + 64, p * 128 : p * 128 + 128])
                    rows = dot_nt(block, weights[g, :, j * 128 : j * 128 + 128])
                    target[half * 2 + g, j * 128 : j * 128 + 128] = rows.astype(BF)

    to_latent(r.q, r.v_upkey, r.qs)
    for half in range(2):
        for p in range(6):
            pair = r.qr[half * 64 : half * 64 + 64, p * 128 : p * 128 + 128].astype(F32)
            turned = pltpu.roll(pair, 64, 1)
            for odd in range(2):
                front, back = (turned, pair) if odd else (pair, turned)
                at = (p % 3) * 128 + odd * 64
                here = (half * 2 + p // 3, slice(at, at + 64))
                r.qrx[(0,) + here] = jnp.where(low64(64), front, 0.0).astype(BF)
                r.qrx[(1,) + here] = jnp.where(low64(64), 0.0, back).astype(BF)

    for part in (1, 0):
        for copy in gather(part, 0):
            copy.wait()
        for copy in gather(part, 1):
            copy.start()

    def transpose_latents():
        def body(step, carried):
            j, c = lax.div(step, 4), lax.rem(step, 4)
            r.latt[j, c] = r.lat[j, c].reshape(256, 256).T.reshape(4, 64, 256)
            return carried

        lax.fori_loop(0, 16, body, 0)

    query_blk = (blk, 31 - blk)

    counts = (y + 1, 4 - y)

    def masks(half, step):
        first = query_blk[half] * 64
        near = r.rel[0] <= first - 512 * step - 64 * x_hi
        far = r.rel[1] <= first - 1984 + 512 * (3 - step) + 64 * x_hi
        return (step, near), (3 - step, far)

    def raw_scores(at, far, chunk, g):
        keys = r.lat[far * 2 + g, chunk].reshape(256, 256)
        rot = r.kr[chunk].reshape(256, 128)
        return dot_nt(keys, r.qs[at]) + dot_nt(rot, r.qrx[far, at]), keys

    r.acc[...] = jnp.zeros_like(r.acc)
    for copy in gather(1, 1) + gather(0, 1):
        copy.wait()
    top = lax.broadcasted_iota(jnp.int32, (128, 256), 0) < 64
    for c in range(4):
        turned = r.kr[c].reshape(256, 128).astype(F32).T
        r.krt[0, c] = jnp.where(top, turned, 0.0).astype(BF)
        r.krt[1, c] = jnp.where(top, 0.0, turned).astype(BF)
    transpose_latents()

    def forward(half):
        def chunk_step(step, state):
            places = masks(half, step)
            result = []
            for g in range(2):
                at = half * 2 + g
                high, total = state[g]
                raws = [
                    jnp.where(allowed, raw_scores(at, far, chunk, g)[0], HIDDEN_SCORE)
                    for far, (chunk, allowed) in enumerate(places)
                ]
                new_high = jnp.maximum(high, jnp.max(jnp.maximum(*raws), axis=0, keepdims=True))
                shrink = jnp.exp2((high - new_high) * (FACTOR * LOG2E))
                weights = [jnp.exp2((raw - new_high) * (FACTOR * LOG2E)) for raw in raws]
                total = total * shrink + jnp.sum(weights[0] + weights[1], axis=0, keepdims=True)
                mixed = r.acc[at] * shrink
                for far, (chunk, _) in enumerate(places):
                    value = r.latt[far * 2 + g, chunk].reshape(256, 256)
                    mixed = mixed + dot(value, weights[far].astype(BF))
                r.acc[at] = mixed
                result.append((new_high, total))
            return tuple(result)

        empty = (jnp.full((1, 384), HIDDEN_SCORE, F32), jnp.zeros((1, 384), F32))
        state = lax.fori_loop(0, counts[half], chunk_step, (empty, empty))
        for g in range(2):
            high, total = state[g]
            at = half * 2 + g
            r.ctx[at] = (r.acc[at] * (1.0 / total)).astype(BF)
            r.logs[at, 0:1] = high * (FACTOR * LOG2E) + jnp.log2(total)

    forward(0)
    forward(1)
    loads["w_upval"].wait()

    def from_latent(source, weights, half, p):
        g, j = p // 3, p % 3
        lanes = slice(j * 128, j * 128 + 128)
        return pick(dot_tn(source[half * 2 + g, :, lanes].astype(BF), weights[g, :, lanes]))

    for half in range(2):
        for p in range(6):
            r.aof[half * 64 : half * 64 + 64, p * 128 : p * 128 + 128] = from_latent(r.ctx, r.v_upval, half, p)
    r.ao2[0:128] = r.aof[...].astype(BF)
    send_ao = paired(1, r.ao2.at[pl.ds(0, 128)], r.ao2.at[pl.ds(128, 128)])
    send_ao.start()

    loads["w_out"].wait()
    middle = r.xbuf[...].astype(F32) + dot(r.ao2[0:128], r.v_out[...])
    r.middle[...] = middle
    unit_mlp = unit_of(middle)[0]
    r.nm2[0:128] = (unit_mlp * gain_of(r.norm_mlp)).astype(BF)
    send_nm = paired(2, r.nm2.at[pl.ds(0, 128)], r.nm2.at[pl.ds(128, 128)])
    send_nm.start()
    swap_c.wait()
    group = jnp.where(x_hi == 0, r.group_of_seq[0], r.group_of_seq[1])
    weight = r.group_weight[0]
    for g in range(1, GROUPS):
        weight = jnp.where(group == g, r.group_weight[g], weight)
    r.gb2[0:128] = (r.cbuf[...].astype(F32) * weight).astype(BF)
    send_gb = paired(3, r.gb2.at[pl.ds(0, 128)], r.gb2.at[pl.ds(128, 128)])
    send_gb.start()
    r.outacc[...] = jnp.zeros_like(r.outacc)
    r.gnm[...] = jnp.zeros_like(r.gnm)
    for name in ("w_gate", "w_up", "w_down"):
        loads[name].wait()
    send_nm.wait()
    send_gb.wait()

    def tile(step, carried):
        at = rows_at(step * 256, 256, 256)
        act = r.nm2[...]
        gate = dot(act, r.v_gate[:, at])
        up = dot(act, r.v_up[:, at])
        sig = jax.nn.sigmoid(gate)
        silu = gate * sig
        hidden = (silu * up).astype(BF)
        grad_hidden = dot_nt(r.gb2[...], r.v_down[at, :])
        grad_gate = (grad_hidden * up * sig * (1.0 + gate * (1.0 - sig))).astype(BF)
        grad_up = (grad_hidden * silu).astype(BF)
        r.acts[0, :, at] = hidden
        r.acts[1, :, at] = grad_gate
        r.acts[2, :, at] = grad_up
        r.outacc[...] += dot(hidden, r.v_down[at, :])
        r.gnm[...] += dot_nt(grad_gate, r.v_gate[:, at]) + dot_nt(grad_up, r.v_up[:, at])
        return carried

    lax.fori_loop(0, 4, tile, 0)
    send_gnm = paired(4, r.gnm.at[pl.ds(128, 128)], r.gnmx)
    send_out = paired(10, r.outacc.at[pl.ds(128, 128)], r.outx)
    send_gnm.start()
    send_out.start()

    wide = Reduction(r, "wide", place, r.g_wide, True)
    outer = Reduction(r, "out", place, r.g_out, False)
    early = Reduction(r, "early", place, r.g_early, False, True)
    late = Reduction(r, "late", place, r.g_late, False, True)
    r.nmt[...] = r.nm2[...].T
    r.hidt[...] = r.acts[0].T
    for o in range(3):

        def wide_tile(i, carried):
            cols = rows_at(i * 256, 256, 256)
            left = r.nmt[o * 256 : o * 256 + 256]
            r.wide_total[o, i, 0] = dot(left, r.acts[1, :, cols]).astype(BF)
            r.wide_total[o, i, 1] = dot(left, r.acts[2, :, cols]).astype(BF)
            r.wide_total[o, i, 2] = dot(r.hidt[cols, :], r.gb2[:, o * 256 : o * 256 + 256]).astype(BF)
            return carried

        lax.fori_loop(0, 4, wide_tile, 0)
        wide.start(0, (o,))

    def norm_back(grads, values, gain):
        unit_rows, inverse = unit_of(values)
        scaled = grads * gain
        gain_grad = jnp.sum(grads * unit_rows, axis=0, keepdims=True)
        mean = jnp.mean(scaled * unit_rows, axis=-1, keepdims=True)
        return inverse * (scaled - unit_rows * mean), gain_grad

    send_gnm.wait()
    back, gain_mlp = norm_back(r.gnm[0:128] + r.gnmx[...], r.middle[...], gain_of(r.norm_mlp))
    r.gmid[...] = r.cbuf[...].astype(F32) * weight + back
    gain_row = lax.broadcasted_iota(jnp.int32, (16, 128), 0)
    gains = jnp.zeros((16, 128), F32)
    for p in range(6):
        gains = gains + jnp.where(gain_row == 6 + p, gain_mlp[:, p * 128 : p * 128 + 128], 0.0)
    r.gains[...] = gains
    grad_attn = r.gmid[...].astype(BF)
    for half in range(2):
        r.gattn[half, 0:128] = grad_attn[:, half * 384 : half * 384 + 384]
    send_ga = paired(5, r.gattn.at[1 - core, pl.ds(0, 128)], r.gattn.at[1 - core, pl.ds(128, 128)])
    send_ga.start()
    mixed = dot_nt(grad_attn, r.v_out[...])
    r.gmix[...] = mixed.astype(BF)
    to_latent(r.gmix, r.v_upval, r.ga)
    send_out.wait()
    r.outbf[...] = (r.middle[...] + r.outacc[0:128] + r.outx[...]).astype(BF)
    r.layer_out[x_hi] = r.outbf[0:64]
    swap_out = swap(2, r.outbf.at[pl.ds(64, 64)], r.layer_out.at[x_hi])
    swap_out.start()
    ones = jnp.ones((8, 128), F32)
    for half in range(2):
        for p in range(6):
            here = (slice(half * 64, half * 64 + 64), slice(p * 128, p * 128 + 128))
            block = both(r.gmix[here].astype(F32) * r.aof[here])
            sums = lax.dot_general(
                ones, block, (((1,), (1,)), ((), ())), precision=lax.Precision.HIGHEST, preferred_element_type=F32
            )
            r.delta[half * 2 + p // 3, :, (p % 3) * 128 : (p % 3) * 128 + 128] = sums

    send_ao.wait()
    send_ga.wait()
    r.nmt[...] = r.ao2[...].T
    for o in range(3):
        block = dot(r.nmt[o * 256 : o * 256 + 256], r.gattn[core]).astype(BF)
        for i in range(3):
            r.out_total[o, i, 0] = block[:, i * 128 : i * 128 + 128]
        r.out_total[o, 3, 0] = jnp.zeros((256, 128), BF)
    outer.start(0)

    r.acc[...] = jnp.zeros_like(r.acc)
    r.dqr[...] = jnp.zeros_like(r.dqr)
    r.dlat[...] = jnp.zeros_like(r.dlat)
    r.dkr[...] = jnp.zeros_like(r.dkr)

    def backward(half):
        def chunk_step(step, carried):
            places = masks(half, step)
            for g in range(2):
                at = half * 2 + g
                mixed, turned = r.acc[at], r.dqr[at]
                for far, (chunk, allowed) in enumerate(places):
                    raw, keys = raw_scores(at, far, chunk, g)
                    weights = jnp.exp2(raw * (FACTOR * LOG2E) - r.logs[at, 0:1])
                    weights = jnp.where(allowed, weights, 0.0)
                    dprob = dot_nt(keys, r.ga[at])
                    dscore = (weights * (dprob - r.delta[at, 0:1])).astype(BF)
                    weights = weights.astype(BF)
                    mixed = mixed + dot(r.latt[far * 2 + g, chunk].reshape(256, 256), dscore)
                    turned = turned + dot(r.krt[far, chunk], dscore)
                    r.dlat[far * 2 + g, chunk] += FACTOR * dot(dscore, r.qs[at]) + dot(weights, r.ga[at])
                    r.dkr[chunk] += FACTOR * dot(dscore, r.qrx[far, at])
                r.acc[at], r.dqr[at] = mixed, turned
            return carried

        lax.fori_loop(0, counts[half], chunk_step, 0)

    def narrow(step, carried):
        j, c = lax.div(step, 4), lax.rem(step, 4)
        r.latt[j, c] = r.dlat[j, c].astype(BF).reshape(4, 64, 256)
        return carried

    def scatter(part, phase):
        made = []
        axis = (1, 2)[(part + phase) % 2]
        for step in (1, 2, 3):
            peer = on_ring(place, axis, step)
            to = lax.rem(place[axis] + step, 4)
            at = step - 1
            if part == 0 and phase == 0:
                pieces = [(r.latt.at[pl.ds(0, 2), to], r.ro1.at[at]), (r.skr.at[to], r.rk1.at[at])]
            elif part == 0:
                pieces = [(r.so1.at[:, to], r.ro2.at[at]), (r.ks1.at[to], r.rk2.at[at])]
            elif phase == 0:
                pieces = [(r.latt.at[pl.ds(2, 2), :, to], r.rt1.at[at])]
            else:
                pieces = [(r.st1.at[:, to], r.rt2.at[at])]
            for k, (src, dst) in enumerate(pieces):
                send = r.lat_send.at[part, k, at]
                made.append(remote(src, dst, send, r.lat_recv.at[1, part, phase, k, at], peer))
        return made

    backward(0)
    wide.step(0)
    backward(1)
    lax.fori_loop(0, 16, narrow, 0)
    for c in range(4):
        r.skr[c] = r.dkr[c].astype(BF).reshape(4, 64, 128)
    for copy in scatter(1, 0) + scatter(0, 0):
        copy.start()
    wide.step(1)
    outer.step(0, 1)

    for half in range(2):
        for p in range(6):
            rows, lanes = slice(half * 64, half * 64 + 64), slice((p % 3) * 128, (p % 3) * 128 + 128)
            at = half * 2 + p // 3
            piece = (FACTOR * from_latent(r.acc, r.v_upkey, half, p)).astype(BF)
            r.gq2[p // 3, rows, lanes] = piece
            turned = FACTOR * r.dqr[at, :, lanes].T
            turned = pick(turned + pltpu.roll(turned, 64, 1))
            turned = turned * r.cosine[rows, :] - swap_halves(turned) * r.sine[rows, :]
            r.gqp2[p // 3, rows, lanes] = turned.astype(BF)
    send_gq = paired(6, r.gq2.at[1 - core, pl.ds(0, 128)], r.gq2.at[1 - core, pl.ds(128, 128)])
    send_gqp = paired(7, r.gqp2.at[1 - core, pl.ds(0, 128)], r.gqp2.at[1 - core, pl.ds(128, 128)])
    send_gq.start()
    send_gqp.start()
    for g in range(2):
        for j in range(3):
            lanes = slice(j * 128, j * 128 + 128)
            wide_lanes = slice((g * 3 + j) * 128, (g * 3 + j) * 128 + 128)
            key_sum, value_sum = jnp.zeros((256, 128), F32), jnp.zeros((256, 128), F32)
            for half in range(2):
                rows = slice(half * 64, half * 64 + 64)
                key_sum += FACTOR * dot(r.acc[half * 2 + g, :, lanes].astype(BF), both(r.q[rows, wide_lanes]))
                value_sum += dot(r.ctx[half * 2 + g, :, lanes], both(r.gmix[rows, wide_lanes]))
            r.dup[g, 0, j] = key_sum.astype(BF)
            r.dup[g, 1, j] = value_sum.astype(BF)
    send_up = paired(8, r.dup.at[1 - core], r.sup)
    send_up.start()
    grad_normed = dot_nt(r.gq2[0, 0:128], r.v_query[:, 0:384]) + dot_nt(r.gq2[1, 0:128], r.v_query[:, 384:768])
    grad_normed += dot_nt(r.gqp2[0, 0:128], r.v_qrope[:, 0:384]) + dot_nt(r.gqp2[1, 0:128], r.v_qrope[:, 384:768])
    r.gnm[0:128] = grad_normed
    send_norm.wait()
    r.normt[...] = r.norm2[...].T
    send_gq.wait()
    send_gqp.wait()
    send_up.wait()
    for o in range(3):
        rows = slice(o * 256, o * 256 + 256)
        for m, right in enumerate((r.gq2, r.gqp2)):
            block = dot(r.normt[rows], right[core]).astype(BF)
            for i in range(3):
                r.early_total[o, i, m] = block[:, i * 128 : i * 128 + 128]
            r.early_total[o, 3, m] = (r.dup[core, m, o].astype(F32) + r.sup[m, o].astype(F32)).astype(BF)
        early.start(0, (o,))

    outer.step(2)
    wide.step(2, 3)

    def fold_near(at, carried):
        for g in range(2):
            near = r.dlat[g, y, rows_at(at * 64, 64), :]
            for k in range(3):
                near = near + r.ro1[k, g, at].astype(F32)
            r.so1[g, at] = near.astype(BF)
        return carried

    def fold_far(at, carried):
        for g in range(2):
            far = r.dlat[2 + g, at, rows_at(z * 64, 64), :]
            for k in range(3):
                far = far + r.rt1[k, g, at].astype(F32)
            r.st1[g, at] = far.astype(BF)
        rot = r.dkr[y, rows_at(at * 64, 64), :]
        for k in range(3):
            rot = rot + r.rk1[k, at].astype(F32)
        r.ks1[at] = rot.astype(BF)
        return carried

    for copy in scatter(0, 0)[0::2]:
        copy.wait()
    lax.fori_loop(0, 4, fold_near, 0)
    for copy in scatter(0, 1)[0::2]:
        copy.start()
    outer.step(3)
    for copy in scatter(1, 0) + scatter(0, 0)[1::2]:
        copy.wait()
    lax.fori_loop(0, 4, fold_far, 0)
    for copy in scatter(1, 1) + scatter(0, 1)[1::2]:
        copy.start()
    wide.step(4)
    early.step(0, 1)
    for copy in scatter(0, 1) + scatter(1, 1):
        copy.wait()
    grad_latents = []
    for g in range(2):
        near = r.so1[g, z].astype(F32)
        far = r.st1[g, y].astype(F32)
        for k in range(3):
            near = near + r.ro2[k, g].astype(F32)
            far = far + r.rt2[k, g].astype(F32)
        piece = jnp.concatenate([near, far], axis=0).astype(BF)
        grad_latents.append(piece)
        r.gl2[g, 0:128] = piece
    send_gl = paired(9, r.gl2.at[1 - core, pl.ds(0, 128)], r.gl2.at[1 - core, pl.ds(128, 128)])
    send_gl.start()
    rot = r.ks1[z].astype(F32)
    for k in range(3):
        rot = rot + r.rk2[k].astype(F32)
    turned = pltpu.roll(rot, 64, 1)
    rot = jnp.concatenate([jnp.where(low64(64), rot, turned), jnp.where(low64(64), turned, rot)], axis=0)
    grad_kpre = (rot * r.cosine[...] - swap_halves(rot) * r.sine[...]).astype(BF)
    grad_normed = r.gnm[0:128] + dot(grad_kpre[:, 0:64], r.v_krope[...])
    for g in range(2):
        grad_normed = grad_normed + dot_nt(grad_latents[g], r.v_latent[:, g * 256 : g * 256 + 256])
    back, gain_attn = norm_back(grad_normed, r.xbuf[...].astype(F32), gain_of(r.norm_attn))
    r.outacc[0:128] = r.gmid[...] + back
    r.grad_tokens[x_hi] = r.outacc[0:64]
    swap_grad = swap(3, r.outacc.at[pl.ds(64, 64)], r.grad_tokens.at[x_hi])
    swap_grad.start()
    gains = r.gains[...]
    for p in range(6):
        gains = gains + jnp.where(gain_row == p, gain_attn[:, p * 128 : p * 128 + 128], 0.0)
    for o in range(3):
        r.late_total[o, 3, 0] = jnp.zeros((256, 128), BF)
    r.late_total[0, 3, 0, 0:16] = gains.astype(BF)
    grad_krope = dot_tn(grad_kpre, r.norm2[0:128]).astype(BF)
    send_gl.wait()
    for o in range(3):
        rows = slice(o * 256, o * 256 + 256)
        block = dot(r.normt[rows], r.gl2[core]).astype(BF)
        for i in range(2):
            r.late_total[o, i, 0] = block[:, i * 128 : i * 128 + 128]
        for part in range(2):
            at = o * 256 + part * 128
            r.late_total[o, 2, 0, part * 64 : part * 64 + 64] = grad_krope[0:64, at : at + 128]
        r.late_total[o, 2, 0, 128:256] = jnp.zeros((128, 128), BF)
        late.start(0, (o,))
    wide.step(5)
    early.step(2)
    late.step(0, 1)
    outer.step(4)
    wide.step(6)
    early.step(3, 4)
    late.step(2)
    early.step(5, 6)
    late.step(3, 4)
    outer.step(5, 6)
    wide.step(7)
    late.step(5, 6)
    outer.step(7)
    early.step(7)
    late.step(7)
    swap_out.wait()
    swap_grad.wait()
    for reduction in (wide, outer, early, late):
        reduction.finish(8)


def layer(small, weights):
    vmem = pl.BlockSpec(memory_space=pltpu.VMEM)
    hbm = pl.BlockSpec(memory_space=pl.ANY)
    smem = pl.BlockSpec(memory_space=pltpu.SMEM)
    return pl.pallas_call(
        layer_kernel,
        out_shape=[jax.ShapeDtypeStruct(shape, kind) for shape, kind in OUTS.values()],
        in_specs=[vmem] * 4 + [smem] * 2 + [hbm] * (1 + len(weights)),
        out_specs=[vmem, vmem] + [hbm] * (len(OUTS) - 2),
        scratch_shapes=list(scratch().values()),
        compiler_params=pltpu.CompilerParams(
            collective_id=1, has_side_effects=True, vmem_limit_bytes=63 * 2**20
        ),
    )(*small, jnp.asarray(rotary_table()), *weights)


def rotary_table():
    halves = ROPE // 2
    powers = -(np.arange(halves, dtype=np.float32) * np.float32(2.0) / np.float32(ROPE))
    freq_list = np.power(np.float32(10000.0), powers, dtype=np.float32)
    phases = (np.arange(2048, dtype=np.float32)[:, None] * freq_list[None, :]).astype(np.float32)
    cosine, sine = np.cos(phases), np.sin(phases)
    return np.concatenate([cosine, cosine, -sine, sine], axis=1).astype(np.float32)


CAST_STEPS = 12


def cast_kernel(
    wide, down, out, early, late, layer_out, grad_tokens,
    o_gate, o_up, o_down, o_query, o_qrope, o_out, o_latent, o_krope, o_upkey, o_upval, o_attn, o_mlp, o_layer, o_tokens,
):
    o_gate[...] = wide[0].astype(F32)
    o_up[...] = wide[1].astype(F32)
    o_down[0:256] = down[0, :, 0:256].astype(F32)
    o_down[256:512] = down[0, :, 256:512].astype(F32)
    for source, m, target, width in (
        (early, 0, o_query, 384), (early, 1, o_qrope, 384), (out, 0, o_out, 384), (late, 0, o_latent, 256)
    ):
        target[:, 0:width] = source[m, :, 0:width].astype(F32)
        target[:, width : 2 * width] = source[m, :, 512 : 512 + width].astype(F32)
    for m, target in ((0, o_upkey), (1, o_upval)):
        target[0] = early[m, :, 384:512].astype(F32)
        target[1] = early[m, :, 896:1024].astype(F32)
    step = pl.program_id(0)

    @pl.when(lax.rem(step, 4) < 2)
    def _():
        lanes = rows_at(lax.div(step, 4) * 256 + lax.rem(step, 4) * 128, 128, 128)
        o_krope[:, lanes] = late[0, :, 256:384].astype(F32) + late[0, :, 768:896].astype(F32)

    @pl.when(step == 0)
    def _():
        gains = late[0, 0:16, 384:512].astype(F32) + late[0, 0:16, 896:1024].astype(F32)
        for p in range(6):
            o_attn[p * 128 : p * 128 + 128] = gains[p]
            o_mlp[p * 128 : p * 128 + 128] = gains[6 + p]
        o_layer[...] = layer_out[...]
        o_tokens[...] = grad_tokens[...]


def cast_sums(layer_out, grad_tokens, wide, out, early, late):
    rows = lambda width: pl.BlockSpec((64, width), lambda i: (i, 0))
    group = lambda n, width: pl.BlockSpec((n, 64, width), lambda i: (0, i, 0))
    ups = pl.BlockSpec((2, 64, 128), lambda i: (0, lax.rem(i, 4), lax.div(i, 4)))
    shapes = (
        (768, 2048), (768, 2048), (2048, 768), (768, 768), (768, 768), (768, 768), (768, 512), (64, 768),
        (2, 256, 384), (2, 256, 384), (768,), (768,),
    )
    whole = lambda shape: pl.BlockSpec(shape, lambda i: (0,) * len(shape))
    rows_out = (layer_out, grad_tokens)
    return pl.pallas_call(
        cast_kernel,
        grid=(CAST_STEPS,),
        out_shape=[jax.ShapeDtypeStruct(shape, F32) for shape in shapes]
        + [jax.ShapeDtypeStruct(array.shape, array.dtype) for array in rows_out],
        in_specs=[
            group(2, 2048),
            pl.BlockSpec((1, 256, 512), lambda i: (2, lax.div(i, 4), lax.rem(i, 4))),
            group(1, 1024),
            group(2, 1024),
            group(1, 1024),
        ]
        + [whole(array.shape) for array in rows_out],
        out_specs=[
            rows(2048),
            rows(2048),
            pl.BlockSpec((512, 256), lambda i: (lax.rem(i, 4), lax.div(i, 4))),
            rows(768),
            rows(768),
            rows(768),
            rows(512),
            whole((64, 768)),
            ups,
            ups,
            whole((768,)),
            whole((768,)),
        ]
        + [whole(array.shape) for array in rows_out],
        compiler_params=pltpu.CompilerParams(vmem_limit_bytes=63 * 2**20),
    )(wide, wide, out, early, late, layer_out, grad_tokens)


def local(
    tokens, cotangent, group_of_seq, group_weight, norm_attn, w_query, w_qrope, w_latent, w_krope, w_upkey, w_upval,
    w_out, norm_mlp, w_gate, w_up, w_down,
):
    small = (tokens, cotangent, norm_attn, norm_mlp, group_of_seq, group_weight)
    weights = (w_latent, w_krope.T, w_query, w_qrope, w_upkey, w_upval, w_out, w_gate, w_up, w_down)
    gate, up, down, query, qrope, out, latent, krope, upkey, upval, attn, mlp, layer_out, grad_tokens = cast_sums(
        *layer(small, weights)
    )
    return (
        layer_out, grad_tokens, attn, query, qrope, latent, krope.T, upkey, upval, out, mlp, gate, up, down,
    )


def solution(mesh):
    split = P("seq", "blk", None)
    in_specs = (split, split, P("seq")) + (P(),) * 13
    out_specs = (split, split) + (P(),) * 12
    return jax.shard_map(local, mesh=mesh, in_specs=in_specs, out_specs=out_specs, check_vma=False)
```

```python
import jax
import jax.numpy as jnp
import numpy as np
from jax import lax
from jax.sharding import PartitionSpec as P
from jax.experimental import pallas as pl
from jax.experimental.pallas import tpu as pltpu

MESH = pl.DeviceIdType.MESH
BF = jnp.bfloat16
F32 = jnp.float32
EPSILON = 1e-06
ROPE = 64
GROUPS = 4
FACTOR = 128.0**-0.5
LOG2E = 1.4426950408889634
HIDDEN_SCORE = -1e30
ORDERS = ((0, 1, 2), (1, 2, 0), (2, 0, 1))
X_FIRST = ((0, 1, 2), (0, 2, 1), (0, 1, 2))


def coords():
    s = lax.axis_index("seq")
    b = lax.axis_index("blk")
    x = lax.rem(b, 2) * 2 + lax.div(s, 2)
    return x, lax.div(b, 8), lax.rem(lax.div(b, 2), 4), lax.rem(s, 2)


def device(x, y, z, core):
    return (lax.rem(x, 2) * 2 + core, y * 8 + z * 2 + lax.div(x, 2))


def on_ring(place, axis, step):
    spot = list(place)
    spot[axis] = lax.rem(place[axis] + step, 4)
    return device(*spot)


def remote(src, dst, send, recv, peer):
    return pltpu.make_async_remote_copy(
        src_ref=src, dst_ref=dst, send_sem=send, recv_sem=recv, device_id=peer, device_id_type=MESH
    )


def rows_at(start, size, multiple=16):
    return pl.ds(pl.multiple_of(start, multiple), size)


def dot(left, right):
    return jnp.dot(left, right, preferred_element_type=F32)


def dot_nt(left, right):
    return lax.dot_general(left, right, (((1,), (1,)), ((), ())), preferred_element_type=F32)


def dot_tn(left, right):
    return lax.dot_general(left, right, (((0,), (0,)), ((), ())), preferred_element_type=F32)


class Reduction:
    def __init__(self, r, name, place, out, halving, flat=False, orders=ORDERS):
        self.place, self.out, self.halving, self.flat, self.orders = place, out, halving, flat, orders
        for part in ("total", "first", "second", "third", "chunk", "send", "recv", "keep"):
            setattr(self, part, getattr(r, name + "_" + part))
        self.n, self.width = self.total.shape[2], self.total.shape[4]
        counts = stage_counts(halving, flat)
        self.base = [sum(counts[:stage]) for stage in range(9)]

    def spots(self, o):
        a, b, c = self.orders[o]
        return self.place[a], self.place[b], self.place[c]

    def sides(self, o, s):
        me = self.place[self.orders[o][0]]
        odd = lax.rem(me, 2)
        near, far = 1 + 2 * odd, 3 - 2 * odd
        steps = (near, far) if s == 0 else (far, near)
        return steps, lax.rem(me + steps[0], 4), lax.rem(me + steps[1], 4), lax.rem(me + 2, 4)

    def region(self, o, i, row, rows, count=1):
        core, width = self.place[3], self.width
        return self.out.at[:, rows_at(o * 256 + row, rows), rows_at((core * 4 + i) * width, count * width, 128)]

    def moves(self, o, stage):
        i, j, k = self.spots(o)
        if stage == 8:
            x, y, z, core = self.place
            here = self.region(o, 0, 0, 256, 4)
            return [(here, here, device(x, y, z, 1 - core))]
        made = []
        axis = self.orders[o][(0, 0, 1, 2, 2, 1, 0, 0)[stage]]
        if stage in (0, 1, 6, 7) and self.halving:
            for s in range(2):
                steps, front, last, across = self.sides(o, s)
                half = pl.ds(s * 128, 128)
                peer = on_ring(self.place, axis, steps[0 if stage in (0, 7) else 1])
                if stage == 0:
                    made.append((self.total.at[o, front, :, half], self.first.at[o, s, 0], peer))
                    made.append((self.total.at[o, across, :, half], self.first.at[o, s, 1], peer))
                elif stage == 1:
                    made.append((self.total.at[o, last, :, half], self.first.at[o, s, 2], peer))
                else:
                    for spot in (i, last) if stage == 7 else (i,):
                        here = self.region(o, spot, s * 128, 128)
                        made.append((here, here, peer))
            return made
        if stage in (1, 6) or (stage == 4 and self.flat):
            return made
        for step in (1, 2, 3):
            to = lax.rem(self.place[axis] + step, 4)
            peer = on_ring(self.place, axis, step)
            at = step - 1
            if stage == 0:
                made.append((self.total.at[o, to], self.first.at[o, at], peer))
            elif stage == 2:
                made.append((self.total.at[o, i, :, rows_at(to * 64, 64)], self.second.at[o, at], peer))
            elif stage == 3 and self.flat:
                made.append((self.total.at[o, i, :, rows_at(j * 64, 64)], self.third.at[o, k], peer))
            elif stage == 3:
                made.append((self.total.at[o, i, :, rows_at(j * 64 + to * 16, 16)], self.third.at[o, at], peer))
            elif stage == 4:
                made.append((self.chunk.at[o], self.region(o, i, j * 64 + k * 16, 16), peer))
            elif stage == 5:
                here = self.region(o, i, j * 64, 64)
                made.append((self.chunk.at[o] if self.flat else here, here, peer))
            else:
                here = self.region(o, i, 0, 256)
                made.append((here, here, peer))
        return made

    def copies(self, o, stage):
        return [
            remote(src, dst, self.send.at[o, at], self.recv.at[o, self.base[stage] + at], peer)
            for at, (src, dst, peer) in enumerate(self.moves(o, stage))
        ]

    def kept(self, o):
        i, j, k = self.spots(o)
        row, rows = (j * 64, 64) if self.flat else (j * 64 + k * 16, 16)
        return pltpu.make_async_copy(self.chunk.at[o], self.region(o, i, row, rows), self.keep.at[o])

    def start(self, stage, orders=(0, 1, 2)):
        for o in orders:
            for copy in self.copies(o, stage):
                copy.start()
            if stage == 4:
                self.kept(o).start()

    def finish(self, stage, orders=(0, 1, 2)):
        for o in orders:
            for copy in self.copies(o, stage):
                copy.wait()
            if stage == 4:
                self.kept(o).wait()
            if stage < 4:
                self.add(o, stage)

    def step(self, *stages):
        for stage in stages:
            for o in range(3):
                self.finish(stage, (o,))
                self.start(stage + 1, (o,))

    def add(self, o, stage):
        i, j, k = self.spots(o)
        if stage == 1 and not self.halving:
            return

        def body(m, carried):
            if stage < 2 and self.halving:
                for s in range(2):
                    _, _, last, _ = self.sides(o, s)
                    half = slice(s * 128, s * 128 + 128)
                    for spot, slot in ((i, 0), (last, 1)) if stage == 0 else ((i, 2),):
                        acc = self.total[o, spot, m, half, :].astype(F32) + self.first[o, s, slot, m].astype(F32)
                        self.total[o, spot, m, half, :] = acc.astype(BF)
            elif stage == 0:
                for part in range(4):
                    rows = slice(part * 64, part * 64 + 64)
                    acc = self.total[o, i, m, rows, :].astype(F32)
                    for slot in range(3):
                        acc = acc + self.first[o, slot, m, rows, :].astype(F32)
                    self.total[o, i, m, rows, :] = acc.astype(BF)
            elif stage == 2:
                rows = rows_at(j * 64, 64)
                acc = self.total[o, i, m, rows, :].astype(F32)
                for slot in range(3):
                    acc = acc + self.second[o, slot, m].astype(F32)
                self.total[o, i, m, rows, :] = acc.astype(BF)
            elif self.flat:
                self.third[o, k, m] = self.total[o, i, m, rows_at(j * 64, 64), :]
                acc = self.third[o, 0, m].astype(F32)
                for slot in range(1, 4):
                    acc = acc + self.third[o, slot, m].astype(F32)
                self.chunk[o, m] = acc.astype(BF)
            else:
                acc = self.total[o, i, m, rows_at(j * 64 + k * 16, 16), :].astype(F32)
                for slot in range(3):
                    acc = acc + self.third[o, slot, m].astype(F32)
                self.chunk[o, m] = acc.astype(BF)
            return carried

        lax.fori_loop(0, self.n, body, 0)


def stage_counts(halving, flat):
    return (4 if halving else 3, 2 if halving else 0, 3, 3, 0 if flat else 3, 3, 2 if halving else 0, 4 if halving else 3, 1)


def reduction_scratch(name, n, width, halving, flat=False):
    return {
        name + "_total": pltpu.VMEM((3, 4, n, 256, width), BF),
        name + "_first": pltpu.VMEM((3, 2, 3, n, 128, width) if halving else (3, 3, n, 256, width), BF),
        name + "_second": pltpu.VMEM((3, 3, n, 64, width), BF),
        name + "_third": pltpu.VMEM((3, 4, n, 64, width) if flat else (3, 3, n, 16, width), BF),
        name + "_chunk": pltpu.VMEM((3, n, 64 if flat else 16, width), BF),
        name + "_send": pltpu.SemaphoreType.DMA((3, 4)),
        name + "_recv": pltpu.SemaphoreType.DMA((3, sum(stage_counts(halving, flat)))),
        name + "_keep": pltpu.SemaphoreType.DMA((3,)),
    }


WEIGHTS = {
    "w_latent": (768, 512),
    "w_krope": (64, 768),
    "w_query": (768, 768),
    "w_qrope": (768, 768),
    "w_upkey": (2, 256, 384),
    "w_upval": (2, 256, 384),
    "w_out": (768, 768),
    "w_gate": (768, 1024),
    "w_up": (768, 1024),
    "w_down": (1024, 768),
}
SMALL = ("tokens", "cotangent", "norm_attn", "norm_mlp", "group_of_seq", "group_weight")
OUTS = {
    "layer_out": ((2, 64, 768), BF),
    "grad_tokens": ((2, 64, 768), F32),
    "g_wide": ((3, 768, 2048), BF),
    "g_out": ((1, 768, 1024), BF),
    "g_early": ((2, 768, 1024), BF),
    "g_late": ((1, 768, 1024), BF),
}


def scratch():
    vmem, dma = pltpu.VMEM, pltpu.SemaphoreType.DMA
    made = {"v" + name[1:]: vmem(shape, BF) for name, shape in WEIGHTS.items()}
    made.update(
        load_sem=dma((len(WEIGHTS),)),
        table_sem=dma((2,)),
        turns=vmem((128, 128), F32),
        cosine=vmem((128, 128), F32),
        sine=vmem((128, 128), F32),
        swap_sem=dma((4, 2)),
        pair_sem=dma((12, 2)),
        lat_send=dma((2, 2, 3)),
        lat_recv=dma((2, 2, 2, 2, 3)),
        xbuf=vmem((128, 768), BF),
        cbuf=vmem((128, 768), BF),
        norm2=vmem((256, 768), BF),
        normt=vmem((768, 256), BF),
        krd=vmem((128, 128), F32),
        q=vmem((128, 768), BF),
        qr=vmem((128, 768), BF),
        lat=vmem((4, 4, 4, 64, 256), BF),
        kr=vmem((4, 4, 64, 128), BF),
        latt=vmem((4, 4, 4, 64, 256), BF),
        krt=vmem((2, 4, 128, 256), BF),
        rel=vmem((2, 256, 384), jnp.int32),
        qs=vmem((4, 384, 256), BF),
        ga=vmem((4, 384, 256), BF),
        qrx=vmem((2, 4, 384, 128), BF),
        acc=vmem((4, 256, 384), F32),
        ctx=vmem((4, 256, 384), BF),
        dqa=vmem((4, 256, 384), F32),
        logs=vmem((4, 8, 384), F32),
        delta=vmem((4, 8, 384), F32),
        aof=vmem((128, 768), F32),
        ao2=vmem((256, 768), BF),
        middle=vmem((128, 768), F32),
        nm2=vmem((256, 768), BF),
        nmt=vmem((768, 256), BF),
        gb2=vmem((256, 768), BF),
        acts=vmem((3, 256, 1024), BF),
        hidt=vmem((1024, 256), BF),
        outacc=vmem((256, 768), F32),
        gnm=vmem((256, 768), F32),
        outx=vmem((128, 768), F32),
        gnmx=vmem((128, 768), F32),
        outbf=vmem((128, 768), BF),
        gattn=vmem((2, 256, 384), BF),
        gmix=vmem((128, 768), BF),
        dqr=vmem((4, 128, 384), F32),
        dlat=vmem((4, 4, 256, 256), F32),
        dkr=vmem((4, 256, 128), F32),
        skr=vmem((4, 4, 64, 128), BF),
        ro1=vmem((3, 2, 4, 64, 256), BF),
        rk1=vmem((3, 4, 64, 128), BF),
        rt1=vmem((3, 2, 4, 64, 256), BF),
        so1=vmem((2, 4, 64, 256), BF),
        ks1=vmem((4, 64, 128), BF),
        st1=vmem((2, 4, 64, 256), BF),
        ro2=vmem((3, 2, 64, 256), BF),
        rk2=vmem((3, 64, 128), BF),
        rt2=vmem((3, 2, 64, 256), BF),
        gq2=vmem((2, 256, 384), BF),
        gqp2=vmem((2, 256, 384), BF),
        gl2=vmem((2, 256, 256), BF),
        dup=vmem((2, 2, 3, 256, 128), BF),
        sup=vmem((2, 3, 256, 128), BF),
        gmid=vmem((128, 768), F32),
        gains=vmem((16, 128), F32),
    )
    made.update(reduction_scratch("wide", 3, 256, True))
    made.update(reduction_scratch("out", 1, 128, False))
    made.update(reduction_scratch("early", 2, 128, False, True))
    made.update(reduction_scratch("late", 1, 128, False, True))
    return made


class Refs:
    pass


def swap_halves(values):
    lanes = values.shape[-1]
    low = lax.rem(lax.broadcasted_iota(jnp.int32, values.shape, 1), 64) < 32
    return jnp.where(low, pltpu.roll(values, lanes - 32, 1), pltpu.roll(values, 32, 1))


def layer_kernel(*args):
    r = Refs()
    shapes = scratch()
    names = list(SMALL) + ["table"] + list(WEIGHTS) + list(OUTS) + list(shapes)
    for name, ref in zip(names, args, strict=True):
        setattr(r, name, ref)
    place = coords()
    x, y, z, core = place
    x_hi = lax.div(x, 2)
    blk = y * 8 + z * 2 + x_hi
    slot = y * 4 + z
    sibling = device(x, y, z, 1 - core)
    partner = device(lax.rem(x + 2, 4), 3 - y, 3 - z, core)
    peers = [on_ring(place, axis, step) for axis in range(3) for step in (1, 2, 3)] + [sibling, partner]
    low64 = lambda rows: lax.broadcasted_iota(jnp.int32, (rows, 128), 1) < 64
    diagonal = (lax.broadcasted_iota(jnp.int32, (128, 128), 0) < 64) == low64(128)

    def gain_of(ref):
        return ref[...].reshape(1, 768)

    def both(value):
        return jnp.where(diagonal, jnp.concatenate([value, value], axis=0), jnp.zeros((), value.dtype))

    def pick(value):
        return jnp.where(low64(64), value[0:64], value[64:128])

    loads = {}
    for at, name in enumerate(WEIGHTS):
        source = getattr(r, name)
        if name in ("w_gate", "w_up"):
            source = source.at[:, rows_at(core * 1024, 1024, 128)]
        elif name == "w_down":
            source = source.at[rows_at(core * 1024, 1024), :]
        loads[name] = pltpu.make_async_copy(source, getattr(r, "v" + name[1:]), r.load_sem.at[at])
    tables = [
        pltpu.make_async_copy(
            r.table.at[rows_at(where * 64, 64)], r.turns.at[pl.ds(half * 64, 64)], r.table_sem.at[half]
        )
        for half, where in enumerate((blk, 31 - blk))
    ]
    loads["w_latent"].start()
    loads["w_krope"].start()
    for table in tables:
        table.start()
    barrier = pltpu.get_barrier_semaphore()
    for peer in peers:
        pl.semaphore_signal(barrier, inc=1, device_id=peer, device_id_type=MESH)
    pl.semaphore_wait(barrier, len(peers))

    def swap(at, src, dst):
        return remote(src, dst, r.swap_sem.at[at, 0], r.swap_sem.at[at, 1], partner)

    def paired(at, src, dst):
        return remote(src, dst, r.pair_sem.at[at, 0], r.pair_sem.at[at, 1], sibling)

    swap_x = swap(0, r.tokens.at[1 - x_hi], r.xbuf.at[pl.ds(64, 64)])
    swap_c = swap(1, r.cotangent.at[1 - x_hi], r.cbuf.at[pl.ds(64, 64)])
    swap_x.start()
    swap_c.start()
    for name in ("w_query", "w_qrope", "w_upkey"):
        loads[name].start()
    r.xbuf[0:64] = r.tokens[x_hi]
    r.cbuf[0:64] = r.cotangent[x_hi]
    key_row = lax.broadcasted_iota(jnp.int32, (256, 384), 0)
    query_lane = lax.rem(lax.broadcasted_iota(jnp.int32, (256, 384), 1), 64)
    within = lax.rem(key_row, 64) - query_lane
    r.rel[0] = 128 * lax.div(key_row, 64) + within
    r.rel[1] = within - 128 * lax.div(key_row, 64)
    for table in tables:
        table.wait()
    turns = r.turns[...]
    other = pltpu.roll(turns, 64, 1)
    r.cosine[...] = jnp.where(low64(128), turns, other)
    r.sine[...] = jnp.where(low64(128), other, turns)
    swap_x.wait()

    def unit_of(values):
        inverse = lax.rsqrt(jnp.mean(values * values, axis=-1, keepdims=True) + EPSILON)
        return values * inverse, inverse

    unit = unit_of(r.xbuf[...].astype(F32))[0]
    normed = (unit * gain_of(r.norm_attn)).astype(BF)
    r.norm2[0:128] = normed
    send_norm = paired(0, r.norm2.at[pl.ds(0, 128)], r.norm2.at[pl.ds(128, 128)])
    send_norm.start()
    loads["w_latent"].wait()
    loads["w_krope"].wait()
    key_pre = dot_nt(normed, r.v_krope[...])
    r.krd[:, 0:64] = key_pre
    r.krd[:, 64:128] = key_pre
    key_pre = r.krd[...]
    key_rot = (key_pre * r.cosine[...] + swap_halves(key_pre) * r.sine[...]).astype(BF)
    r.kr[y, z] = pick(key_rot)
    latents = dot(normed, r.v_latent[...]).astype(BF)
    for half in range(2):
        for g in range(2):
            r.lat[half * 2 + g, y, z] = latents[half * 64 : half * 64 + 64, g * 256 : g * 256 + 256]

    def gather(part, phase):
        made = []
        axis = (2, 1)[(part + phase) % 2]
        for step in (1, 2, 3):
            peer = on_ring(place, axis, step)
            two = pl.ds(part * 2, 2)
            if phase == 0:
                pieces = [r.lat.at[two, y, z], r.kr.at[y, z]]
            elif part == 0:
                pieces = [r.lat.at[two, y], r.kr.at[y]]
            else:
                pieces = [r.lat.at[two, :, z], None]
            for at, piece in enumerate(pieces if part == 0 else pieces[:1]):
                send = r.lat_send.at[part, at, step - 1]
                made.append(remote(piece, piece, send, r.lat_recv.at[0, part, phase, at, step - 1], peer))
        return made

    for part in range(2):
        for copy in gather(part, 0):
            copy.start()
    for name in ("w_upval", "w_out", "w_gate", "w_up", "w_down"):
        loads[name].start()

    loads["w_query"].wait()
    r.q[...] = dot(normed, r.v_query[...]).astype(BF)
    loads["w_qrope"].wait()
    query_pre = dot(normed, r.v_qrope[...])
    for p in range(6):
        lanes = slice(p * 128, p * 128 + 128)
        piece = query_pre[:, lanes]
        r.qr[:, lanes] = (piece * r.cosine[...] + swap_halves(piece) * r.sine[...]).astype(BF)
    loads["w_upkey"].wait()

    def to_latent(source, weights, target):
        for half in range(2):
            for g in range(2):
                for j in range(3):
                    p = g * 3 + j
                    block = both(source[half * 64 : half * 64 + 64, p * 128 : p * 128 + 128])
                    rows = dot_nt(block, weights[g, :, j * 128 : j * 128 + 128])
                    target[half * 2 + g, j * 128 : j * 128 + 128] = rows.astype(BF)

    to_latent(r.q, r.v_upkey, r.qs)
    for half in range(2):
        for p in range(6):
            pair = r.qr[half * 64 : half * 64 + 64, p * 128 : p * 128 + 128].astype(F32)
            turned = pltpu.roll(pair, 64, 1)
            for odd in range(2):
                front, back = (turned, pair) if odd else (pair, turned)
                at = (p % 3) * 128 + odd * 64
                here = (half * 2 + p // 3, slice(at, at + 64))
                r.qrx[(0,) + here] = jnp.where(low64(64), front, 0.0).astype(BF)
                r.qrx[(1,) + here] = jnp.where(low64(64), 0.0, back).astype(BF)

    swap_c.wait()
    group = jnp.where(x_hi == 0, r.group_of_seq[0], r.group_of_seq[1])
    weight = r.group_weight[0]
    for g in range(1, GROUPS):
        weight = jnp.where(group == g, r.group_weight[g], weight)
    r.gb2[0:128] = (r.cbuf[...].astype(F32) * weight).astype(BF)
    send_gb = paired(3, r.gb2.at[pl.ds(0, 128)], r.gb2.at[pl.ds(128, 128)])
    send_gb.start()
    for ref in (r.outacc, r.gnm, r.acc, r.dqa, r.dqr, r.dlat, r.dkr):
        ref[...] = jnp.zeros_like(ref)

    for part in (1, 0):
        for copy in gather(part, 0):
            copy.wait()
        for copy in gather(part, 1):
            copy.start()

    def transpose_latents():
        def body(step, carried):
            j, c = lax.div(step, 4), lax.rem(step, 4)
            r.latt[j, c] = r.lat[j, c].reshape(256, 256).T.reshape(4, 64, 256)
            return carried

        lax.fori_loop(0, 16, body, 0)

    query_blk = (blk, 31 - blk)

    counts = (y + 1, 4 - y)

    def masks(half, step):
        first = query_blk[half] * 64
        near = r.rel[0] <= first - 512 * step - 64 * x_hi
        far = r.rel[1] <= first - 1984 + 512 * (3 - step) + 64 * x_hi
        return (step, near), (3 - step, far)

    def raw_scores(at, far, chunk, g):
        keys = r.lat[far * 2 + g, chunk].reshape(256, 256)
        rot = r.kr[chunk].reshape(256, 128)
        return dot_nt(keys, r.qs[at]) + dot_nt(rot, r.qrx[far, at]), keys

    for copy in gather(1, 1) + gather(0, 1):
        copy.wait()
    top = lax.broadcasted_iota(jnp.int32, (128, 256), 0) < 64
    for c in range(4):
        turned = r.kr[c].reshape(256, 128).astype(F32).T
        r.krt[0, c] = jnp.where(top, turned, 0.0).astype(BF)
        r.krt[1, c] = jnp.where(top, 0.0, turned).astype(BF)
    transpose_latents()

    def forward(half):
        def chunk_step(step, state):
            places = masks(half, step)
            result = []
            for g in range(2):
                at = half * 2 + g
                high, total = state[g]
                raws = [
                    jnp.where(allowed, raw_scores(at, far, chunk, g)[0], HIDDEN_SCORE)
                    for far, (chunk, allowed) in enumerate(places)
                ]
                new_high = jnp.maximum(high, jnp.max(jnp.maximum(*raws), axis=0, keepdims=True))
                shrink = jnp.exp2((high - new_high) * (FACTOR * LOG2E))
                weights = [jnp.exp2((raw - new_high) * (FACTOR * LOG2E)) for raw in raws]
                total = total * shrink + jnp.sum(weights[0] + weights[1], axis=0, keepdims=True)
                mixed = r.acc[at] * shrink
                for far, (chunk, _) in enumerate(places):
                    value = r.latt[far * 2 + g, chunk].reshape(256, 256)
                    mixed = mixed + dot(value, weights[far].astype(BF))
                r.acc[at] = mixed
                result.append((new_high, total))
            return tuple(result)

        empty = (jnp.full((1, 384), HIDDEN_SCORE, F32), jnp.zeros((1, 384), F32))
        state = lax.fori_loop(0, counts[half], chunk_step, (empty, empty))
        for g in range(2):
            high, total = state[g]
            at = half * 2 + g
            r.ctx[at] = (r.acc[at] * (1.0 / total)).astype(BF)
            r.logs[at, 0:1] = high * (FACTOR * LOG2E) + jnp.log2(total)

    forward(0)
    forward(1)
    loads["w_upval"].wait()

    def from_latent(source, weights, half, p):
        g, j = p // 3, p % 3
        lanes = slice(j * 128, j * 128 + 128)
        return pick(dot_tn(source[half * 2 + g, :, lanes].astype(BF), weights[g, :, lanes]))

    for half in range(2):
        for p in range(6):
            r.aof[half * 64 : half * 64 + 64, p * 128 : p * 128 + 128] = from_latent(r.ctx, r.v_upval, half, p)
    r.ao2[0:128] = r.aof[...].astype(BF)
    send_ao = paired(1, r.ao2.at[pl.ds(0, 128)], r.ao2.at[pl.ds(128, 128)])
    send_ao.start()

    loads["w_out"].wait()
    middle = r.xbuf[...].astype(F32) + dot(r.ao2[0:128], r.v_out[...])
    r.middle[...] = middle
    unit_mlp = unit_of(middle)[0]
    r.nm2[0:128] = (unit_mlp * gain_of(r.norm_mlp)).astype(BF)
    send_nm = paired(2, r.nm2.at[pl.ds(0, 128)], r.nm2.at[pl.ds(128, 128)])
    send_nm.start()
    for name in ("w_gate", "w_up", "w_down"):
        loads[name].wait()
    send_nm.wait()
    send_gb.wait()

    def tile(step, carried):
        at = rows_at(step * 512, 512, 512)
        act = r.nm2[...]
        gate = dot(act, r.v_gate[:, at])
        up = dot(act, r.v_up[:, at])
        sig = jax.nn.sigmoid(gate)
        silu = gate * sig
        hidden = (silu * up).astype(BF)
        grad_hidden = dot_nt(r.gb2[...], r.v_down[at, :])
        grad_gate = (grad_hidden * up * sig * (1.0 + gate * (1.0 - sig))).astype(BF)
        grad_up = (grad_hidden * silu).astype(BF)
        r.acts[0, :, at] = hidden
        r.acts[1, :, at] = grad_gate
        r.acts[2, :, at] = grad_up
        r.outacc[...] += dot(hidden, r.v_down[at, :])
        r.gnm[...] += dot_nt(grad_gate, r.v_gate[:, at]) + dot_nt(grad_up, r.v_up[:, at])
        return carried

    lax.fori_loop(0, 2, tile, 0)
    send_gnm = paired(4, r.gnm.at[pl.ds(128, 128)], r.gnmx)
    send_out = paired(10, r.outacc.at[pl.ds(128, 128)], r.outx)
    send_gnm.start()
    send_out.start()

    wide = Reduction(r, "wide", place, r.g_wide, True)
    outer = Reduction(r, "out", place, r.g_out, False)
    early = Reduction(r, "early", place, r.g_early, False, True)
    late = Reduction(r, "late", place, r.g_late, False, True)
    r.nmt[...] = r.nm2[...].T
    r.hidt[...] = r.acts[0].T
    for o in range(3):
        left = r.nmt[o * 256 : o * 256 + 256]
        for i in range(4):
            cols = slice(i * 256, i * 256 + 256)
            r.wide_total[o, i, 0] = dot(left, r.acts[1, :, cols]).astype(BF)
            r.wide_total[o, i, 1] = dot(left, r.acts[2, :, cols]).astype(BF)
            r.wide_total[o, i, 2] = dot(r.hidt[cols, :], r.gb2[:, o * 256 : o * 256 + 256]).astype(BF)
        wide.start(0, (o,))

    def norm_back(grads, values, gain):
        unit_rows, inverse = unit_of(values)
        scaled = grads * gain
        gain_grad = jnp.sum(grads * unit_rows, axis=0, keepdims=True)
        mean = jnp.mean(scaled * unit_rows, axis=-1, keepdims=True)
        return inverse * (scaled - unit_rows * mean), gain_grad

    send_gnm.wait()
    back, gain_mlp = norm_back(r.gnm[0:128] + r.gnmx[...], r.middle[...], gain_of(r.norm_mlp))
    r.gmid[...] = r.cbuf[...].astype(F32) * weight + back
    gain_row = lax.broadcasted_iota(jnp.int32, (16, 128), 0)
    gains = jnp.zeros((16, 128), F32)
    for p in range(6):
        gains = gains + jnp.where(gain_row == 6 + p, gain_mlp[:, p * 128 : p * 128 + 128], 0.0)
    r.gains[...] = gains
    grad_attn = r.gmid[...].astype(BF)
    for half in range(2):
        r.gattn[half, 0:128] = grad_attn[:, half * 384 : half * 384 + 384]
    send_ga = paired(5, r.gattn.at[1 - core, pl.ds(0, 128)], r.gattn.at[1 - core, pl.ds(128, 128)])
    send_ga.start()
    mixed = dot_nt(grad_attn, r.v_out[...])
    r.gmix[...] = mixed.astype(BF)
    to_latent(r.gmix, r.v_upval, r.ga)
    send_out.wait()
    r.outbf[...] = (r.middle[...] + r.outacc[0:128] + r.outx[...]).astype(BF)
    r.layer_out[x_hi] = r.outbf[0:64]
    swap_out = swap(2, r.outbf.at[pl.ds(64, 64)], r.layer_out.at[x_hi])
    swap_out.start()
    ones = jnp.ones((8, 128), F32)
    for half in range(2):
        for p in range(6):
            here = (slice(half * 64, half * 64 + 64), slice(p * 128, p * 128 + 128))
            block = both(r.gmix[here].astype(F32) * r.aof[here])
            sums = lax.dot_general(
                ones, block, (((1,), (1,)), ((), ())), precision=lax.Precision.HIGHEST, preferred_element_type=F32
            )
            r.delta[half * 2 + p // 3, :, (p % 3) * 128 : (p % 3) * 128 + 128] = sums

    send_ao.wait()
    send_ga.wait()
    r.nmt[...] = r.ao2[...].T
    for o in range(3):
        block = dot(r.nmt[o * 256 : o * 256 + 256], r.gattn[core]).astype(BF)
        for i in range(3):
            r.out_total[o, i, 0] = block[:, i * 128 : i * 128 + 128]
        r.out_total[o, 3, 0] = jnp.zeros((256, 128), BF)
    outer.start(0)

    def backward(half):
        def chunk_step(step, carried):
            places = masks(half, step)
            for g in range(2):
                at = half * 2 + g
                mixed, turned = r.dqa[at], r.dqr[at]
                for far, (chunk, allowed) in enumerate(places):
                    raw, keys = raw_scores(at, far, chunk, g)
                    weights = jnp.exp2(raw * (FACTOR * LOG2E) - r.logs[at, 0:1])
                    weights = jnp.where(allowed, weights, 0.0)
                    dprob = dot_nt(keys, r.ga[at])
                    dscore = (weights * (dprob - r.delta[at, 0:1])).astype(BF)
                    weights = weights.astype(BF)
                    mixed = mixed + dot(r.latt[far * 2 + g, chunk].reshape(256, 256), dscore)
                    turned = turned + dot(r.krt[far, chunk], dscore)
                    r.dlat[far * 2 + g, chunk] += FACTOR * dot(dscore, r.qs[at]) + dot(weights, r.ga[at])
                    r.dkr[chunk] += FACTOR * dot(dscore, r.qrx[far, at])
                r.dqa[at], r.dqr[at] = mixed, turned
            return carried

        lax.fori_loop(0, counts[half], chunk_step, 0)

    def narrow(step, carried):
        j, c = lax.div(step, 4), lax.rem(step, 4)
        r.latt[j, c] = r.dlat[j, c].astype(BF).reshape(4, 64, 256)
        return carried

    def scatter(part, phase):
        made = []
        axis = (1, 2)[(part + phase) % 2]
        for step in (1, 2, 3):
            peer = on_ring(place, axis, step)
            to = lax.rem(place[axis] + step, 4)
            at = step - 1
            if part == 0 and phase == 0:
                pieces = [(r.latt.at[pl.ds(0, 2), to], r.ro1.at[at]), (r.skr.at[to], r.rk1.at[at])]
            elif part == 0:
                pieces = [(r.so1.at[:, to], r.ro2.at[at]), (r.ks1.at[to], r.rk2.at[at])]
            elif phase == 0:
                pieces = [(r.latt.at[pl.ds(2, 2), :, to], r.rt1.at[at])]
            else:
                pieces = [(r.st1.at[:, to], r.rt2.at[at])]
            for k, (src, dst) in enumerate(pieces):
                send = r.lat_send.at[part, k, at]
                made.append(remote(src, dst, send, r.lat_recv.at[1, part, phase, k, at], peer))
        return made

    backward(0)
    wide.step(0)
    backward(1)
    lax.fori_loop(0, 16, narrow, 0)
    for c in range(4):
        r.skr[c] = r.dkr[c].astype(BF).reshape(4, 64, 128)
    for copy in scatter(1, 0) + scatter(0, 0):
        copy.start()
    wide.step(1)
    outer.step(0, 1)

    for half in range(2):
        for p in range(6):
            rows, lanes = slice(half * 64, half * 64 + 64), slice((p % 3) * 128, (p % 3) * 128 + 128)
            at = half * 2 + p // 3
            piece = (FACTOR * from_latent(r.dqa, r.v_upkey, half, p)).astype(BF)
            r.gq2[p // 3, rows, lanes] = piece
            turned = FACTOR * r.dqr[at, :, lanes].T
            turned = pick(turned + pltpu.roll(turned, 64, 1))
            turned = turned * r.cosine[rows, :] - swap_halves(turned) * r.sine[rows, :]
            r.gqp2[p // 3, rows, lanes] = turned.astype(BF)
    send_gq = paired(6, r.gq2.at[1 - core, pl.ds(0, 128)], r.gq2.at[1 - core, pl.ds(128, 128)])
    send_gqp = paired(7, r.gqp2.at[1 - core, pl.ds(0, 128)], r.gqp2.at[1 - core, pl.ds(128, 128)])
    send_gq.start()
    send_gqp.start()
    for g in range(2):
        for j in range(3):
            lanes = slice(j * 128, j * 128 + 128)
            wide_lanes = slice((g * 3 + j) * 128, (g * 3 + j) * 128 + 128)
            key_sum, value_sum = jnp.zeros((256, 128), F32), jnp.zeros((256, 128), F32)
            for half in range(2):
                rows = slice(half * 64, half * 64 + 64)
                key_sum += FACTOR * dot(r.dqa[half * 2 + g, :, lanes].astype(BF), both(r.q[rows, wide_lanes]))
                value_sum += dot(r.ctx[half * 2 + g, :, lanes], both(r.gmix[rows, wide_lanes]))
            r.dup[g, 0, j] = key_sum.astype(BF)
            r.dup[g, 1, j] = value_sum.astype(BF)
    send_up = paired(8, r.dup.at[1 - core], r.sup)
    send_up.start()
    grad_normed = dot_nt(r.gq2[0, 0:128], r.v_query[:, 0:384]) + dot_nt(r.gq2[1, 0:128], r.v_query[:, 384:768])
    grad_normed += dot_nt(r.gqp2[0, 0:128], r.v_qrope[:, 0:384]) + dot_nt(r.gqp2[1, 0:128], r.v_qrope[:, 384:768])
    r.gnm[0:128] = grad_normed
    send_norm.wait()
    r.normt[...] = r.norm2[...].T
    send_gq.wait()
    send_gqp.wait()
    send_up.wait()
    for o in range(3):
        rows = slice(o * 256, o * 256 + 256)
        for m, right in enumerate((r.gq2, r.gqp2)):
            block = dot(r.normt[rows], right[core]).astype(BF)
            for i in range(3):
                r.early_total[o, i, m] = block[:, i * 128 : i * 128 + 128]
            r.early_total[o, 3, m] = (r.dup[core, m, o].astype(F32) + r.sup[m, o].astype(F32)).astype(BF)
        early.start(0, (o,))

    outer.step(2)
    wide.step(2, 3)

    def fold_near(at, carried):
        for g in range(2):
            near = r.dlat[g, y, rows_at(at * 64, 64), :]
            for k in range(3):
                near = near + r.ro1[k, g, at].astype(F32)
            r.so1[g, at] = near.astype(BF)
        return carried

    def fold_far(at, carried):
        for g in range(2):
            far = r.dlat[2 + g, at, rows_at(z * 64, 64), :]
            for k in range(3):
                far = far + r.rt1[k, g, at].astype(F32)
            r.st1[g, at] = far.astype(BF)
        rot = r.dkr[y, rows_at(at * 64, 64), :]
        for k in range(3):
            rot = rot + r.rk1[k, at].astype(F32)
        r.ks1[at] = rot.astype(BF)
        return carried

    for copy in scatter(0, 0)[0::2]:
        copy.wait()
    lax.fori_loop(0, 4, fold_near, 0)
    for copy in scatter(0, 1)[0::2]:
        copy.start()
    outer.step(3)
    for copy in scatter(1, 0) + scatter(0, 0)[1::2]:
        copy.wait()
    lax.fori_loop(0, 4, fold_far, 0)
    for copy in scatter(1, 1) + scatter(0, 1)[1::2]:
        copy.start()
    wide.step(4)
    early.step(0, 1)
    for copy in scatter(0, 1) + scatter(1, 1):
        copy.wait()
    grad_latents = []
    for g in range(2):
        near = r.so1[g, z].astype(F32)
        far = r.st1[g, y].astype(F32)
        for k in range(3):
            near = near + r.ro2[k, g].astype(F32)
            far = far + r.rt2[k, g].astype(F32)
        piece = jnp.concatenate([near, far], axis=0).astype(BF)
        grad_latents.append(piece)
        r.gl2[g, 0:128] = piece
    send_gl = paired(9, r.gl2.at[1 - core, pl.ds(0, 128)], r.gl2.at[1 - core, pl.ds(128, 128)])
    send_gl.start()
    rot = r.ks1[z].astype(F32)
    for k in range(3):
        rot = rot + r.rk2[k].astype(F32)
    turned = pltpu.roll(rot, 64, 1)
    rot = jnp.concatenate([jnp.where(low64(64), rot, turned), jnp.where(low64(64), turned, rot)], axis=0)
    grad_kpre = (rot * r.cosine[...] - swap_halves(rot) * r.sine[...]).astype(BF)
    grad_normed = r.gnm[0:128] + dot(grad_kpre[:, 0:64], r.v_krope[...])
    for g in range(2):
        grad_normed = grad_normed + dot_nt(grad_latents[g], r.v_latent[:, g * 256 : g * 256 + 256])
    back, gain_attn = norm_back(grad_normed, r.xbuf[...].astype(F32), gain_of(r.norm_attn))
    r.outacc[0:128] = r.gmid[...] + back
    r.grad_tokens[x_hi] = r.outacc[0:64]
    swap_grad = swap(3, r.outacc.at[pl.ds(64, 64)], r.grad_tokens.at[x_hi])
    swap_grad.start()
    gains = r.gains[...]
    for p in range(6):
        gains = gains + jnp.where(gain_row == p, gain_attn[:, p * 128 : p * 128 + 128], 0.0)
    for o in range(3):
        r.late_total[o, 3, 0] = jnp.zeros((256, 128), BF)
    r.late_total[0, 3, 0, 0:16] = gains.astype(BF)
    grad_krope = dot_tn(grad_kpre, r.norm2[0:128]).astype(BF)
    send_gl.wait()
    for o in range(3):
        rows = slice(o * 256, o * 256 + 256)
        block = dot(r.normt[rows], r.gl2[core]).astype(BF)
        for i in range(2):
            r.late_total[o, i, 0] = block[:, i * 128 : i * 128 + 128]
        for part in range(2):
            at = o * 256 + part * 128
            r.late_total[o, 2, 0, part * 64 : part * 64 + 64] = grad_krope[0:64, at : at + 128]
        r.late_total[o, 2, 0, 128:256] = jnp.zeros((128, 128), BF)
        late.start(0, (o,))
    wide.step(5)
    early.step(2)
    late.step(0, 1)
    outer.step(4)
    wide.step(6)
    early.step(3, 4)
    late.step(2)
    early.step(5, 6)
    late.step(3, 4)
    outer.step(5, 6)
    wide.step(7)
    late.step(5, 6)
    outer.step(7)
    early.step(7)
    late.step(7)
    swap_out.wait()
    swap_grad.wait()
    for reduction in (wide, outer, early, late):
        reduction.finish(8)


def layer(small, weights):
    vmem = pl.BlockSpec(memory_space=pltpu.VMEM)
    hbm = pl.BlockSpec(memory_space=pl.ANY)
    smem = pl.BlockSpec(memory_space=pltpu.SMEM)
    return pl.pallas_call(
        layer_kernel,
        out_shape=[jax.ShapeDtypeStruct(shape, kind) for shape, kind in OUTS.values()],
        in_specs=[vmem] * 4 + [smem] * 2 + [hbm] * (1 + len(weights)),
        out_specs=[vmem, vmem] + [hbm] * (len(OUTS) - 2),
        scratch_shapes=list(scratch().values()),
        compiler_params=pltpu.CompilerParams(
            collective_id=1, has_side_effects=True, vmem_limit_bytes=63 * 2**20
        ),
    )(*small, jnp.asarray(rotary_table()), *weights)


def rotary_table():
    halves = ROPE // 2
    powers = -(np.arange(halves, dtype=np.float32) * np.float32(2.0) / np.float32(ROPE))
    freq_list = np.power(np.float32(10000.0), powers, dtype=np.float32)
    phases = (np.arange(2048, dtype=np.float32)[:, None] * freq_list[None, :]).astype(np.float32)
    cosine, sine = np.cos(phases), np.sin(phases)
    return np.concatenate([cosine, cosine, -sine, sine], axis=1).astype(np.float32)


CAST_STEPS = 3


def cast_kernel(
    wide, down, out, early, late, layer_out, grad_tokens,
    o_gate, o_up, o_down, o_query, o_qrope, o_out, o_latent, o_krope, o_upkey, o_upval, o_attn, o_mlp, o_layer, o_tokens,
):
    o_gate[...] = wide[0].astype(F32)
    o_up[...] = wide[1].astype(F32)
    for k in range(8):
        o_down[k * 256 : k * 256 + 256] = down[0, :, k * 256 : k * 256 + 256].astype(F32)
    for source, m, target, width in (
        (early, 0, o_query, 384), (early, 1, o_qrope, 384), (out, 0, o_out, 384), (late, 0, o_latent, 256)
    ):
        target[:, 0:width] = source[m, :, 0:width].astype(F32)
        target[:, width : 2 * width] = source[m, :, 512 : 512 + width].astype(F32)
    for m, target in ((0, o_upkey), (1, o_upval)):
        target[0] = early[m, :, 384:512].astype(F32)
        target[1] = early[m, :, 896:1024].astype(F32)
    step = pl.program_id(0)
    for part in range(2):
        rows = slice(part * 64, part * 64 + 64)
        lanes = rows_at(step * 256 + part * 128, 128, 128)
        o_krope[:, lanes] = late[0, rows, 256:384].astype(F32) + late[0, rows, 768:896].astype(F32)

    @pl.when(step == 0)
    def _():
        gains = late[0, 0:16, 384:512].astype(F32) + late[0, 0:16, 896:1024].astype(F32)
        for p in range(6):
            o_attn[p * 128 : p * 128 + 128] = gains[p]
            o_mlp[p * 128 : p * 128 + 128] = gains[6 + p]
        o_layer[...] = layer_out[...]
        o_tokens[...] = grad_tokens[...]


def cast_sums(layer_out, grad_tokens, wide, out, early, late):
    rows = lambda width: pl.BlockSpec((256, width), lambda i: (i, 0))
    group = lambda n, width: pl.BlockSpec((n, 256, width), lambda i: (0, i, 0))
    ups = pl.BlockSpec((2, 256, 128), lambda i: (0, 0, i))
    whole = lambda shape: pl.BlockSpec(shape, lambda i: (0,) * len(shape))
    shapes = (
        (768, 2048), (768, 2048), (2048, 768), (768, 768), (768, 768), (768, 768), (768, 512), (64, 768),
        (2, 256, 384), (2, 256, 384), (768,), (768,),
    )
    rows_out = (layer_out, grad_tokens)
    return pl.pallas_call(
        cast_kernel,
        grid=(CAST_STEPS,),
        out_shape=[jax.ShapeDtypeStruct(shape, F32) for shape in shapes]
        + [jax.ShapeDtypeStruct(array.shape, array.dtype) for array in rows_out],
        in_specs=[
            group(2, 2048),
            pl.BlockSpec((1, 256, 2048), lambda i: (2, i, 0)),
            group(1, 1024),
            group(2, 1024),
            group(1, 1024),
        ]
        + [whole(array.shape) for array in rows_out],
        out_specs=[rows(2048), rows(2048), pl.BlockSpec((2048, 256), lambda i: (0, i))]
        + [rows(768)] * 3
        + [rows(512), whole((64, 768)), ups, ups, whole((768,)), whole((768,))]
        + [whole(array.shape) for array in rows_out],
        compiler_params=pltpu.CompilerParams(vmem_limit_bytes=63 * 2**20),
    )(wide, wide, out, early, late, layer_out, grad_tokens)


def local(
    tokens, cotangent, group_of_seq, group_weight, norm_attn, w_query, w_qrope, w_latent, w_krope, w_upkey, w_upval,
    w_out, norm_mlp, w_gate, w_up, w_down,
):
    small = (tokens, cotangent, norm_attn, norm_mlp, group_of_seq, group_weight)
    weights = (w_latent, w_krope.T, w_query, w_qrope, w_upkey, w_upval, w_out, w_gate, w_up, w_down)
    gate, up, down, query, qrope, out, latent, krope, upkey, upval, attn, mlp, layer_out, grad_tokens = cast_sums(
        *layer(small, weights)
    )
    return (
        layer_out, grad_tokens, attn, query, qrope, latent, krope.T, upkey, upval, out, mlp, gate, up, down,
    )


def solution(mesh):
    split = P("seq", "blk", None)
    in_specs = (split, split, P("seq")) + (P(),) * 13
    out_specs = (split, split) + (P(),) * 12
    return jax.shard_map(local, mesh=mesh, in_specs=in_specs, out_specs=out_specs, check_vma=False)
```

```python
import jax
import jax.numpy as jnp
import numpy as np
from jax import lax
from jax.sharding import PartitionSpec as P
from jax.experimental import pallas as pl
from jax.experimental.pallas import tpu as pltpu

MESH = pl.DeviceIdType.MESH
BF = jnp.bfloat16
F32 = jnp.float32
EPSILON = 1e-06
ROPE = 64
GROUPS = 4
FACTOR = 128.0**-0.5
LOG2E = 1.4426950408889634
HIDDEN_SCORE = -1e30
ORDERS = ((0, 1, 2), (1, 2, 0), (2, 0, 1))
X_FIRST = ((0, 1, 2), (0, 2, 1), (0, 1, 2))


def coords():
    s = lax.axis_index("seq")
    b = lax.axis_index("blk")
    x = lax.rem(b, 2) * 2 + lax.div(s, 2)
    return x, lax.div(b, 8), lax.rem(lax.div(b, 2), 4), lax.rem(s, 2)


def device(x, y, z, core):
    return (lax.rem(x, 2) * 2 + core, y * 8 + z * 2 + lax.div(x, 2))


def on_ring(place, axis, step):
    spot = list(place)
    spot[axis] = lax.rem(place[axis] + step, 4)
    return device(*spot)


def remote(src, dst, send, recv, peer):
    return pltpu.make_async_remote_copy(
        src_ref=src, dst_ref=dst, send_sem=send, recv_sem=recv, device_id=peer, device_id_type=MESH
    )


def rows_at(start, size, multiple=16):
    return pl.ds(pl.multiple_of(start, multiple), size)


def dot(left, right):
    return jnp.dot(left, right, preferred_element_type=F32)


def dot_nt(left, right):
    return lax.dot_general(left, right, (((1,), (1,)), ((), ())), preferred_element_type=F32)


def dot_tn(left, right):
    return lax.dot_general(left, right, (((0,), (0,)), ((), ())), preferred_element_type=F32)


class Reduction:
    def __init__(self, r, name, place, out, halving, flat=False, orders=ORDERS):
        self.place, self.out, self.halving, self.flat, self.orders = place, out, halving, flat, orders
        for part in ("total", "first", "second", "third", "chunk", "send", "recv", "keep"):
            setattr(self, part, getattr(r, name + "_" + part))
        self.n, self.width = self.total.shape[2], self.total.shape[4]
        counts = stage_counts(halving, flat)
        self.base = [sum(counts[:stage]) for stage in range(9)]

    def spots(self, o):
        a, b, c = self.orders[o]
        return self.place[a], self.place[b], self.place[c]

    def sides(self, o, s):
        me = self.place[self.orders[o][0]]
        odd = lax.rem(me, 2)
        near, far = 1 + 2 * odd, 3 - 2 * odd
        steps = (near, far) if s == 0 else (far, near)
        return steps, lax.rem(me + steps[0], 4), lax.rem(me + steps[1], 4), lax.rem(me + 2, 4)

    def region(self, o, i, row, rows, count=1):
        core, width = self.place[3], self.width
        return self.out.at[:, rows_at(o * 256 + row, rows), rows_at((core * 4 + i) * width, count * width, 128)]

    def moves(self, o, stage):
        i, j, k = self.spots(o)
        if stage == 8:
            x, y, z, core = self.place
            here = self.region(o, 0, 0, 256, 4)
            return [(here, here, device(x, y, z, 1 - core))]
        made = []
        axis = self.orders[o][(0, 0, 1, 2, 2, 1, 0, 0)[stage]]
        if stage in (0, 1, 6, 7) and self.halving:
            for s in range(2):
                steps, front, last, across = self.sides(o, s)
                half = pl.ds(s * 128, 128)
                peer = on_ring(self.place, axis, steps[0 if stage in (0, 7) else 1])
                if stage == 0:
                    made.append((self.total.at[o, front, :, half], self.first.at[o, s, 0], peer))
                    made.append((self.total.at[o, across, :, half], self.first.at[o, s, 1], peer))
                elif stage == 1:
                    made.append((self.total.at[o, last, :, half], self.first.at[o, s, 2], peer))
                else:
                    for spot in (i, last) if stage == 7 else (i,):
                        here = self.region(o, spot, s * 128, 128)
                        made.append((here, here, peer))
            return made
        if stage in (1, 6) or (stage == 4 and self.flat):
            return made
        for step in (1, 2, 3):
            to = lax.rem(self.place[axis] + step, 4)
            peer = on_ring(self.place, axis, step)
            at = step - 1
            if stage == 0:
                made.append((self.total.at[o, to], self.first.at[o, at], peer))
            elif stage == 2:
                made.append((self.total.at[o, i, :, rows_at(to * 64, 64)], self.second.at[o, at], peer))
            elif stage == 3 and self.flat:
                made.append((self.total.at[o, i, :, rows_at(j * 64, 64)], self.third.at[o, k], peer))
            elif stage == 3:
                made.append((self.total.at[o, i, :, rows_at(j * 64 + to * 16, 16)], self.third.at[o, at], peer))
            elif stage == 4:
                made.append((self.chunk.at[o], self.region(o, i, j * 64 + k * 16, 16), peer))
            elif stage == 5:
                here = self.region(o, i, j * 64, 64)
                made.append((self.chunk.at[o] if self.flat else here, here, peer))
            else:
                here = self.region(o, i, 0, 256)
                made.append((here, here, peer))
        return made

    def copies(self, o, stage):
        return [
            remote(src, dst, self.send.at[o, at], self.recv.at[o, self.base[stage] + at], peer)
            for at, (src, dst, peer) in enumerate(self.moves(o, stage))
        ]

    def kept(self, o):
        i, j, k = self.spots(o)
        row, rows = (j * 64, 64) if self.flat else (j * 64 + k * 16, 16)
        return pltpu.make_async_copy(self.chunk.at[o], self.region(o, i, row, rows), self.keep.at[o])

    def start(self, stage, orders=(0, 1, 2)):
        for o in orders:
            for copy in self.copies(o, stage):
                copy.start()
            if stage == 4:
                self.kept(o).start()

    def finish(self, stage, orders=(0, 1, 2)):
        for o in orders:
            for copy in self.copies(o, stage):
                copy.wait()
            if stage == 4:
                self.kept(o).wait()
            if stage < 4:
                self.add(o, stage)

    def step(self, *stages):
        for stage in stages:
            for o in range(3):
                self.finish(stage, (o,))
                self.start(stage + 1, (o,))

    def add(self, o, stage):
        i, j, k = self.spots(o)
        if stage == 1 and not self.halving:
            return

        def body(m, carried):
            if stage < 2 and self.halving:
                for s in range(2):
                    _, _, last, _ = self.sides(o, s)
                    half = slice(s * 128, s * 128 + 128)
                    for spot, slot in ((i, 0), (last, 1)) if stage == 0 else ((i, 2),):
                        acc = self.total[o, spot, m, half, :].astype(F32) + self.first[o, s, slot, m].astype(F32)
                        self.total[o, spot, m, half, :] = acc.astype(BF)
            elif stage == 0:
                for part in range(4):
                    rows = slice(part * 64, part * 64 + 64)
                    acc = self.total[o, i, m, rows, :].astype(F32)
                    for slot in range(3):
                        acc = acc + self.first[o, slot, m, rows, :].astype(F32)
                    self.total[o, i, m, rows, :] = acc.astype(BF)
            elif stage == 2:
                rows = rows_at(j * 64, 64)
                acc = self.total[o, i, m, rows, :].astype(F32)
                for slot in range(3):
                    acc = acc + self.second[o, slot, m].astype(F32)
                self.total[o, i, m, rows, :] = acc.astype(BF)
            elif self.flat:
                self.third[o, k, m] = self.total[o, i, m, rows_at(j * 64, 64), :]
                acc = self.third[o, 0, m].astype(F32)
                for slot in range(1, 4):
                    acc = acc + self.third[o, slot, m].astype(F32)
                self.chunk[o, m] = acc.astype(BF)
            else:
                acc = self.total[o, i, m, rows_at(j * 64 + k * 16, 16), :].astype(F32)
                for slot in range(3):
                    acc = acc + self.third[o, slot, m].astype(F32)
                self.chunk[o, m] = acc.astype(BF)
            return carried

        lax.fori_loop(0, self.n, body, 0)


def stage_counts(halving, flat):
    return (4 if halving else 3, 2 if halving else 0, 3, 3, 0 if flat else 3, 3, 2 if halving else 0, 4 if halving else 3, 1)


def reduction_scratch(name, n, width, halving, flat=False):
    return {
        name + "_total": pltpu.VMEM((3, 4, n, 256, width), BF),
        name + "_first": pltpu.VMEM((3, 2, 3, n, 128, width) if halving else (3, 3, n, 256, width), BF),
        name + "_second": pltpu.VMEM((3, 3, n, 64, width), BF),
        name + "_third": pltpu.VMEM((3, 4, n, 64, width) if flat else (3, 3, n, 16, width), BF),
        name + "_chunk": pltpu.VMEM((3, n, 64 if flat else 16, width), BF),
        name + "_send": pltpu.SemaphoreType.DMA((3, 4)),
        name + "_recv": pltpu.SemaphoreType.DMA((3, sum(stage_counts(halving, flat)))),
        name + "_keep": pltpu.SemaphoreType.DMA((3,)),
    }


WEIGHTS = {
    "w_latent": (768, 512),
    "w_krope": (64, 768),
    "w_query": (768, 768),
    "w_qrope": (768, 768),
    "w_upkey": (2, 256, 384),
    "w_upval": (2, 256, 384),
    "w_out": (768, 768),
    "w_gate": (768, 1024),
    "w_up": (768, 1024),
    "w_down": (1024, 768),
}
SMALL = ("tokens", "cotangent", "norm_attn", "norm_mlp", "group_of_seq", "group_weight")
OUTS = {
    "layer_out": ((2, 64, 768), BF),
    "grad_tokens": ((2, 64, 768), F32),
    "g_wide": ((3, 768, 2048), BF),
    "g_out": ((1, 768, 1024), BF),
    "g_early": ((2, 768, 1024), BF),
    "g_late": ((1, 768, 1024), BF),
}


def scratch():
    vmem, dma = pltpu.VMEM, pltpu.SemaphoreType.DMA
    made = {"v" + name[1:]: vmem(shape, BF) for name, shape in WEIGHTS.items()}
    made.update(
        load_sem=dma((len(WEIGHTS),)),
        table_sem=dma((2,)),
        turns=vmem((128, 128), F32),
        cosine=vmem((128, 128), F32),
        sine=vmem((128, 128), F32),
        swap_sem=dma((4, 2)),
        pair_sem=dma((11, 2)),
        lat_send=dma((2, 2, 3)),
        ag_recv=dma((2, 2, 3)),
        lat_recv=dma((2, 2, 2, 3)),
        fw_sem=dma((2, 7, 2)),
        xbuf=vmem((128, 768), BF),
        cbuf=vmem((128, 768), BF),
        norm2=vmem((256, 768), BF),
        normt=vmem((768, 256), BF),
        krd=vmem((128, 128), F32),
        q=vmem((128, 768), BF),
        qr=vmem((128, 768), BF),
        lat=vmem((4, 4, 4, 64, 256), BF),
        kr=vmem((4, 4, 64, 128), BF),
        latt=vmem((4, 4, 4, 64, 256), BF),
        krt=vmem((2, 4, 128, 256), BF),
        rel=vmem((2, 256, 384), jnp.int32),
        qs=vmem((4, 384, 256), BF),
        ga=vmem((4, 384, 256), BF),
        qrx=vmem((4, 384, 128), BF),
        krm=vmem((2, 4, 256, 128), BF),
        gh=vmem((256, 1024), F32),
        acc=vmem((4, 256, 384), F32),
        ctx=vmem((4, 256, 384), BF),
        dqa=vmem((4, 256, 384), F32),
        logs=vmem((4, 8, 384), F32),
        delta=vmem((4, 8, 384), F32),
        aof=vmem((128, 768), F32),
        ao2=vmem((256, 768), BF),
        middle=vmem((128, 768), F32),
        nm2=vmem((256, 768), BF),
        nmt=vmem((768, 256), BF),
        gb2=vmem((256, 768), BF),
        acts=vmem((3, 256, 1024), BF),
        hidt=vmem((1024, 256), BF),
        outacc=vmem((256, 768), F32),
        gnm=vmem((256, 768), F32),
        outx=vmem((128, 768), F32),
        gnmx=vmem((128, 768), F32),
        outbf=vmem((128, 768), BF),
        gattn=vmem((2, 256, 384), BF),
        gmix=vmem((128, 768), BF),
        dqr=vmem((4, 128, 384), F32),
        dlat=vmem((4, 4, 256, 256), F32),
        dkr=vmem((4, 256, 128), F32),
        skr=vmem((4, 4, 64, 128), BF),
        ro1=vmem((3, 2, 4, 64, 256), BF),
        rk1=vmem((3, 4, 64, 128), BF),
        rt1=vmem((3, 2, 4, 64, 256), BF),
        so1=vmem((2, 4, 64, 256), BF),
        ks1=vmem((4, 64, 128), BF),
        st1=vmem((2, 4, 64, 256), BF),
        ro2=vmem((3, 2, 64, 256), BF),
        rk2=vmem((3, 64, 128), BF),
        rt2=vmem((3, 2, 64, 256), BF),
        gq2=vmem((2, 256, 384), BF),
        gqp2=vmem((2, 256, 384), BF),
        gl2=vmem((2, 256, 256), BF),
        dup=vmem((2, 2, 3, 256, 128), BF),
        sup=vmem((2, 3, 256, 128), BF),
        gmid=vmem((128, 768), F32),
        gains=vmem((16, 128), F32),
    )
    made.update(reduction_scratch("wide", 3, 256, True))
    made.update(reduction_scratch("out", 1, 128, False))
    made.update(reduction_scratch("early", 2, 128, False, True))
    made.update(reduction_scratch("late", 1, 128, False, True))
    return made


class Refs:
    pass


def swap_halves(values):
    lanes = values.shape[-1]
    low = lax.rem(lax.broadcasted_iota(jnp.int32, values.shape, 1), 64) < 32
    return jnp.where(low, pltpu.roll(values, lanes - 32, 1), pltpu.roll(values, 32, 1))


def layer_kernel(*args):
    r = Refs()
    shapes = scratch()
    names = list(SMALL) + ["table"] + list(WEIGHTS) + list(OUTS) + list(shapes)
    for name, ref in zip(names, args, strict=True):
        setattr(r, name, ref)
    place = coords()
    x, y, z, core = place
    x_hi = lax.div(x, 2)
    blk = y * 8 + z * 2 + x_hi
    slot = y * 4 + z
    sibling = device(x, y, z, 1 - core)
    partner = device(lax.rem(x + 2, 4), 3 - y, 3 - z, core)
    peers = [on_ring(place, axis, step) for axis in range(3) for step in (1, 2, 3)] + [sibling, partner]
    low64 = lambda rows: lax.broadcasted_iota(jnp.int32, (rows, 128), 1) < 64
    diagonal = (lax.broadcasted_iota(jnp.int32, (128, 128), 0) < 64) == low64(128)

    def gain_of(ref):
        return ref[...].reshape(1, 768)

    def both(value):
        return jnp.where(diagonal, jnp.concatenate([value, value], axis=0), jnp.zeros((), value.dtype))

    def pick(value):
        return jnp.where(low64(64), value[0:64], value[64:128])

    loads = {}
    for at, name in enumerate(WEIGHTS):
        source = getattr(r, name)
        if name in ("w_gate", "w_up"):
            source = source.at[:, rows_at(core * 1024, 1024, 128)]
        elif name == "w_down":
            source = source.at[rows_at(core * 1024, 1024), :]
        loads[name] = pltpu.make_async_copy(source, getattr(r, "v" + name[1:]), r.load_sem.at[at])
    tables = [
        pltpu.make_async_copy(
            r.table.at[rows_at(where * 64, 64)], r.turns.at[pl.ds(half * 64, 64)], r.table_sem.at[half]
        )
        for half, where in enumerate((blk, 31 - blk))
    ]
    loads["w_latent"].start()
    loads["w_krope"].start()
    for table in tables:
        table.start()
    barrier = pltpu.get_barrier_semaphore()
    for peer in peers:
        pl.semaphore_signal(barrier, inc=1, device_id=peer, device_id_type=MESH)
    pl.semaphore_wait(barrier, len(peers))

    def swap(at, src, dst):
        return remote(src, dst, r.swap_sem.at[at, 0], r.swap_sem.at[at, 1], partner)

    def paired(at, src, dst):
        return remote(src, dst, r.pair_sem.at[at, 0], r.pair_sem.at[at, 1], sibling)

    swap_x = swap(0, r.tokens.at[1 - x_hi], r.xbuf.at[pl.ds(64, 64)])
    swap_c = swap(1, r.cotangent.at[1 - x_hi], r.cbuf.at[pl.ds(64, 64)])
    swap_x.start()
    swap_c.start()
    for name in ("w_query", "w_qrope", "w_upkey"):
        loads[name].start()
    r.xbuf[0:64] = r.tokens[x_hi]
    r.cbuf[0:64] = r.cotangent[x_hi]
    key_row = lax.broadcasted_iota(jnp.int32, (256, 384), 0)
    query_lane = lax.rem(lax.broadcasted_iota(jnp.int32, (256, 384), 1), 64)
    within = lax.rem(key_row, 64) - query_lane
    r.rel[0] = 128 * lax.div(key_row, 64) + within
    r.rel[1] = within - 128 * lax.div(key_row, 64)
    for table in tables:
        table.wait()
    turns = r.turns[...]
    other = pltpu.roll(turns, 64, 1)
    r.cosine[...] = jnp.where(low64(128), turns, other)
    r.sine[...] = jnp.where(low64(128), other, turns)
    swap_x.wait()

    def unit_of(values):
        inverse = lax.rsqrt(jnp.mean(values * values, axis=-1, keepdims=True) + EPSILON)
        return values * inverse, inverse

    unit = unit_of(r.xbuf[...].astype(F32))[0]
    normed = (unit * gain_of(r.norm_attn)).astype(BF)
    r.norm2[0:128] = normed
    send_norm = paired(0, r.norm2.at[pl.ds(0, 128)], r.norm2.at[pl.ds(128, 128)])
    send_norm.start()
    loads["w_latent"].wait()
    loads["w_krope"].wait()
    key_pre = dot_nt(normed, r.v_krope[...])
    r.krd[:, 0:64] = key_pre
    r.krd[:, 64:128] = key_pre
    key_pre = r.krd[...]
    key_rot = (key_pre * r.cosine[...] + swap_halves(key_pre) * r.sine[...]).astype(BF)
    r.kr[y, z] = pick(key_rot)
    latents = dot(normed, r.v_latent[...]).astype(BF)
    for half in range(2):
        for g in range(2):
            r.lat[half * 2 + g, y, z] = latents[half * 64 : half * 64 + 64, g * 256 : g * 256 + 256]

    def gather(part):
        made = []
        axis = (2, 1)[part]
        for step in (1, 2, 3):
            pieces = [r.lat.at[pl.ds(part * 2, 2), y, z]] + ([r.kr.at[y, z]] if part == 0 else [])
            for at, piece in enumerate(pieces):
                send, recv = r.lat_send.at[part, at, step - 1], r.ag_recv.at[part, at, step - 1]
                made.append(remote(piece, piece, send, recv, on_ring(place, axis, step)))
        return made

    for part in range(2):
        for copy in gather(part):
            copy.start()
    for name in ("w_upval", "w_out", "w_gate", "w_up", "w_down"):
        loads[name].start()

    loads["w_query"].wait()
    r.q[...] = dot(normed, r.v_query[...]).astype(BF)
    loads["w_qrope"].wait()
    query_pre = dot(normed, r.v_qrope[...])
    for p in range(6):
        lanes = slice(p * 128, p * 128 + 128)
        piece = query_pre[:, lanes]
        r.qr[:, lanes] = (piece * r.cosine[...] + swap_halves(piece) * r.sine[...]).astype(BF)
    loads["w_upkey"].wait()

    def to_latent(source, weights, target):
        for half in range(2):
            for g in range(2):
                for j in range(3):
                    p = g * 3 + j
                    block = both(source[half * 64 : half * 64 + 64, p * 128 : p * 128 + 128])
                    rows = dot_nt(block, weights[g, :, j * 128 : j * 128 + 128])
                    target[half * 2 + g, j * 128 : j * 128 + 128] = rows.astype(BF)

    to_latent(r.q, r.v_upkey, r.qs)
    for half in range(2):
        for p in range(6):
            pair = r.qr[half * 64 : half * 64 + 64, p * 128 : p * 128 + 128].astype(F32)
            turned = pltpu.roll(pair, 64, 1)
            for odd in range(2):
                front, back = (turned, pair) if odd else (pair, turned)
                at = (p % 3) * 128 + odd * 64
                r.qrx[half * 2 + p // 3, at : at + 64] = jnp.where(low64(64), front, back).astype(BF)

    swap_c.wait()
    group = jnp.where(x_hi == 0, r.group_of_seq[0], r.group_of_seq[1])
    weight = r.group_weight[0]
    for g in range(1, GROUPS):
        weight = jnp.where(group == g, r.group_weight[g], weight)
    r.gb2[0:128] = (r.cbuf[...].astype(F32) * weight).astype(BF)
    send_gb = paired(3, r.gb2.at[pl.ds(0, 128)], r.gb2.at[pl.ds(128, 128)])
    send_gb.start()
    def spread(part, stage):
        axis = (1, 2)[part]
        me = place[axis]
        right, left = on_ring(place, axis, 1), on_ring(place, axis, 3)
        before, after = lax.rem(me + 3, 4), lax.rem(me + 1, 4)

        def plane(which, where):
            return r.lat.at[which, where] if part == 0 else r.lat.at[which, :, where]

        if stage == 0:
            mine = plane(pl.ds(part * 2, 2), me)
            pieces = [(mine, right), (mine, left)]
            if part == 0:
                pieces += [(r.kr.at[me], right), (r.kr.at[me], left)]
        else:
            pieces = [(plane(part * 2, before), right), (plane(part * 2 + 1, after), left)]
            if part == 0:
                pieces += [(r.kr.at[after], left)]
        return [
            remote(piece, piece, r.fw_sem.at[part, stage * 4 + at, 0], r.fw_sem.at[part, stage * 4 + at, 1], peer)
            for at, (piece, peer) in enumerate(pieces)
        ]

    for part in (1, 0):
        for copy in gather(part):
            copy.wait()
        for copy in spread(part, 0):
            copy.start()
    loads["w_down"].wait()
    send_gb.wait()
    for part in range(4):
        cols = slice(part * 256, part * 256 + 256)
        r.gh[:, cols] = dot_nt(r.gb2[...], r.v_down[cols, :])
    for ref in (r.outacc, r.gnm, r.acc, r.dqa, r.dqr, r.dlat, r.dkr):
        ref[...] = jnp.zeros_like(ref)

    for part in (1, 0):
        for copy in spread(part, 0):
            copy.wait()
        for copy in spread(part, 1):
            copy.start()

    def transpose_latents():
        def body(step, carried):
            j, c = lax.div(step, 4), lax.rem(step, 4)
            r.latt[j, c] = r.lat[j, c].reshape(256, 256).T.reshape(4, 64, 256)
            return carried

        lax.fori_loop(0, 16, body, 0)

    query_blk = (blk, 31 - blk)

    counts = (y + 1, 4 - y)

    def masks(half, step):
        first = query_blk[half] * 64
        near = r.rel[0] <= first - 512 * step - 64 * x_hi
        far = r.rel[1] <= first - 1984 + 512 * (3 - step) + 64 * x_hi
        return near, far

    def pair_keys(g, step):
        keys = [r.lat[far * 2 + g, chunk].reshape(256, 256) for far, chunk in ((0, step), (1, 3 - step))]
        return jnp.concatenate(keys, axis=0)

    def pair_scores(at, keys, step):
        rot = jnp.concatenate([r.krm[0, step], r.krm[1, 3 - step]], axis=0)
        return dot_nt(keys, r.qs[at]) + dot_nt(rot, r.qrx[at])

    def pair_turned(g, step):
        turned = [r.latt[far * 2 + g, chunk].reshape(256, 256) for far, chunk in ((0, step), (1, 3 - step))]
        return jnp.concatenate(turned, axis=1)

    for copy in spread(1, 1) + spread(0, 1):
        copy.wait()
    top = lax.broadcasted_iota(jnp.int32, (128, 256), 0) < 64
    for c in range(4):
        rot = r.kr[c].reshape(256, 128).astype(F32)
        r.krm[0, c] = jnp.where(low64(256), rot, 0.0).astype(BF)
        r.krm[1, c] = jnp.where(low64(256), 0.0, rot).astype(BF)
        turned = rot.T
        r.krt[0, c] = jnp.where(top, turned, 0.0).astype(BF)
        r.krt[1, c] = jnp.where(top, 0.0, turned).astype(BF)
    transpose_latents()

    def forward(half):
        def chunk_step(step, state):
            near, far = masks(half, step)
            result = []
            for g in range(2):
                at = half * 2 + g
                high, total = state[g]
                raw = pair_scores(at, pair_keys(g, step), step)
                raws = [jnp.where(near, raw[0:256], HIDDEN_SCORE), jnp.where(far, raw[256:512], HIDDEN_SCORE)]
                new_high = jnp.maximum(high, jnp.max(jnp.maximum(*raws), axis=0, keepdims=True))
                shrink = jnp.exp2((high - new_high) * (FACTOR * LOG2E))
                weights = [jnp.exp2((raw - new_high) * (FACTOR * LOG2E)) for raw in raws]
                total = total * shrink + jnp.sum(weights[0] + weights[1], axis=0, keepdims=True)
                weights = jnp.concatenate([weight.astype(BF) for weight in weights], axis=0)
                mixed = r.acc[at] * shrink + dot(pair_turned(g, step), weights)
                r.acc[at] = mixed
                result.append((new_high, total))
            return tuple(result)

        empty = (jnp.full((1, 384), HIDDEN_SCORE, F32), jnp.zeros((1, 384), F32))
        state = lax.fori_loop(0, counts[half], chunk_step, (empty, empty))
        for g in range(2):
            high, total = state[g]
            at = half * 2 + g
            r.ctx[at] = (r.acc[at] * (1.0 / total)).astype(BF)
            r.logs[at, 0:1] = high * (FACTOR * LOG2E) + jnp.log2(total)

    forward(0)
    forward(1)
    loads["w_upval"].wait()

    def from_latent(source, weights, half, p):
        g, j = p // 3, p % 3
        lanes = slice(j * 128, j * 128 + 128)
        return pick(dot_tn(source[half * 2 + g, :, lanes].astype(BF), weights[g, :, lanes]))

    for half in range(2):
        for p in range(6):
            r.aof[half * 64 : half * 64 + 64, p * 128 : p * 128 + 128] = from_latent(r.ctx, r.v_upval, half, p)
    r.ao2[0:128] = r.aof[...].astype(BF)
    send_ao = paired(1, r.ao2.at[pl.ds(0, 128)], r.ao2.at[pl.ds(128, 128)])
    send_ao.start()

    loads["w_out"].wait()
    middle = r.xbuf[...].astype(F32) + dot(r.ao2[0:128], r.v_out[...])
    r.middle[...] = middle
    unit_mlp = unit_of(middle)[0]
    r.nm2[0:128] = (unit_mlp * gain_of(r.norm_mlp)).astype(BF)
    send_nm = paired(2, r.nm2.at[pl.ds(0, 128)], r.nm2.at[pl.ds(128, 128)])
    send_nm.start()
    loads["w_gate"].wait()
    loads["w_up"].wait()
    send_nm.wait()

    def tile(step, carried):
        at = rows_at(step * 512, 512, 512)
        act = r.nm2[...]
        gate = dot(act, r.v_gate[:, at])
        up = dot(act, r.v_up[:, at])
        sig = jax.nn.sigmoid(gate)
        silu = gate * sig
        hidden = (silu * up).astype(BF)
        grad_hidden = r.gh[:, at]
        grad_gate = (grad_hidden * up * sig * (1.0 + gate * (1.0 - sig))).astype(BF)
        grad_up = (grad_hidden * silu).astype(BF)
        r.acts[0, :, at] = hidden
        r.acts[1, :, at] = grad_gate
        r.acts[2, :, at] = grad_up
        r.outacc[...] += dot(hidden, r.v_down[at, :])
        r.gnm[...] += dot_nt(grad_gate, r.v_gate[:, at]) + dot_nt(grad_up, r.v_up[:, at])
        return carried

    lax.fori_loop(0, 2, tile, 0)
    send_gnm = paired(4, r.gnm.at[pl.ds(128, 128)], r.gnmx)
    send_out = paired(10, r.outacc.at[pl.ds(128, 128)], r.outx)
    send_gnm.start()
    send_out.start()

    wide = Reduction(r, "wide", place, r.g_wide, True)
    outer = Reduction(r, "out", place, r.g_out, False)
    early = Reduction(r, "early", place, r.g_early, False, True)
    late = Reduction(r, "late", place, r.g_late, False, True)
    r.nmt[...] = r.nm2[...].T
    r.hidt[...] = r.acts[0].T
    for o in range(3):
        left = r.nmt[o * 256 : o * 256 + 256]
        for i in range(4):
            cols = slice(i * 256, i * 256 + 256)
            r.wide_total[o, i, 0] = dot(left, r.acts[1, :, cols]).astype(BF)
            r.wide_total[o, i, 1] = dot(left, r.acts[2, :, cols]).astype(BF)
            r.wide_total[o, i, 2] = dot(r.hidt[cols, :], r.gb2[:, o * 256 : o * 256 + 256]).astype(BF)
        wide.start(0, (o,))

    def norm_back(grads, values, gain):
        unit_rows, inverse = unit_of(values)
        scaled = grads * gain
        gain_grad = jnp.sum(grads * unit_rows, axis=0, keepdims=True)
        mean = jnp.mean(scaled * unit_rows, axis=-1, keepdims=True)
        return inverse * (scaled - unit_rows * mean), gain_grad

    send_gnm.wait()
    back, gain_mlp = norm_back(r.gnm[0:128] + r.gnmx[...], r.middle[...], gain_of(r.norm_mlp))
    r.gmid[...] = r.cbuf[...].astype(F32) * weight + back
    gain_row = lax.broadcasted_iota(jnp.int32, (16, 128), 0)
    gains = jnp.zeros((16, 128), F32)
    for p in range(6):
        gains = gains + jnp.where(gain_row == 6 + p, gain_mlp[:, p * 128 : p * 128 + 128], 0.0)
    r.gains[...] = gains
    grad_attn = r.gmid[...].astype(BF)
    for half in range(2):
        r.gattn[half, 0:128] = grad_attn[:, half * 384 : half * 384 + 384]
    send_ga = paired(5, r.gattn.at[1 - core, pl.ds(0, 128)], r.gattn.at[1 - core, pl.ds(128, 128)])
    send_ga.start()
    mixed = dot_nt(grad_attn, r.v_out[...])
    r.gmix[...] = mixed.astype(BF)
    to_latent(r.gmix, r.v_upval, r.ga)
    send_out.wait()
    r.outbf[...] = (r.middle[...] + r.outacc[0:128] + r.outx[...]).astype(BF)
    r.layer_out[x_hi] = r.outbf[0:64]
    swap_out = swap(2, r.outbf.at[pl.ds(64, 64)], r.layer_out.at[x_hi])
    swap_out.start()
    ones = jnp.ones((8, 128), F32)
    for half in range(2):
        for p in range(6):
            here = (slice(half * 64, half * 64 + 64), slice(p * 128, p * 128 + 128))
            block = both(r.gmix[here].astype(F32) * r.aof[here])
            sums = lax.dot_general(
                ones, block, (((1,), (1,)), ((), ())), precision=lax.Precision.HIGHEST, preferred_element_type=F32
            )
            r.delta[half * 2 + p // 3, :, (p % 3) * 128 : (p % 3) * 128 + 128] = sums

    send_ao.wait()
    send_ga.wait()
    r.nmt[...] = r.ao2[...].T
    for o in range(3):
        block = dot(r.nmt[o * 256 : o * 256 + 256], r.gattn[core]).astype(BF)
        for i in range(3):
            r.out_total[o, i, 0] = block[:, i * 128 : i * 128 + 128]
        r.out_total[o, 3, 0] = jnp.zeros((256, 128), BF)
    outer.start(0)

    def backward(half):
        def chunk_step(step, carried):
            near, far = masks(half, step)
            rot_turned = jnp.concatenate([r.krt[0, step], r.krt[1, 3 - step]], axis=1)
            rot_sum = None
            for g in range(2):
                at = half * 2 + g
                keys = pair_keys(g, step)
                raw = pair_scores(at, keys, step)
                weights = jnp.exp2(raw * (FACTOR * LOG2E) - r.logs[at, 0:1])
                weights = [jnp.where(near, weights[0:256], 0.0), jnp.where(far, weights[256:512], 0.0)]
                dprob = dot_nt(keys, r.ga[at]) - r.delta[at, 0:1]
                dscore = [weights[0] * dprob[0:256], weights[1] * dprob[256:512]]
                dscore = jnp.concatenate([part.astype(BF) for part in dscore], axis=0)
                weights = jnp.concatenate([part.astype(BF) for part in weights], axis=0)
                r.dqa[at] += dot(pair_turned(g, step), dscore)
                r.dqr[at] += dot(rot_turned, dscore)
                grads = FACTOR * dot(dscore, r.qs[at]) + dot(weights, r.ga[at])
                r.dlat[g, step] += grads[0:256]
                r.dlat[2 + g, 3 - step] += grads[256:512]
                rots = dot(dscore, r.qrx[at])
                rot_sum = rots if rot_sum is None else rot_sum + rots
            r.dkr[step] += jnp.where(low64(256), FACTOR * rot_sum[0:256], 0.0)
            r.dkr[3 - step] += jnp.where(low64(256), 0.0, FACTOR * rot_sum[256:512])
            return carried

        lax.fori_loop(0, counts[half], chunk_step, 0)

    def narrow(step, carried):
        j, c = lax.div(step, 4), lax.rem(step, 4)
        r.latt[j, c] = r.dlat[j, c].astype(BF).reshape(4, 64, 256)
        return carried

    def scatter(part, phase):
        made = []
        axis = (1, 2)[(part + phase) % 2]
        for step in (1, 2, 3):
            peer = on_ring(place, axis, step)
            to = lax.rem(place[axis] + step, 4)
            at = step - 1
            if part == 0 and phase == 0:
                pieces = [(r.latt.at[pl.ds(0, 2), to], r.ro1.at[at]), (r.skr.at[to], r.rk1.at[at])]
            elif part == 0:
                pieces = [(r.so1.at[:, to], r.ro2.at[at]), (r.ks1.at[to], r.rk2.at[at])]
            elif phase == 0:
                pieces = [(r.latt.at[pl.ds(2, 2), :, to], r.rt1.at[at])]
            else:
                pieces = [(r.st1.at[:, to], r.rt2.at[at])]
            for k, (src, dst) in enumerate(pieces):
                send = r.lat_send.at[part, k, at]
                made.append(remote(src, dst, send, r.lat_recv.at[part, phase, k, at], peer))
        return made

    backward(0)
    wide.step(0)
    backward(1)
    lax.fori_loop(0, 16, narrow, 0)
    for c in range(4):
        r.skr[c] = r.dkr[c].astype(BF).reshape(4, 64, 128)
    for copy in scatter(1, 0) + scatter(0, 0):
        copy.start()
    wide.step(1)
    outer.step(0, 1)

    for half in range(2):
        for p in range(6):
            rows, lanes = slice(half * 64, half * 64 + 64), slice((p % 3) * 128, (p % 3) * 128 + 128)
            at = half * 2 + p // 3
            piece = (FACTOR * from_latent(r.dqa, r.v_upkey, half, p)).astype(BF)
            r.gq2[p // 3, rows, lanes] = piece
            turned = FACTOR * r.dqr[at, :, lanes].T
            turned = pick(turned + pltpu.roll(turned, 64, 1))
            turned = turned * r.cosine[rows, :] - swap_halves(turned) * r.sine[rows, :]
            r.gqp2[p // 3, rows, lanes] = turned.astype(BF)
    send_gq = paired(6, r.gq2.at[1 - core, pl.ds(0, 128)], r.gq2.at[1 - core, pl.ds(128, 128)])
    send_gqp = paired(7, r.gqp2.at[1 - core, pl.ds(0, 128)], r.gqp2.at[1 - core, pl.ds(128, 128)])
    send_gq.start()
    send_gqp.start()
    for g in range(2):
        for j in range(3):
            lanes = slice(j * 128, j * 128 + 128)
            wide_lanes = slice((g * 3 + j) * 128, (g * 3 + j) * 128 + 128)
            key_sum, value_sum = jnp.zeros((256, 128), F32), jnp.zeros((256, 128), F32)
            for half in range(2):
                rows = slice(half * 64, half * 64 + 64)
                key_sum += FACTOR * dot(r.dqa[half * 2 + g, :, lanes].astype(BF), both(r.q[rows, wide_lanes]))
                value_sum += dot(r.ctx[half * 2 + g, :, lanes], both(r.gmix[rows, wide_lanes]))
            r.dup[g, 0, j] = key_sum.astype(BF)
            r.dup[g, 1, j] = value_sum.astype(BF)
    send_up = paired(8, r.dup.at[1 - core], r.sup)
    send_up.start()
    grad_normed = dot_nt(r.gq2[0, 0:128], r.v_query[:, 0:384]) + dot_nt(r.gq2[1, 0:128], r.v_query[:, 384:768])
    grad_normed += dot_nt(r.gqp2[0, 0:128], r.v_qrope[:, 0:384]) + dot_nt(r.gqp2[1, 0:128], r.v_qrope[:, 384:768])
    r.gnm[0:128] = grad_normed
    send_norm.wait()
    r.normt[...] = r.norm2[...].T
    send_gq.wait()
    send_gqp.wait()
    send_up.wait()
    for o in range(3):
        rows = slice(o * 256, o * 256 + 256)
        for m, right in enumerate((r.gq2, r.gqp2)):
            block = dot(r.normt[rows], right[core]).astype(BF)
            for i in range(3):
                r.early_total[o, i, m] = block[:, i * 128 : i * 128 + 128]
            r.early_total[o, 3, m] = (r.dup[core, m, o].astype(F32) + r.sup[m, o].astype(F32)).astype(BF)
        early.start(0, (o,))

    outer.step(2)
    wide.step(2, 3)

    def fold_near(at, carried):
        for g in range(2):
            near = r.dlat[g, y, rows_at(at * 64, 64), :]
            for k in range(3):
                near = near + r.ro1[k, g, at].astype(F32)
            r.so1[g, at] = near.astype(BF)
        return carried

    def fold_far(at, carried):
        for g in range(2):
            far = r.dlat[2 + g, at, rows_at(z * 64, 64), :]
            for k in range(3):
                far = far + r.rt1[k, g, at].astype(F32)
            r.st1[g, at] = far.astype(BF)
        rot = r.dkr[y, rows_at(at * 64, 64), :]
        for k in range(3):
            rot = rot + r.rk1[k, at].astype(F32)
        r.ks1[at] = rot.astype(BF)
        return carried

    for copy in scatter(0, 0)[0::2]:
        copy.wait()
    lax.fori_loop(0, 4, fold_near, 0)
    for copy in scatter(0, 1)[0::2]:
        copy.start()
    outer.step(3)
    for copy in scatter(1, 0) + scatter(0, 0)[1::2]:
        copy.wait()
    lax.fori_loop(0, 4, fold_far, 0)
    for copy in scatter(1, 1) + scatter(0, 1)[1::2]:
        copy.start()
    wide.step(4)
    early.step(0, 1)
    for copy in scatter(0, 1) + scatter(1, 1):
        copy.wait()
    grad_latents = []
    for g in range(2):
        near = r.so1[g, z].astype(F32)
        far = r.st1[g, y].astype(F32)
        for k in range(3):
            near = near + r.ro2[k, g].astype(F32)
            far = far + r.rt2[k, g].astype(F32)
        piece = jnp.concatenate([near, far], axis=0).astype(BF)
        grad_latents.append(piece)
        r.gl2[g, 0:128] = piece
    send_gl = paired(9, r.gl2.at[1 - core, pl.ds(0, 128)], r.gl2.at[1 - core, pl.ds(128, 128)])
    send_gl.start()
    rot = r.ks1[z].astype(F32)
    for k in range(3):
        rot = rot + r.rk2[k].astype(F32)
    turned = pltpu.roll(rot, 64, 1)
    rot = jnp.concatenate([jnp.where(low64(64), rot, turned), jnp.where(low64(64), turned, rot)], axis=0)
    grad_kpre = (rot * r.cosine[...] - swap_halves(rot) * r.sine[...]).astype(BF)
    grad_normed = r.gnm[0:128] + dot(grad_kpre[:, 0:64], r.v_krope[...])
    for g in range(2):
        grad_normed = grad_normed + dot_nt(grad_latents[g], r.v_latent[:, g * 256 : g * 256 + 256])
    back, gain_attn = norm_back(grad_normed, r.xbuf[...].astype(F32), gain_of(r.norm_attn))
    r.outacc[0:128] = r.gmid[...] + back
    r.grad_tokens[x_hi] = r.outacc[0:64]
    swap_grad = swap(3, r.outacc.at[pl.ds(64, 64)], r.grad_tokens.at[x_hi])
    swap_grad.start()
    gains = r.gains[...]
    for p in range(6):
        gains = gains + jnp.where(gain_row == p, gain_attn[:, p * 128 : p * 128 + 128], 0.0)
    for o in range(3):
        r.late_total[o, 3, 0] = jnp.zeros((256, 128), BF)
    r.late_total[0, 3, 0, 0:16] = gains.astype(BF)
    grad_krope = dot_tn(grad_kpre, r.norm2[0:128]).astype(BF)
    send_gl.wait()
    for o in range(3):
        rows = slice(o * 256, o * 256 + 256)
        block = dot(r.normt[rows], r.gl2[core]).astype(BF)
        for i in range(2):
            r.late_total[o, i, 0] = block[:, i * 128 : i * 128 + 128]
        for part in range(2):
            at = o * 256 + part * 128
            r.late_total[o, 2, 0, part * 64 : part * 64 + 64] = grad_krope[0:64, at : at + 128]
        r.late_total[o, 2, 0, 128:256] = jnp.zeros((128, 128), BF)
        late.start(0, (o,))
    wide.step(5)
    early.step(2)
    late.step(0, 1)
    outer.step(4)
    wide.step(6)
    early.step(3, 4)
    late.step(2)
    early.step(5, 6)
    late.step(3, 4)
    outer.step(5, 6)
    wide.step(7)
    late.step(5, 6)
    outer.step(7)
    early.step(7)
    late.step(7)
    swap_out.wait()
    swap_grad.wait()
    for reduction in (wide, outer, early, late):
        reduction.finish(8)


def layer(small, weights):
    vmem = pl.BlockSpec(memory_space=pltpu.VMEM)
    hbm = pl.BlockSpec(memory_space=pl.ANY)
    smem = pl.BlockSpec(memory_space=pltpu.SMEM)
    return pl.pallas_call(
        layer_kernel,
        out_shape=[jax.ShapeDtypeStruct(shape, kind) for shape, kind in OUTS.values()],
        in_specs=[vmem] * 4 + [smem] * 2 + [hbm] * (1 + len(weights)),
        out_specs=[vmem, vmem] + [hbm] * (len(OUTS) - 2),
        scratch_shapes=list(scratch().values()),
        compiler_params=pltpu.CompilerParams(
            collective_id=1, has_side_effects=True, vmem_limit_bytes=63 * 2**20
        ),
    )(*small, jnp.asarray(rotary_table()), *weights)


def rotary_table():
    halves = ROPE // 2
    powers = -(np.arange(halves, dtype=np.float32) * np.float32(2.0) / np.float32(ROPE))
    freq_list = np.power(np.float32(10000.0), powers, dtype=np.float32)
    phases = (np.arange(2048, dtype=np.float32)[:, None] * freq_list[None, :]).astype(np.float32)
    cosine, sine = np.cos(phases), np.sin(phases)
    return np.concatenate([cosine, cosine, -sine, sine], axis=1).astype(np.float32)


CAST_STEPS = 3


def cast_kernel(
    wide, down, out, early, late, layer_out, grad_tokens,
    o_gate, o_up, o_down, o_query, o_qrope, o_out, o_latent, o_krope, o_upkey, o_upval, o_attn, o_mlp, o_layer, o_tokens,
):
    o_gate[...] = wide[0].astype(F32)
    o_up[...] = wide[1].astype(F32)
    for k in range(8):
        o_down[k * 256 : k * 256 + 256] = down[0, :, k * 256 : k * 256 + 256].astype(F32)
    for source, m, target, width in (
        (early, 0, o_query, 384), (early, 1, o_qrope, 384), (out, 0, o_out, 384), (late, 0, o_latent, 256)
    ):
        target[:, 0:width] = source[m, :, 0:width].astype(F32)
        target[:, width : 2 * width] = source[m, :, 512 : 512 + width].astype(F32)
    for m, target in ((0, o_upkey), (1, o_upval)):
        target[0] = early[m, :, 384:512].astype(F32)
        target[1] = early[m, :, 896:1024].astype(F32)
    step = pl.program_id(0)
    for part in range(2):
        rows = slice(part * 64, part * 64 + 64)
        lanes = rows_at(step * 256 + part * 128, 128, 128)
        o_krope[:, lanes] = late[0, rows, 256:384].astype(F32) + late[0, rows, 768:896].astype(F32)

    @pl.when(step == 0)
    def _():
        gains = late[0, 0:16, 384:512].astype(F32) + late[0, 0:16, 896:1024].astype(F32)
        for p in range(6):
            o_attn[p * 128 : p * 128 + 128] = gains[p]
            o_mlp[p * 128 : p * 128 + 128] = gains[6 + p]
        o_layer[...] = layer_out[...]
        o_tokens[...] = grad_tokens[...]


def cast_sums(layer_out, grad_tokens, wide, out, early, late):
    rows = lambda width: pl.BlockSpec((256, width), lambda i: (i, 0))
    group = lambda n, width: pl.BlockSpec((n, 256, width), lambda i: (0, i, 0))
    ups = pl.BlockSpec((2, 256, 128), lambda i: (0, 0, i))
    whole = lambda shape: pl.BlockSpec(shape, lambda i: (0,) * len(shape))
    shapes = (
        (768, 2048), (768, 2048), (2048, 768), (768, 768), (768, 768), (768, 768), (768, 512), (64, 768),
        (2, 256, 384), (2, 256, 384), (768,), (768,),
    )
    rows_out = (layer_out, grad_tokens)
    return pl.pallas_call(
        cast_kernel,
        grid=(CAST_STEPS,),
        out_shape=[jax.ShapeDtypeStruct(shape, F32) for shape in shapes]
        + [jax.ShapeDtypeStruct(array.shape, array.dtype) for array in rows_out],
        in_specs=[
            group(2, 2048),
            pl.BlockSpec((1, 256, 2048), lambda i: (2, i, 0)),
            group(1, 1024),
            group(2, 1024),
            group(1, 1024),
        ]
        + [whole(array.shape) for array in rows_out],
        out_specs=[rows(2048), rows(2048), pl.BlockSpec((2048, 256), lambda i: (0, i))]
        + [rows(768)] * 3
        + [rows(512), whole((64, 768)), ups, ups, whole((768,)), whole((768,))]
        + [whole(array.shape) for array in rows_out],
        compiler_params=pltpu.CompilerParams(vmem_limit_bytes=63 * 2**20),
    )(wide, wide, out, early, late, layer_out, grad_tokens)


def local(
    tokens, cotangent, group_of_seq, group_weight, norm_attn, w_query, w_qrope, w_latent, w_krope, w_upkey, w_upval,
    w_out, norm_mlp, w_gate, w_up, w_down,
):
    small = (tokens, cotangent, norm_attn, norm_mlp, group_of_seq, group_weight)
    weights = (w_latent, w_krope.T, w_query, w_qrope, w_upkey, w_upval, w_out, w_gate, w_up, w_down)
    gate, up, down, query, qrope, out, latent, krope, upkey, upval, attn, mlp, layer_out, grad_tokens = cast_sums(
        *layer(small, weights)
    )
    return (
        layer_out, grad_tokens, attn, query, qrope, latent, krope.T, upkey, upval, out, mlp, gate, up, down,
    )


def solution(mesh):
    split = P("seq", "blk", None)
    in_specs = (split, split, P("seq")) + (P(),) * 13
    out_specs = (split, split) + (P(),) * 12
    return jax.shard_map(local, mesh=mesh, in_specs=in_specs, out_specs=out_specs, check_vma=False)
```

```python
import jax
import jax.numpy as jnp
import numpy as np
from jax import lax
from jax.sharding import PartitionSpec as P
from jax.experimental import pallas as pl
from jax.experimental.pallas import tpu as pltpu

MESH = pl.DeviceIdType.MESH
BF = jnp.bfloat16
F32 = jnp.float32
EPSILON = 1e-06
ROPE = 64
GROUPS = 4
FACTOR = 128.0**-0.5
LOG2E = 1.4426950408889634
HIDDEN_SCORE = -1e30
ORDERS = ((0, 1, 2), (1, 2, 0), (2, 0, 1))
X_FIRST = ((0, 1, 2), (0, 2, 1), (0, 1, 2))


def coords():
    s = lax.axis_index("seq")
    b = lax.axis_index("blk")
    x = lax.rem(b, 2) * 2 + lax.div(s, 2)
    return x, lax.div(b, 8), lax.rem(lax.div(b, 2), 4), lax.rem(s, 2)


def device(x, y, z, core):
    return (lax.rem(x, 2) * 2 + core, y * 8 + z * 2 + lax.div(x, 2))


def on_ring(place, axis, step):
    spot = list(place)
    spot[axis] = lax.rem(place[axis] + step, 4)
    return device(*spot)


def remote(src, dst, send, recv, peer):
    return pltpu.make_async_remote_copy(
        src_ref=src, dst_ref=dst, send_sem=send, recv_sem=recv, device_id=peer, device_id_type=MESH
    )


def rows_at(start, size, multiple=16):
    return pl.ds(pl.multiple_of(start, multiple), size)


def dot(left, right):
    return jnp.dot(left, right, preferred_element_type=F32)


def dot_nt(left, right):
    return lax.dot_general(left, right, (((1,), (1,)), ((), ())), preferred_element_type=F32)


def dot_tn(left, right):
    return lax.dot_general(left, right, (((0,), (0,)), ((), ())), preferred_element_type=F32)


class Reduction:
    def __init__(self, r, name, place, out, halving, flat=False, orders=ORDERS):
        self.place, self.out, self.halving, self.flat, self.orders = place, out, halving, flat, orders
        for part in ("total", "first", "second", "third", "chunk", "send", "recv", "keep"):
            setattr(self, part, getattr(r, name + "_" + part))
        self.n, self.width = self.total.shape[2], self.total.shape[4]
        counts = stage_counts(halving, flat)
        self.base = [sum(counts[:stage]) for stage in range(9)]

    def spots(self, o):
        a, b, c = self.orders[o]
        return self.place[a], self.place[b], self.place[c]

    def sides(self, o, s):
        me = self.place[self.orders[o][0]]
        odd = lax.rem(me, 2)
        near, far = 1 + 2 * odd, 3 - 2 * odd
        steps = (near, far) if s == 0 else (far, near)
        return steps, lax.rem(me + steps[0], 4), lax.rem(me + steps[1], 4), lax.rem(me + 2, 4)

    def region(self, o, i, row, rows, count=1):
        core, width = self.place[3], self.width
        return self.out.at[:, rows_at(o * 256 + row, rows), rows_at((core * 4 + i) * width, count * width, 128)]

    def moves(self, o, stage):
        i, j, k = self.spots(o)
        if stage == 8:
            x, y, z, core = self.place
            here = self.region(o, 0, 0, 256, 4)
            return [(here, here, device(x, y, z, 1 - core))]
        made = []
        axis = self.orders[o][(0, 0, 1, 2, 2, 1, 0, 0)[stage]]
        if stage in (0, 1, 6, 7) and self.halving:
            for s in range(2):
                steps, front, last, across = self.sides(o, s)
                half = pl.ds(s * 128, 128)
                peer = on_ring(self.place, axis, steps[0 if stage in (0, 7) else 1])
                if stage == 0:
                    made.append((self.total.at[o, front, :, half], self.first.at[o, s, 0], peer))
                    made.append((self.total.at[o, across, :, half], self.first.at[o, s, 1], peer))
                elif stage == 1:
                    made.append((self.total.at[o, last, :, half], self.first.at[o, s, 2], peer))
                else:
                    for spot in (i, last) if stage == 7 else (i,):
                        here = self.region(o, spot, s * 128, 128)
                        made.append((here, here, peer))
            return made
        if stage in (1, 6) or (stage == 4 and self.flat):
            return made
        for step in (1, 2, 3):
            to = lax.rem(self.place[axis] + step, 4)
            peer = on_ring(self.place, axis, step)
            at = step - 1
            if stage == 0:
                made.append((self.total.at[o, to], self.first.at[o, at], peer))
            elif stage == 2:
                made.append((self.total.at[o, i, :, rows_at(to * 64, 64)], self.second.at[o, at], peer))
            elif stage == 3 and self.flat:
                made.append((self.total.at[o, i, :, rows_at(j * 64, 64)], self.third.at[o, k], peer))
            elif stage == 3:
                made.append((self.total.at[o, i, :, rows_at(j * 64 + to * 16, 16)], self.third.at[o, at], peer))
            elif stage == 4:
                made.append((self.chunk.at[o], self.region(o, i, j * 64 + k * 16, 16), peer))
            elif stage == 5:
                here = self.region(o, i, j * 64, 64)
                made.append((self.chunk.at[o] if self.flat else here, here, peer))
            else:
                here = self.region(o, i, 0, 256)
                made.append((here, here, peer))
        return made

    def copies(self, o, stage):
        return [
            remote(src, dst, self.send.at[o, at], self.recv.at[o, self.base[stage] + at], peer)
            for at, (src, dst, peer) in enumerate(self.moves(o, stage))
        ]

    def kept(self, o):
        i, j, k = self.spots(o)
        row, rows = (j * 64, 64) if self.flat else (j * 64 + k * 16, 16)
        return pltpu.make_async_copy(self.chunk.at[o], self.region(o, i, row, rows), self.keep.at[o])

    def start(self, stage, orders=(0, 1, 2)):
        for o in orders:
            for copy in self.copies(o, stage):
                copy.start()
            if stage == 4:
                self.kept(o).start()

    def finish(self, stage, orders=(0, 1, 2)):
        for o in orders:
            for copy in self.copies(o, stage):
                copy.wait()
            if stage == 4:
                self.kept(o).wait()
            if stage < 4:
                self.add(o, stage)

    def step(self, *stages):
        for stage in stages:
            for o in range(3):
                self.finish(stage, (o,))
                self.start(stage + 1, (o,))

    def add(self, o, stage):
        i, j, k = self.spots(o)
        if stage == 1 and not self.halving:
            return

        def body(m, carried):
            if stage < 2 and self.halving:
                for s in range(2):
                    _, _, last, _ = self.sides(o, s)
                    half = slice(s * 128, s * 128 + 128)
                    for spot, slot in ((i, 0), (last, 1)) if stage == 0 else ((i, 2),):
                        acc = self.total[o, spot, m, half, :].astype(F32) + self.first[o, s, slot, m].astype(F32)
                        self.total[o, spot, m, half, :] = acc.astype(BF)
            elif stage == 0:
                for part in range(4):
                    rows = slice(part * 64, part * 64 + 64)
                    acc = self.total[o, i, m, rows, :].astype(F32)
                    for slot in range(3):
                        acc = acc + self.first[o, slot, m, rows, :].astype(F32)
                    self.total[o, i, m, rows, :] = acc.astype(BF)
            elif stage == 2:
                rows = rows_at(j * 64, 64)
                acc = self.total[o, i, m, rows, :].astype(F32)
                for slot in range(3):
                    acc = acc + self.second[o, slot, m].astype(F32)
                self.total[o, i, m, rows, :] = acc.astype(BF)
            elif self.flat:
                self.third[o, k, m] = self.total[o, i, m, rows_at(j * 64, 64), :]
                acc = self.third[o, 0, m].astype(F32)
                for slot in range(1, 4):
                    acc = acc + self.third[o, slot, m].astype(F32)
                self.chunk[o, m] = acc.astype(BF)
            else:
                acc = self.total[o, i, m, rows_at(j * 64 + k * 16, 16), :].astype(F32)
                for slot in range(3):
                    acc = acc + self.third[o, slot, m].astype(F32)
                self.chunk[o, m] = acc.astype(BF)
            return carried

        lax.fori_loop(0, self.n, body, 0)


def stage_counts(halving, flat):
    return (4 if halving else 3, 2 if halving else 0, 3, 3, 0 if flat else 3, 3, 2 if halving else 0, 4 if halving else 3, 1)


def reduction_scratch(name, n, width, halving, flat=False):
    return {
        name + "_total": pltpu.VMEM((3, 4, n, 256, width), BF),
        name + "_first": pltpu.VMEM((3, 2, 3, n, 128, width) if halving else (3, 3, n, 256, width), BF),
        name + "_second": pltpu.VMEM((3, 3, n, 64, width), BF),
        name + "_third": pltpu.VMEM((3, 4, n, 64, width) if flat else (3, 3, n, 16, width), BF),
        name + "_chunk": pltpu.VMEM((3, n, 64 if flat else 16, width), BF),
        name + "_send": pltpu.SemaphoreType.DMA((3, 4)),
        name + "_recv": pltpu.SemaphoreType.DMA((3, sum(stage_counts(halving, flat)))),
        name + "_keep": pltpu.SemaphoreType.DMA((3,)),
    }


WEIGHTS = {
    "w_latent": (768, 512),
    "w_krope": (64, 768),
    "w_query": (768, 768),
    "w_qrope": (768, 768),
    "w_upkey": (2, 256, 384),
    "w_upval": (2, 256, 384),
    "w_out": (768, 768),
    "w_gate": (768, 1024),
    "w_up": (768, 1024),
    "w_down": (1024, 768),
}
SMALL = ("tokens", "cotangent", "norm_attn", "norm_mlp", "group_of_seq", "group_weight")
OUTS = {
    "layer_out": ((2, 64, 768), BF),
    "grad_tokens": ((2, 64, 768), F32),
    "g_wide": ((3, 768, 2048), BF),
    "g_out": ((1, 768, 1024), BF),
    "g_early": ((2, 768, 1024), BF),
    "g_late": ((1, 768, 1024), BF),
}


def scratch():
    vmem, dma = pltpu.VMEM, pltpu.SemaphoreType.DMA
    made = {"v" + name[1:]: vmem(shape, BF) for name, shape in WEIGHTS.items()}
    made.update(
        load_sem=dma((len(WEIGHTS),)),
        table_sem=dma((2,)),
        turns=vmem((128, 128), F32),
        cosine=vmem((128, 128), F32),
        sine=vmem((128, 128), F32),
        swap_sem=dma((4, 2)),
        pair_sem=dma((11, 2)),
        lat_send=dma((2, 2, 3)),
        ag_recv=dma((2, 2, 3)),
        lat_recv=dma((2, 2, 2, 3)),
        fw_sem=dma((2, 7, 2)),
        xbuf=vmem((128, 768), BF),
        cbuf=vmem((128, 768), BF),
        norm2=vmem((256, 768), BF),
        normt=vmem((768, 256), BF),
        krd=vmem((128, 128), F32),
        q=vmem((128, 768), BF),
        qr=vmem((128, 768), BF),
        lat=vmem((4, 4, 4, 64, 256), BF),
        kr=vmem((4, 4, 64, 128), BF),
        latt=vmem((4, 4, 4, 64, 256), BF),
        krt=vmem((2, 4, 128, 256), BF),
        rel=vmem((2, 256, 384), jnp.int32),
        qs=vmem((4, 384, 256), BF),
        ga=vmem((4, 384, 256), BF),
        qrx=vmem((4, 384, 128), BF),
        krm=vmem((2, 4, 256, 128), BF),
        gh=vmem((256, 1024), F32),
        acc=vmem((4, 256, 384), F32),
        ctx=vmem((4, 256, 384), BF),
        dqa=vmem((4, 256, 384), F32),
        logs=vmem((4, 8, 384), F32),
        delta=vmem((4, 8, 384), F32),
        aof=vmem((128, 768), F32),
        ao2=vmem((256, 768), BF),
        middle=vmem((128, 768), F32),
        nm2=vmem((256, 768), BF),
        nmt=vmem((768, 256), BF),
        gb2=vmem((256, 768), BF),
        acts=vmem((3, 256, 1024), BF),
        hidt=vmem((1024, 256), BF),
        outacc=vmem((256, 768), F32),
        gnm=vmem((256, 768), F32),
        outx=vmem((128, 768), F32),
        gnmx=vmem((128, 768), F32),
        outbf=vmem((128, 768), BF),
        gattn=vmem((2, 256, 384), BF),
        gmix=vmem((128, 768), BF),
        dqr=vmem((4, 128, 384), F32),
        dlat=vmem((4, 4, 256, 256), F32),
        dkr=vmem((4, 256, 128), F32),
        skr=vmem((4, 4, 64, 128), BF),
        ro1=vmem((3, 2, 4, 64, 256), BF),
        rk1=vmem((3, 4, 64, 128), BF),
        rt1=vmem((3, 2, 4, 64, 256), BF),
        so1=vmem((2, 4, 64, 256), BF),
        ks1=vmem((4, 64, 128), BF),
        st1=vmem((2, 4, 64, 256), BF),
        ro2=vmem((3, 2, 64, 256), BF),
        rk2=vmem((3, 64, 128), BF),
        rt2=vmem((3, 2, 64, 256), BF),
        gq2=vmem((2, 256, 384), BF),
        gqp2=vmem((2, 256, 384), BF),
        gl2=vmem((2, 256, 256), BF),
        dup=vmem((2, 2, 3, 256, 128), BF),
        sup=vmem((2, 3, 256, 128), BF),
        gmid=vmem((128, 768), F32),
        gains=vmem((16, 128), F32),
    )
    made.update(reduction_scratch("wide", 3, 256, True))
    made.update(reduction_scratch("out", 1, 128, False))
    made.update(reduction_scratch("early", 2, 128, False, True))
    made.update(reduction_scratch("late", 1, 128, False, True))
    return made


class Refs:
    pass


def swap_halves(values):
    lanes = values.shape[-1]
    low = lax.rem(lax.broadcasted_iota(jnp.int32, values.shape, 1), 64) < 32
    return jnp.where(low, pltpu.roll(values, lanes - 32, 1), pltpu.roll(values, 32, 1))


def layer_kernel(*args):
    r = Refs()
    shapes = scratch()
    names = list(SMALL) + ["table"] + list(WEIGHTS) + list(OUTS) + list(shapes)
    for name, ref in zip(names, args, strict=True):
        setattr(r, name, ref)
    place = coords()
    x, y, z, core = place
    x_hi = lax.div(x, 2)
    blk = y * 8 + z * 2 + x_hi
    slot = y * 4 + z
    sibling = device(x, y, z, 1 - core)
    partner = device(lax.rem(x + 2, 4), 3 - y, 3 - z, core)
    peers = [on_ring(place, axis, step) for axis in range(3) for step in (1, 2, 3)] + [sibling, partner]
    low64 = lambda rows: lax.broadcasted_iota(jnp.int32, (rows, 128), 1) < 64
    diagonal = (lax.broadcasted_iota(jnp.int32, (128, 128), 0) < 64) == low64(128)

    def gain_of(ref):
        return ref[...].reshape(1, 768)

    def both(value):
        return jnp.where(diagonal, jnp.concatenate([value, value], axis=0), jnp.zeros((), value.dtype))

    def pick(value):
        return jnp.where(low64(64), value[0:64], value[64:128])

    loads = {}
    for at, name in enumerate(WEIGHTS):
        source = getattr(r, name)
        if name in ("w_gate", "w_up"):
            source = source.at[:, rows_at(core * 1024, 1024, 128)]
        elif name == "w_down":
            source = source.at[rows_at(core * 1024, 1024), :]
        loads[name] = pltpu.make_async_copy(source, getattr(r, "v" + name[1:]), r.load_sem.at[at])
    tables = [
        pltpu.make_async_copy(
            r.table.at[rows_at(where * 64, 64)], r.turns.at[pl.ds(half * 64, 64)], r.table_sem.at[half]
        )
        for half, where in enumerate((blk, 31 - blk))
    ]
    loads["w_latent"].start()
    loads["w_krope"].start()
    for table in tables:
        table.start()
    barrier = pltpu.get_barrier_semaphore()
    for peer in peers:
        pl.semaphore_signal(barrier, inc=1, device_id=peer, device_id_type=MESH)
    pl.semaphore_wait(barrier, len(peers))

    def swap(at, src, dst):
        return remote(src, dst, r.swap_sem.at[at, 0], r.swap_sem.at[at, 1], partner)

    def paired(at, src, dst):
        return remote(src, dst, r.pair_sem.at[at, 0], r.pair_sem.at[at, 1], sibling)

    swap_x = swap(0, r.tokens.at[1 - x_hi], r.xbuf.at[pl.ds(64, 64)])
    swap_c = swap(1, r.cotangent.at[1 - x_hi], r.cbuf.at[pl.ds(64, 64)])
    swap_x.start()
    swap_c.start()
    for name in ("w_query", "w_qrope", "w_upkey"):
        loads[name].start()
    r.xbuf[0:64] = r.tokens[x_hi]
    r.cbuf[0:64] = r.cotangent[x_hi]
    key_row = lax.broadcasted_iota(jnp.int32, (256, 384), 0)
    query_lane = lax.rem(lax.broadcasted_iota(jnp.int32, (256, 384), 1), 64)
    within = lax.rem(key_row, 64) - query_lane
    r.rel[0] = 128 * lax.div(key_row, 64) + within
    r.rel[1] = within - 128 * lax.div(key_row, 64)
    for table in tables:
        table.wait()
    turns = r.turns[...]
    other = pltpu.roll(turns, 64, 1)
    r.cosine[...] = jnp.where(low64(128), turns, other)
    r.sine[...] = jnp.where(low64(128), other, turns)
    def unit_of(values):
        inverse = lax.rsqrt(jnp.mean(values * values, axis=-1, keepdims=True) + EPSILON)
        return values * inverse, inverse

    def start_half(half):
        rows = slice(half * 64, half * 64 + 64)
        unit = unit_of(r.xbuf[rows].astype(F32))[0]
        normed = (unit * gain_of(r.norm_attn)).astype(BF)
        r.norm2[rows] = normed
        latents = dot(normed, r.v_latent[...]).astype(BF)
        for g in range(2):
            r.lat[half * 2 + g, y, z] = latents[:, g * 256 : g * 256 + 256]

    def gather(part):
        made = []
        axis = (2, 1)[part]
        for step in (1, 2, 3):
            pieces = [r.lat.at[pl.ds(part * 2, 2), y, z]] + ([r.kr.at[y, z]] if part == 0 else [])
            for at, piece in enumerate(pieces):
                send, recv = r.lat_send.at[part, at, step - 1], r.ag_recv.at[part, at, step - 1]
                made.append(remote(piece, piece, send, recv, on_ring(place, axis, step)))
        return made

    loads["w_latent"].wait()
    start_half(0)
    for copy in gather(0)[0::2]:
        copy.start()
    swap_x.wait()
    start_half(1)
    for copy in gather(1):
        copy.start()
    loads["w_krope"].wait()
    key_pre = dot_nt(r.norm2[0:128], r.v_krope[...])
    r.krd[:, 0:64] = key_pre
    r.krd[:, 64:128] = key_pre
    key_pre = r.krd[...]
    key_rot = (key_pre * r.cosine[...] + swap_halves(key_pre) * r.sine[...]).astype(BF)
    r.kr[y, z] = pick(key_rot)
    for copy in gather(0)[1::2]:
        copy.start()
    send_norm = paired(0, r.norm2.at[pl.ds(0, 128)], r.norm2.at[pl.ds(128, 128)])
    send_norm.start()
    normed = r.norm2[0:128]
    for name in ("w_upval", "w_out", "w_gate", "w_up", "w_down"):
        loads[name].start()

    loads["w_query"].wait()
    r.q[...] = dot(normed, r.v_query[...]).astype(BF)
    loads["w_qrope"].wait()
    query_pre = dot(normed, r.v_qrope[...])
    for p in range(6):
        lanes = slice(p * 128, p * 128 + 128)
        piece = query_pre[:, lanes]
        r.qr[:, lanes] = (piece * r.cosine[...] + swap_halves(piece) * r.sine[...]).astype(BF)
    loads["w_upkey"].wait()

    def to_latent(source, weights, target):
        for half in range(2):
            for g in range(2):
                for j in range(3):
                    p = g * 3 + j
                    block = both(source[half * 64 : half * 64 + 64, p * 128 : p * 128 + 128])
                    rows = dot_nt(block, weights[g, :, j * 128 : j * 128 + 128])
                    target[half * 2 + g, j * 128 : j * 128 + 128] = rows.astype(BF)

    to_latent(r.q, r.v_upkey, r.qs)
    for half in range(2):
        for p in range(6):
            pair = r.qr[half * 64 : half * 64 + 64, p * 128 : p * 128 + 128].astype(F32)
            turned = pltpu.roll(pair, 64, 1)
            for odd in range(2):
                front, back = (turned, pair) if odd else (pair, turned)
                at = (p % 3) * 128 + odd * 64
                r.qrx[half * 2 + p // 3, at : at + 64] = jnp.where(low64(64), front, back).astype(BF)

    swap_c.wait()
    group = jnp.where(x_hi == 0, r.group_of_seq[0], r.group_of_seq[1])
    weight = r.group_weight[0]
    for g in range(1, GROUPS):
        weight = jnp.where(group == g, r.group_weight[g], weight)
    r.gb2[0:128] = (r.cbuf[...].astype(F32) * weight).astype(BF)
    send_gb = paired(3, r.gb2.at[pl.ds(0, 128)], r.gb2.at[pl.ds(128, 128)])
    send_gb.start()
    def spread(part, stage):
        axis = (1, 2)[part]
        me = place[axis]
        right, left = on_ring(place, axis, 1), on_ring(place, axis, 3)
        before, after = lax.rem(me + 3, 4), lax.rem(me + 1, 4)

        def plane(which, where):
            return r.lat.at[which, where] if part == 0 else r.lat.at[which, :, where]

        if stage == 0:
            mine = plane(pl.ds(part * 2, 2), me)
            pieces = [(mine, right), (mine, left)]
            if part == 0:
                pieces += [(r.kr.at[me], right), (r.kr.at[me], left)]
        else:
            pieces = [(plane(part * 2, before), right), (plane(part * 2 + 1, after), left)]
            if part == 0:
                pieces += [(r.kr.at[after], left)]
        return [
            remote(piece, piece, r.fw_sem.at[part, stage * 4 + at, 0], r.fw_sem.at[part, stage * 4 + at, 1], peer)
            for at, (piece, peer) in enumerate(pieces)
        ]

    for part in (1, 0):
        for copy in gather(part):
            copy.wait()
        for copy in spread(part, 0):
            copy.start()
    loads["w_down"].wait()
    send_gb.wait()
    for part in range(4):
        cols = slice(part * 256, part * 256 + 256)
        r.gh[:, cols] = dot_nt(r.gb2[...], r.v_down[cols, :])
    for ref in (r.acc, r.dqa, r.dqr, r.dlat, r.dkr):
        ref[...] = jnp.zeros_like(ref)

    for part in (1, 0):
        for copy in spread(part, 0):
            copy.wait()
        for copy in spread(part, 1):
            copy.start()

    top = lax.broadcasted_iota(jnp.int32, (128, 256), 0) < 64

    def turn(j, c):
        r.latt[j, c] = r.lat[j, c].reshape(256, 256).T.reshape(4, 64, 256)

    def turn_rot(c):
        rot = r.kr[c].reshape(256, 128).astype(F32)
        r.krm[0, c] = jnp.where(low64(256), rot, 0.0).astype(BF)
        r.krm[1, c] = jnp.where(low64(256), 0.0, rot).astype(BF)
        turned = rot.T
        r.krt[0, c] = jnp.where(top, turned, 0.0).astype(BF)
        r.krt[1, c] = jnp.where(top, 0.0, turned).astype(BF)

    for step in (0, 1, 3):
        plane = lax.rem(y + step, 4)
        turn(0, plane)
        turn(1, plane)
        turn_rot(plane)

    query_blk = (blk, 31 - blk)

    counts = (y + 1, 4 - y)

    def masks(half, step):
        first = query_blk[half] * 64
        near = r.rel[0] <= first - 512 * step - 64 * x_hi
        far = r.rel[1] <= first - 1984 + 512 * (3 - step) + 64 * x_hi
        return near, far

    def pair_keys(g, step):
        keys = [r.lat[far * 2 + g, chunk].reshape(256, 256) for far, chunk in ((0, step), (1, 3 - step))]
        return jnp.concatenate(keys, axis=0)

    def pair_scores(at, keys, step):
        rot = jnp.concatenate([r.krm[0, step], r.krm[1, 3 - step]], axis=0)
        return dot_nt(keys, r.qs[at]) + dot_nt(rot, r.qrx[at])

    def pair_turned(g, step):
        turned = [r.latt[far * 2 + g, chunk].reshape(256, 256) for far, chunk in ((0, step), (1, 3 - step))]
        return jnp.concatenate(turned, axis=1)

    for copy in spread(1, 1) + spread(0, 1):
        copy.wait()
    across = lax.rem(y + 2, 4)
    turn(0, across)
    turn(1, across)
    turn_rot(across)
    for c in range(4):
        turn(2, c)
        turn(3, c)

    def forward(half):
        def chunk_step(step, state):
            near, far = masks(half, step)
            result = []
            for g in range(2):
                at = half * 2 + g
                high, total = state[g]
                raw = pair_scores(at, pair_keys(g, step), step)
                raws = [jnp.where(near, raw[0:256], HIDDEN_SCORE), jnp.where(far, raw[256:512], HIDDEN_SCORE)]
                new_high = jnp.maximum(high, jnp.max(jnp.maximum(*raws), axis=0, keepdims=True))
                shrink = jnp.exp2((high - new_high) * (FACTOR * LOG2E))
                weights = [jnp.exp2((raw - new_high) * (FACTOR * LOG2E)) for raw in raws]
                total = total * shrink + jnp.sum(weights[0] + weights[1], axis=0, keepdims=True)
                weights = jnp.concatenate([weight.astype(BF) for weight in weights], axis=0)
                mixed = r.acc[at] * shrink + dot(pair_turned(g, step), weights)
                r.acc[at] = mixed
                result.append((new_high, total))
            return tuple(result)

        empty = (jnp.full((1, 384), HIDDEN_SCORE, F32), jnp.zeros((1, 384), F32))
        state = lax.fori_loop(0, counts[half], chunk_step, (empty, empty))
        for g in range(2):
            high, total = state[g]
            at = half * 2 + g
            r.ctx[at] = (r.acc[at] * (1.0 / total)).astype(BF)
            r.logs[at, 0:1] = high * (FACTOR * LOG2E) + jnp.log2(total)

    forward(0)
    forward(1)
    loads["w_upval"].wait()

    def from_latent(source, weights, half, p):
        g, j = p // 3, p % 3
        lanes = slice(j * 128, j * 128 + 128)
        return pick(dot_tn(source[half * 2 + g, :, lanes].astype(BF), weights[g, :, lanes]))

    for half in range(2):
        for p in range(6):
            r.aof[half * 64 : half * 64 + 64, p * 128 : p * 128 + 128] = from_latent(r.ctx, r.v_upval, half, p)
    r.ao2[0:128] = r.aof[...].astype(BF)
    send_ao = paired(1, r.ao2.at[pl.ds(0, 128)], r.ao2.at[pl.ds(128, 128)])
    send_ao.start()

    loads["w_out"].wait()
    middle = r.xbuf[...].astype(F32) + dot(r.ao2[0:128], r.v_out[...])
    r.middle[...] = middle
    unit_mlp = unit_of(middle)[0]
    r.nm2[0:128] = (unit_mlp * gain_of(r.norm_mlp)).astype(BF)
    send_nm = paired(2, r.nm2.at[pl.ds(0, 128)], r.nm2.at[pl.ds(128, 128)])
    send_nm.start()
    loads["w_gate"].wait()
    loads["w_up"].wait()
    r.nmt[:, 0:128] = r.nm2[0:128].T
    send_nm.wait()

    def tile(step, carried):
        at = rows_at(step * 512, 512, 512)
        act = r.nm2[...]
        gate = dot(act, r.v_gate[:, at])
        up = dot(act, r.v_up[:, at])
        sig = jax.nn.sigmoid(gate)
        silu = gate * sig
        hidden = (silu * up).astype(BF)
        grad_hidden = r.gh[:, at]
        grad_gate = (grad_hidden * up * sig * (1.0 + gate * (1.0 - sig))).astype(BF)
        grad_up = (grad_hidden * silu).astype(BF)
        r.acts[0, :, at] = hidden
        r.acts[1, :, at] = grad_gate
        r.acts[2, :, at] = grad_up
        return carried

    lax.fori_loop(0, 2, tile, 0)
    wide = Reduction(r, "wide", place, r.g_wide, True)
    outer = Reduction(r, "out", place, r.g_out, False)
    early = Reduction(r, "early", place, r.g_early, False, True)
    late = Reduction(r, "late", place, r.g_late, False, True)
    r.nmt[:, 128:256] = r.nm2[128:256].T
    r.hidt[...] = r.acts[0].T
    for o in range(3):
        left = r.nmt[o * 256 : o * 256 + 256]
        for i in range(4):
            cols = slice(i * 256, i * 256 + 256)
            r.wide_total[o, i, 0] = dot(left, r.acts[1, :, cols]).astype(BF)
            r.wide_total[o, i, 1] = dot(left, r.acts[2, :, cols]).astype(BF)
            r.wide_total[o, i, 2] = dot(r.hidt[cols, :], r.gb2[:, o * 256 : o * 256 + 256]).astype(BF)
        wide.start(0, (o,))

    r.gnm[...] = dot_nt(r.acts[1], r.v_gate[...]) + dot_nt(r.acts[2], r.v_up[...])
    send_gnm = paired(4, r.gnm.at[pl.ds(128, 128)], r.gnmx)
    send_gnm.start()
    r.outacc[...] = dot(r.acts[0], r.v_down[...])
    send_out = paired(10, r.outacc.at[pl.ds(128, 128)], r.outx)
    send_out.start()

    def norm_back(grads, values, gain):
        unit_rows, inverse = unit_of(values)
        scaled = grads * gain
        gain_grad = jnp.sum(grads * unit_rows, axis=0, keepdims=True)
        mean = jnp.mean(scaled * unit_rows, axis=-1, keepdims=True)
        return inverse * (scaled - unit_rows * mean), gain_grad

    send_gnm.wait()
    back, gain_mlp = norm_back(r.gnm[0:128] + r.gnmx[...], r.middle[...], gain_of(r.norm_mlp))
    r.gmid[...] = r.cbuf[...].astype(F32) * weight + back
    gain_row = lax.broadcasted_iota(jnp.int32, (16, 128), 0)
    gains = jnp.zeros((16, 128), F32)
    for p in range(6):
        gains = gains + jnp.where(gain_row == 6 + p, gain_mlp[:, p * 128 : p * 128 + 128], 0.0)
    r.gains[...] = gains
    grad_attn = r.gmid[...].astype(BF)
    for half in range(2):
        r.gattn[half, 0:128] = grad_attn[:, half * 384 : half * 384 + 384]
    send_ga = paired(5, r.gattn.at[1 - core, pl.ds(0, 128)], r.gattn.at[1 - core, pl.ds(128, 128)])
    send_ga.start()
    mixed = dot_nt(grad_attn, r.v_out[...])
    r.gmix[...] = mixed.astype(BF)
    to_latent(r.gmix, r.v_upval, r.ga)
    send_out.wait()
    r.outbf[...] = (r.middle[...] + r.outacc[0:128] + r.outx[...]).astype(BF)
    r.layer_out[x_hi] = r.outbf[0:64]
    swap_out = swap(2, r.outbf.at[pl.ds(64, 64)], r.layer_out.at[x_hi])
    swap_out.start()
    ones = jnp.ones((8, 128), F32)
    for half in range(2):
        for p in range(6):
            here = (slice(half * 64, half * 64 + 64), slice(p * 128, p * 128 + 128))
            block = both(r.gmix[here].astype(F32) * r.aof[here])
            sums = lax.dot_general(
                ones, block, (((1,), (1,)), ((), ())), precision=lax.Precision.HIGHEST, preferred_element_type=F32
            )
            r.delta[half * 2 + p // 3, :, (p % 3) * 128 : (p % 3) * 128 + 128] = sums

    send_ao.wait()
    send_ga.wait()
    r.nmt[...] = r.ao2[...].T
    for o in range(3):
        block = dot(r.nmt[o * 256 : o * 256 + 256], r.gattn[core]).astype(BF)
        for i in range(3):
            r.out_total[o, i, 0] = block[:, i * 128 : i * 128 + 128]
        r.out_total[o, 3, 0] = jnp.zeros((256, 128), BF)
    outer.start(0)

    def backward(half):
        def chunk_step(step, carried):
            near, far = masks(half, step)
            rot_turned = jnp.concatenate([r.krt[0, step], r.krt[1, 3 - step]], axis=1)
            rot_sum = None
            for g in range(2):
                at = half * 2 + g
                keys = pair_keys(g, step)
                raw = pair_scores(at, keys, step)
                weights = jnp.exp2(raw * (FACTOR * LOG2E) - r.logs[at, 0:1])
                weights = [jnp.where(near, weights[0:256], 0.0), jnp.where(far, weights[256:512], 0.0)]
                dprob = dot_nt(keys, r.ga[at]) - r.delta[at, 0:1]
                dscore = [weights[0] * dprob[0:256], weights[1] * dprob[256:512]]
                dscore = jnp.concatenate([part.astype(BF) for part in dscore], axis=0)
                weights = jnp.concatenate([part.astype(BF) for part in weights], axis=0)
                r.dqa[at] += dot(pair_turned(g, step), dscore)
                r.dqr[at] += dot(rot_turned, dscore)
                grads = FACTOR * dot(dscore, r.qs[at]) + dot(weights, r.ga[at])
                r.dlat[g, step] += grads[0:256]
                r.dlat[2 + g, 3 - step] += grads[256:512]
                rots = dot(dscore, r.qrx[at])
                rot_sum = rots if rot_sum is None else rot_sum + rots
            r.dkr[step] += jnp.where(low64(256), FACTOR * rot_sum[0:256], 0.0)
            r.dkr[3 - step] += jnp.where(low64(256), 0.0, FACTOR * rot_sum[256:512])
            return carried

        lax.fori_loop(0, counts[half], chunk_step, 0)

    def narrow(step, carried):
        j, c = lax.div(step, 4), lax.rem(step, 4)
        r.latt[j, c] = r.dlat[j, c].astype(BF).reshape(4, 64, 256)
        return carried

    def scatter(part, phase):
        made = []
        axis = (1, 2)[(part + phase) % 2]
        for step in (1, 2, 3):
            peer = on_ring(place, axis, step)
            to = lax.rem(place[axis] + step, 4)
            at = step - 1
            if part == 0 and phase == 0:
                pieces = [(r.latt.at[pl.ds(0, 2), to], r.ro1.at[at]), (r.skr.at[to], r.rk1.at[at])]
            elif part == 0:
                pieces = [(r.so1.at[:, to], r.ro2.at[at]), (r.ks1.at[to], r.rk2.at[at])]
            elif phase == 0:
                pieces = [(r.latt.at[pl.ds(2, 2), :, to], r.rt1.at[at])]
            else:
                pieces = [(r.st1.at[:, to], r.rt2.at[at])]
            for k, (src, dst) in enumerate(pieces):
                send = r.lat_send.at[part, k, at]
                made.append(remote(src, dst, send, r.lat_recv.at[part, phase, k, at], peer))
        return made

    backward(0)
    wide.step(0)
    backward(1)
    lax.fori_loop(0, 16, narrow, 0)
    for c in range(4):
        r.skr[c] = r.dkr[c].astype(BF).reshape(4, 64, 128)
    for copy in scatter(1, 0) + scatter(0, 0):
        copy.start()
    wide.step(1)
    outer.step(0, 1)

    for half in range(2):
        for p in range(6):
            rows, lanes = slice(half * 64, half * 64 + 64), slice((p % 3) * 128, (p % 3) * 128 + 128)
            at = half * 2 + p // 3
            piece = (FACTOR * from_latent(r.dqa, r.v_upkey, half, p)).astype(BF)
            r.gq2[p // 3, rows, lanes] = piece
            turned = FACTOR * r.dqr[at, :, lanes].T
            turned = pick(turned + pltpu.roll(turned, 64, 1))
            turned = turned * r.cosine[rows, :] - swap_halves(turned) * r.sine[rows, :]
            r.gqp2[p // 3, rows, lanes] = turned.astype(BF)
    send_gq = paired(6, r.gq2.at[1 - core, pl.ds(0, 128)], r.gq2.at[1 - core, pl.ds(128, 128)])
    send_gqp = paired(7, r.gqp2.at[1 - core, pl.ds(0, 128)], r.gqp2.at[1 - core, pl.ds(128, 128)])
    send_gq.start()
    send_gqp.start()
    for g in range(2):
        for j in range(3):
            lanes = slice(j * 128, j * 128 + 128)
            wide_lanes = slice((g * 3 + j) * 128, (g * 3 + j) * 128 + 128)
            key_sum, value_sum = jnp.zeros((256, 128), F32), jnp.zeros((256, 128), F32)
            for half in range(2):
                rows = slice(half * 64, half * 64 + 64)
                key_sum += FACTOR * dot(r.dqa[half * 2 + g, :, lanes].astype(BF), both(r.q[rows, wide_lanes]))
                value_sum += dot(r.ctx[half * 2 + g, :, lanes], both(r.gmix[rows, wide_lanes]))
            r.dup[g, 0, j] = key_sum.astype(BF)
            r.dup[g, 1, j] = value_sum.astype(BF)
    send_up = paired(8, r.dup.at[1 - core], r.sup)
    send_up.start()
    grad_normed = dot_nt(r.gq2[0, 0:128], r.v_query[:, 0:384]) + dot_nt(r.gq2[1, 0:128], r.v_query[:, 384:768])
    grad_normed += dot_nt(r.gqp2[0, 0:128], r.v_qrope[:, 0:384]) + dot_nt(r.gqp2[1, 0:128], r.v_qrope[:, 384:768])
    r.gnm[0:128] = grad_normed
    send_norm.wait()
    r.normt[...] = r.norm2[...].T
    send_gq.wait()
    send_gqp.wait()
    send_up.wait()
    for o in range(3):
        rows = slice(o * 256, o * 256 + 256)
        for m, right in enumerate((r.gq2, r.gqp2)):
            block = dot(r.normt[rows], right[core]).astype(BF)
            for i in range(3):
                r.early_total[o, i, m] = block[:, i * 128 : i * 128 + 128]
            r.early_total[o, 3, m] = (r.dup[core, m, o].astype(F32) + r.sup[m, o].astype(F32)).astype(BF)
        early.start(0, (o,))

    outer.step(2)
    wide.step(2, 3)

    def fold_near(at, carried):
        for g in range(2):
            near = r.dlat[g, y, rows_at(at * 64, 64), :]
            for k in range(3):
                near = near + r.ro1[k, g, at].astype(F32)
            r.so1[g, at] = near.astype(BF)
        return carried

    def fold_far(at, carried):
        for g in range(2):
            far = r.dlat[2 + g, at, rows_at(z * 64, 64), :]
            for k in range(3):
                far = far + r.rt1[k, g, at].astype(F32)
            r.st1[g, at] = far.astype(BF)
        rot = r.dkr[y, rows_at(at * 64, 64), :]
        for k in range(3):
            rot = rot + r.rk1[k, at].astype(F32)
        r.ks1[at] = rot.astype(BF)
        return carried

    for copy in scatter(0, 0)[0::2]:
        copy.wait()
    lax.fori_loop(0, 4, fold_near, 0)
    for copy in scatter(0, 1)[0::2]:
        copy.start()
    outer.step(3)
    for copy in scatter(1, 0) + scatter(0, 0)[1::2]:
        copy.wait()
    lax.fori_loop(0, 4, fold_far, 0)
    for copy in scatter(1, 1) + scatter(0, 1)[1::2]:
        copy.start()
    wide.step(4)
    early.step(0, 1)
    for copy in scatter(0, 1) + scatter(1, 1):
        copy.wait()
    grad_latents = []
    for g in range(2):
        near = r.so1[g, z].astype(F32)
        far = r.st1[g, y].astype(F32)
        for k in range(3):
            near = near + r.ro2[k, g].astype(F32)
            far = far + r.rt2[k, g].astype(F32)
        piece = jnp.concatenate([near, far], axis=0).astype(BF)
        grad_latents.append(piece)
        r.gl2[g, 0:128] = piece
    send_gl = paired(9, r.gl2.at[1 - core, pl.ds(0, 128)], r.gl2.at[1 - core, pl.ds(128, 128)])
    send_gl.start()
    rot = r.ks1[z].astype(F32)
    for k in range(3):
        rot = rot + r.rk2[k].astype(F32)
    turned = pltpu.roll(rot, 64, 1)
    rot = jnp.concatenate([jnp.where(low64(64), rot, turned), jnp.where(low64(64), turned, rot)], axis=0)
    grad_kpre = (rot * r.cosine[...] - swap_halves(rot) * r.sine[...]).astype(BF)
    grad_normed = r.gnm[0:128] + dot(grad_kpre[:, 0:64], r.v_krope[...])
    for g in range(2):
        grad_normed = grad_normed + dot_nt(grad_latents[g], r.v_latent[:, g * 256 : g * 256 + 256])
    back, gain_attn = norm_back(grad_normed, r.xbuf[...].astype(F32), gain_of(r.norm_attn))
    r.outacc[0:128] = r.gmid[...] + back
    r.grad_tokens[x_hi] = r.outacc[0:64]
    swap_grad = swap(3, r.outacc.at[pl.ds(64, 64)], r.grad_tokens.at[x_hi])
    swap_grad.start()
    gains = r.gains[...]
    for p in range(6):
        gains = gains + jnp.where(gain_row == p, gain_attn[:, p * 128 : p * 128 + 128], 0.0)
    for o in range(3):
        r.late_total[o, 3, 0] = jnp.zeros((256, 128), BF)
    r.late_total[0, 3, 0, 0:16] = gains.astype(BF)
    grad_krope = dot_tn(grad_kpre, r.norm2[0:128]).astype(BF)
    send_gl.wait()
    for o in range(3):
        rows = slice(o * 256, o * 256 + 256)
        block = dot(r.normt[rows], r.gl2[core]).astype(BF)
        for i in range(2):
            r.late_total[o, i, 0] = block[:, i * 128 : i * 128 + 128]
        for part in range(2):
            at = o * 256 + part * 128
            r.late_total[o, 2, 0, part * 64 : part * 64 + 64] = grad_krope[0:64, at : at + 128]
        r.late_total[o, 2, 0, 128:256] = jnp.zeros((128, 128), BF)
        late.start(0, (o,))
    wide.step(5)
    early.step(2)
    late.step(0, 1)
    outer.step(4)
    wide.step(6)
    early.step(3, 4)
    late.step(2)
    early.step(5, 6)
    late.step(3, 4)
    outer.step(5, 6)
    wide.step(7)
    late.step(5, 6)
    outer.step(7)
    early.step(7)
    late.step(7)
    swap_out.wait()
    swap_grad.wait()
    for reduction in (wide, outer, early, late):
        reduction.finish(8)


def layer(small, weights):
    vmem = pl.BlockSpec(memory_space=pltpu.VMEM)
    hbm = pl.BlockSpec(memory_space=pl.ANY)
    smem = pl.BlockSpec(memory_space=pltpu.SMEM)
    return pl.pallas_call(
        layer_kernel,
        out_shape=[jax.ShapeDtypeStruct(shape, kind) for shape, kind in OUTS.values()],
        in_specs=[vmem] * 4 + [smem] * 2 + [hbm] * (1 + len(weights)),
        out_specs=[vmem, vmem] + [hbm] * (len(OUTS) - 2),
        scratch_shapes=list(scratch().values()),
        compiler_params=pltpu.CompilerParams(
            collective_id=1, has_side_effects=True, vmem_limit_bytes=63 * 2**20
        ),
    )(*small, jnp.asarray(rotary_table()), *weights)


def rotary_table():
    halves = ROPE // 2
    powers = -(np.arange(halves, dtype=np.float32) * np.float32(2.0) / np.float32(ROPE))
    freq_list = np.power(np.float32(10000.0), powers, dtype=np.float32)
    phases = (np.arange(2048, dtype=np.float32)[:, None] * freq_list[None, :]).astype(np.float32)
    cosine, sine = np.cos(phases), np.sin(phases)
    return np.concatenate([cosine, cosine, -sine, sine], axis=1).astype(np.float32)


CAST_STEPS = 3


def cast_kernel(
    wide, down, out, early, late, layer_out, grad_tokens,
    o_gate, o_up, o_down, o_query, o_qrope, o_out, o_latent, o_krope, o_upkey, o_upval, o_attn, o_mlp, o_layer, o_tokens,
):
    o_gate[...] = wide[0].astype(F32)
    o_up[...] = wide[1].astype(F32)
    for k in range(8):
        o_down[k * 256 : k * 256 + 256] = down[0, :, k * 256 : k * 256 + 256].astype(F32)
    for source, m, target, width in (
        (early, 0, o_query, 384), (early, 1, o_qrope, 384), (out, 0, o_out, 384), (late, 0, o_latent, 256)
    ):
        target[:, 0:width] = source[m, :, 0:width].astype(F32)
        target[:, width : 2 * width] = source[m, :, 512 : 512 + width].astype(F32)
    for m, target in ((0, o_upkey), (1, o_upval)):
        target[0] = early[m, :, 384:512].astype(F32)
        target[1] = early[m, :, 896:1024].astype(F32)
    step = pl.program_id(0)
    for part in range(2):
        rows = slice(part * 64, part * 64 + 64)
        lanes = rows_at(step * 256 + part * 128, 128, 128)
        o_krope[:, lanes] = late[0, rows, 256:384].astype(F32) + late[0, rows, 768:896].astype(F32)

    @pl.when(step == 0)
    def _():
        gains = late[0, 0:16, 384:512].astype(F32) + late[0, 0:16, 896:1024].astype(F32)
        for p in range(6):
            o_attn[p * 128 : p * 128 + 128] = gains[p]
            o_mlp[p * 128 : p * 128 + 128] = gains[6 + p]
        o_layer[...] = layer_out[...]
        o_tokens[...] = grad_tokens[...]


def cast_sums(layer_out, grad_tokens, wide, out, early, late):
    rows = lambda width: pl.BlockSpec((256, width), lambda i: (i, 0))
    group = lambda n, width: pl.BlockSpec((n, 256, width), lambda i: (0, i, 0))
    ups = pl.BlockSpec((2, 256, 128), lambda i: (0, 0, i))
    whole = lambda shape: pl.BlockSpec(shape, lambda i: (0,) * len(shape))
    shapes = (
        (768, 2048), (768, 2048), (2048, 768), (768, 768), (768, 768), (768, 768), (768, 512), (64, 768),
        (2, 256, 384), (2, 256, 384), (768,), (768,),
    )
    rows_out = (layer_out, grad_tokens)
    return pl.pallas_call(
        cast_kernel,
        grid=(CAST_STEPS,),
        out_shape=[jax.ShapeDtypeStruct(shape, F32) for shape in shapes]
        + [jax.ShapeDtypeStruct(array.shape, array.dtype) for array in rows_out],
        in_specs=[
            group(2, 2048),
            pl.BlockSpec((1, 256, 2048), lambda i: (2, i, 0)),
            group(1, 1024),
            group(2, 1024),
            group(1, 1024),
        ]
        + [whole(array.shape) for array in rows_out],
        out_specs=[rows(2048), rows(2048), pl.BlockSpec((2048, 256), lambda i: (0, i))]
        + [rows(768)] * 3
        + [rows(512), whole((64, 768)), ups, ups, whole((768,)), whole((768,))]
        + [whole(array.shape) for array in rows_out],
        compiler_params=pltpu.CompilerParams(vmem_limit_bytes=63 * 2**20),
    )(wide, wide, out, early, late, layer_out, grad_tokens)


def local(
    tokens, cotangent, group_of_seq, group_weight, norm_attn, w_query, w_qrope, w_latent, w_krope, w_upkey, w_upval,
    w_out, norm_mlp, w_gate, w_up, w_down,
):
    small = (tokens, cotangent, norm_attn, norm_mlp, group_of_seq, group_weight)
    weights = (w_latent, w_krope.T, w_query, w_qrope, w_upkey, w_upval, w_out, w_gate, w_up, w_down)
    gate, up, down, query, qrope, out, latent, krope, upkey, upval, attn, mlp, layer_out, grad_tokens = cast_sums(
        *layer(small, weights)
    )
    return (
        layer_out, grad_tokens, attn, query, qrope, latent, krope.T, upkey, upval, out, mlp, gate, up, down,
    )


def solution(mesh):
    split = P("seq", "blk", None)
    in_specs = (split, split, P("seq")) + (P(),) * 13
    out_specs = (split, split) + (P(),) * 12
    return jax.shard_map(local, mesh=mesh, in_specs=in_specs, out_specs=out_specs, check_vma=False)
```

```python
import jax
import jax.numpy as jnp
import numpy as np
from jax import lax
from jax.sharding import PartitionSpec as P
from jax.experimental import pallas as pl
from jax.experimental.pallas import tpu as pltpu

MESH = pl.DeviceIdType.MESH
BF = jnp.bfloat16
F32 = jnp.float32
EPSILON = 1e-06
ROPE = 64
GROUPS = 4
FACTOR = 128.0**-0.5
LOG2E = 1.4426950408889634
HIDDEN_SCORE = -1e30
ORDERS = ((0, 1, 2), (1, 2, 0), (2, 0, 1))
X_FIRST = ((0, 1, 2), (0, 2, 1), (0, 1, 2))


def coords():
    s = lax.axis_index("seq")
    b = lax.axis_index("blk")
    x = lax.rem(b, 2) * 2 + lax.div(s, 2)
    return x, lax.div(b, 8), lax.rem(lax.div(b, 2), 4), lax.rem(s, 2)


def device(x, y, z, core):
    return (lax.rem(x, 2) * 2 + core, y * 8 + z * 2 + lax.div(x, 2))


def on_ring(place, axis, step):
    spot = list(place)
    spot[axis] = lax.rem(place[axis] + step, 4)
    return device(*spot)


def remote(src, dst, send, recv, peer):
    return pltpu.make_async_remote_copy(
        src_ref=src, dst_ref=dst, send_sem=send, recv_sem=recv, device_id=peer, device_id_type=MESH
    )


def rows_at(start, size, multiple=16):
    return pl.ds(pl.multiple_of(start, multiple), size)


def dot(left, right):
    return jnp.dot(left, right, preferred_element_type=F32)


def dot_nt(left, right):
    return lax.dot_general(left, right, (((1,), (1,)), ((), ())), preferred_element_type=F32)


def dot_tn(left, right):
    return lax.dot_general(left, right, (((0,), (0,)), ((), ())), preferred_element_type=F32)


class Reduction:
    def __init__(self, r, name, place, out, halving, flat=False, orders=ORDERS):
        self.place, self.out, self.halving, self.flat, self.orders = place, out, halving, flat, orders
        for part in ("total", "first", "second", "third", "chunk", "send", "recv", "keep"):
            setattr(self, part, getattr(r, name + "_" + part))
        self.n, self.width = self.total.shape[2], self.total.shape[4]
        counts = stage_counts(halving, flat)
        self.base = [sum(counts[:stage]) for stage in range(9)]

    def spots(self, o):
        a, b, c = self.orders[o]
        return self.place[a], self.place[b], self.place[c]

    def sides(self, o, s):
        me = self.place[self.orders[o][0]]
        odd = lax.rem(me, 2)
        near, far = 1 + 2 * odd, 3 - 2 * odd
        steps = (near, far) if s == 0 else (far, near)
        return steps, lax.rem(me + steps[0], 4), lax.rem(me + steps[1], 4), lax.rem(me + 2, 4)

    def region(self, o, i, row, rows, count=1):
        core, width = self.place[3], self.width
        return self.out.at[:, rows_at(o * 256 + row, rows), rows_at((core * 4 + i) * width, count * width, 128)]

    def moves(self, o, stage):
        i, j, k = self.spots(o)
        if stage == 8:
            x, y, z, core = self.place
            here = self.region(o, 0, 0, 256, 4)
            return [(here, here, device(x, y, z, 1 - core))]
        made = []
        axis = self.orders[o][(0, 0, 1, 2, 2, 1, 0, 0)[stage]]
        if stage in (0, 1, 6, 7) and self.halving:
            for s in range(2):
                steps, front, last, across = self.sides(o, s)
                half = pl.ds(s * 128, 128)
                peer = on_ring(self.place, axis, steps[0 if stage in (0, 7) else 1])
                if stage == 0:
                    made.append((self.total.at[o, front, :, half], self.first.at[o, s, 0], peer))
                    made.append((self.total.at[o, across, :, half], self.first.at[o, s, 1], peer))
                elif stage == 1:
                    made.append((self.total.at[o, last, :, half], self.first.at[o, s, 2], peer))
                else:
                    for spot in (i, last) if stage == 7 else (i,):
                        here = self.region(o, spot, s * 128, 128)
                        made.append((here, here, peer))
            return made
        if stage in (1, 6) or (stage == 4 and self.flat):
            return made
        for step in (1, 2, 3):
            to = lax.rem(self.place[axis] + step, 4)
            peer = on_ring(self.place, axis, step)
            at = step - 1
            if stage == 0:
                made.append((self.total.at[o, to], self.first.at[o, at], peer))
            elif stage == 2:
                made.append((self.total.at[o, i, :, rows_at(to * 64, 64)], self.second.at[o, at], peer))
            elif stage == 3 and self.flat:
                made.append((self.total.at[o, i, :, rows_at(j * 64, 64)], self.third.at[o, k], peer))
            elif stage == 3:
                made.append((self.total.at[o, i, :, rows_at(j * 64 + to * 16, 16)], self.third.at[o, at], peer))
            elif stage == 4:
                made.append((self.chunk.at[o], self.region(o, i, j * 64 + k * 16, 16), peer))
            elif stage == 5:
                here = self.region(o, i, j * 64, 64)
                made.append((self.chunk.at[o] if self.flat else here, here, peer))
            else:
                here = self.region(o, i, 0, 256)
                made.append((here, here, peer))
        return made

    def copies(self, o, stage):
        return [
            remote(src, dst, self.send.at[o, at], self.recv.at[o, self.base[stage] + at], peer)
            for at, (src, dst, peer) in enumerate(self.moves(o, stage))
        ]

    def kept(self, o):
        i, j, k = self.spots(o)
        row, rows = (j * 64, 64) if self.flat else (j * 64 + k * 16, 16)
        return pltpu.make_async_copy(self.chunk.at[o], self.region(o, i, row, rows), self.keep.at[o])

    def start(self, stage, orders=(0, 1, 2)):
        for o in orders:
            for copy in self.copies(o, stage):
                copy.start()
            if stage == 4:
                self.kept(o).start()

    def finish(self, stage, orders=(0, 1, 2)):
        for o in orders:
            for copy in self.copies(o, stage):
                copy.wait()
            if stage == 4:
                self.kept(o).wait()
            if stage < 4:
                self.add(o, stage)

    def step(self, *stages):
        for stage in stages:
            for o in range(3):
                self.finish(stage, (o,))
                self.start(stage + 1, (o,))

    def add(self, o, stage):
        i, j, k = self.spots(o)
        if stage == 1 and not self.halving:
            return

        def body(m, carried):
            if stage < 2 and self.halving:
                for s in range(2):
                    _, _, last, _ = self.sides(o, s)
                    half = slice(s * 128, s * 128 + 128)
                    for spot, slot in ((i, 0), (last, 1)) if stage == 0 else ((i, 2),):
                        acc = self.total[o, spot, m, half, :].astype(F32) + self.first[o, s, slot, m].astype(F32)
                        self.total[o, spot, m, half, :] = acc.astype(BF)
            elif stage == 0:
                for part in range(4):
                    rows = slice(part * 64, part * 64 + 64)
                    acc = self.total[o, i, m, rows, :].astype(F32)
                    for slot in range(3):
                        acc = acc + self.first[o, slot, m, rows, :].astype(F32)
                    self.total[o, i, m, rows, :] = acc.astype(BF)
            elif stage == 2:
                rows = rows_at(j * 64, 64)
                acc = self.total[o, i, m, rows, :].astype(F32)
                for slot in range(3):
                    acc = acc + self.second[o, slot, m].astype(F32)
                self.total[o, i, m, rows, :] = acc.astype(BF)
            elif self.flat:
                self.third[o, k, m] = self.total[o, i, m, rows_at(j * 64, 64), :]
                acc = self.third[o, 0, m].astype(F32)
                for slot in range(1, 4):
                    acc = acc + self.third[o, slot, m].astype(F32)
                self.chunk[o, m] = acc.astype(BF)
            else:
                acc = self.total[o, i, m, rows_at(j * 64 + k * 16, 16), :].astype(F32)
                for slot in range(3):
                    acc = acc + self.third[o, slot, m].astype(F32)
                self.chunk[o, m] = acc.astype(BF)
            return carried

        lax.fori_loop(0, self.n, body, 0)


def stage_counts(halving, flat):
    return (4 if halving else 3, 2 if halving else 0, 3, 3, 0 if flat else 3, 3, 2 if halving else 0, 4 if halving else 3, 1)


def reduction_scratch(name, n, width, halving, flat=False):
    return {
        name + "_total": pltpu.VMEM((3, 4, n, 256, width), BF),
        name + "_first": pltpu.VMEM((3, 2, 3, n, 128, width) if halving else (3, 3, n, 256, width), BF),
        name + "_second": pltpu.VMEM((3, 3, n, 64, width), BF),
        name + "_third": pltpu.VMEM((3, 4, n, 64, width) if flat else (3, 3, n, 16, width), BF),
        name + "_chunk": pltpu.VMEM((3, n, 64 if flat else 16, width), BF),
        name + "_send": pltpu.SemaphoreType.DMA((3, 4)),
        name + "_recv": pltpu.SemaphoreType.DMA((3, sum(stage_counts(halving, flat)))),
        name + "_keep": pltpu.SemaphoreType.DMA((3,)),
    }


WEIGHTS = {
    "w_latent": (768, 512),
    "w_krope": (64, 768),
    "w_query": (768, 768),
    "w_qrope": (768, 768),
    "w_upkey": (2, 256, 384),
    "w_upval": (2, 256, 384),
    "w_out": (768, 768),
    "w_gate": (768, 1024),
    "w_up": (768, 1024),
    "w_down": (1024, 768),
}
SMALL = ("tokens", "cotangent", "norm_attn", "norm_mlp", "group_of_seq", "group_weight")
OUTS = {
    "layer_out": ((2, 64, 768), BF),
    "grad_tokens": ((2, 64, 768), F32),
    "g_wide": ((3, 768, 2048), BF),
    "g_out": ((1, 768, 1024), BF),
    "g_early": ((2, 768, 1024), BF),
    "g_late": ((1, 768, 1024), BF),
}


def scratch():
    vmem, dma = pltpu.VMEM, pltpu.SemaphoreType.DMA
    made = {"v" + name[1:]: vmem(shape, BF) for name, shape in WEIGHTS.items()}
    made.update(
        load_sem=dma((len(WEIGHTS),)),
        table_sem=dma((2,)),
        turns=vmem((128, 128), F32),
        cosine=vmem((128, 128), F32),
        sine=vmem((128, 128), F32),
        swap_sem=dma((4, 2)),
        pair_sem=dma((11, 2)),
        lat_send=dma((2, 2, 3)),
        ag_recv=dma((2, 2, 3)),
        lat_recv=dma((2, 2, 2, 3)),
        fw_sem=dma((2, 7, 2)),
        xbuf=vmem((128, 768), BF),
        cbuf=vmem((128, 768), BF),
        norm2=vmem((256, 768), BF),
        normt=vmem((768, 256), BF),
        krd=vmem((128, 128), F32),
        q=vmem((128, 768), BF),
        qr=vmem((128, 768), BF),
        lat=vmem((4, 4, 4, 64, 256), BF),
        kr=vmem((4, 4, 64, 128), BF),
        latt=vmem((4, 4, 4, 64, 256), BF),
        krt=vmem((2, 4, 128, 256), BF),
        rel=vmem((2, 256, 384), jnp.int32),
        qs=vmem((4, 384, 256), BF),
        ga=vmem((4, 384, 256), BF),
        qrx=vmem((4, 384, 128), BF),
        krm=vmem((2, 4, 256, 128), BF),
        gh=vmem((256, 1024), F32),
        acc=vmem((4, 256, 384), F32),
        ctx=vmem((4, 256, 384), BF),
        dqa=vmem((4, 256, 384), F32),
        logs=vmem((4, 8, 384), F32),
        delta=vmem((4, 8, 384), F32),
        aof=vmem((128, 768), F32),
        ao2=vmem((256, 768), BF),
        middle=vmem((128, 768), F32),
        nm2=vmem((256, 768), BF),
        nmt=vmem((768, 256), BF),
        gb2=vmem((256, 768), BF),
        acts=vmem((3, 256, 1024), BF),
        hidt=vmem((1024, 256), BF),
        outacc=vmem((256, 768), F32),
        gnm=vmem((256, 768), F32),
        outx=vmem((128, 768), F32),
        gnmx=vmem((128, 768), F32),
        outbf=vmem((128, 768), BF),
        gattn=vmem((2, 256, 384), BF),
        gmix=vmem((128, 768), BF),
        dqr=vmem((4, 128, 384), F32),
        dlat=vmem((4, 4, 256, 256), F32),
        dkr=vmem((4, 256, 128), F32),
        skr=vmem((4, 4, 64, 128), BF),
        ro1=vmem((3, 2, 4, 64, 256), BF),
        rk1=vmem((3, 4, 64, 128), BF),
        rt1=vmem((3, 2, 4, 64, 256), BF),
        so1=vmem((2, 4, 64, 256), BF),
        ks1=vmem((4, 64, 128), BF),
        st1=vmem((2, 4, 64, 256), BF),
        ro2=vmem((3, 2, 64, 256), BF),
        rk2=vmem((3, 64, 128), BF),
        rt2=vmem((3, 2, 64, 256), BF),
        gq2=vmem((2, 256, 384), BF),
        gqp2=vmem((2, 256, 384), BF),
        gl2=vmem((2, 256, 256), BF),
        dup=vmem((2, 2, 3, 256, 128), BF),
        sup=vmem((2, 3, 256, 128), BF),
        gmid=vmem((128, 768), F32),
        gains=vmem((16, 128), F32),
    )
    made.update(reduction_scratch("wide", 3, 256, True))
    made.update(reduction_scratch("out", 1, 128, False))
    made.update(reduction_scratch("early", 2, 128, False, True))
    made.update(reduction_scratch("late", 1, 128, False, True))
    return made


class Refs:
    pass


def swap_halves(values):
    lanes = values.shape[-1]
    low = lax.rem(lax.broadcasted_iota(jnp.int32, values.shape, 1), 64) < 32
    return jnp.where(low, pltpu.roll(values, lanes - 32, 1), pltpu.roll(values, 32, 1))


def layer_kernel(*args):
    r = Refs()
    shapes = scratch()
    names = list(SMALL) + ["table"] + list(WEIGHTS) + list(OUTS) + list(shapes)
    for name, ref in zip(names, args, strict=True):
        setattr(r, name, ref)
    place = coords()
    x, y, z, core = place
    x_hi = lax.div(x, 2)
    blk = y * 8 + z * 2 + x_hi
    slot = y * 4 + z
    sibling = device(x, y, z, 1 - core)
    partner = device(lax.rem(x + 2, 4), 3 - y, 3 - z, core)
    peers = [on_ring(place, axis, step) for axis in range(3) for step in (1, 2, 3)] + [sibling, partner]
    low64 = lambda rows: lax.broadcasted_iota(jnp.int32, (rows, 128), 1) < 64
    diagonal = (lax.broadcasted_iota(jnp.int32, (128, 128), 0) < 64) == low64(128)

    def gain_of(ref):
        return ref[...].reshape(1, 768)

    def both(value):
        return jnp.where(diagonal, jnp.concatenate([value, value], axis=0), jnp.zeros((), value.dtype))

    def pick(value):
        return jnp.where(low64(64), value[0:64], value[64:128])

    barrier = pltpu.get_barrier_semaphore()
    for peer in peers:
        pl.semaphore_signal(barrier, inc=1, device_id=peer, device_id_type=MESH)
    loads = {}
    for at, name in enumerate(WEIGHTS):
        source = getattr(r, name)
        if name in ("w_gate", "w_up"):
            source = source.at[:, rows_at(core * 1024, 1024, 128)]
        elif name == "w_down":
            source = source.at[rows_at(core * 1024, 1024), :]
        loads[name] = pltpu.make_async_copy(source, getattr(r, "v" + name[1:]), r.load_sem.at[at])
    tables = [
        pltpu.make_async_copy(
            r.table.at[rows_at(where * 64, 64)], r.turns.at[pl.ds(half * 64, 64)], r.table_sem.at[half]
        )
        for half, where in enumerate((blk, 31 - blk))
    ]
    loads["w_latent"].start()
    loads["w_krope"].start()
    for table in tables:
        table.start()
    pl.semaphore_wait(barrier, len(peers))

    def swap(at, src, dst):
        return remote(src, dst, r.swap_sem.at[at, 0], r.swap_sem.at[at, 1], partner)

    def paired(at, src, dst):
        return remote(src, dst, r.pair_sem.at[at, 0], r.pair_sem.at[at, 1], sibling)

    swap_x = swap(0, r.tokens.at[1 - x_hi], r.xbuf.at[pl.ds(64, 64)])
    swap_c = swap(1, r.cotangent.at[1 - x_hi], r.cbuf.at[pl.ds(64, 64)])
    swap_x.start()
    for name in ("w_query", "w_qrope", "w_upkey"):
        loads[name].start()
    r.xbuf[0:64] = r.tokens[x_hi]
    r.cbuf[0:64] = r.cotangent[x_hi]
    key_row = lax.broadcasted_iota(jnp.int32, (256, 384), 0)
    query_lane = lax.rem(lax.broadcasted_iota(jnp.int32, (256, 384), 1), 64)
    within = lax.rem(key_row, 64) - query_lane
    r.rel[0] = 128 * lax.div(key_row, 64) + within
    r.rel[1] = within - 128 * lax.div(key_row, 64)
    for table in tables:
        table.wait()
    turns = r.turns[...]
    other = pltpu.roll(turns, 64, 1)
    r.cosine[...] = jnp.where(low64(128), turns, other)
    r.sine[...] = jnp.where(low64(128), other, turns)
    def unit_of(values):
        inverse = lax.rsqrt(jnp.mean(values * values, axis=-1, keepdims=True) + EPSILON)
        return values * inverse, inverse

    def start_half(half):
        rows = slice(half * 64, half * 64 + 64)
        unit = unit_of(r.xbuf[rows].astype(F32))[0]
        normed = (unit * gain_of(r.norm_attn)).astype(BF)
        r.norm2[rows] = normed
        latents = dot(normed, r.v_latent[...]).astype(BF)
        for g in range(2):
            r.lat[half * 2 + g, y, z] = latents[:, g * 256 : g * 256 + 256]

    def gather(part):
        made = []
        axis = (2, 1)[part]
        for step in (1, 2, 3):
            pieces = [r.lat.at[pl.ds(part * 2, 2), y, z]] + ([r.kr.at[y, z]] if part == 0 else [])
            for at, piece in enumerate(pieces):
                send, recv = r.lat_send.at[part, at, step - 1], r.ag_recv.at[part, at, step - 1]
                made.append(remote(piece, piece, send, recv, on_ring(place, axis, step)))
        return made

    loads["w_latent"].wait()
    start_half(0)
    for copy in gather(0)[0::2]:
        copy.start()
    swap_x.wait()
    start_half(1)
    for copy in gather(1):
        copy.start()
    loads["w_krope"].wait()
    key_pre = dot_nt(r.norm2[0:128], r.v_krope[...])
    r.krd[:, 0:64] = key_pre
    r.krd[:, 64:128] = key_pre
    key_pre = r.krd[...]
    key_rot = (key_pre * r.cosine[...] + swap_halves(key_pre) * r.sine[...]).astype(BF)
    r.kr[y, z] = pick(key_rot)
    for copy in gather(0)[1::2]:
        copy.start()
    swap_c.start()
    send_norm = paired(0, r.norm2.at[pl.ds(0, 128)], r.norm2.at[pl.ds(128, 128)])
    send_norm.start()
    normed = r.norm2[0:128]
    for name in ("w_upval", "w_out", "w_gate", "w_up", "w_down"):
        loads[name].start()

    loads["w_query"].wait()
    r.q[...] = dot(normed, r.v_query[...]).astype(BF)
    loads["w_qrope"].wait()
    query_pre = dot(normed, r.v_qrope[...])
    for p in range(6):
        lanes = slice(p * 128, p * 128 + 128)
        piece = query_pre[:, lanes]
        r.qr[:, lanes] = (piece * r.cosine[...] + swap_halves(piece) * r.sine[...]).astype(BF)
    def to_latent(source, weights, target):
        for half in range(2):
            for g in range(2):
                for j in range(3):
                    p = g * 3 + j
                    block = both(source[half * 64 : half * 64 + 64, p * 128 : p * 128 + 128])
                    rows = dot_nt(block, weights[g, :, j * 128 : j * 128 + 128])
                    target[half * 2 + g, j * 128 : j * 128 + 128] = rows.astype(BF)

    def spread(part, stage):
        axis = (1, 2)[part]
        me = place[axis]
        right, left = on_ring(place, axis, 1), on_ring(place, axis, 3)
        before, after = lax.rem(me + 3, 4), lax.rem(me + 1, 4)

        def plane(which, where):
            return r.lat.at[which, where] if part == 0 else r.lat.at[which, :, where]

        if stage == 0:
            mine = plane(pl.ds(part * 2, 2), me)
            pieces = [(mine, right), (mine, left)]
            if part == 0:
                pieces += [(r.kr.at[me], right), (r.kr.at[me], left)]
        else:
            pieces = [(plane(part * 2, before), right), (plane(part * 2 + 1, after), left)]
            if part == 0:
                pieces += [(r.kr.at[after], left)]
        return [
            remote(piece, piece, r.fw_sem.at[part, stage * 4 + at, 0], r.fw_sem.at[part, stage * 4 + at, 1], peer)
            for at, (piece, peer) in enumerate(pieces)
        ]

    for part in (1, 0):
        for copy in gather(part):
            copy.wait()
        for copy in spread(part, 0):
            copy.start()
    loads["w_upkey"].wait()
    to_latent(r.q, r.v_upkey, r.qs)
    for half in range(2):
        for p in range(6):
            pair = r.qr[half * 64 : half * 64 + 64, p * 128 : p * 128 + 128].astype(F32)
            turned = pltpu.roll(pair, 64, 1)
            for odd in range(2):
                front, back = (turned, pair) if odd else (pair, turned)
                at = (p % 3) * 128 + odd * 64
                r.qrx[half * 2 + p // 3, at : at + 64] = jnp.where(low64(64), front, back).astype(BF)

    swap_c.wait()
    group = jnp.where(x_hi == 0, r.group_of_seq[0], r.group_of_seq[1])
    weight = r.group_weight[0]
    for g in range(1, GROUPS):
        weight = jnp.where(group == g, r.group_weight[g], weight)
    r.gb2[0:128] = (r.cbuf[...].astype(F32) * weight).astype(BF)
    send_gb = paired(3, r.gb2.at[pl.ds(0, 128)], r.gb2.at[pl.ds(128, 128)])
    send_gb.start()

    for ref in (r.acc, r.dqa, r.dqr, r.dlat, r.dkr):
        ref[...] = jnp.zeros_like(ref)
    loads["w_down"].wait()
    send_gb.wait()
    for part in range(4):
        cols = slice(part * 256, part * 256 + 256)
        r.gh[:, cols] = dot_nt(r.gb2[...], r.v_down[cols, :])

    for part in (1, 0):
        for copy in spread(part, 0):
            copy.wait()
        for copy in spread(part, 1):
            copy.start()

    top = lax.broadcasted_iota(jnp.int32, (128, 256), 0) < 64

    def turn(j, c):
        r.latt[j, c] = r.lat[j, c].reshape(256, 256).T.reshape(4, 64, 256)

    def turn_rot(c):
        rot = r.kr[c].reshape(256, 128).astype(F32)
        r.krm[0, c] = jnp.where(low64(256), rot, 0.0).astype(BF)
        r.krm[1, c] = jnp.where(low64(256), 0.0, rot).astype(BF)
        turned = rot.T
        r.krt[0, c] = jnp.where(top, turned, 0.0).astype(BF)
        r.krt[1, c] = jnp.where(top, 0.0, turned).astype(BF)

    for step in (0, 1, 3):
        plane = lax.rem(y + step, 4)
        turn(0, plane)
        turn(1, plane)
        turn_rot(plane)

    query_blk = (blk, 31 - blk)

    counts = (y + 1, 4 - y)

    def masks(half, step):
        first = query_blk[half] * 64
        near = r.rel[0] <= first - 512 * step - 64 * x_hi
        far = r.rel[1] <= first - 1984 + 512 * (3 - step) + 64 * x_hi
        return near, far

    def pair_keys(g, step):
        keys = [r.lat[far * 2 + g, chunk].reshape(256, 256) for far, chunk in ((0, step), (1, 3 - step))]
        return jnp.concatenate(keys, axis=0)

    def pair_scores(at, keys, step):
        rot = jnp.concatenate([r.krm[0, step], r.krm[1, 3 - step]], axis=0)
        return dot_nt(keys, r.qs[at]) + dot_nt(rot, r.qrx[at])

    def pair_turned(g, step):
        turned = [r.latt[far * 2 + g, chunk].reshape(256, 256) for far, chunk in ((0, step), (1, 3 - step))]
        return jnp.concatenate(turned, axis=1)

    for copy in spread(1, 1) + spread(0, 1):
        copy.wait()
    across = lax.rem(y + 2, 4)
    turn(0, across)
    turn(1, across)
    turn_rot(across)
    for c in range(4):
        turn(2, c)
        turn(3, c)

    def forward(half):
        def chunk_step(step, state):
            near, far = masks(half, step)
            result = []
            for g in range(2):
                at = half * 2 + g
                high, total = state[g]
                raw = pair_scores(at, pair_keys(g, step), step)
                raws = [jnp.where(near, raw[0:256], HIDDEN_SCORE), jnp.where(far, raw[256:512], HIDDEN_SCORE)]
                new_high = jnp.maximum(high, jnp.max(jnp.maximum(*raws), axis=0, keepdims=True))
                shrink = jnp.exp2((high - new_high) * (FACTOR * LOG2E))
                weights = [jnp.exp2((raw - new_high) * (FACTOR * LOG2E)) for raw in raws]
                total = total * shrink + jnp.sum(weights[0] + weights[1], axis=0, keepdims=True)
                weights = jnp.concatenate([weight.astype(BF) for weight in weights], axis=0)
                mixed = r.acc[at] * shrink + dot(pair_turned(g, step), weights)
                r.acc[at] = mixed
                result.append((new_high, total))
            return tuple(result)

        empty = (jnp.full((1, 384), HIDDEN_SCORE, F32), jnp.zeros((1, 384), F32))
        state = lax.fori_loop(0, counts[half], chunk_step, (empty, empty))
        for g in range(2):
            high, total = state[g]
            at = half * 2 + g
            r.ctx[at] = (r.acc[at] * (1.0 / total)).astype(BF)
            r.logs[at, 0:1] = high * (FACTOR * LOG2E) + jnp.log2(total)

    forward(0)
    forward(1)
    loads["w_upval"].wait()

    def from_latent(source, weights, half, p):
        g, j = p // 3, p % 3
        lanes = slice(j * 128, j * 128 + 128)
        return pick(dot_tn(source[half * 2 + g, :, lanes].astype(BF), weights[g, :, lanes]))

    for half in range(2):
        for p in range(6):
            r.aof[half * 64 : half * 64 + 64, p * 128 : p * 128 + 128] = from_latent(r.ctx, r.v_upval, half, p)
    r.ao2[0:128] = r.aof[...].astype(BF)
    send_ao = paired(1, r.ao2.at[pl.ds(0, 128)], r.ao2.at[pl.ds(128, 128)])
    send_ao.start()

    loads["w_out"].wait()
    middle = r.xbuf[...].astype(F32) + dot(r.ao2[0:128], r.v_out[...])
    r.middle[...] = middle
    unit_mlp = unit_of(middle)[0]
    r.nm2[0:128] = (unit_mlp * gain_of(r.norm_mlp)).astype(BF)
    send_nm = paired(2, r.nm2.at[pl.ds(0, 128)], r.nm2.at[pl.ds(128, 128)])
    send_nm.start()
    loads["w_gate"].wait()
    loads["w_up"].wait()
    r.nmt[:, 0:128] = r.nm2[0:128].T
    send_nm.wait()

    for part in range(2):
        at = slice(part * 512, part * 512 + 512)
        act = r.nm2[...]
        gate = dot(act, r.v_gate[:, at])
        up = dot(act, r.v_up[:, at])
        sig = jax.nn.sigmoid(gate)
        silu = gate * sig
        hidden = (silu * up).astype(BF)
        grad_hidden = r.gh[:, at]
        grad_gate = (grad_hidden * up * sig * (1.0 + gate * (1.0 - sig))).astype(BF)
        grad_up = (grad_hidden * silu).astype(BF)
        r.acts[0, :, at] = hidden
        r.acts[1, :, at] = grad_gate
        r.acts[2, :, at] = grad_up

    wide = Reduction(r, "wide", place, r.g_wide, True)
    outer = Reduction(r, "out", place, r.g_out, False)
    early = Reduction(r, "early", place, r.g_early, False, True)
    late = Reduction(r, "late", place, r.g_late, False, True)
    r.nmt[:, 128:256] = r.nm2[128:256].T
    r.hidt[...] = r.acts[0].T
    for o in range(3):
        left = r.nmt[o * 256 : o * 256 + 256]
        for i in range(4):
            cols = slice(i * 256, i * 256 + 256)
            r.wide_total[o, i, 0] = dot(left, r.acts[1, :, cols]).astype(BF)
            r.wide_total[o, i, 1] = dot(left, r.acts[2, :, cols]).astype(BF)
            r.wide_total[o, i, 2] = dot(r.hidt[cols, :], r.gb2[:, o * 256 : o * 256 + 256]).astype(BF)
        wide.start(0, (o,))

    r.gnm[...] = dot_nt(r.acts[1], r.v_gate[...]) + dot_nt(r.acts[2], r.v_up[...])
    send_gnm = paired(4, r.gnm.at[pl.ds(128, 128)], r.gnmx)
    send_gnm.start()
    r.outacc[...] = dot(r.acts[0], r.v_down[...])
    send_out = paired(10, r.outacc.at[pl.ds(128, 128)], r.outx)
    send_out.start()

    def norm_back(grads, values, gain):
        unit_rows, inverse = unit_of(values)
        scaled = grads * gain
        gain_grad = jnp.sum(grads * unit_rows, axis=0, keepdims=True)
        mean = jnp.mean(scaled * unit_rows, axis=-1, keepdims=True)
        return inverse * (scaled - unit_rows * mean), gain_grad

    send_gnm.wait()
    back, gain_mlp = norm_back(r.gnm[0:128] + r.gnmx[...], r.middle[...], gain_of(r.norm_mlp))
    r.gmid[...] = r.cbuf[...].astype(F32) * weight + back
    gain_row = lax.broadcasted_iota(jnp.int32, (16, 128), 0)
    gains = jnp.zeros((16, 128), F32)
    for p in range(6):
        gains = gains + jnp.where(gain_row == 6 + p, gain_mlp[:, p * 128 : p * 128 + 128], 0.0)
    r.gains[...] = gains
    grad_attn = r.gmid[...].astype(BF)
    for half in range(2):
        r.gattn[half, 0:128] = grad_attn[:, half * 384 : half * 384 + 384]
    send_ga = paired(5, r.gattn.at[1 - core, pl.ds(0, 128)], r.gattn.at[1 - core, pl.ds(128, 128)])
    send_ga.start()
    mixed = dot_nt(grad_attn, r.v_out[...])
    r.gmix[...] = mixed.astype(BF)
    to_latent(r.gmix, r.v_upval, r.ga)
    send_out.wait()
    r.outbf[...] = (r.middle[...] + r.outacc[0:128] + r.outx[...]).astype(BF)
    r.layer_out[x_hi] = r.outbf[0:64]
    swap_out = swap(2, r.outbf.at[pl.ds(64, 64)], r.layer_out.at[x_hi])
    swap_out.start()
    ones = jnp.ones((8, 128), F32)
    for half in range(2):
        for p in range(6):
            here = (slice(half * 64, half * 64 + 64), slice(p * 128, p * 128 + 128))
            block = both(r.gmix[here].astype(F32) * r.aof[here])
            sums = lax.dot_general(
                ones, block, (((1,), (1,)), ((), ())), precision=lax.Precision.HIGHEST, preferred_element_type=F32
            )
            r.delta[half * 2 + p // 3, :, (p % 3) * 128 : (p % 3) * 128 + 128] = sums

    send_ao.wait()
    send_ga.wait()
    r.nmt[...] = r.ao2[...].T
    for o in range(3):
        block = dot(r.nmt[o * 256 : o * 256 + 256], r.gattn[core]).astype(BF)
        for i in range(3):
            r.out_total[o, i, 0] = block[:, i * 128 : i * 128 + 128]
        r.out_total[o, 3, 0] = jnp.zeros((256, 128), BF)
    outer.start(0)

    def backward(half):
        def chunk_step(step, carried):
            near, far = masks(half, step)
            rot_turned = jnp.concatenate([r.krt[0, step], r.krt[1, 3 - step]], axis=1)
            rot_sum = None
            for g in range(2):
                at = half * 2 + g
                keys = pair_keys(g, step)
                raw = pair_scores(at, keys, step)
                weights = jnp.exp2(raw * (FACTOR * LOG2E) - r.logs[at, 0:1])
                weights = [jnp.where(near, weights[0:256], 0.0), jnp.where(far, weights[256:512], 0.0)]
                dprob = dot_nt(keys, r.ga[at]) - r.delta[at, 0:1]
                dscore = [weights[0] * dprob[0:256], weights[1] * dprob[256:512]]
                dscore = jnp.concatenate([part.astype(BF) for part in dscore], axis=0)
                weights = jnp.concatenate([part.astype(BF) for part in weights], axis=0)
                r.dqa[at] += dot(pair_turned(g, step), dscore)
                r.dqr[at] += dot(rot_turned, dscore)
                grads = FACTOR * dot(dscore, r.qs[at]) + dot(weights, r.ga[at])
                r.dlat[g, step] += grads[0:256]
                r.dlat[2 + g, 3 - step] += grads[256:512]
                rots = dot(dscore, r.qrx[at])
                rot_sum = rots if rot_sum is None else rot_sum + rots
            r.dkr[step] += jnp.where(low64(256), FACTOR * rot_sum[0:256], 0.0)
            r.dkr[3 - step] += jnp.where(low64(256), 0.0, FACTOR * rot_sum[256:512])
            return carried

        lax.fori_loop(0, counts[half], chunk_step, 0)

    def narrow(step, carried):
        j, c = lax.div(step, 4), lax.rem(step, 4)
        r.latt[j, c] = r.dlat[j, c].astype(BF).reshape(4, 64, 256)
        return carried

    def scatter(part, phase):
        made = []
        axis = (1, 2)[(part + phase) % 2]
        for step in (1, 2, 3):
            peer = on_ring(place, axis, step)
            to = lax.rem(place[axis] + step, 4)
            at = step - 1
            if part == 0 and phase == 0:
                pieces = [(r.latt.at[pl.ds(0, 2), to], r.ro1.at[at]), (r.skr.at[to], r.rk1.at[at])]
            elif part == 0:
                pieces = [(r.so1.at[:, to], r.ro2.at[at]), (r.ks1.at[to], r.rk2.at[at])]
            elif phase == 0:
                pieces = [(r.latt.at[pl.ds(2, 2), :, to], r.rt1.at[at])]
            else:
                pieces = [(r.st1.at[:, to], r.rt2.at[at])]
            for k, (src, dst) in enumerate(pieces):
                send = r.lat_send.at[part, k, at]
                made.append(remote(src, dst, send, r.lat_recv.at[part, phase, k, at], peer))
        return made

    backward(0)
    wide.step(0)
    backward(1)
    lax.fori_loop(0, 16, narrow, 0)
    for c in range(4):
        r.skr[c] = r.dkr[c].astype(BF).reshape(4, 64, 128)
    for copy in scatter(1, 0) + scatter(0, 0):
        copy.start()
    wide.step(1)
    outer.step(0, 1)

    for half in range(2):
        for p in range(6):
            rows, lanes = slice(half * 64, half * 64 + 64), slice((p % 3) * 128, (p % 3) * 128 + 128)
            at = half * 2 + p // 3
            piece = (FACTOR * from_latent(r.dqa, r.v_upkey, half, p)).astype(BF)
            r.gq2[p // 3, rows, lanes] = piece
            turned = FACTOR * r.dqr[at, :, lanes].T
            turned = pick(turned + pltpu.roll(turned, 64, 1))
            turned = turned * r.cosine[rows, :] - swap_halves(turned) * r.sine[rows, :]
            r.gqp2[p // 3, rows, lanes] = turned.astype(BF)
    send_gq = paired(6, r.gq2.at[1 - core, pl.ds(0, 128)], r.gq2.at[1 - core, pl.ds(128, 128)])
    send_gqp = paired(7, r.gqp2.at[1 - core, pl.ds(0, 128)], r.gqp2.at[1 - core, pl.ds(128, 128)])
    send_gq.start()
    send_gqp.start()
    for g in range(2):
        for j in range(3):
            lanes = slice(j * 128, j * 128 + 128)
            wide_lanes = slice((g * 3 + j) * 128, (g * 3 + j) * 128 + 128)
            key_sum, value_sum = jnp.zeros((256, 128), F32), jnp.zeros((256, 128), F32)
            for half in range(2):
                rows = slice(half * 64, half * 64 + 64)
                key_sum += FACTOR * dot(r.dqa[half * 2 + g, :, lanes].astype(BF), both(r.q[rows, wide_lanes]))
                value_sum += dot(r.ctx[half * 2 + g, :, lanes], both(r.gmix[rows, wide_lanes]))
            r.dup[g, 0, j] = key_sum.astype(BF)
            r.dup[g, 1, j] = value_sum.astype(BF)
    send_up = paired(8, r.dup.at[1 - core], r.sup)
    send_up.start()
    grad_normed = dot_nt(r.gq2[0, 0:128], r.v_query[:, 0:384]) + dot_nt(r.gq2[1, 0:128], r.v_query[:, 384:768])
    grad_normed += dot_nt(r.gqp2[0, 0:128], r.v_qrope[:, 0:384]) + dot_nt(r.gqp2[1, 0:128], r.v_qrope[:, 384:768])
    r.gnm[0:128] = grad_normed
    send_norm.wait()
    r.normt[...] = r.norm2[...].T
    send_gq.wait()
    send_gqp.wait()
    send_up.wait()
    for o in range(3):
        rows = slice(o * 256, o * 256 + 256)
        for m, right in enumerate((r.gq2, r.gqp2)):
            block = dot(r.normt[rows], right[core]).astype(BF)
            for i in range(3):
                r.early_total[o, i, m] = block[:, i * 128 : i * 128 + 128]
            r.early_total[o, 3, m] = (r.dup[core, m, o].astype(F32) + r.sup[m, o].astype(F32)).astype(BF)
        early.start(0, (o,))

    outer.step(2)
    wide.step(2, 3)

    def fold_near(at, carried):
        for g in range(2):
            near = r.dlat[g, y, rows_at(at * 64, 64), :]
            for k in range(3):
                near = near + r.ro1[k, g, at].astype(F32)
            r.so1[g, at] = near.astype(BF)
        return carried

    def fold_far(at, carried):
        for g in range(2):
            far = r.dlat[2 + g, at, rows_at(z * 64, 64), :]
            for k in range(3):
                far = far + r.rt1[k, g, at].astype(F32)
            r.st1[g, at] = far.astype(BF)
        rot = r.dkr[y, rows_at(at * 64, 64), :]
        for k in range(3):
            rot = rot + r.rk1[k, at].astype(F32)
        r.ks1[at] = rot.astype(BF)
        return carried

    for copy in scatter(0, 0)[0::2]:
        copy.wait()
    lax.fori_loop(0, 4, fold_near, 0)
    for copy in scatter(0, 1)[0::2]:
        copy.start()
    outer.step(3)
    for copy in scatter(1, 0) + scatter(0, 0)[1::2]:
        copy.wait()
    lax.fori_loop(0, 4, fold_far, 0)
    for copy in scatter(1, 1) + scatter(0, 1)[1::2]:
        copy.start()
    wide.step(4)
    early.step(0, 1)
    for copy in scatter(0, 1) + scatter(1, 1):
        copy.wait()
    grad_latents = []
    for g in range(2):
        near = r.so1[g, z].astype(F32)
        far = r.st1[g, y].astype(F32)
        for k in range(3):
            near = near + r.ro2[k, g].astype(F32)
            far = far + r.rt2[k, g].astype(F32)
        piece = jnp.concatenate([near, far], axis=0).astype(BF)
        grad_latents.append(piece)
        r.gl2[g, 0:128] = piece
    send_gl = paired(9, r.gl2.at[1 - core, pl.ds(0, 128)], r.gl2.at[1 - core, pl.ds(128, 128)])
    send_gl.start()
    rot = r.ks1[z].astype(F32)
    for k in range(3):
        rot = rot + r.rk2[k].astype(F32)
    turned = pltpu.roll(rot, 64, 1)
    rot = jnp.concatenate([jnp.where(low64(64), rot, turned), jnp.where(low64(64), turned, rot)], axis=0)
    grad_kpre = (rot * r.cosine[...] - swap_halves(rot) * r.sine[...]).astype(BF)
    grad_normed = r.gnm[0:128] + dot(grad_kpre[:, 0:64], r.v_krope[...])
    for g in range(2):
        grad_normed = grad_normed + dot_nt(grad_latents[g], r.v_latent[:, g * 256 : g * 256 + 256])
    back, gain_attn = norm_back(grad_normed, r.xbuf[...].astype(F32), gain_of(r.norm_attn))
    r.outacc[0:128] = r.gmid[...] + back
    r.grad_tokens[x_hi] = r.outacc[0:64]
    swap_grad = swap(3, r.outacc.at[pl.ds(64, 64)], r.grad_tokens.at[x_hi])
    swap_grad.start()
    gains = r.gains[...]
    for p in range(6):
        gains = gains + jnp.where(gain_row == p, gain_attn[:, p * 128 : p * 128 + 128], 0.0)
    for o in range(3):
        r.late_total[o, 3, 0] = jnp.zeros((256, 128), BF)
    r.late_total[0, 3, 0, 0:16] = gains.astype(BF)
    grad_krope = dot_tn(grad_kpre, r.norm2[0:128]).astype(BF)
    send_gl.wait()
    for o in range(3):
        rows = slice(o * 256, o * 256 + 256)
        block = dot(r.normt[rows], r.gl2[core]).astype(BF)
        for i in range(2):
            r.late_total[o, i, 0] = block[:, i * 128 : i * 128 + 128]
        for part in range(2):
            at = o * 256 + part * 128
            r.late_total[o, 2, 0, part * 64 : part * 64 + 64] = grad_krope[0:64, at : at + 128]
        r.late_total[o, 2, 0, 128:256] = jnp.zeros((128, 128), BF)
        late.start(0, (o,))
    wide.step(5)
    early.step(2)
    late.step(0, 1)
    outer.step(4)
    wide.step(6)
    early.step(3, 4)
    late.step(2)
    early.step(5, 6)
    late.step(3, 4)
    outer.step(5, 6)
    wide.step(7)
    late.step(5, 6)
    outer.step(7)
    early.step(7)
    late.step(7)
    swap_out.wait()
    swap_grad.wait()
    for reduction in (wide, outer, early, late):
        reduction.finish(8)


def layer(small, weights):
    vmem = pl.BlockSpec(memory_space=pltpu.VMEM)
    hbm = pl.BlockSpec(memory_space=pl.ANY)
    smem = pl.BlockSpec(memory_space=pltpu.SMEM)
    return pl.pallas_call(
        layer_kernel,
        out_shape=[jax.ShapeDtypeStruct(shape, kind) for shape, kind in OUTS.values()],
        in_specs=[vmem] * 4 + [smem] * 2 + [hbm] * (1 + len(weights)),
        out_specs=[vmem, vmem] + [hbm] * (len(OUTS) - 2),
        scratch_shapes=list(scratch().values()),
        compiler_params=pltpu.CompilerParams(
            collective_id=1, has_side_effects=True, vmem_limit_bytes=63 * 2**20
        ),
    )(*small, jnp.asarray(rotary_table()), *weights)


def rotary_table():
    halves = ROPE // 2
    powers = -(np.arange(halves, dtype=np.float32) * np.float32(2.0) / np.float32(ROPE))
    freq_list = np.power(np.float32(10000.0), powers, dtype=np.float32)
    phases = (np.arange(2048, dtype=np.float32)[:, None] * freq_list[None, :]).astype(np.float32)
    cosine, sine = np.cos(phases), np.sin(phases)
    return np.concatenate([cosine, cosine, -sine, sine], axis=1).astype(np.float32)


CAST_STEPS = 3


def cast_kernel(
    wide, down, out, early, late, layer_out, grad_tokens,
    o_gate, o_up, o_down, o_query, o_qrope, o_out, o_latent, o_krope, o_upkey, o_upval, o_attn, o_mlp, o_layer, o_tokens,
):
    o_gate[...] = wide[0].astype(F32)
    o_up[...] = wide[1].astype(F32)
    for k in range(8):
        o_down[k * 256 : k * 256 + 256] = down[0, :, k * 256 : k * 256 + 256].astype(F32)
    for source, m, target, width in (
        (early, 0, o_query, 384), (early, 1, o_qrope, 384), (out, 0, o_out, 384), (late, 0, o_latent, 256)
    ):
        target[:, 0:width] = source[m, :, 0:width].astype(F32)
        target[:, width : 2 * width] = source[m, :, 512 : 512 + width].astype(F32)
    for m, target in ((0, o_upkey), (1, o_upval)):
        target[0] = early[m, :, 384:512].astype(F32)
        target[1] = early[m, :, 896:1024].astype(F32)
    step = pl.program_id(0)
    for part in range(2):
        rows = slice(part * 64, part * 64 + 64)
        lanes = rows_at(step * 256 + part * 128, 128, 128)
        o_krope[:, lanes] = late[0, rows, 256:384].astype(F32) + late[0, rows, 768:896].astype(F32)

    @pl.when(step == 0)
    def _():
        gains = late[0, 0:16, 384:512].astype(F32) + late[0, 0:16, 896:1024].astype(F32)
        for p in range(6):
            o_attn[p * 128 : p * 128 + 128] = gains[p]
            o_mlp[p * 128 : p * 128 + 128] = gains[6 + p]
        o_layer[...] = layer_out[...]
        o_tokens[...] = grad_tokens[...]


def cast_sums(layer_out, grad_tokens, wide, out, early, late):
    rows = lambda width: pl.BlockSpec((256, width), lambda i: (i, 0))
    group = lambda n, width: pl.BlockSpec((n, 256, width), lambda i: (0, i, 0))
    ups = pl.BlockSpec((2, 256, 128), lambda i: (0, 0, i))
    whole = lambda shape: pl.BlockSpec(shape, lambda i: (0,) * len(shape))
    shapes = (
        (768, 2048), (768, 2048), (2048, 768), (768, 768), (768, 768), (768, 768), (768, 512), (64, 768),
        (2, 256, 384), (2, 256, 384), (768,), (768,),
    )
    rows_out = (layer_out, grad_tokens)
    return pl.pallas_call(
        cast_kernel,
        grid=(CAST_STEPS,),
        out_shape=[jax.ShapeDtypeStruct(shape, F32) for shape in shapes]
        + [jax.ShapeDtypeStruct(array.shape, array.dtype) for array in rows_out],
        in_specs=[
            group(2, 2048),
            pl.BlockSpec((1, 256, 2048), lambda i: (2, i, 0)),
            group(1, 1024),
            group(2, 1024),
            group(1, 1024),
        ]
        + [whole(array.shape) for array in rows_out],
        out_specs=[rows(2048), rows(2048), pl.BlockSpec((2048, 256), lambda i: (0, i))]
        + [rows(768)] * 3
        + [rows(512), whole((64, 768)), ups, ups, whole((768,)), whole((768,))]
        + [whole(array.shape) for array in rows_out],
        compiler_params=pltpu.CompilerParams(vmem_limit_bytes=63 * 2**20),
    )(wide, wide, out, early, late, layer_out, grad_tokens)


def local(
    tokens, cotangent, group_of_seq, group_weight, norm_attn, w_query, w_qrope, w_latent, w_krope, w_upkey, w_upval,
    w_out, norm_mlp, w_gate, w_up, w_down,
):
    small = (tokens, cotangent, norm_attn, norm_mlp, group_of_seq, group_weight)
    weights = (w_latent, w_krope.T, w_query, w_qrope, w_upkey, w_upval, w_out, w_gate, w_up, w_down)
    gate, up, down, query, qrope, out, latent, krope, upkey, upval, attn, mlp, layer_out, grad_tokens = cast_sums(
        *layer(small, weights)
    )
    return (
        layer_out, grad_tokens, attn, query, qrope, latent, krope.T, upkey, upval, out, mlp, gate, up, down,
    )


def solution(mesh):
    split = P("seq", "blk", None)
    in_specs = (split, split, P("seq")) + (P(),) * 13
    out_specs = (split, split) + (P(),) * 12
    return jax.shard_map(local, mesh=mesh, in_specs=in_specs, out_specs=out_specs, check_vma=False)
```

```python
import jax
import jax.numpy as jnp
import numpy as np
from jax import lax
from jax.sharding import PartitionSpec as P
from jax.experimental import pallas as pl
from jax.experimental.pallas import tpu as pltpu

MESH = pl.DeviceIdType.MESH
BF = jnp.bfloat16
F32 = jnp.float32
EPSILON = 1e-06
ROPE = 64
GROUPS = 4
FACTOR = 128.0**-0.5
LOG2E = 1.4426950408889634
HIDDEN_SCORE = -1e30
ORDERS = ((0, 1, 2), (1, 2, 0), (2, 0, 1))
X_FIRST = ((0, 1, 2), (0, 2, 1), (0, 1, 2))


def coords():
    s = lax.axis_index("seq")
    b = lax.axis_index("blk")
    x = lax.rem(b, 2) * 2 + lax.div(s, 2)
    return x, lax.div(b, 8), lax.rem(lax.div(b, 2), 4), lax.rem(s, 2)


def device(x, y, z, core):
    return (lax.rem(x, 2) * 2 + core, y * 8 + z * 2 + lax.div(x, 2))


def on_ring(place, axis, step):
    spot = list(place)
    spot[axis] = lax.rem(place[axis] + step, 4)
    return device(*spot)


def remote(src, dst, send, recv, peer):
    return pltpu.make_async_remote_copy(
        src_ref=src, dst_ref=dst, send_sem=send, recv_sem=recv, device_id=peer, device_id_type=MESH
    )


def rows_at(start, size, multiple=16):
    return pl.ds(pl.multiple_of(start, multiple), size)


def dot(left, right):
    return jnp.dot(left, right, preferred_element_type=F32)


def dot_nt(left, right):
    return lax.dot_general(left, right, (((1,), (1,)), ((), ())), preferred_element_type=F32)


def dot_tn(left, right):
    return lax.dot_general(left, right, (((0,), (0,)), ((), ())), preferred_element_type=F32)


class Reduction:
    def __init__(self, r, name, place, out, halving, flat=False, orders=ORDERS):
        self.place, self.out, self.halving, self.flat, self.orders = place, out, halving, flat, orders
        for part in ("total", "first", "second", "third", "chunk", "send", "recv", "keep"):
            setattr(self, part, getattr(r, name + "_" + part))
        self.n, self.width = self.total.shape[2], self.total.shape[4]
        counts = stage_counts(halving, flat)
        self.base = [sum(counts[:stage]) for stage in range(9)]

    def spots(self, o):
        a, b, c = self.orders[o]
        return self.place[a], self.place[b], self.place[c]

    def sides(self, o, s):
        me = self.place[self.orders[o][0]]
        odd = lax.rem(me, 2)
        near, far = 1 + 2 * odd, 3 - 2 * odd
        steps = (near, far) if s == 0 else (far, near)
        return steps, lax.rem(me + steps[0], 4), lax.rem(me + steps[1], 4), lax.rem(me + 2, 4)

    def region(self, o, i, row, rows, count=1):
        core, width = self.place[3], self.width
        return self.out.at[:, rows_at(o * 256 + row, rows), rows_at((core * 4 + i) * width, count * width, 128)]

    def moves(self, o, stage):
        i, j, k = self.spots(o)
        if stage == 8:
            x, y, z, core = self.place
            here = self.region(o, 0, 0, 256, 4)
            return [(here, here, device(x, y, z, 1 - core))]
        made = []
        axis = self.orders[o][(0, 0, 1, 2, 2, 1, 0, 0)[stage]]
        if stage in (0, 1, 6, 7) and self.halving:
            for s in range(2):
                steps, front, last, across = self.sides(o, s)
                half = pl.ds(s * 128, 128)
                peer = on_ring(self.place, axis, steps[0 if stage in (0, 7) else 1])
                if stage == 0:
                    made.append((self.total.at[o, front, :, half], self.first.at[o, s, 0], peer))
                    made.append((self.total.at[o, across, :, half], self.first.at[o, s, 1], peer))
                elif stage == 1:
                    made.append((self.total.at[o, last, :, half], self.first.at[o, s, 2], peer))
                else:
                    for spot in (i, last) if stage == 7 else (i,):
                        here = self.region(o, spot, s * 128, 128)
                        made.append((here, here, peer))
            return made
        if stage in (1, 6) or (stage == 4 and self.flat):
            return made
        for step in (1, 2, 3):
            to = lax.rem(self.place[axis] + step, 4)
            peer = on_ring(self.place, axis, step)
            at = step - 1
            if stage == 0:
                made.append((self.total.at[o, to], self.first.at[o, at], peer))
            elif stage == 2:
                made.append((self.total.at[o, i, :, rows_at(to * 64, 64)], self.second.at[o, at], peer))
            elif stage == 3 and self.flat:
                made.append((self.total.at[o, i, :, rows_at(j * 64, 64)], self.third.at[o, k], peer))
            elif stage == 3:
                made.append((self.total.at[o, i, :, rows_at(j * 64 + to * 16, 16)], self.third.at[o, at], peer))
            elif stage == 4:
                made.append((self.chunk.at[o], self.region(o, i, j * 64 + k * 16, 16), peer))
            elif stage == 5:
                here = self.region(o, i, j * 64, 64)
                made.append((self.chunk.at[o] if self.flat else here, here, peer))
            else:
                here = self.region(o, i, 0, 256)
                made.append((here, here, peer))
        return made

    def copies(self, o, stage):
        return [
            remote(src, dst, self.send.at[o, at], self.recv.at[o, self.base[stage] + at], peer)
            for at, (src, dst, peer) in enumerate(self.moves(o, stage))
        ]

    def kept(self, o):
        i, j, k = self.spots(o)
        row, rows = (j * 64, 64) if self.flat else (j * 64 + k * 16, 16)
        return pltpu.make_async_copy(self.chunk.at[o], self.region(o, i, row, rows), self.keep.at[o])

    def start(self, stage, orders=(0, 1, 2)):
        for o in orders:
            for copy in self.copies(o, stage):
                copy.start()
            if stage == 4:
                self.kept(o).start()

    def finish(self, stage, orders=(0, 1, 2)):
        for o in orders:
            for copy in self.copies(o, stage):
                copy.wait()
            if stage == 4:
                self.kept(o).wait()
            if stage < 4:
                self.add(o, stage)

    def step(self, *stages):
        for stage in stages:
            for o in (1, 2, 0):
                self.finish(stage, (o,))
                self.start(stage + 1, (o,))

    def add(self, o, stage):
        i, j, k = self.spots(o)
        if stage == 1 and not self.halving:
            return

        def body(m, carried):
            if stage < 2 and self.halving:
                for s in range(2):
                    _, _, last, _ = self.sides(o, s)
                    half = slice(s * 128, s * 128 + 128)
                    for spot, slot in ((i, 0), (last, 1)) if stage == 0 else ((i, 2),):
                        acc = self.total[o, spot, m, half, :].astype(F32) + self.first[o, s, slot, m].astype(F32)
                        self.total[o, spot, m, half, :] = acc.astype(BF)
            elif stage == 0:
                for part in range(4):
                    rows = slice(part * 64, part * 64 + 64)
                    acc = self.total[o, i, m, rows, :].astype(F32)
                    for slot in range(3):
                        acc = acc + self.first[o, slot, m, rows, :].astype(F32)
                    self.total[o, i, m, rows, :] = acc.astype(BF)
            elif stage == 2:
                rows = rows_at(j * 64, 64)
                acc = self.total[o, i, m, rows, :].astype(F32)
                for slot in range(3):
                    acc = acc + self.second[o, slot, m].astype(F32)
                self.total[o, i, m, rows, :] = acc.astype(BF)
            elif self.flat:
                self.third[o, k, m] = self.total[o, i, m, rows_at(j * 64, 64), :]
                acc = self.third[o, 0, m].astype(F32)
                for slot in range(1, 4):
                    acc = acc + self.third[o, slot, m].astype(F32)
                self.chunk[o, m] = acc.astype(BF)
            else:
                acc = self.total[o, i, m, rows_at(j * 64 + k * 16, 16), :].astype(F32)
                for slot in range(3):
                    acc = acc + self.third[o, slot, m].astype(F32)
                self.chunk[o, m] = acc.astype(BF)
            return carried

        lax.fori_loop(0, self.n, body, 0)


def stage_counts(halving, flat):
    return (4 if halving else 3, 2 if halving else 0, 3, 3, 0 if flat else 3, 3, 2 if halving else 0, 4 if halving else 3, 1)


def reduction_scratch(name, n, width, halving, flat=False):
    return {
        name + "_total": pltpu.VMEM((3, 4, n, 256, width), BF),
        name + "_first": pltpu.VMEM((3, 2, 3, n, 128, width) if halving else (3, 3, n, 256, width), BF),
        name + "_second": pltpu.VMEM((3, 3, n, 64, width), BF),
        name + "_third": pltpu.VMEM((3, 4, n, 64, width) if flat else (3, 3, n, 16, width), BF),
        name + "_chunk": pltpu.VMEM((3, n, 64 if flat else 16, width), BF),
        name + "_send": pltpu.SemaphoreType.DMA((3, 4)),
        name + "_recv": pltpu.SemaphoreType.DMA((3, sum(stage_counts(halving, flat)))),
        name + "_keep": pltpu.SemaphoreType.DMA((3,)),
    }


WEIGHTS = {
    "w_latent": (768, 512),
    "w_krope": (64, 768),
    "w_query": (768, 768),
    "w_qrope": (768, 768),
    "w_upkey": (2, 256, 384),
    "w_upval": (2, 256, 384),
    "w_out": (768, 768),
    "w_gate": (768, 1024),
    "w_up": (768, 1024),
    "w_down": (1024, 768),
}
SMALL = ("tokens", "cotangent", "norm_attn", "norm_mlp", "group_of_seq", "group_weight")
OUTS = {
    "layer_out": ((2, 64, 768), BF),
    "grad_tokens": ((2, 64, 768), F32),
    "g_wide": ((3, 768, 2048), BF),
    "g_out": ((1, 768, 1024), BF),
    "g_early": ((2, 768, 1024), BF),
    "g_late": ((1, 768, 1024), BF),
}


def scratch():
    vmem, dma = pltpu.VMEM, pltpu.SemaphoreType.DMA
    made = {"v" + name[1:]: vmem(shape, BF) for name, shape in WEIGHTS.items()}
    made.update(
        load_sem=dma((len(WEIGHTS),)),
        table_sem=dma((2,)),
        turns=vmem((128, 128), F32),
        cosine=vmem((128, 128), F32),
        sine=vmem((128, 128), F32),
        swap_sem=dma((4, 2)),
        pair_sem=dma((11, 2)),
        lat_send=dma((2, 2, 3)),
        ag_recv=dma((2, 2, 3)),
        lat_recv=dma((2, 2, 2, 3)),
        fw_sem=dma((2, 7, 2)),
        xbuf=vmem((128, 768), BF),
        cbuf=vmem((128, 768), BF),
        norm2=vmem((256, 768), BF),
        normt=vmem((768, 256), BF),
        krd=vmem((128, 128), F32),
        q=vmem((128, 768), BF),
        qr=vmem((128, 768), BF),
        lat=vmem((4, 4, 4, 64, 256), BF),
        kr=vmem((4, 4, 64, 128), BF),
        latt=vmem((4, 4, 4, 64, 256), BF),
        krt=vmem((2, 4, 128, 256), BF),
        rel=vmem((2, 256, 384), jnp.int32),
        qs=vmem((4, 384, 256), BF),
        ga=vmem((4, 384, 256), BF),
        qrx=vmem((4, 384, 128), BF),
        krm=vmem((2, 4, 256, 128), BF),
        gh=vmem((256, 1024), F32),
        acc=vmem((4, 256, 384), F32),
        ctx=vmem((4, 256, 384), BF),
        dqa=vmem((4, 256, 384), F32),
        logs=vmem((4, 8, 384), F32),
        delta=vmem((4, 8, 384), F32),
        aof=vmem((128, 768), F32),
        ao2=vmem((256, 768), BF),
        middle=vmem((128, 768), F32),
        nm2=vmem((256, 768), BF),
        nmt=vmem((768, 256), BF),
        gb2=vmem((256, 768), BF),
        acts=vmem((3, 256, 1024), BF),
        hidt=vmem((1024, 256), BF),
        outacc=vmem((256, 768), F32),
        gnm=vmem((256, 768), F32),
        outx=vmem((128, 768), F32),
        gnmx=vmem((128, 768), F32),
        outbf=vmem((128, 768), BF),
        gattn=vmem((2, 256, 384), BF),
        gmix=vmem((128, 768), BF),
        dqr=vmem((4, 128, 384), F32),
        dlat=vmem((4, 4, 256, 256), F32),
        dkr=vmem((4, 256, 128), F32),
        skr=vmem((4, 4, 64, 128), BF),
        ro1=vmem((3, 2, 4, 64, 256), BF),
        rk1=vmem((3, 4, 64, 128), BF),
        rt1=vmem((3, 2, 4, 64, 256), BF),
        so1=vmem((2, 4, 64, 256), BF),
        ks1=vmem((4, 64, 128), BF),
        st1=vmem((2, 4, 64, 256), BF),
        ro2=vmem((3, 2, 64, 256), BF),
        rk2=vmem((3, 64, 128), BF),
        rt2=vmem((3, 2, 64, 256), BF),
        gq2=vmem((2, 256, 384), BF),
        gqp2=vmem((2, 256, 384), BF),
        gl2=vmem((2, 256, 256), BF),
        dup=vmem((2, 2, 3, 256, 128), BF),
        sup=vmem((2, 3, 256, 128), BF),
        gmid=vmem((128, 768), F32),
        gains=vmem((16, 128), F32),
    )
    made.update(reduction_scratch("wide", 3, 256, True))
    made.update(reduction_scratch("out", 1, 128, False))
    made.update(reduction_scratch("early", 2, 128, False, True))
    made.update(reduction_scratch("late", 1, 128, False, True))
    return made


class Refs:
    pass


def swap_halves(values):
    lanes = values.shape[-1]
    low = lax.rem(lax.broadcasted_iota(jnp.int32, values.shape, 1), 64) < 32
    return jnp.where(low, pltpu.roll(values, lanes - 32, 1), pltpu.roll(values, 32, 1))


def layer_kernel(*args):
    r = Refs()
    shapes = scratch()
    names = list(SMALL) + ["table"] + list(WEIGHTS) + list(OUTS) + list(shapes)
    for name, ref in zip(names, args, strict=True):
        setattr(r, name, ref)
    place = coords()
    x, y, z, core = place
    x_hi = lax.div(x, 2)
    blk = y * 8 + z * 2 + x_hi
    slot = y * 4 + z
    sibling = device(x, y, z, 1 - core)
    partner = device(lax.rem(x + 2, 4), 3 - y, 3 - z, core)
    peers = [on_ring(place, axis, step) for axis in range(3) for step in (1, 2, 3)] + [sibling, partner]
    low64 = lambda rows: lax.broadcasted_iota(jnp.int32, (rows, 128), 1) < 64
    diagonal = (lax.broadcasted_iota(jnp.int32, (128, 128), 0) < 64) == low64(128)

    def gain_of(ref):
        return ref[...].reshape(1, 768)

    def both(value):
        return jnp.where(diagonal, jnp.concatenate([value, value], axis=0), jnp.zeros((), value.dtype))

    def pick(value):
        return jnp.where(low64(64), value[0:64], value[64:128])

    barrier = pltpu.get_barrier_semaphore()
    for peer in peers:
        pl.semaphore_signal(barrier, inc=1, device_id=peer, device_id_type=MESH)
    loads = {}
    for at, name in enumerate(WEIGHTS):
        source = getattr(r, name)
        if name in ("w_gate", "w_up"):
            source = source.at[:, rows_at(core * 1024, 1024, 128)]
        elif name == "w_down":
            source = source.at[rows_at(core * 1024, 1024), :]
        loads[name] = pltpu.make_async_copy(source, getattr(r, "v" + name[1:]), r.load_sem.at[at])
    tables = [
        pltpu.make_async_copy(
            r.table.at[rows_at(where * 64, 64)], r.turns.at[pl.ds(half * 64, 64)], r.table_sem.at[half]
        )
        for half, where in enumerate((blk, 31 - blk))
    ]
    loads["w_latent"].start()
    loads["w_krope"].start()
    for table in tables:
        table.start()
    pl.semaphore_wait(barrier, len(peers))

    def swap(at, src, dst):
        return remote(src, dst, r.swap_sem.at[at, 0], r.swap_sem.at[at, 1], partner)

    def paired(at, src, dst):
        return remote(src, dst, r.pair_sem.at[at, 0], r.pair_sem.at[at, 1], sibling)

    swap_x = swap(0, r.tokens.at[1 - x_hi], r.xbuf.at[pl.ds(64, 64)])
    swap_c = swap(1, r.cotangent.at[1 - x_hi], r.cbuf.at[pl.ds(64, 64)])
    swap_x.start()
    for name in ("w_query", "w_qrope", "w_upkey"):
        loads[name].start()
    r.xbuf[0:64] = r.tokens[x_hi]
    r.cbuf[0:64] = r.cotangent[x_hi]
    key_row = lax.broadcasted_iota(jnp.int32, (256, 384), 0)
    query_lane = lax.rem(lax.broadcasted_iota(jnp.int32, (256, 384), 1), 64)
    within = lax.rem(key_row, 64) - query_lane
    r.rel[0] = 128 * lax.div(key_row, 64) + within
    r.rel[1] = within - 128 * lax.div(key_row, 64)
    for table in tables:
        table.wait()
    turns = r.turns[...]
    other = pltpu.roll(turns, 64, 1)
    r.cosine[...] = jnp.where(low64(128), turns, other)
    r.sine[...] = jnp.where(low64(128), other, turns)
    def unit_of(values):
        inverse = lax.rsqrt(jnp.mean(values * values, axis=-1, keepdims=True) + EPSILON)
        return values * inverse, inverse

    def start_half(half):
        rows = slice(half * 64, half * 64 + 64)
        unit = unit_of(r.xbuf[rows].astype(F32))[0]
        normed = (unit * gain_of(r.norm_attn)).astype(BF)
        r.norm2[rows] = normed
        latents = dot(normed, r.v_latent[...]).astype(BF)
        for g in range(2):
            r.lat[half * 2 + g, y, z] = latents[:, g * 256 : g * 256 + 256]

    def gather(part):
        made = []
        axis = (2, 1)[part]
        for step in (1, 2, 3):
            pieces = [r.lat.at[pl.ds(part * 2, 2), y, z]] + ([r.kr.at[y, z]] if part == 0 else [])
            for at, piece in enumerate(pieces):
                send, recv = r.lat_send.at[part, at, step - 1], r.ag_recv.at[part, at, step - 1]
                made.append(remote(piece, piece, send, recv, on_ring(place, axis, step)))
        return made

    loads["w_latent"].wait()
    start_half(0)
    for copy in gather(0)[0::2]:
        copy.start()
    swap_x.wait()
    start_half(1)
    for copy in gather(1):
        copy.start()
    loads["w_krope"].wait()
    key_pre = dot_nt(r.norm2[0:128], r.v_krope[...])
    r.krd[:, 0:64] = key_pre
    r.krd[:, 64:128] = key_pre
    key_pre = r.krd[...]
    key_rot = (key_pre * r.cosine[...] + swap_halves(key_pre) * r.sine[...]).astype(BF)
    r.kr[y, z] = pick(key_rot)
    for copy in gather(0)[1::2]:
        copy.start()
    swap_c.start()
    send_norm = paired(0, r.norm2.at[pl.ds(0, 128)], r.norm2.at[pl.ds(128, 128)])
    send_norm.start()
    normed = r.norm2[0:128]
    for name in ("w_upval", "w_out", "w_gate", "w_up", "w_down"):
        loads[name].start()

    loads["w_query"].wait()
    r.q[...] = dot(normed, r.v_query[...]).astype(BF)
    loads["w_qrope"].wait()
    query_pre = dot(normed, r.v_qrope[...])
    for p in range(6):
        lanes = slice(p * 128, p * 128 + 128)
        piece = query_pre[:, lanes]
        r.qr[:, lanes] = (piece * r.cosine[...] + swap_halves(piece) * r.sine[...]).astype(BF)
    def to_latent(source, weights, target):
        for half in range(2):
            for g in range(2):
                for j in range(3):
                    p = g * 3 + j
                    block = both(source[half * 64 : half * 64 + 64, p * 128 : p * 128 + 128])
                    rows = dot_nt(block, weights[g, :, j * 128 : j * 128 + 128])
                    target[half * 2 + g, j * 128 : j * 128 + 128] = rows.astype(BF)

    def spread(part, stage):
        axis = (1, 2)[part]
        me = place[axis]
        right, left = on_ring(place, axis, 1), on_ring(place, axis, 3)
        before, after = lax.rem(me + 3, 4), lax.rem(me + 1, 4)

        def plane(which, where):
            return r.lat.at[which, where] if part == 0 else r.lat.at[which, :, where]

        if stage == 0:
            mine = plane(pl.ds(part * 2, 2), me)
            pieces = [(mine, right), (mine, left)]
            if part == 0:
                pieces += [(r.kr.at[me], right), (r.kr.at[me], left)]
        else:
            pieces = [(plane(part * 2, before), right), (plane(part * 2 + 1, after), left)]
            if part == 0:
                pieces += [(r.kr.at[after], left)]
        return [
            remote(piece, piece, r.fw_sem.at[part, stage * 4 + at, 0], r.fw_sem.at[part, stage * 4 + at, 1], peer)
            for at, (piece, peer) in enumerate(pieces)
        ]

    for part in (1, 0):
        for copy in gather(part):
            copy.wait()
        for copy in spread(part, 0):
            copy.start()
    loads["w_upkey"].wait()
    to_latent(r.q, r.v_upkey, r.qs)
    for half in range(2):
        for p in range(6):
            pair = r.qr[half * 64 : half * 64 + 64, p * 128 : p * 128 + 128].astype(F32)
            turned = pltpu.roll(pair, 64, 1)
            for odd in range(2):
                front, back = (turned, pair) if odd else (pair, turned)
                at = (p % 3) * 128 + odd * 64
                r.qrx[half * 2 + p // 3, at : at + 64] = jnp.where(low64(64), front, back).astype(BF)

    swap_c.wait()
    group = jnp.where(x_hi == 0, r.group_of_seq[0], r.group_of_seq[1])
    weight = r.group_weight[0]
    for g in range(1, GROUPS):
        weight = jnp.where(group == g, r.group_weight[g], weight)
    r.gb2[0:128] = (r.cbuf[...].astype(F32) * weight).astype(BF)
    send_gb = paired(3, r.gb2.at[pl.ds(0, 128)], r.gb2.at[pl.ds(128, 128)])
    send_gb.start()

    for ref in (r.acc, r.dqa, r.dqr, r.dlat, r.dkr):
        ref[...] = jnp.zeros_like(ref)
    loads["w_down"].wait()
    send_gb.wait()
    for part in range(4):
        cols = slice(part * 256, part * 256 + 256)
        r.gh[:, cols] = dot_nt(r.gb2[...], r.v_down[cols, :])

    for part in (1, 0):
        for copy in spread(part, 0):
            copy.wait()
        for copy in spread(part, 1):
            copy.start()

    top = lax.broadcasted_iota(jnp.int32, (128, 256), 0) < 64

    def turn(j, c):
        r.latt[j, c] = r.lat[j, c].reshape(256, 256).T.reshape(4, 64, 256)

    def turn_rot(c):
        rot = r.kr[c].reshape(256, 128).astype(F32)
        r.krm[0, c] = jnp.where(low64(256), rot, 0.0).astype(BF)
        r.krm[1, c] = jnp.where(low64(256), 0.0, rot).astype(BF)
        turned = rot.T
        r.krt[0, c] = jnp.where(top, turned, 0.0).astype(BF)
        r.krt[1, c] = jnp.where(top, 0.0, turned).astype(BF)

    for step in (0, 1, 3):
        plane = lax.rem(y + step, 4)
        turn(0, plane)
        turn(1, plane)
        turn_rot(plane)

    query_blk = (blk, 31 - blk)

    counts = (y + 1, 4 - y)

    def masks(half, step):
        first = query_blk[half] * 64
        near = r.rel[0] <= first - 512 * step - 64 * x_hi
        far = r.rel[1] <= first - 1984 + 512 * (3 - step) + 64 * x_hi
        return near, far

    def pair_keys(g, step):
        keys = [r.lat[far * 2 + g, chunk].reshape(256, 256) for far, chunk in ((0, step), (1, 3 - step))]
        return jnp.concatenate(keys, axis=0)

    def pair_scores(at, keys, step):
        rot = jnp.concatenate([r.krm[0, step], r.krm[1, 3 - step]], axis=0)
        return dot_nt(keys, r.qs[at]) + dot_nt(rot, r.qrx[at])

    def pair_turned(g, step):
        turned = [r.latt[far * 2 + g, chunk].reshape(256, 256) for far, chunk in ((0, step), (1, 3 - step))]
        return jnp.concatenate(turned, axis=1)

    for copy in spread(1, 1) + spread(0, 1):
        copy.wait()
    across = lax.rem(y + 2, 4)
    turn(0, across)
    turn(1, across)
    turn_rot(across)
    for c in range(4):
        turn(2, c)
        turn(3, c)

    def forward(half):
        def chunk_step(step, state):
            near, far = masks(half, step)
            result = []
            for g in range(2):
                at = half * 2 + g
                high, total = state[g]
                raw = pair_scores(at, pair_keys(g, step), step)
                raws = [jnp.where(near, raw[0:256], HIDDEN_SCORE), jnp.where(far, raw[256:512], HIDDEN_SCORE)]
                new_high = jnp.maximum(high, jnp.max(jnp.maximum(*raws), axis=0, keepdims=True))
                shrink = jnp.exp2((high - new_high) * (FACTOR * LOG2E))
                weights = [jnp.exp2((raw - new_high) * (FACTOR * LOG2E)) for raw in raws]
                total = total * shrink + jnp.sum(weights[0] + weights[1], axis=0, keepdims=True)
                weights = jnp.concatenate([weight.astype(BF) for weight in weights], axis=0)
                mixed = r.acc[at] * shrink + dot(pair_turned(g, step), weights)
                r.acc[at] = mixed
                result.append((new_high, total))
            return tuple(result)

        empty = (jnp.full((1, 384), HIDDEN_SCORE, F32), jnp.zeros((1, 384), F32))
        state = lax.fori_loop(0, counts[half], chunk_step, (empty, empty))
        for g in range(2):
            high, total = state[g]
            at = half * 2 + g
            r.ctx[at] = (r.acc[at] * (1.0 / total)).astype(BF)
            r.logs[at, 0:1] = high * (FACTOR * LOG2E) + jnp.log2(total)

    forward(0)
    forward(1)
    loads["w_upval"].wait()

    def from_latent(source, weights, half, p):
        g, j = p // 3, p % 3
        lanes = slice(j * 128, j * 128 + 128)
        return pick(dot_tn(source[half * 2 + g, :, lanes].astype(BF), weights[g, :, lanes]))

    for half in range(2):
        for p in range(6):
            r.aof[half * 64 : half * 64 + 64, p * 128 : p * 128 + 128] = from_latent(r.ctx, r.v_upval, half, p)
    r.ao2[0:128] = r.aof[...].astype(BF)
    send_ao = paired(1, r.ao2.at[pl.ds(0, 128)], r.ao2.at[pl.ds(128, 128)])
    send_ao.start()

    loads["w_out"].wait()
    middle = r.xbuf[...].astype(F32) + dot(r.ao2[0:128], r.v_out[...])
    r.middle[...] = middle
    unit_mlp = unit_of(middle)[0]
    r.nm2[0:128] = (unit_mlp * gain_of(r.norm_mlp)).astype(BF)
    send_nm = paired(2, r.nm2.at[pl.ds(0, 128)], r.nm2.at[pl.ds(128, 128)])
    send_nm.start()
    loads["w_gate"].wait()
    loads["w_up"].wait()
    r.nmt[:, 0:128] = r.nm2[0:128].T
    send_nm.wait()

    for part in range(2):
        at = slice(part * 512, part * 512 + 512)
        act = r.nm2[...]
        gate = dot(act, r.v_gate[:, at])
        up = dot(act, r.v_up[:, at])
        sig = jax.nn.sigmoid(gate)
        silu = gate * sig
        hidden = (silu * up).astype(BF)
        grad_hidden = r.gh[:, at]
        grad_gate = (grad_hidden * up * sig * (1.0 + gate * (1.0 - sig))).astype(BF)
        grad_up = (grad_hidden * silu).astype(BF)
        r.acts[0, :, at] = hidden
        r.acts[1, :, at] = grad_gate
        r.acts[2, :, at] = grad_up

    wide = Reduction(r, "wide", place, r.g_wide, True)
    outer = Reduction(r, "out", place, r.g_out, False)
    early = Reduction(r, "early", place, r.g_early, False, True)
    late = Reduction(r, "late", place, r.g_late, False, True)
    r.nmt[:, 128:256] = r.nm2[128:256].T
    r.hidt[...] = r.acts[0].T
    for o in range(3):
        left = r.nmt[o * 256 : o * 256 + 256]
        for i in range(4):
            cols = slice(i * 256, i * 256 + 256)
            r.wide_total[o, i, 0] = dot(left, r.acts[1, :, cols]).astype(BF)
            r.wide_total[o, i, 1] = dot(left, r.acts[2, :, cols]).astype(BF)
            r.wide_total[o, i, 2] = dot(r.hidt[cols, :], r.gb2[:, o * 256 : o * 256 + 256]).astype(BF)
        wide.start(0, (o,))

    r.gnm[...] = dot_nt(r.acts[1], r.v_gate[...]) + dot_nt(r.acts[2], r.v_up[...])
    send_gnm = paired(4, r.gnm.at[pl.ds(128, 128)], r.gnmx)
    send_gnm.start()
    r.outacc[...] = dot(r.acts[0], r.v_down[...])
    send_out = paired(10, r.outacc.at[pl.ds(128, 128)], r.outx)
    send_out.start()

    def norm_back(grads, values, gain):
        unit_rows, inverse = unit_of(values)
        scaled = grads * gain
        gain_grad = jnp.sum(grads * unit_rows, axis=0, keepdims=True)
        mean = jnp.mean(scaled * unit_rows, axis=-1, keepdims=True)
        return inverse * (scaled - unit_rows * mean), gain_grad

    send_gnm.wait()
    back, gain_mlp = norm_back(r.gnm[0:128] + r.gnmx[...], r.middle[...], gain_of(r.norm_mlp))
    r.gmid[...] = r.cbuf[...].astype(F32) * weight + back
    gain_row = lax.broadcasted_iota(jnp.int32, (16, 128), 0)
    gains = jnp.zeros((16, 128), F32)
    for p in range(6):
        gains = gains + jnp.where(gain_row == 6 + p, gain_mlp[:, p * 128 : p * 128 + 128], 0.0)
    r.gains[...] = gains
    grad_attn = r.gmid[...].astype(BF)
    for half in range(2):
        r.gattn[half, 0:128] = grad_attn[:, half * 384 : half * 384 + 384]
    send_ga = paired(5, r.gattn.at[1 - core, pl.ds(0, 128)], r.gattn.at[1 - core, pl.ds(128, 128)])
    send_ga.start()
    mixed = dot_nt(grad_attn, r.v_out[...])
    r.gmix[...] = mixed.astype(BF)
    to_latent(r.gmix, r.v_upval, r.ga)
    send_out.wait()
    r.outbf[...] = (r.middle[...] + r.outacc[0:128] + r.outx[...]).astype(BF)
    r.layer_out[x_hi] = r.outbf[0:64]
    swap_out = swap(2, r.outbf.at[pl.ds(64, 64)], r.layer_out.at[x_hi])
    swap_out.start()
    ones = jnp.ones((8, 128), F32)
    for half in range(2):
        for p in range(6):
            here = (slice(half * 64, half * 64 + 64), slice(p * 128, p * 128 + 128))
            block = both(r.gmix[here].astype(F32) * r.aof[here])
            sums = lax.dot_general(
                ones, block, (((1,), (1,)), ((), ())), precision=lax.Precision.HIGHEST, preferred_element_type=F32
            )
            r.delta[half * 2 + p // 3, :, (p % 3) * 128 : (p % 3) * 128 + 128] = sums

    send_ao.wait()
    send_ga.wait()
    r.nmt[...] = r.ao2[...].T
    for o in range(3):
        block = dot(r.nmt[o * 256 : o * 256 + 256], r.gattn[core]).astype(BF)
        for i in range(3):
            r.out_total[o, i, 0] = block[:, i * 128 : i * 128 + 128]
        r.out_total[o, 3, 0] = jnp.zeros((256, 128), BF)
    outer.start(0)

    def backward(half):
        def chunk_step(step, carried):
            near, far = masks(half, step)
            rot_turned = jnp.concatenate([r.krt[0, step], r.krt[1, 3 - step]], axis=1)
            rot_sum = None
            for g in range(2):
                at = half * 2 + g
                keys = pair_keys(g, step)
                raw = pair_scores(at, keys, step)
                weights = jnp.exp2(raw * (FACTOR * LOG2E) - r.logs[at, 0:1])
                weights = [jnp.where(near, weights[0:256], 0.0), jnp.where(far, weights[256:512], 0.0)]
                dprob = dot_nt(keys, r.ga[at]) - r.delta[at, 0:1]
                dscore = [weights[0] * dprob[0:256], weights[1] * dprob[256:512]]
                dscore = jnp.concatenate([part.astype(BF) for part in dscore], axis=0)
                weights = jnp.concatenate([part.astype(BF) for part in weights], axis=0)
                r.dqa[at] += dot(pair_turned(g, step), dscore)
                r.dqr[at] += dot(rot_turned, dscore)
                grads = FACTOR * dot(dscore, r.qs[at]) + dot(weights, r.ga[at])
                r.dlat[g, step] += grads[0:256]
                r.dlat[2 + g, 3 - step] += grads[256:512]
                rots = dot(dscore, r.qrx[at])
                rot_sum = rots if rot_sum is None else rot_sum + rots
            r.dkr[step] += jnp.where(low64(256), FACTOR * rot_sum[0:256], 0.0)
            r.dkr[3 - step] += jnp.where(low64(256), 0.0, FACTOR * rot_sum[256:512])
            return carried

        lax.fori_loop(0, counts[half], chunk_step, 0)

    def narrow(step, carried):
        j, c = lax.div(step, 4), lax.rem(step, 4)
        r.latt[j, c] = r.dlat[j, c].astype(BF).reshape(4, 64, 256)
        return carried

    def scatter(part, phase):
        made = []
        axis = (1, 2)[(part + phase) % 2]
        for step in (1, 2, 3):
            peer = on_ring(place, axis, step)
            to = lax.rem(place[axis] + step, 4)
            at = step - 1
            if part == 0 and phase == 0:
                pieces = [(r.latt.at[pl.ds(0, 2), to], r.ro1.at[at]), (r.skr.at[to], r.rk1.at[at])]
            elif part == 0:
                pieces = [(r.so1.at[:, to], r.ro2.at[at]), (r.ks1.at[to], r.rk2.at[at])]
            elif phase == 0:
                pieces = [(r.latt.at[pl.ds(2, 2), :, to], r.rt1.at[at])]
            else:
                pieces = [(r.st1.at[:, to], r.rt2.at[at])]
            for k, (src, dst) in enumerate(pieces):
                send = r.lat_send.at[part, k, at]
                made.append(remote(src, dst, send, r.lat_recv.at[part, phase, k, at], peer))
        return made

    backward(0)
    wide.step(0)
    backward(1)
    lax.fori_loop(0, 16, narrow, 0)
    for c in range(4):
        r.skr[c] = r.dkr[c].astype(BF).reshape(4, 64, 128)
    for copy in scatter(1, 0) + scatter(0, 0):
        copy.start()
    wide.step(1)
    outer.step(0, 1)

    for half in range(2):
        for p in range(6):
            rows, lanes = slice(half * 64, half * 64 + 64), slice((p % 3) * 128, (p % 3) * 128 + 128)
            at = half * 2 + p // 3
            piece = (FACTOR * from_latent(r.dqa, r.v_upkey, half, p)).astype(BF)
            r.gq2[p // 3, rows, lanes] = piece
            turned = FACTOR * r.dqr[at, :, lanes].T
            turned = pick(turned + pltpu.roll(turned, 64, 1))
            turned = turned * r.cosine[rows, :] - swap_halves(turned) * r.sine[rows, :]
            r.gqp2[p // 3, rows, lanes] = turned.astype(BF)
    send_gq = paired(6, r.gq2.at[1 - core, pl.ds(0, 128)], r.gq2.at[1 - core, pl.ds(128, 128)])
    send_gqp = paired(7, r.gqp2.at[1 - core, pl.ds(0, 128)], r.gqp2.at[1 - core, pl.ds(128, 128)])
    send_gq.start()
    send_gqp.start()
    for g in range(2):
        for j in range(3):
            lanes = slice(j * 128, j * 128 + 128)
            wide_lanes = slice((g * 3 + j) * 128, (g * 3 + j) * 128 + 128)
            key_sum, value_sum = jnp.zeros((256, 128), F32), jnp.zeros((256, 128), F32)
            for half in range(2):
                rows = slice(half * 64, half * 64 + 64)
                key_sum += FACTOR * dot(r.dqa[half * 2 + g, :, lanes].astype(BF), both(r.q[rows, wide_lanes]))
                value_sum += dot(r.ctx[half * 2 + g, :, lanes], both(r.gmix[rows, wide_lanes]))
            r.dup[g, 0, j] = key_sum.astype(BF)
            r.dup[g, 1, j] = value_sum.astype(BF)
    send_up = paired(8, r.dup.at[1 - core], r.sup)
    send_up.start()
    grad_normed = dot_nt(r.gq2[0, 0:128], r.v_query[:, 0:384]) + dot_nt(r.gq2[1, 0:128], r.v_query[:, 384:768])
    grad_normed += dot_nt(r.gqp2[0, 0:128], r.v_qrope[:, 0:384]) + dot_nt(r.gqp2[1, 0:128], r.v_qrope[:, 384:768])
    r.gnm[0:128] = grad_normed
    send_norm.wait()
    r.normt[...] = r.norm2[...].T
    send_gq.wait()
    send_gqp.wait()
    send_up.wait()
    for o in range(3):
        rows = slice(o * 256, o * 256 + 256)
        for m, right in enumerate((r.gq2, r.gqp2)):
            block = dot(r.normt[rows], right[core]).astype(BF)
            for i in range(3):
                r.early_total[o, i, m] = block[:, i * 128 : i * 128 + 128]
            r.early_total[o, 3, m] = (r.dup[core, m, o].astype(F32) + r.sup[m, o].astype(F32)).astype(BF)
        early.start(0, (o,))

    outer.step(2)
    wide.step(2, 3)

    def fold_near(at, carried):
        for g in range(2):
            near = r.dlat[g, y, rows_at(at * 64, 64), :]
            for k in range(3):
                near = near + r.ro1[k, g, at].astype(F32)
            r.so1[g, at] = near.astype(BF)
        return carried

    def fold_far(at, carried):
        for g in range(2):
            far = r.dlat[2 + g, at, rows_at(z * 64, 64), :]
            for k in range(3):
                far = far + r.rt1[k, g, at].astype(F32)
            r.st1[g, at] = far.astype(BF)
        rot = r.dkr[y, rows_at(at * 64, 64), :]
        for k in range(3):
            rot = rot + r.rk1[k, at].astype(F32)
        r.ks1[at] = rot.astype(BF)
        return carried

    for copy in scatter(0, 0)[0::2]:
        copy.wait()
    lax.fori_loop(0, 4, fold_near, 0)
    for copy in scatter(0, 1)[0::2]:
        copy.start()
    outer.step(3)
    for copy in scatter(1, 0) + scatter(0, 0)[1::2]:
        copy.wait()
    lax.fori_loop(0, 4, fold_far, 0)
    for copy in scatter(1, 1) + scatter(0, 1)[1::2]:
        copy.start()
    wide.step(4)
    early.step(0, 1)
    for copy in scatter(0, 1) + scatter(1, 1):
        copy.wait()
    grad_latents = []
    for g in range(2):
        near = r.so1[g, z].astype(F32)
        far = r.st1[g, y].astype(F32)
        for k in range(3):
            near = near + r.ro2[k, g].astype(F32)
            far = far + r.rt2[k, g].astype(F32)
        piece = jnp.concatenate([near, far], axis=0).astype(BF)
        grad_latents.append(piece)
        r.gl2[g, 0:128] = piece
    send_gl = paired(9, r.gl2.at[1 - core, pl.ds(0, 128)], r.gl2.at[1 - core, pl.ds(128, 128)])
    send_gl.start()
    rot = r.ks1[z].astype(F32)
    for k in range(3):
        rot = rot + r.rk2[k].astype(F32)
    turned = pltpu.roll(rot, 64, 1)
    rot = jnp.concatenate([jnp.where(low64(64), rot, turned), jnp.where(low64(64), turned, rot)], axis=0)
    grad_kpre = (rot * r.cosine[...] - swap_halves(rot) * r.sine[...]).astype(BF)
    for o in range(3):
        r.late_total[o, 3, 0] = jnp.zeros((256, 128), BF)
    grad_krope = dot_tn(grad_kpre, r.norm2[0:128]).astype(BF)
    send_gl.wait()
    for o in range(3):
        rows = slice(o * 256, o * 256 + 256)
        block = dot(r.normt[rows], r.gl2[core]).astype(BF)
        for i in range(2):
            r.late_total[o, i, 0] = block[:, i * 128 : i * 128 + 128]
        for part in range(2):
            at = o * 256 + part * 128
            r.late_total[o, 2, 0, part * 64 : part * 64 + 64] = grad_krope[0:64, at : at + 128]
        r.late_total[o, 2, 0, 128:256] = jnp.zeros((128, 128), BF)
        if o > 0:
            late.start(0, (o,))
    grad_normed = r.gnm[0:128] + dot(grad_kpre[:, 0:64], r.v_krope[...])
    for g in range(2):
        grad_normed = grad_normed + dot_nt(grad_latents[g], r.v_latent[:, g * 256 : g * 256 + 256])
    back, gain_attn = norm_back(grad_normed, r.xbuf[...].astype(F32), gain_of(r.norm_attn))
    r.outacc[0:128] = r.gmid[...] + back
    r.grad_tokens[x_hi] = r.outacc[0:64]
    swap_grad = swap(3, r.outacc.at[pl.ds(64, 64)], r.grad_tokens.at[x_hi])
    swap_grad.start()
    gains = r.gains[...]
    for p in range(6):
        gains = gains + jnp.where(gain_row == p, gain_attn[:, p * 128 : p * 128 + 128], 0.0)
    r.late_total[0, 3, 0, 0:16] = gains.astype(BF)
    late.start(0, (0,))
    wide.step(5)
    early.step(2)
    late.step(0, 1)
    outer.step(4)
    wide.step(6)
    early.step(3, 4)
    late.step(2)
    early.step(5, 6)
    late.step(3, 4)
    outer.step(5, 6)
    wide.step(7)
    late.step(5, 6)
    outer.step(7)
    early.step(7)
    late.step(7)
    swap_out.wait()
    swap_grad.wait()
    for reduction in (wide, outer, early, late):
        reduction.finish(8)


def layer(small, weights):
    vmem = pl.BlockSpec(memory_space=pltpu.VMEM)
    hbm = pl.BlockSpec(memory_space=pl.ANY)
    smem = pl.BlockSpec(memory_space=pltpu.SMEM)
    return pl.pallas_call(
        layer_kernel,
        out_shape=[jax.ShapeDtypeStruct(shape, kind) for shape, kind in OUTS.values()],
        in_specs=[vmem] * 4 + [smem] * 2 + [hbm] * (1 + len(weights)),
        out_specs=[vmem, vmem] + [hbm] * (len(OUTS) - 2),
        scratch_shapes=list(scratch().values()),
        compiler_params=pltpu.CompilerParams(
            collective_id=1, has_side_effects=True, vmem_limit_bytes=63 * 2**20
        ),
    )(*small, jnp.asarray(rotary_table()), *weights)


def rotary_table():
    halves = ROPE // 2
    powers = -(np.arange(halves, dtype=np.float32) * np.float32(2.0) / np.float32(ROPE))
    freq_list = np.power(np.float32(10000.0), powers, dtype=np.float32)
    phases = (np.arange(2048, dtype=np.float32)[:, None] * freq_list[None, :]).astype(np.float32)
    cosine, sine = np.cos(phases), np.sin(phases)
    return np.concatenate([cosine, cosine, -sine, sine], axis=1).astype(np.float32)


CAST_STEPS = 3


def cast_kernel(
    wide, down, out, early, late, layer_out, grad_tokens,
    o_gate, o_up, o_down, o_query, o_qrope, o_out, o_latent, o_krope, o_upkey, o_upval, o_attn, o_mlp, o_layer, o_tokens,
):
    o_gate[...] = wide[0].astype(F32)
    o_up[...] = wide[1].astype(F32)
    for k in range(8):
        o_down[k * 256 : k * 256 + 256] = down[0, :, k * 256 : k * 256 + 256].astype(F32)
    for source, m, target, width in (
        (early, 0, o_query, 384), (early, 1, o_qrope, 384), (out, 0, o_out, 384), (late, 0, o_latent, 256)
    ):
        target[:, 0:width] = source[m, :, 0:width].astype(F32)
        target[:, width : 2 * width] = source[m, :, 512 : 512 + width].astype(F32)
    for m, target in ((0, o_upkey), (1, o_upval)):
        target[0] = early[m, :, 384:512].astype(F32)
        target[1] = early[m, :, 896:1024].astype(F32)
    step = pl.program_id(0)
    for part in range(2):
        rows = slice(part * 64, part * 64 + 64)
        lanes = rows_at(step * 256 + part * 128, 128, 128)
        o_krope[:, lanes] = late[0, rows, 256:384].astype(F32) + late[0, rows, 768:896].astype(F32)

    @pl.when(step == 0)
    def _():
        gains = late[0, 0:16, 384:512].astype(F32) + late[0, 0:16, 896:1024].astype(F32)
        for p in range(6):
            o_attn[p * 128 : p * 128 + 128] = gains[p]
            o_mlp[p * 128 : p * 128 + 128] = gains[6 + p]
        o_layer[...] = layer_out[...]
        o_tokens[...] = grad_tokens[...]


def cast_sums(layer_out, grad_tokens, wide, out, early, late):
    rows = lambda width: pl.BlockSpec((256, width), lambda i: (i, 0))
    group = lambda n, width: pl.BlockSpec((n, 256, width), lambda i: (0, i, 0))
    ups = pl.BlockSpec((2, 256, 128), lambda i: (0, 0, i))
    whole = lambda shape: pl.BlockSpec(shape, lambda i: (0,) * len(shape))
    shapes = (
        (768, 2048), (768, 2048), (2048, 768), (768, 768), (768, 768), (768, 768), (768, 512), (64, 768),
        (2, 256, 384), (2, 256, 384), (768,), (768,),
    )
    rows_out = (layer_out, grad_tokens)
    return pl.pallas_call(
        cast_kernel,
        grid=(CAST_STEPS,),
        out_shape=[jax.ShapeDtypeStruct(shape, F32) for shape in shapes]
        + [jax.ShapeDtypeStruct(array.shape, array.dtype) for array in rows_out],
        in_specs=[
            group(2, 2048),
            pl.BlockSpec((1, 256, 2048), lambda i: (2, i, 0)),
            group(1, 1024),
            group(2, 1024),
            group(1, 1024),
        ]
        + [whole(array.shape) for array in rows_out],
        out_specs=[rows(2048), rows(2048), pl.BlockSpec((2048, 256), lambda i: (0, i))]
        + [rows(768)] * 3
        + [rows(512), whole((64, 768)), ups, ups, whole((768,)), whole((768,))]
        + [whole(array.shape) for array in rows_out],
        compiler_params=pltpu.CompilerParams(vmem_limit_bytes=63 * 2**20),
    )(wide, wide, out, early, late, layer_out, grad_tokens)


def local(
    tokens, cotangent, group_of_seq, group_weight, norm_attn, w_query, w_qrope, w_latent, w_krope, w_upkey, w_upval,
    w_out, norm_mlp, w_gate, w_up, w_down,
):
    small = (tokens, cotangent, norm_attn, norm_mlp, group_of_seq, group_weight)
    weights = (w_latent, w_krope.T, w_query, w_qrope, w_upkey, w_upval, w_out, w_gate, w_up, w_down)
    gate, up, down, query, qrope, out, latent, krope, upkey, upval, attn, mlp, layer_out, grad_tokens = cast_sums(
        *layer(small, weights)
    )
    return (
        layer_out, grad_tokens, attn, query, qrope, latent, krope.T, upkey, upval, out, mlp, gate, up, down,
    )


def solution(mesh):
    split = P("seq", "blk", None)
    in_specs = (split, split, P("seq")) + (P(),) * 13
    out_specs = (split, split) + (P(),) * 12
    return jax.shard_map(local, mesh=mesh, in_specs=in_specs, out_specs=out_specs, check_vma=False)
```
